32 devices in a mesh: dp: 4 (over x, core), context: 2 (over y), experts: 4 (over z).
Axes of the slice: x: 2, y: 2, z: 4, core: 2. Of those that a mesh axis runs over, the one named last changes fastest.
Arguments:
- activations: bfloat16 [2, 16, 256, 1024], P(None, ('dp', 'experts'), 'context'), may hold values from -6 to 6
- cotangent: bfloat16 [2, 16, 256, 1024], P(None, ('dp', 'experts'), 'context'), may hold values from -6 to 6
- dealing: int32 [2, 16, 256], P(None, ('dp', 'experts')), may hold values from 0 to 255, each once within a row
- lengths: int32 [2, 16], P(None, ('dp', 'experts')), may hold values from 128 to 256, as said below
- routes: int32 [2, 16, 256, 2], P(None, ('dp', 'experts'), 'context'), may hold values from 0 to 3, all different within a row
- buckets: int32 [256], replicated, may hold values from 0 to 31, as said below
- w_query: bfloat16 [1024, 1024], P(('dp', 'context', 'experts')), may hold values from -0.1875 to 0.1875
- w_key: bfloat16 [1024, 1024], P(('dp', 'context', 'experts')), may hold values from -0.1875 to 0.1875
- w_value: bfloat16 [1024, 1024], P(('dp', 'context', 'experts')), may hold values from -0.1875 to 0.1875
- w_out: bfloat16 [1024, 1024], P(('dp', 'context', 'experts')), may hold values from -1.5 to 1.5
- w_router: bfloat16 [1024, 4], P(('dp', 'context', 'experts')), may hold values from -0.125 to 0.125
- norm_first: bfloat16 [1024], P(('dp', 'context', 'experts')), may hold values from 0.099609375 to 1.8984375
- norm_second: bfloat16 [1024], P(('dp', 'context', 'experts')), may hold values from 0.099609375 to 1.8984375
- bias_table: bfloat16 [32, 16], replicated, may hold values from -4 to 4
- w_gate: bfloat16 [4, 1024, 2816], P('experts', ('dp', 'context')), may hold values from -0.1875 to 0.1875
- w_up: bfloat16 [4, 1024, 2816], P('experts', ('dp', 'context')), may hold values from -0.1875 to 0.1875
- w_down: bfloat16 [4, 2816, 1024], P('experts', ('dp', 'context')), may hold values from -0.15625 to 0.15625
Outputs:
- output: bfloat16 [2, 16, 256, 1024], P(None, ('dp', 'experts'), 'context')
- grad_input: bfloat16 [2, 16, 256, 1024], P(None, ('dp', 'experts'), 'context')
- grad_query: float32 [1024, 1024], P(('dp', 'context', 'experts'))
- grad_key: float32 [1024, 1024], P(('dp', 'context', 'experts'))
- grad_value: float32 [1024, 1024], P(('dp', 'context', 'experts'))
- grad_out: float32 [1024, 1024], P(('dp', 'context', 'experts'))
- grad_router: float32 [1024, 4], P(('dp', 'context', 'experts'))
- grad_first: float32 [1024], P(('dp', 'context', 'experts'))
- grad_second: float32 [1024], P(('dp', 'context', 'experts'))
- grad_table: float32 [32, 16], replicated
- grad_gate: float32 [4, 1024, 2816], P('experts', ('dp', 'context'))
- grad_up: float32 [4, 1024, 2816], P('experts', ('dp', 'context'))
- grad_down: float32 [4, 2816, 1024], P('experts', ('dp', 'context'))
The draws below stay inside these ranges and needn't reach their ends.
Inputs may be any that keep to these rules, and one draw needn't show every extreme that they name: `dealing`: each row is a permutation. `lengths`: some sequence has length 256. `routes`: the two experts of a slot differ. `buckets`: non-decreasing in the offset; an offset o below 16 has bucket o; offset 256 - 1 has bucket 32 - 1.
All inputs are finite; a program needn't handle non-finite values.
Results may differ from the reference program's by a relative error of at most 0.015.
Values may be sent and summed in bfloat16 or wider, within the bound.
A program may use at most 512 MiB of HBM per device.

```python
import jax
import jax.numpy as jnp
from jax import lax

D = 1024
HEADS = 16
HEAD_DIM = 64
FF = 2816
BUCKETS = 32
EXPERTS = 4
TOP = 2
TOK_DEV = 128
MB = 2
SEQ = 256
GROUPS = 16
CAP = 80
N_CONTEXT = 2


def draw_lengths(key, part):
    key = jax.random.fold_in(key, 11)
    first_key, second_key = jax.random.split(key)
    drawn_len = jax.random.randint(first_key, (MB, GROUPS), SEQ // 2, SEQ + 1, dtype=jnp.int32)
    chosen_cell = jax.random.randint(second_key, (), 0, MB * GROUPS, dtype=jnp.int32)
    cell_index = jnp.arange(MB * GROUPS, dtype=jnp.int32).reshape(MB, GROUPS)
    return jnp.where(cell_index == chosen_cell, SEQ, drawn_len).astype(jnp.int32)


def draw_buckets(key, part):
    key = jax.random.fold_in(key, 23)
    offsets = jnp.arange(SEQ, dtype=jnp.int32)
    half_count = BUCKETS // 2
    random_bits = jax.random.randint(key, (SEQ,), 0, 1 << 20, dtype=jnp.int32)
    far_step = (random_bits % (4 * (offsets + 1)) < half_count).astype(jnp.int32)
    step_up = jnp.where(offsets == 0, 0, jnp.where(offsets < half_count, 1, far_step))
    bucket_ids = jnp.minimum(jnp.cumsum(step_up), BUCKETS - 1)
    bucket_ids = jnp.where(offsets == SEQ - 1, BUCKETS - 1, bucket_ids)
    return bucket_ids.astype(jnp.int32)


def block_levels(own_key, shape, cuts, least, largest):
    level, own = 1.0, jax.random.fold_in(own_key, 6)
    for position, blocks in cuts:
        steps = jnp.exp(jax.random.uniform(jax.random.fold_in(own, position), (blocks,), jnp.float32, least / len(cuts), largest / len(cuts)))
        level = level * jnp.repeat(steps, shape[position] // blocks).reshape([-1 if axis == position else 1 for axis in range(len(shape))])
    return level


def picks_of(stream_key, rows, count, top, lift):
    ranking = jax.random.permutation(jax.random.fold_in(stream_key, 1), count)
    pull = ranking
    for power in range(3):
        pull = pull * pull // count
    pull = pull * lift // count
    tickets = jax.random.randint(jax.random.fold_in(stream_key, 2), (rows, count), 0, 4096) + pull
    fixed_rows = jax.random.permutation(jax.random.fold_in(stream_key, 3), rows)[jnp.arange(count) % rows]
    tickets = jnp.where(jnp.arange(rows)[:, None] == fixed_rows[None, :], 1 << 14, tickets)
    score = tickets * count + jnp.arange(count)
    return lax.top_k(score.astype(jnp.int32), top)[1].astype(jnp.int32)


def scatter_about(rng, extent, deviation, bound, cuts=(), kind=jnp.bfloat16):
    factor_of = block_levels(rng, extent, cuts, -0.22, 0.18) if cuts else 1.0
    values = jax.random.normal(rng, extent, jnp.float32) * deviation * factor_of
    return jnp.minimum(jnp.maximum(values, -bound), bound).astype(kind)


def setup_inputs(seed: int = 0) -> dict:
    splits = jax.random.split(jax.random.key(seed), 18)
    return {
        "activations": scatter_about(splits[0], (MB, GROUPS, SEQ, D), 1.0, 6.0, ((1, 16), (2, 2))),
        "cotangent": scatter_about(splits[1], (MB, GROUPS, SEQ, D), 1.0, 6.0, ((1, 16), (2, 2))),
        "dealing": jax.vmap(lambda own: jax.random.permutation(own, SEQ))(jax.random.split(splits[2], MB * GROUPS)).reshape((MB, GROUPS, SEQ)).astype(jnp.int32),
        "lengths": draw_lengths(jax.random.fold_in(splits[17], 71), 0),
        "routes": picks_of(splits[4], MB * GROUPS * SEQ, EXPERTS, TOP, 4096).reshape((MB, GROUPS, SEQ, TOP)),
        "buckets": draw_buckets(jax.random.fold_in(splits[17], 71), 0),
        "w_query": scatter_about(splits[6], (D, D), D ** -0.5, 0.1875, ((0, 32),)),
        "w_key": scatter_about(splits[7], (D, D), D ** -0.5, 0.1875, ((0, 32),)),
        "w_value": scatter_about(splits[8], (D, D), D ** -0.5, 0.1875, ((0, 32),)),
        "w_out": scatter_about(splits[9], (D, D), (D // 64) ** -0.5, 1.5, ((0, 32),)),
        "w_router": scatter_about(splits[10], (D, EXPERTS), (0.75 / D ** 0.5), 0.125, ((0, 32),)),
        "norm_first": jnp.clip(1.0 + 0.18 * jax.random.normal(splits[11], (D,), jnp.float32), 0.099609375, 1.8984375).astype(jnp.bfloat16),
        "norm_second": jnp.clip(1.0 + 0.18 * jax.random.normal(splits[12], (D,), jnp.float32), 0.099609375, 1.8984375).astype(jnp.bfloat16),
        "bias_table": scatter_about(splits[13], (BUCKETS, HEADS), 1.0, 4.0),
        "w_gate": scatter_about(splits[14], (EXPERTS, D, FF), D ** -0.5, 0.1875, ((0, 4), (1, 8))),
        "w_up": scatter_about(splits[15], (EXPERTS, D, FF), D ** -0.5, 0.1875, ((0, 4), (1, 8))),
        "w_down": scatter_about(splits[16], (EXPERTS, FF, D), (FF // 2) ** -0.5, 0.15625, ((0, 4), (1, 8))),
    }


epsilon = 1e-06
masked_score = -1e+30
precise = lax.Precision.HIGHEST

@jax.custom_vjp
def low(v):
    return lax.optimization_barrier(v.astype(jnp.bfloat16)).astype(jnp.float32)

@jax.custom_vjp
def low_back(v):
    return v

def low_keep(v):
    return (low(v), None)

def low_pass(kept, grad):
    return (grad,)

def back_keep(v):
    return (v, None)

def back_low(kept, grad):
    return (low(grad),)
low.defvjp(low_keep, low_pass)
low_back.defvjp(back_keep, back_low)

def product(left_side, right_side):
    return jnp.dot(left_side, right_side, precision=precise)

def rms_scale(features, gain_vec):
    inverse = lax.rsqrt(lax.optimization_barrier(jnp.mean(features * features, axis=-1, keepdims=True)) + epsilon)
    return features * inverse * gain_vec

def slot_plan(route_seq, is_live):
    expert_ids = jnp.arange(EXPERTS, dtype=jnp.int32)
    onehot = (route_seq[:, :, None] == expert_ids[None, None, :]).astype(jnp.int32)
    onehot = onehot * is_live.astype(jnp.int32)[:, None, None]
    blocks = onehot.reshape(N_CONTEXT, TOK_DEV * TOP, EXPERTS)
    earlier = jnp.cumsum(blocks, axis=1).astype(jnp.int32) - blocks
    slot_rank = lax.optimization_barrier(jnp.sum(earlier * blocks, axis=2)).astype(jnp.int32).reshape(SEQ, TOP)
    kept_pair = is_live[:, None] & (slot_rank < CAP)
    block_of = (jnp.arange(SEQ, dtype=jnp.int32) // TOK_DEV)[:, None]
    target = block_of * (EXPERTS * CAP) + route_seq * CAP + slot_rank
    target = jnp.where(kept_pair, target, N_CONTEXT * EXPERTS * CAP).astype(jnp.int32)
    return (kept_pair, target)

def block_forward(activation, positions, length, route_seq, buckets, w_query, w_key, w_value, w_out, w_router, norm_first, norm_second, bias_table, w_gate, w_up, w_down):
    is_live = positions < length
    live_rows = is_live.astype(jnp.float32)[:, None]
    rows_in = jnp.take(activation, positions, axis=0)
    normed = low(rms_scale(rows_in, norm_first))
    query_rows = low_back(low(product(normed, w_query))).reshape(SEQ, HEADS, HEAD_DIM)
    key_rows = low_back(low(product(normed, w_key))).reshape(SEQ, HEADS, HEAD_DIM)
    value_rows = low_back(low(product(normed, w_value))).reshape(SEQ, HEADS, HEAD_DIM)
    offset = positions[:, None] - positions[None, :]
    allowed = (offset >= 0) & is_live[None, :]
    bias_rows = jnp.take(bias_table, buckets, axis=0)
    bias_full = jnp.take(bias_rows, jnp.maximum(offset, 0).astype(jnp.int32), axis=0)
    scores = jnp.einsum('shd,thd->hst', query_rows, key_rows, precision=precise) * HEAD_DIM ** (-0.5)
    scores = low_back(scores + jnp.transpose(bias_full, (2, 0, 1)))
    scores = jnp.where(allowed[None], scores, masked_score)
    attn_probs = low(jax.nn.softmax(scores, axis=-1))
    mixed_rows = jnp.einsum('hst,thd->shd', attn_probs, value_rows, precision=precise).reshape(SEQ, D)
    mixed_rows = low_back(low(mixed_rows))
    branch = low_back(product(mixed_rows, w_out)) * live_rows
    hidden = rows_in + branch
    normed_two = low(rms_scale(hidden, norm_second))
    logits = low_back(product(normed_two, w_router))
    chosen = jnp.take_along_axis(logits, route_seq, axis=1)
    gate_probs = jax.nn.softmax(chosen, axis=-1)
    kept_pair, target = slot_plan(route_seq, is_live)
    slot_count = N_CONTEXT * EXPERTS * CAP
    pair_ids = jnp.arange(SEQ * TOP, dtype=jnp.int32)
    slot_pair = jnp.full((slot_count + 1,), SEQ * TOP, jnp.int32).at[target.reshape(-1)].set(pair_ids)[:slot_count]
    padded = jnp.concatenate([normed_two, jnp.zeros((1, D), jnp.float32)], axis=0)
    expert_in = low_back(jnp.take(padded, (slot_pair // TOP).astype(jnp.int32), axis=0))
    expert_in = expert_in.reshape(N_CONTEXT, EXPERTS, CAP, D)
    gate_pre = low_back(jnp.einsum('becd,edf->becf', expert_in, w_gate, precision=precise))
    up_part = low_back(jnp.einsum('becd,edf->becf', expert_in, w_up, precision=precise))
    activated = low(jax.nn.gelu(gate_pre, approximate=True) * up_part)
    expert_out = low_back(low(jnp.einsum('becf,efd->becd', activated, w_down, precision=precise)))
    out_rows = jnp.concatenate([expert_out.reshape(slot_count, D), jnp.zeros((1, D), jnp.float32)], axis=0)
    pair_out = jnp.take(out_rows, target, axis=0)
    pair_weight = gate_probs * kept_pair.astype(jnp.float32)
    result = hidden + lax.optimization_barrier(jnp.sum(pair_weight[:, :, None] * pair_out, axis=1))
    inverse = jnp.zeros((SEQ,), jnp.int32).at[positions].set(jnp.arange(SEQ, dtype=jnp.int32))
    return jnp.take(result, inverse, axis=0)

def reference(activations, cotangent, dealing, lengths, routes, buckets, w_query, w_key, w_value, w_out, w_router, norm_first, norm_second, bias_table, w_gate, w_up, w_down):
    weight_list = tuple((weight.astype(jnp.float32) for weight in (w_query, w_key, w_value, w_out, w_router, norm_first, norm_second, bias_table, w_gate, w_up, w_down)))
    seq_count = MB * GROUPS
    flat_act = activations.reshape(seq_count, SEQ, D)
    flat_cot = cotangent.reshape(seq_count, SEQ, D)
    flat_deal = dealing.reshape(seq_count, SEQ)
    flat_len = lengths.reshape(seq_count)
    flat_route = routes.reshape(seq_count, SEQ, TOP)

    def one_sequence(totals, pieces):
        act_seq, cot_seq, deal_seq, length, route_seq = pieces

        def forward(act_in, *weight_args):
            return block_forward(act_in, deal_seq, length, route_seq, buckets, *weight_args)
        result, pullback = jax.vjp(forward, act_seq.astype(jnp.float32), *weight_list)
        gradients = pullback(cot_seq.astype(jnp.float32))
        totals = tuple((total_old + grad_new for total_old, grad_new in zip(totals, gradients[1:])))
        return (totals, (result.astype(jnp.bfloat16), gradients[0].astype(jnp.bfloat16)))
    initial = tuple((jnp.zeros_like(weight) for weight in weight_list))
    totals, (outputs, grad_rows) = lax.scan(one_sequence, initial, (flat_act, flat_cot, flat_deal, flat_len, flat_route))
    return (outputs.reshape(MB, GROUPS, SEQ, D), grad_rows.reshape(MB, GROUPS, SEQ, D), totals[0], totals[1], totals[2], totals[3], totals[4], totals[5], totals[6], totals[7], totals[8], totals[9], totals[10])
```

```python
import functools

import jax
import jax.numpy as jnp
from jax import lax
from jax.experimental import pallas as pl
from jax.experimental.pallas import tpu as pltpu
from jax.sharding import PartitionSpec as P

epsilon = 1e-06
masked_score = -1e30
ALL = ("dp", "context", "experts")
F32 = jnp.float32
BF16 = jnp.bfloat16


def dot_f32(spec, left, right):
    return jnp.einsum(spec, left, right, preferred_element_type=F32)


def swap(value, axis, offset):
    size = lax.axis_size(axis)
    return lax.ppermute(value, axis, [(i, i ^ offset) for i in range(size)])


def reorder(pieces, index):
    pieces = list(pieces)
    bit = 1
    while bit < len(pieces):
        flag = (index // bit) % 2 == 1
        pieces = [jnp.where(flag, pieces[j ^ bit], pieces[j]) for j in range(len(pieces))]
        bit *= 2
    return pieces


def reorder_lanes(value, blocks, index):
    return jnp.concatenate(reorder(jnp.split(value, blocks, axis=-1), index), axis=-1)


def toeplitz_bias(line, size):
    rows = jnp.broadcast_to(line, (size, 2 * size))
    return pltpu.roll(rows, 0, 1, stride=1, stride_axis=0)[:, :size]


def masked_scores(query, key, line, length, scale):
    size = query.shape[0]
    scores = lax.dot_general(query, key, (((1,), (1,)), ((), ())), preferred_element_type=F32)
    scores = scores * scale + toeplitz_bias(line, size)
    row_id = lax.broadcasted_iota(jnp.int32, (size, size), 0)
    col_id = lax.broadcasted_iota(jnp.int32, (size, size), 1)
    allowed = (row_id >= col_id) & (col_id < length)
    return jnp.where(allowed, scores, masked_score)


def soft(scores):
    top_score = jnp.max(scores, axis=-1, keepdims=True)
    raised = jnp.exp(scores - top_score)
    return raised / jnp.sum(raised, axis=-1, keepdims=True)


def attend_kernel(heads, head_size, length_ref, line_ref, qkv_ref, mixed_ref):
    scale = head_size ** (-0.5)
    width = heads * head_size
    length = length_ref[pl.program_id(0)]
    for head in range(heads):
        query = qkv_ref[0, :, head * head_size : (head + 1) * head_size]
        key = qkv_ref[0, :, width + head * head_size : width + (head + 1) * head_size]
        value = qkv_ref[0, :, 2 * width + head * head_size : 2 * width + (head + 1) * head_size]
        scores = masked_scores(query, key, line_ref[head : head + 1, :], length, scale)
        probs = soft(scores).astype(BF16)
        mixed = jnp.dot(probs, value, preferred_element_type=F32)
        mixed_ref[0, :, head * head_size : (head + 1) * head_size] = mixed.astype(BF16)


def attend(qkv, lines, lengths, heads):
    micro, seq, width = qkv.shape
    width = width // 3
    head_size = width // heads
    return pl.pallas_call(
        functools.partial(attend_kernel, heads, head_size),
        grid=(micro,),
        out_shape=jax.ShapeDtypeStruct((micro, seq, width), BF16),
        in_specs=[
            pl.BlockSpec(memory_space=pltpu.SMEM),
            pl.BlockSpec(lines.shape, lambda i: (0, 0)),
            pl.BlockSpec((1, seq, 3 * width), lambda i: (i, 0, 0)),
        ],
        out_specs=pl.BlockSpec((1, seq, width), lambda i: (i, 0, 0)),
        compiler_params=pltpu.CompilerParams(vmem_limit_bytes=32 * 2**20),
    )(lengths, lines, qkv)


def diagonal_sums(grad):
    size = grad.shape[0]
    wide = jnp.concatenate([grad, jnp.zeros_like(grad)], axis=1)
    rows = size
    while rows > 1:
        rows //= 2
        lower = pltpu.roll(wide[rows:], 2 * size - rows, 1)
        wide = wide[:rows] + lower
    return wide


def attend_back_kernel(
    heads, head_size, length_ref, line_ref, qkv_ref, grad_ref, out_ref, diag_ref
):
    scale = head_size ** (-0.5)
    width = heads * head_size
    length = length_ref[pl.program_id(0)]

    @pl.when(pl.program_id(0) == 0)
    def _():
        diag_ref[...] = jnp.zeros_like(diag_ref)

    for head in range(heads):
        at = [
            slice(part * width + head * head_size, part * width + (head + 1) * head_size)
            for part in range(3)
        ]
        query, key, value = (qkv_ref[0, :, part] for part in at)
        grad = grad_ref[0, :, at[0]]
        scores = masked_scores(query, key, line_ref[head : head + 1, :], length, scale)
        probs = soft(scores)
        prob_grad = lax.dot_general(
            grad, value, (((1,), (1,)), ((), ())), preferred_element_type=F32
        )
        delta = jnp.sum(probs * prob_grad, axis=-1, keepdims=True)
        score_grad = (probs * (prob_grad - delta)).astype(BF16)
        diag_ref[head : head + 1, :] += diagonal_sums(score_grad.astype(F32))
        query_grad = jnp.dot(score_grad, key, preferred_element_type=F32) * scale
        key_grad = (
            lax.dot_general(
                score_grad, query, (((0,), (0,)), ((), ())), preferred_element_type=F32
            )
            * scale
        )
        value_grad = lax.dot_general(
            probs.astype(BF16), grad, (((0,), (0,)), ((), ())), preferred_element_type=F32
        )
        out_ref[0, :, at[0]] = query_grad.astype(BF16)
        out_ref[0, :, at[1]] = key_grad.astype(BF16)
        out_ref[0, :, at[2]] = value_grad.astype(BF16)


def attend_back(qkv, grad, lines, lengths, heads):
    micro, seq, width = grad.shape
    head_size = width // heads
    return pl.pallas_call(
        functools.partial(attend_back_kernel, heads, head_size),
        grid=(micro,),
        out_shape=(
            jax.ShapeDtypeStruct(qkv.shape, BF16),
            jax.ShapeDtypeStruct(lines.shape, F32),
        ),
        in_specs=[
            pl.BlockSpec(memory_space=pltpu.SMEM),
            pl.BlockSpec(lines.shape, lambda i: (0, 0)),
            pl.BlockSpec((1, seq, 3 * width), lambda i: (i, 0, 0)),
            pl.BlockSpec((1, seq, width), lambda i: (i, 0, 0)),
        ],
        out_specs=(
            pl.BlockSpec((1, seq, 3 * width), lambda i: (i, 0, 0)),
            pl.BlockSpec(lines.shape, lambda i: (0, 0)),
        ),
        compiler_params=pltpu.CompilerParams(vmem_limit_bytes=32 * 2**20),
    )(lengths, lines, qkv, grad)


def halve(value, axis, bit, flag):
    kept = jnp.where(flag, value[1], value[0])
    sent = jnp.where(flag, value[0], value[1]).astype(BF16)
    return kept + swap(sent, axis, bit).astype(F32)


def scatter_sum(value, dp_index, expert_index):
    dp_count, ctx_count, expert_count = value.shape[:3]
    rest = value.shape[3:]
    count, bit = dp_count, 1
    while count > 1:
        shaped = value.reshape((count // 2, 2, -1))
        value = halve(jnp.moveaxis(shaped, 1, 0), "dp", bit, (dp_index // bit) % 2 == 1)
        count //= 2
        bit *= 2
    value = value.reshape((ctx_count, expert_count) + rest)
    count, bit = expert_count, 1
    while count > 1:
        shaped = value.reshape((ctx_count, count // 2, 2) + rest)
        value = halve(jnp.moveaxis(shaped, 2, 0), "experts", bit, (expert_index // bit) % 2 == 1)
        count //= 2
        bit *= 2
    return value.reshape((ctx_count,) + rest)


def norm_pull(features, inverse, gain, grad):
    lifted = gain * grad
    mean_part = jnp.mean(lifted * features, axis=-1, keepdims=True)
    back = inverse * lifted - features * (inverse * inverse * inverse) * mean_part
    gain_grad = jnp.sum(grad * features * inverse, axis=(0, 1))
    return back, gain_grad


def gelu_parts(pre):
    root = 0.7978845608028654
    cubic = 0.044715
    square = pre * pre
    wave = jnp.tanh(root * (pre + cubic * pre * square))
    value = 0.5 * pre * (1.0 + wave)
    slope = 0.5 * (1.0 + wave) + 0.5 * pre * (1.0 - wave * wave) * root * (
        1.0 + 3.0 * cubic * square
    )
    return value, slope


def down_routes(dp_count, ctx_count, expert_count, core, ctx_offset):
    pairs = []
    for dp in range(dp_count):
        for ctx in range(ctx_count):
            for expert in range(expert_count):
                high, low = dp // 2, dp % 2
                to_high = high if low == core else high ^ 1
                target = ((to_high * 2 + high) * ctx_count + (ctx ^ ctx_offset)) * expert_count
                pairs.append(((dp * ctx_count + ctx) * expert_count + expert, target + expert))
    return pairs


def body(
    activations,
    cotangent,
    dealing,
    lengths,
    routes,
    buckets,
    w_query,
    w_key,
    w_value,
    w_out,
    w_router,
    norm_first,
    norm_second,
    bias_table,
    w_gate,
    w_up,
    w_down,
):
    micro, _, rows_dev, width = activations.shape
    seq = dealing.shape[2]
    bucket_count, head_count = bias_table.shape
    dp_count, ctx_count, expert_count = (lax.axis_size(name) for name in ALL)
    dp_index, ctx_index, expert_index = (lax.axis_index(name) for name in ALL)
    high, low = dp_index // 2, dp_index % 2
    heads = head_count // ctx_count
    head_size = width // head_count
    own_width = heads * head_size
    experts = w_router.shape[1]
    top_count = routes.shape[3]
    capacity = (5 * rows_dev * top_count + 4 * experts - 1) // (4 * experts)
    slots = -(-capacity // 16) * 16
    ff = w_gate.shape[2]
    half_ff = ff // 2
    weight_rows = w_query.shape[0]
    plane = dp_count * ctx_count
    plane_index = dp_index * ctx_count + ctx_index
    act = activations[:, 0]
    cot = cotangent[:, 0]
    deal = dealing[:, 0]
    length = lengths[:, 0]
    route = routes[:, 0]

    extras = jnp.concatenate(
        [w_router, norm_first[:, None], norm_second[:, None]], axis=1
    )
    extras = jnp.pad(extras, ((0, 0), (0, 128 - extras.shape[1])))
    column_parts = [
        jnp.split(weight, ctx_count, axis=1) for weight in (w_query, w_key, w_value)
    ]
    packs = [
        jnp.concatenate([part[c] for part in column_parts] + [extras], axis=1)
        for c in range(ctx_count)
    ]
    packs = reorder(packs, ctx_index)
    packs = [packs[0]] + [swap(packs[k], "context", k) for k in range(1, ctx_count)]
    packs = jnp.stack(reorder(packs, ctx_index))
    dense = lax.all_gather(packs, ("dp", "experts"), axis=0, tiled=False)
    dense = dense.reshape((dp_count, expert_count) + packs.shape)
    dense = jnp.transpose(dense, (0, 2, 1, 3, 4)).reshape(width, -1)
    qkv_w = dense[:, : 3 * own_width]
    router_w = dense[:, 3 * own_width : 3 * own_width + experts]
    gain_one = dense[:, 3 * own_width + experts].astype(F32)
    gain_two = dense[:, 3 * own_width + experts + 1].astype(F32)
    out_w = lax.all_gather(w_out, ALL, axis=0, tiled=True)

    gate_up = [
        jnp.concatenate([w_gate[0, :, h * half_ff : (h + 1) * half_ff], w_up[0, :, h * half_ff : (h + 1) * half_ff]], axis=1)
        for h in range(2)
    ]
    halves = reorder(gate_up, low)
    gate_blocks = []
    for j in range(plane):
        dp_offset, ctx_offset = j // ctx_count, j % ctx_count
        piece = halves[dp_offset % 2]
        if dp_offset:
            piece = swap(piece, "dp", dp_offset)
        if ctx_offset:
            piece = swap(piece, "context", ctx_offset) if not dp_offset else piece
        gate_blocks.append(piece)
    for j in range(plane):
        dp_offset, ctx_offset = j // ctx_count, j % ctx_count
        if dp_offset and ctx_offset:
            gate_blocks[j] = swap(gate_blocks[dp_offset * ctx_count], "context", ctx_offset)
    gate_up_w = jnp.concatenate(gate_blocks, axis=0)
    down_w = jnp.zeros((half_ff, width), BF16)
    down_rows = w_down.shape[1]
    for ctx_offset in range(ctx_count):
        for core in range(2):
            pairs = down_routes(dp_count, ctx_count, expert_count, core, ctx_offset)
            piece = lax.ppermute(w_down[0], ALL, pairs)
            from_core = jnp.where(low == high, core, 1 - core)
            place = (from_core * ctx_count + (ctx_index ^ ctx_offset)) * down_rows
            down_w = lax.dynamic_update_slice(down_w, piece, (place, 0))

    act_all = jnp.concatenate(
        reorder([act] + [swap(act, "context", k) for k in range(1, ctx_count)], ctx_index), axis=1
    )
    cot_all = jnp.concatenate(
        reorder([cot] + [swap(cot, "context", k) for k in range(1, ctx_count)], ctx_index), axis=1
    )
    position_ids = jnp.arange(seq, dtype=jnp.int32)
    slot_blocks = [
        lax.dynamic_slice_in_dim(deal, (ctx_index ^ k) * rows_dev, rows_dev, axis=1)
        for k in range(ctx_count)
    ]
    hot = [
        (block[:, :, None] == position_ids[None, None, :]).astype(BF16) for block in slot_blocks
    ]
    my_positions = ctx_index * rows_dev + jnp.arange(rows_dev, dtype=jnp.int32)
    hot_mine = [
        (block[:, :, None] == my_positions[None, None, :]).astype(BF16) for block in slot_blocks
    ]
    live = slot_blocks[0] < length[:, None]
    live_rows = live.astype(F32)[:, :, None]
    bucket_hot = (buckets[:, None] == jnp.arange(bucket_count)[None, :]).astype(BF16)
    own_table = lax.dynamic_slice_in_dim(bias_table, ctx_index * heads, heads, axis=1)
    lookup = dot_f32("sb,bh->hs", bucket_hot, own_table)
    lines = jnp.concatenate(
        [lookup[:, :1], jnp.zeros((heads, seq), F32), lookup[:, :0:-1]], axis=1
    )

    rows_all = act_all.astype(F32)
    inverse_one = lax.rsqrt(jnp.mean(rows_all * rows_all, axis=-1, keepdims=True) + epsilon)
    normed = (rows_all * inverse_one * gain_one).astype(BF16)
    qkv = dot_f32("mpd,dw->mpw", normed, qkv_w).astype(BF16)
    mixed_own = attend(qkv, lines, length, heads)
    mixed_parts = [
        dot_f32("msp,mpw->msw", hot[k], mixed_own).astype(BF16) for k in range(ctx_count)
    ]
    mixed_parts = [mixed_parts[0]] + [
        swap(mixed_parts[k], "context", k) for k in range(1, ctx_count)
    ]
    mixed = jnp.concatenate(reorder(mixed_parts, ctx_index), axis=-1)

    rows_in = dot_f32("msp,mpd->msd", hot[0], act_all)
    cot_rows = dot_f32("msp,mpd->msd", hot[0], cot_all)
    branch = dot_f32("msi,io->mso", mixed, out_w)
    hidden = rows_in + branch * live_rows
    inverse_two = lax.rsqrt(jnp.mean(hidden * hidden, axis=-1, keepdims=True) + epsilon)
    normed_two = (hidden * inverse_two * gain_two).astype(BF16)
    logits = dot_f32("msd,de->mse", normed_two, router_w)
    route_hot = (route[..., None] == jnp.arange(experts)).astype(F32)
    chosen = jnp.sum(route_hot * logits[:, :, None, :], axis=3)
    gate_probs = jax.nn.softmax(chosen, axis=-1)

    flat_hot = (route_hot * live_rows[..., None]).reshape(micro, rows_dev * top_count, experts)
    pair_ids = jnp.arange(rows_dev * top_count)
    before = (pair_ids[:, None] > pair_ids[None, :]).astype(BF16)
    earlier = dot_f32("ab,mbe->mae", before, flat_hot.astype(BF16))
    rank = jnp.sum(earlier * flat_hot, axis=2).astype(jnp.int32).reshape(route.shape)
    kept = live[:, :, None] & (rank < capacity)
    target = jnp.where(kept, (route ^ expert_index) * slots + rank, -1)
    place_ids = jnp.arange(experts * slots, dtype=jnp.int32)
    pick = [
        (target[:, None, :, j] == place_ids[None, :, None]) for j in range(top_count)
    ]
    pick_any = functools.reduce(jnp.logical_or, pick).astype(BF16)
    pick_bf = [p.astype(BF16) for p in pick]
    prob_rows = sum(
        jnp.sum(jnp.where(pick[j], gate_probs[:, None, :, j], 0.0), axis=2)
        for j in range(top_count)
    )

    def by_expert(value):
        shaped = value.reshape((micro, experts, slots) + value.shape[2:])
        return jnp.moveaxis(shaped, 1, 0)

    def exchange(value):
        parts = [value[0]] + [swap(value[k], "experts", k) for k in range(1, expert_count)]
        return jnp.stack(parts)

    normed_rel = reorder_lanes(normed_two, plane, plane_index)
    sent_rows = by_expert(dot_f32("mrs,msd->mrd", pick_any, normed_rel).astype(BF16))
    sent_up = by_expert(
        dot_f32("mrs,msd->mrd", pick_any, cot_rows.astype(BF16)).astype(BF16)
    )
    row_count = expert_count * micro * slots
    own_x = exchange(sent_rows).reshape(row_count, width)
    own_u = exchange(sent_up).reshape(row_count, width)
    own_p = exchange(by_expert(prob_rows)).reshape(row_count, 1)
    own_g = (own_p * own_u.astype(F32)).astype(BF16)

    def core_swap(value):
        blocks = jnp.split(value, plane, axis=-1)
        return jnp.concatenate([blocks[j ^ ctx_count] for j in range(plane)], axis=-1)

    all_x = jnp.concatenate([own_x, core_swap(swap(own_x, "dp", 1))], axis=0)
    all_g = jnp.concatenate([own_g, swap(own_g, "dp", 1)], axis=0)

    pre_up = dot_f32("rd,df->rf", all_x, gate_up_w)
    gelu_value, gelu_slope = gelu_parts(pre_up[:, :half_ff])
    up_part = pre_up[:, half_ff:]
    activated = (gelu_value * up_part).astype(BF16)
    act_grad = dot_f32("rd,fd->rf", all_g, down_w)
    pre_grad = (act_grad * up_part * gelu_slope).astype(BF16)
    up_grad = (act_grad * gelu_value).astype(BF16)
    both_grad = jnp.concatenate([pre_grad, up_grad], axis=1)
    back_part = dot_f32("rf,df->rd", both_grad, gate_up_w)
    out_part = dot_f32("rf,fd->rd", activated, down_w)
    out_own = (
        out_part[:row_count] + swap(out_part[row_count:].astype(BF16), "dp", 1).astype(F32)
    ).astype(BF16)
    back_own = (
        back_part[:row_count]
        + swap(core_swap(back_part[row_count:].astype(BF16)), "dp", 1).astype(F32)
    ).astype(BF16)
    gate_rows = jnp.sum(own_u.astype(F32) * out_own.astype(F32), axis=-1)

    def to_source(value):
        parts = value.reshape((expert_count, micro, slots) + value.shape[1:])
        parts = exchange(parts)
        return jnp.moveaxis(parts, 0, 1).reshape((micro, experts * slots) + value.shape[1:])

    back_rows = to_source(back_own)
    gate_back = to_source(gate_rows)
    out_rows = to_source(out_own)

    gate_up_total = dot_f32("rd,rf->df", all_x, both_grad)
    down_total = dot_f32("rf,rd->fd", activated, all_g)

    gate_up_sums = [0.0, 0.0]
    for j in range(plane):
        dp_offset, ctx_offset = j // ctx_count, j % ctx_count
        block = gate_up_total[j * (width // plane) : (j + 1) * (width // plane)].astype(BF16)
        pairs = [
            (
                (d * ctx_count + c) * expert_count + e,
                ((d ^ dp_offset) * ctx_count + (c ^ ctx_offset)) * expert_count + e,
            )
            for d in range(dp_count)
            for c in range(ctx_count)
            for e in range(expert_count)
        ]
        if j:
            block = lax.ppermute(block, ALL, pairs)
        gate_up_sums[dp_offset % 2] = gate_up_sums[dp_offset % 2] + block.astype(F32)
    first_half, second_half = reorder(gate_up_sums, low)
    grad_gate = jnp.concatenate([first_half[:, :half_ff], second_half[:, :half_ff]], axis=1)
    grad_up = jnp.concatenate([first_half[:, half_ff:], second_half[:, half_ff:]], axis=1)
    grad_down = 0.0
    for ctx_offset in range(ctx_count):
        for core in range(2):
            pairs = down_routes(dp_count, ctx_count, expert_count, core, ctx_offset)
            from_core = jnp.where(low == high, core, 1 - core)
            place = (from_core * ctx_count + (ctx_index ^ ctx_offset)) * down_rows
            piece = lax.dynamic_slice_in_dim(down_total, place, down_rows, axis=0).astype(BF16)
            arrived = lax.ppermute(piece, ALL, [(b, a) for a, b in pairs])
            grad_down = grad_down + arrived.astype(F32)

    pair_out = [dot_f32("mrs,mrd->msd", pick_bf[j], out_rows) for j in range(top_count)]
    final = hidden + sum(gate_probs[:, :, j, None] * pair_out[j] for j in range(top_count))
    final = final.astype(BF16)
    gate_grad = jnp.stack(
        [
            jnp.sum(jnp.where(pick[j], gate_back[:, :, None], 0.0), axis=1)
            for j in range(top_count)
        ],
        axis=-1,
    )
    chosen_grad = gate_probs * (
        gate_grad - jnp.sum(gate_probs * gate_grad, axis=-1, keepdims=True)
    )
    logit_grad = jnp.sum(route_hot * chosen_grad[..., None], axis=2).astype(BF16)
    normed_grad = reorder_lanes(
        dot_f32("mrs,mrd->msd", pick_any, back_rows), plane, plane_index
    ) + dot_f32("mse,de->msd", logit_grad, router_w)
    router_total = dot_f32("msd,mse->de", normed_two, logit_grad)
    hidden_norm_grad, second_total = norm_pull(hidden, inverse_two, gain_two, normed_grad)
    hidden_grad = cot_rows + hidden_norm_grad
    branch_grad = (hidden_grad * live_rows).astype(BF16)
    hidden_low = hidden_grad.astype(BF16)
    out_total = dot_f32("msi,mso->io", mixed, branch_grad)
    mixed_grad = dot_f32("mso,io->msi", branch_grad, out_w).astype(BF16)
    grad_parts = reorder(jnp.split(mixed_grad, ctx_count, axis=-1), ctx_index)
    grad_parts = [grad_parts[0]] + [
        swap(grad_parts[k], "context", k) for k in range(1, ctx_count)
    ]
    mixed_back = sum(
        dot_f32("msp,msw->mpw", hot[k], grad_parts[k]) for k in range(ctx_count)
    ).astype(BF16)
    qkv_grad, diagonals = attend_back(qkv, mixed_back, lines, length, heads)
    qkv_total = dot_f32("mpd,mpw->dw", normed, qkv_grad)
    first_part = dot_f32("mpw,dw->mpd", qkv_grad, qkv_w)
    first_total = jnp.sum(first_part * rows_all * inverse_one, axis=(0, 1))
    blocks = [
        lax.dynamic_slice_in_dim(first_part, (ctx_index ^ k) * rows_dev, rows_dev, axis=1)
        for k in range(ctx_count)
    ]
    first_grad = blocks[0] + sum(
        swap(blocks[k].astype(BF16), "context", k).astype(F32) for k in range(1, ctx_count)
    )

    def to_positions(value):
        parts = [value] + [swap(value, "context", k) for k in range(1, ctx_count)]
        return sum(dot_f32("msp,msd->mpd", hot_mine[k], parts[k]) for k in range(ctx_count))

    rows_mine = act.astype(F32)
    inverse_mine = lax.rsqrt(jnp.mean(rows_mine * rows_mine, axis=-1, keepdims=True) + epsilon)
    rows_back, _ = norm_pull(rows_mine, inverse_mine, gain_one, first_grad)
    grad_input = (to_positions(hidden_low) + rows_back).astype(BF16)[:, None]
    output = to_positions(final).astype(BF16)[:, None]

    owners = (dp_count, ctx_count, expert_count, weight_rows)
    out_pack = jnp.concatenate(
        [out_total, router_total, second_total[:, None]], axis=1
    )
    out_pack = jnp.pad(out_pack, ((0, 0), (0, width + 128 - out_pack.shape[1])))
    out_pack = scatter_sum(out_pack.reshape(owners + (-1,)), dp_index, expert_index)
    qkv_pack = jnp.pad(
        jnp.concatenate([qkv_total, first_total[:, None]], axis=1), ((0, 0), (0, 127))
    )
    qkv_pack = scatter_sum(qkv_pack.reshape(owners + (-1,)), dp_index, expert_index)

    def across(value):
        parts = reorder([value[c] for c in range(ctx_count)], ctx_index)
        return [parts[0]] + [
            swap(parts[k].astype(BF16), "context", k).astype(F32) for k in range(1, ctx_count)
        ]

    out_sum = sum(across(out_pack))
    qkv_parts = across(qkv_pack)
    grad_first = sum(part[:, 3 * own_width] for part in qkv_parts)
    qkv_parts = reorder(qkv_parts, ctx_index)
    grad_query, grad_key, grad_value = (
        jnp.concatenate(
            [part[:, i * own_width : (i + 1) * own_width] for part in qkv_parts], axis=1
        )
        for i in range(3)
    )
    grad_out = out_sum[:, :width]
    grad_router = out_sum[:, width : width + experts]
    grad_second = out_sum[:, width + experts]
    offsets = jnp.concatenate([diagonals[:, :1], diagonals[:, : seq : -1]], axis=1)
    table_part = jnp.einsum(
        "hs,sb->bh", offsets, bucket_hot.astype(F32), precision=lax.Precision.HIGHEST
    )
    table_full = lax.dynamic_update_slice(
        jnp.zeros(bias_table.shape, F32), table_part, (0, ctx_index * heads)
    )
    grad_table = lax.psum(table_full, ALL)
    return (
        output,
        grad_input,
        grad_query,
        grad_key,
        grad_value,
        grad_out,
        grad_router,
        grad_first,
        grad_second,
        grad_table,
        grad_gate[None],
        grad_up[None],
        grad_down[None],
    )


def solution(mesh):
    tokens = P(None, ("dp", "experts"), "context", None)
    sequences = P(None, ("dp", "experts"))
    rows = P(("dp", "context", "experts"), None)
    gains = P(("dp", "context", "experts"))
    experts = P("experts", ("dp", "context"), None)
    placed = (
        (tokens, tokens, P(None, ("dp", "experts"), None), sequences, tokens, P())
        + (rows,) * 5
        + (gains, gains, P())
        + (experts,) * 3
    )
    return jax.shard_map(
        body,
        mesh=mesh,
        in_specs=placed,
        out_specs=(tokens, tokens) + (rows,) * 5 + (gains, gains, P()) + (experts,) * 3,
        check_vma=False,
    )
```

```python
import functools

import jax
import jax.numpy as jnp
from jax import lax
from jax.experimental import pallas as pl
from jax.experimental.pallas import tpu as pltpu
from jax.sharding import PartitionSpec as P

epsilon = 1e-06
masked_score = -1e30
ALL = ("dp", "context", "experts")
F32 = jnp.float32
BF16 = jnp.bfloat16


def dot_f32(spec, left, right):
    return jnp.einsum(spec, left, right, preferred_element_type=F32)


def swap(value, axis, offset):
    size = lax.axis_size(axis)
    return lax.ppermute(value, axis, [(i, i ^ offset) for i in range(size)])


def reorder(pieces, index):
    pieces = list(pieces)
    bit = 1
    while bit < len(pieces):
        flag = (index // bit) % 2 == 1
        pieces = [jnp.where(flag, pieces[j ^ bit], pieces[j]) for j in range(len(pieces))]
        bit *= 2
    return pieces


def reorder_lanes(value, blocks, index):
    return jnp.concatenate(reorder(jnp.split(value, blocks, axis=-1), index), axis=-1)


def toeplitz_bias(line, size):
    rows = jnp.broadcast_to(line, (size, 2 * size))
    return pltpu.roll(rows, 0, 1, stride=1, stride_axis=0)[:, :size]


def masked_scores(query, key, line, length, scale):
    size = query.shape[0]
    scores = lax.dot_general(query, key, (((1,), (1,)), ((), ())), preferred_element_type=F32)
    scores = scores * scale + toeplitz_bias(line, size)
    row_id = lax.broadcasted_iota(jnp.int32, (size, size), 0)
    col_id = lax.broadcasted_iota(jnp.int32, (size, size), 1)
    allowed = (row_id >= col_id) & (col_id < length)
    return jnp.where(allowed, scores, masked_score)


def soft(scores):
    top_score = jnp.max(scores, axis=-1, keepdims=True)
    raised = jnp.exp(scores - top_score)
    return raised / jnp.sum(raised, axis=-1, keepdims=True)


def attend_kernel(heads, head_size, length_ref, line_ref, qkv_ref, mixed_ref):
    scale = head_size ** (-0.5)
    width = heads * head_size
    length = length_ref[pl.program_id(0)]
    for head in range(heads):
        query = qkv_ref[0, :, head * head_size : (head + 1) * head_size]
        key = qkv_ref[0, :, width + head * head_size : width + (head + 1) * head_size]
        value = qkv_ref[0, :, 2 * width + head * head_size : 2 * width + (head + 1) * head_size]
        scores = masked_scores(query, key, line_ref[head : head + 1, :], length, scale)
        probs = soft(scores).astype(BF16)
        mixed = jnp.dot(probs, value, preferred_element_type=F32)
        mixed_ref[0, :, head * head_size : (head + 1) * head_size] = mixed.astype(BF16)


def attend(qkv, lines, lengths, heads):
    micro, seq, width = qkv.shape
    width = width // 3
    head_size = width // heads
    return pl.pallas_call(
        functools.partial(attend_kernel, heads, head_size),
        grid=(micro,),
        out_shape=jax.ShapeDtypeStruct((micro, seq, width), BF16),
        in_specs=[
            pl.BlockSpec(memory_space=pltpu.SMEM),
            pl.BlockSpec(lines.shape, lambda i: (0, 0)),
            pl.BlockSpec((1, seq, 3 * width), lambda i: (i, 0, 0)),
        ],
        out_specs=pl.BlockSpec((1, seq, width), lambda i: (i, 0, 0)),
        compiler_params=pltpu.CompilerParams(vmem_limit_bytes=32 * 2**20),
    )(lengths, lines, qkv)


def diagonal_sums(grad):
    size = grad.shape[0]
    wide = jnp.concatenate([grad, jnp.zeros_like(grad)], axis=1)
    rows = size
    while rows > 1:
        rows //= 2
        lower = pltpu.roll(wide[rows:], 2 * size - rows, 1)
        wide = wide[:rows] + lower
    return wide


def attend_back_kernel(
    heads, head_size, length_ref, line_ref, qkv_ref, grad_ref, out_ref, diag_ref
):
    scale = head_size ** (-0.5)
    width = heads * head_size
    length = length_ref[pl.program_id(0)]

    @pl.when(pl.program_id(0) == 0)
    def _():
        diag_ref[...] = jnp.zeros_like(diag_ref)

    for head in range(heads):
        at = [
            slice(part * width + head * head_size, part * width + (head + 1) * head_size)
            for part in range(3)
        ]
        query, key, value = (qkv_ref[0, :, part] for part in at)
        grad = grad_ref[0, :, at[0]]
        scores = masked_scores(query, key, line_ref[head : head + 1, :], length, scale)
        probs = soft(scores)
        prob_grad = lax.dot_general(
            grad, value, (((1,), (1,)), ((), ())), preferred_element_type=F32
        )
        delta = jnp.sum(probs * prob_grad, axis=-1, keepdims=True)
        score_grad = (probs * (prob_grad - delta)).astype(BF16)
        diag_ref[head : head + 1, :] += diagonal_sums(score_grad.astype(F32))
        query_grad = jnp.dot(score_grad, key, preferred_element_type=F32) * scale
        key_grad = (
            lax.dot_general(
                score_grad, query, (((0,), (0,)), ((), ())), preferred_element_type=F32
            )
            * scale
        )
        value_grad = lax.dot_general(
            probs.astype(BF16), grad, (((0,), (0,)), ((), ())), preferred_element_type=F32
        )
        out_ref[0, :, at[0]] = query_grad.astype(BF16)
        out_ref[0, :, at[1]] = key_grad.astype(BF16)
        out_ref[0, :, at[2]] = value_grad.astype(BF16)


def attend_back(qkv, grad, lines, lengths, heads):
    micro, seq, width = grad.shape
    head_size = width // heads
    return pl.pallas_call(
        functools.partial(attend_back_kernel, heads, head_size),
        grid=(micro,),
        out_shape=(
            jax.ShapeDtypeStruct(qkv.shape, BF16),
            jax.ShapeDtypeStruct(lines.shape, F32),
        ),
        in_specs=[
            pl.BlockSpec(memory_space=pltpu.SMEM),
            pl.BlockSpec(lines.shape, lambda i: (0, 0)),
            pl.BlockSpec((1, seq, 3 * width), lambda i: (i, 0, 0)),
            pl.BlockSpec((1, seq, width), lambda i: (i, 0, 0)),
        ],
        out_specs=(
            pl.BlockSpec((1, seq, 3 * width), lambda i: (i, 0, 0)),
            pl.BlockSpec(lines.shape, lambda i: (0, 0)),
        ),
        compiler_params=pltpu.CompilerParams(vmem_limit_bytes=32 * 2**20),
    )(lengths, lines, qkv, grad)


def halve(value, axis, bit, flag):
    kept = jnp.where(flag, value[1], value[0])
    sent = jnp.where(flag, value[0], value[1]).astype(BF16)
    return kept + swap(sent, axis, bit).astype(F32)


def scatter_sum(value, dp_index, expert_index):
    dp_count, ctx_count, expert_count = value.shape[:3]
    rest = value.shape[3:]
    count, bit = dp_count, 1
    while count > 1:
        shaped = value.reshape((count // 2, 2, -1))
        value = halve(jnp.moveaxis(shaped, 1, 0), "dp", bit, (dp_index // bit) % 2 == 1)
        count //= 2
        bit *= 2
    value = value.reshape((ctx_count, expert_count) + rest)
    count, bit = expert_count, 1
    while count > 1:
        shaped = value.reshape((ctx_count, count // 2, 2) + rest)
        value = halve(jnp.moveaxis(shaped, 2, 0), "experts", bit, (expert_index // bit) % 2 == 1)
        count //= 2
        bit *= 2
    return value.reshape((ctx_count,) + rest)


MESH = pl.DeviceIdType.MESH


def flip(index, bit):
    return index + bit - 2 * bit * ((index // bit) % 2)


def greet(targets):
    barrier = pltpu.get_barrier_semaphore()
    for target in targets:
        pl.semaphore_signal(barrier, inc=1, device_id=target, device_id_type=MESH)
    pl.semaphore_wait(barrier, len(targets))


def remote(source, place, sends, receives, target):
    return pltpu.make_async_remote_copy(
        src_ref=source,
        dst_ref=place,
        send_sem=sends,
        recv_sem=receives,
        device_id=target,
        device_id_type=MESH,
    )


def reduce_kernel(
    own_width,
    qkv_ref,
    out_ref,
    small_ref,
    diag_ref,
    query_out,
    key_out,
    value_out,
    out_out,
    small_out,
    diag_out,
    *scratch,
):
    dp, ctx, exp = (lax.axis_index(name) for name in ALL)
    high, low = dp // 2, dp % 2
    z_high, z_low = exp // 2, exp % 2
    peers = [
        (flip(dp, 1), ctx, exp),
        (flip(dp, 2), ctx, exp),
        (dp, ctx, flip(exp, 1)),
        (dp, ctx, flip(exp, 2)),
        (dp, 1 - ctx, exp),
    ]
    chunks = []
    for c in range(3):
        chunks.append((qkv_ref, c * own_width, own_width))
    width = out_ref.shape[-1]
    for c in range(width // own_width):
        chunks.append((out_ref, c * own_width, own_width))
    chunks.append((small_ref, 0, small_ref.shape[-1]))
    count = len(chunks)
    per = 9
    bufs = [scratch[i * per : (i + 1) * per] for i in range(count)]
    diag_buf, sends, receives, diag_sends, diag_receives = scratch[count * per :]
    greet(peers)

    flying = []

    def launch(i, stage, source, place):
        copy = remote(source, place, sends.at[i, stage], receives.at[i, stage], peers[stage])
        copy.start()
        flying.append(copy)
        return copy

    copies = {}
    for i, (ref, start, size) in enumerate(chunks):
        copies[i, 0] = launch(
            i, 0, ref.at[:, 1 - low, :, start : start + size], bufs[i][0]
        )
    diag_buf[0] = diag_ref[...]
    diag_copies = []

    def diag_step(stage):
        if stage:
            diag_copies[stage - 1].wait_recv()
        if stage and stage < 5:
            diag_buf[2 * stage] = diag_buf[2 * stage - 2] + diag_buf[2 * stage - 1]
        if stage < 5:
            copy = remote(
                diag_buf.at[2 * stage],
                diag_buf.at[2 * stage + 1],
                diag_sends.at[stage],
                diag_receives.at[stage],
                peers[stage],
            )
            copy.start()
            diag_copies.append(copy)
            flying.append(copy)

    def advance(i, stage):
        ref, start, size = chunks[i]
        recv_a, send_b, recv_b, send_c, recv_c, send_d, recv_d, send_e, recv_e = bufs[i]
        copies[i, stage].wait_recv()
        if stage == 0:
            send_b[...] = (
                ref[1 - high, low, :, start : start + size].astype(F32)
                + recv_a[1 - high].astype(F32)
            ).astype(BF16)
            copies[i, 1] = launch(i, 1, send_b, recv_b)
        elif stage == 1:
            total = (
                ref[high, low, :, start : start + size].astype(F32)
                + recv_a[high].astype(F32)
                + recv_b[...].astype(F32)
            ).astype(BF16)
            send_c[...] = total.reshape(send_c.shape)
            copies[i, 2] = launch(i, 2, send_c.at[:, :, 1 - z_low], recv_c)
        elif stage == 2:
            send_d[...] = (
                send_c[:, :, z_low].astype(F32) + recv_c[...].astype(F32)
            ).astype(BF16)
            copies[i, 3] = launch(i, 3, send_d.at[:, 1 - z_high], recv_d)
        elif stage == 3:
            send_e[...] = (send_d[:, z_high].astype(F32) + recv_d[...].astype(F32)).astype(BF16)
            copies[i, 4] = launch(i, 4, send_e.at[1 - ctx], recv_e)
        else:
            mine, other = send_e[ctx].astype(F32), recv_e[...].astype(F32)
            if i < 3:
                place = (query_out, key_out, value_out)[i]
                place[:, pl.ds(pl.multiple_of(ctx * size, 128), size)] = mine
                place[:, pl.ds(pl.multiple_of((1 - ctx) * size, 128), size)] = other
            elif ref is out_ref:
                out_out[:, start : start + size] = mine + other
            else:
                small_out[...] = mine + other

    for step in range(count + 4):
        if step < 6:
            diag_step(step)
        for stage in range(4, -1, -1):
            if 0 <= step - stage < count:
                advance(step - stage, stage)
    diag_out[ctx] = diag_buf[8]
    diag_out[1 - ctx] = diag_buf[9]
    for copy in flying:
        copy.wait_send()


def reduce_dense(qkv_total, out_total, small, diagonals, own_width):
    rows, width = out_total.shape
    dp_count, ctx_count, expert_count = (lax.axis_size(name) for name in ALL)
    per_row = rows // (dp_count * ctx_count * expert_count)
    shaped = lambda v: v.reshape((2, 2, rows // 4, v.shape[-1]))
    sizes = [own_width] * (3 + width // own_width) + [small.shape[-1]]
    scratch = []
    quarter = rows // 4
    for size in sizes:
        scratch += [
            pltpu.VMEM((2, quarter, size), BF16),
            pltpu.VMEM((quarter, size), BF16),
            pltpu.VMEM((quarter, size), BF16),
            pltpu.VMEM((2, 2, 2, per_row, size), BF16),
            pltpu.VMEM((2, 2, per_row, size), BF16),
            pltpu.VMEM((2, 2, per_row, size), BF16),
            pltpu.VMEM((2, per_row, size), BF16),
            pltpu.VMEM((2, per_row, size), BF16),
            pltpu.VMEM((per_row, size), BF16),
        ]
    scratch += [
        pltpu.VMEM((10,) + diagonals.shape, F32),
        pltpu.SemaphoreType.DMA((len(sizes), 5)),
        pltpu.SemaphoreType.DMA((len(sizes), 5)),
        pltpu.SemaphoreType.DMA((5,)),
        pltpu.SemaphoreType.DMA((5,)),
    ]
    whole = pl.BlockSpec(memory_space=pltpu.VMEM)
    return pl.pallas_call(
        functools.partial(reduce_kernel, own_width),
        out_shape=tuple(jax.ShapeDtypeStruct((per_row, width), F32) for _ in range(4))
        + (
            jax.ShapeDtypeStruct((per_row, small.shape[-1]), F32),
            jax.ShapeDtypeStruct((2,) + diagonals.shape, F32),
        ),
        in_specs=[whole] * 4,
        out_specs=(whole,) * 6,
        scratch_shapes=scratch,
        compiler_params=pltpu.CompilerParams(
            collective_id=0, has_side_effects=True, vmem_limit_bytes=48 * 2**20
        ),
    )(shaped(qkv_total), shaped(out_total), shaped(small), diagonals)


def plain_sums(qkv_total, out_total, router_total, first_total, second_total, own_width):
    width, experts = router_total.shape
    dp_count, ctx_count, expert_count = (lax.axis_size(name) for name in ALL)
    dp_index, ctx_index, expert_index = (lax.axis_index(name) for name in ALL)
    owners = (dp_count, ctx_count, expert_count, -1)
    out_pack = jnp.concatenate([out_total, router_total, second_total[:, None]], axis=1)
    out_pack = jnp.pad(out_pack, ((0, 0), (0, width + 128 - out_pack.shape[1])))
    out_pack = scatter_sum(
        out_pack.reshape(owners + (out_pack.shape[1],)), dp_index, expert_index
    )
    qkv_pack = jnp.pad(
        jnp.concatenate([qkv_total, first_total[:, None]], axis=1), ((0, 0), (0, 127))
    )
    qkv_pack = scatter_sum(
        qkv_pack.reshape(owners + (qkv_pack.shape[1],)), dp_index, expert_index
    )

    def across(value):
        parts = reorder([value[c] for c in range(ctx_count)], ctx_index)
        return [parts[0]] + [
            swap(parts[k].astype(BF16), "context", k).astype(F32) for k in range(1, ctx_count)
        ]

    out_sum = sum(across(out_pack))
    qkv_parts = across(qkv_pack)
    grad_first = sum(part[:, 3 * own_width] for part in qkv_parts)
    qkv_parts = reorder(qkv_parts, ctx_index)
    grads = tuple(
        jnp.concatenate(
            [part[:, i * own_width : (i + 1) * own_width] for part in qkv_parts], axis=1
        )
        for i in range(3)
    )
    return grads + (
        out_sum[:, :width],
        out_sum[:, width : width + experts],
        grad_first,
        out_sum[:, width + experts],
    )


def norm_pull(features, inverse, gain, grad):
    lifted = gain * grad
    mean_part = jnp.mean(lifted * features, axis=-1, keepdims=True)
    back = inverse * lifted - features * (inverse * inverse * inverse) * mean_part
    gain_grad = jnp.sum(grad * features * inverse, axis=(0, 1))
    return back, gain_grad


def gelu_parts(pre):
    root = 0.7978845608028654
    cubic = 0.044715
    square = pre * pre
    wave = jnp.tanh(root * (pre + cubic * pre * square))
    value = 0.5 * pre * (1.0 + wave)
    slope = 0.5 * (1.0 + wave) + 0.5 * pre * (1.0 - wave * wave) * root * (
        1.0 + 3.0 * cubic * square
    )
    return value, slope


def down_routes(dp_count, ctx_count, expert_count, core, ctx_offset):
    pairs = []
    for dp in range(dp_count):
        for ctx in range(ctx_count):
            for expert in range(expert_count):
                high, low = dp // 2, dp % 2
                to_high = high if low == core else high ^ 1
                target = ((to_high * 2 + high) * ctx_count + (ctx ^ ctx_offset)) * expert_count
                pairs.append(((dp * ctx_count + ctx) * expert_count + expert, target + expert))
    return pairs


def body(
    activations,
    cotangent,
    dealing,
    lengths,
    routes,
    buckets,
    w_query,
    w_key,
    w_value,
    w_out,
    w_router,
    norm_first,
    norm_second,
    bias_table,
    w_gate,
    w_up,
    w_down,
):
    micro, _, rows_dev, width = activations.shape
    seq = dealing.shape[2]
    bucket_count, head_count = bias_table.shape
    dp_count, ctx_count, expert_count = (lax.axis_size(name) for name in ALL)
    dp_index, ctx_index, expert_index = (lax.axis_index(name) for name in ALL)
    high, low = dp_index // 2, dp_index % 2
    heads = head_count // ctx_count
    head_size = width // head_count
    own_width = heads * head_size
    experts = w_router.shape[1]
    top_count = routes.shape[3]
    capacity = (5 * rows_dev * top_count + 4 * experts - 1) // (4 * experts)
    slots = -(-capacity // 16) * 16
    ff = w_gate.shape[2]
    half_ff = ff // 2
    weight_rows = w_query.shape[0]
    plane = dp_count * ctx_count
    plane_index = dp_index * ctx_count + ctx_index
    tuned = (
        (dp_count, ctx_count, expert_count) == (4, 2, 4)
        and weight_rows % 16 == 0
        and own_width % 128 == 0
        and width % own_width == 0
    )
    act = activations[:, 0]
    cot = cotangent[:, 0]
    deal = dealing[:, 0]
    length = lengths[:, 0]
    route = routes[:, 0]

    extras = jnp.concatenate(
        [w_router, norm_first[:, None], norm_second[:, None]], axis=1
    )
    extras = jnp.pad(extras, ((0, 0), (0, 128 - extras.shape[1])))
    column_parts = [
        jnp.split(weight, ctx_count, axis=1) for weight in (w_query, w_key, w_value)
    ]
    packs = [
        jnp.concatenate([part[c] for part in column_parts] + [extras], axis=1)
        for c in range(ctx_count)
    ]
    packs = reorder(packs, ctx_index)
    packs = [packs[0]] + [swap(packs[k], "context", k) for k in range(1, ctx_count)]
    packs = jnp.stack(reorder(packs, ctx_index))
    dense = lax.all_gather(packs, ("dp", "experts"), axis=0, tiled=False)
    dense = dense.reshape((dp_count, expert_count) + packs.shape)
    dense = jnp.transpose(dense, (0, 2, 1, 3, 4)).reshape(width, -1)
    qkv_w = dense[:, : 3 * own_width]
    router_w = dense[:, 3 * own_width : 3 * own_width + experts]
    gain_one = dense[:, 3 * own_width + experts].astype(F32)
    gain_two = dense[:, 3 * own_width + experts + 1].astype(F32)
    out_w = lax.all_gather(w_out, ALL, axis=0, tiled=True)

    gate_up = [
        jnp.concatenate([w_gate[0, :, h * half_ff : (h + 1) * half_ff], w_up[0, :, h * half_ff : (h + 1) * half_ff]], axis=1)
        for h in range(2)
    ]
    halves = reorder(gate_up, low)
    gate_blocks = []
    for j in range(plane):
        dp_offset, ctx_offset = j // ctx_count, j % ctx_count
        piece = halves[dp_offset % 2]
        if dp_offset:
            piece = swap(piece, "dp", dp_offset)
        if ctx_offset:
            piece = swap(piece, "context", ctx_offset) if not dp_offset else piece
        gate_blocks.append(piece)
    for j in range(plane):
        dp_offset, ctx_offset = j // ctx_count, j % ctx_count
        if dp_offset and ctx_offset:
            gate_blocks[j] = swap(gate_blocks[dp_offset * ctx_count], "context", ctx_offset)
    gate_up_w = jnp.concatenate(gate_blocks, axis=0)
    down_w = jnp.zeros((half_ff, width), BF16)
    down_rows = w_down.shape[1]
    for ctx_offset in range(ctx_count):
        for core in range(2):
            pairs = down_routes(dp_count, ctx_count, expert_count, core, ctx_offset)
            piece = lax.ppermute(w_down[0], ALL, pairs)
            from_core = jnp.where(low == high, core, 1 - core)
            place = (from_core * ctx_count + (ctx_index ^ ctx_offset)) * down_rows
            down_w = lax.dynamic_update_slice(down_w, piece, (place, 0))

    act_all = jnp.concatenate(
        reorder([act] + [swap(act, "context", k) for k in range(1, ctx_count)], ctx_index), axis=1
    )
    cot_all = jnp.concatenate(
        reorder([cot] + [swap(cot, "context", k) for k in range(1, ctx_count)], ctx_index), axis=1
    )
    position_ids = jnp.arange(seq, dtype=jnp.int32)
    slot_blocks = [
        lax.dynamic_slice_in_dim(deal, (ctx_index ^ k) * rows_dev, rows_dev, axis=1)
        for k in range(ctx_count)
    ]
    hot = [
        (block[:, :, None] == position_ids[None, None, :]).astype(BF16) for block in slot_blocks
    ]
    my_positions = ctx_index * rows_dev + jnp.arange(rows_dev, dtype=jnp.int32)
    hot_mine = [
        (block[:, :, None] == my_positions[None, None, :]).astype(BF16) for block in slot_blocks
    ]
    live = slot_blocks[0] < length[:, None]
    live_rows = live.astype(F32)[:, :, None]
    bucket_hot = (buckets[:, None] == jnp.arange(bucket_count)[None, :]).astype(BF16)
    own_table = lax.dynamic_slice_in_dim(bias_table, ctx_index * heads, heads, axis=1)
    lookup = dot_f32("sb,bh->hs", bucket_hot, own_table)
    lines = jnp.concatenate(
        [lookup[:, :1], jnp.zeros((heads, seq), F32), lookup[:, :0:-1]], axis=1
    )

    rows_all = act_all.astype(F32)
    inverse_one = lax.rsqrt(jnp.mean(rows_all * rows_all, axis=-1, keepdims=True) + epsilon)
    normed = (rows_all * inverse_one * gain_one).astype(BF16)
    qkv = dot_f32("mpd,dw->mpw", normed, qkv_w).astype(BF16)
    mixed_own = attend(qkv, lines, length, heads)
    mixed_parts = [
        dot_f32("msp,mpw->msw", hot[k], mixed_own).astype(BF16) for k in range(ctx_count)
    ]
    mixed_parts = [mixed_parts[0]] + [
        swap(mixed_parts[k], "context", k) for k in range(1, ctx_count)
    ]
    mixed = jnp.concatenate(reorder(mixed_parts, ctx_index), axis=-1)

    rows_in = dot_f32("msp,mpd->msd", hot[0], act_all)
    cot_rows = dot_f32("msp,mpd->msd", hot[0], cot_all)
    branch = dot_f32("msi,io->mso", mixed, out_w)
    hidden = rows_in + branch * live_rows
    inverse_two = lax.rsqrt(jnp.mean(hidden * hidden, axis=-1, keepdims=True) + epsilon)
    normed_two = (hidden * inverse_two * gain_two).astype(BF16)
    logits = dot_f32("msd,de->mse", normed_two, router_w)
    route_hot = (route[..., None] == jnp.arange(experts)).astype(F32)
    chosen = jnp.sum(route_hot * logits[:, :, None, :], axis=3)
    gate_probs = jax.nn.softmax(chosen, axis=-1)

    flat_hot = (route_hot * live_rows[..., None]).reshape(micro, rows_dev * top_count, experts)
    pair_ids = jnp.arange(rows_dev * top_count)
    before = (pair_ids[:, None] > pair_ids[None, :]).astype(BF16)
    earlier = dot_f32("ab,mbe->mae", before, flat_hot.astype(BF16))
    rank = jnp.sum(earlier * flat_hot, axis=2).astype(jnp.int32).reshape(route.shape)
    kept = live[:, :, None] & (rank < capacity)
    target = jnp.where(kept, (route ^ expert_index) * slots + rank, -1)
    place_ids = jnp.arange(experts * slots, dtype=jnp.int32)
    pick = [
        (target[:, None, :, j] == place_ids[None, :, None]) for j in range(top_count)
    ]
    pick_any = functools.reduce(jnp.logical_or, pick).astype(BF16)
    pick_bf = [p.astype(BF16) for p in pick]
    prob_rows = sum(
        jnp.sum(jnp.where(pick[j], gate_probs[:, None, :, j], 0.0), axis=2)
        for j in range(top_count)
    )

    def by_expert(value):
        shaped = value.reshape((micro, experts, slots) + value.shape[2:])
        return jnp.moveaxis(shaped, 1, 0)

    def exchange(value):
        parts = [value[0]] + [swap(value[k], "experts", k) for k in range(1, expert_count)]
        return jnp.stack(parts)

    normed_rel = reorder_lanes(normed_two, plane, plane_index)
    sent_rows = by_expert(dot_f32("mrs,msd->mrd", pick_any, normed_rel).astype(BF16))
    sent_up = by_expert(
        dot_f32("mrs,msd->mrd", pick_any, cot_rows.astype(BF16)).astype(BF16)
    )
    row_count = expert_count * micro * slots
    own_x = exchange(sent_rows).reshape(row_count, width)
    own_u = exchange(sent_up).reshape(row_count, width)
    own_p = exchange(by_expert(prob_rows)).reshape(row_count, 1)
    own_g = (own_p * own_u.astype(F32)).astype(BF16)

    def core_swap(value):
        blocks = jnp.split(value, plane, axis=-1)
        return jnp.concatenate([blocks[j ^ ctx_count] for j in range(plane)], axis=-1)

    all_x = jnp.concatenate([own_x, core_swap(swap(own_x, "dp", 1))], axis=0)
    all_g = jnp.concatenate([own_g, swap(own_g, "dp", 1)], axis=0)

    pre_up = dot_f32("rd,df->rf", all_x, gate_up_w)
    gelu_value, gelu_slope = gelu_parts(pre_up[:, :half_ff])
    up_part = pre_up[:, half_ff:]
    activated = (gelu_value * up_part).astype(BF16)
    act_grad = dot_f32("rd,fd->rf", all_g, down_w)
    pre_grad = (act_grad * up_part * gelu_slope).astype(BF16)
    up_grad = (act_grad * gelu_value).astype(BF16)
    both_grad = jnp.concatenate([pre_grad, up_grad], axis=1)
    back_part = dot_f32("rf,df->rd", both_grad, gate_up_w)
    out_part = dot_f32("rf,fd->rd", activated, down_w)
    out_own = (
        out_part[:row_count] + swap(out_part[row_count:].astype(BF16), "dp", 1).astype(F32)
    ).astype(BF16)
    back_own = (
        back_part[:row_count]
        + swap(core_swap(back_part[row_count:].astype(BF16)), "dp", 1).astype(F32)
    ).astype(BF16)
    gate_rows = jnp.sum(own_u.astype(F32) * out_own.astype(F32), axis=-1)

    def to_source(value):
        parts = value.reshape((expert_count, micro, slots) + value.shape[1:])
        parts = exchange(parts)
        return jnp.moveaxis(parts, 0, 1).reshape((micro, experts * slots) + value.shape[1:])

    back_rows = to_source(back_own)
    gate_back = to_source(gate_rows)
    out_rows = to_source(out_own)

    gate_up_total = dot_f32("rd,rf->df", all_x, both_grad)
    down_total = dot_f32("rf,rd->fd", activated, all_g)

    gate_up_sums = [0.0, 0.0]
    for j in range(plane):
        dp_offset, ctx_offset = j // ctx_count, j % ctx_count
        block = gate_up_total[j * (width // plane) : (j + 1) * (width // plane)].astype(BF16)
        pairs = [
            (
                (d * ctx_count + c) * expert_count + e,
                ((d ^ dp_offset) * ctx_count + (c ^ ctx_offset)) * expert_count + e,
            )
            for d in range(dp_count)
            for c in range(ctx_count)
            for e in range(expert_count)
        ]
        if j:
            block = lax.ppermute(block, ALL, pairs)
        gate_up_sums[dp_offset % 2] = gate_up_sums[dp_offset % 2] + block.astype(F32)
    first_half, second_half = reorder(gate_up_sums, low)
    grad_gate = jnp.concatenate([first_half[:, :half_ff], second_half[:, :half_ff]], axis=1)
    grad_up = jnp.concatenate([first_half[:, half_ff:], second_half[:, half_ff:]], axis=1)
    grad_down = 0.0
    for ctx_offset in range(ctx_count):
        for core in range(2):
            pairs = down_routes(dp_count, ctx_count, expert_count, core, ctx_offset)
            from_core = jnp.where(low == high, core, 1 - core)
            place = (from_core * ctx_count + (ctx_index ^ ctx_offset)) * down_rows
            piece = lax.dynamic_slice_in_dim(down_total, place, down_rows, axis=0).astype(BF16)
            arrived = lax.ppermute(piece, ALL, [(b, a) for a, b in pairs])
            grad_down = grad_down + arrived.astype(F32)

    pair_out = [dot_f32("mrs,mrd->msd", pick_bf[j], out_rows) for j in range(top_count)]
    final = hidden + sum(gate_probs[:, :, j, None] * pair_out[j] for j in range(top_count))
    final = final.astype(BF16)
    gate_grad = jnp.stack(
        [
            jnp.sum(jnp.where(pick[j], gate_back[:, :, None], 0.0), axis=1)
            for j in range(top_count)
        ],
        axis=-1,
    )
    chosen_grad = gate_probs * (
        gate_grad - jnp.sum(gate_probs * gate_grad, axis=-1, keepdims=True)
    )
    logit_grad = jnp.sum(route_hot * chosen_grad[..., None], axis=2).astype(BF16)
    normed_grad = reorder_lanes(
        dot_f32("mrs,mrd->msd", pick_any, back_rows), plane, plane_index
    ) + dot_f32("mse,de->msd", logit_grad, router_w)
    router_total = dot_f32("msd,mse->de", normed_two, logit_grad)
    hidden_norm_grad, second_total = norm_pull(hidden, inverse_two, gain_two, normed_grad)
    hidden_grad = cot_rows + hidden_norm_grad
    branch_grad = (hidden_grad * live_rows).astype(BF16)
    hidden_low = hidden_grad.astype(BF16)
    out_total = dot_f32("msi,mso->io", mixed, branch_grad)
    mixed_grad = dot_f32("mso,io->msi", branch_grad, out_w).astype(BF16)
    grad_parts = reorder(jnp.split(mixed_grad, ctx_count, axis=-1), ctx_index)
    grad_parts = [grad_parts[0]] + [
        swap(grad_parts[k], "context", k) for k in range(1, ctx_count)
    ]
    mixed_back = sum(
        dot_f32("msp,msw->mpw", hot[k], grad_parts[k]) for k in range(ctx_count)
    ).astype(BF16)
    qkv_grad, diagonals = attend_back(qkv, mixed_back, lines, length, heads)
    qkv_total = dot_f32("mpd,mpw->dw", normed, qkv_grad)
    first_part = dot_f32("mpw,dw->mpd", qkv_grad, qkv_w)
    first_total = jnp.sum(first_part * rows_all * inverse_one, axis=(0, 1))
    blocks = [
        lax.dynamic_slice_in_dim(first_part, (ctx_index ^ k) * rows_dev, rows_dev, axis=1)
        for k in range(ctx_count)
    ]
    first_grad = blocks[0] + sum(
        swap(blocks[k].astype(BF16), "context", k).astype(F32) for k in range(1, ctx_count)
    )

    def to_positions(value):
        parts = [value] + [swap(value, "context", k) for k in range(1, ctx_count)]
        return sum(dot_f32("msp,msd->mpd", hot_mine[k], parts[k]) for k in range(ctx_count))

    rows_mine = act.astype(F32)
    inverse_mine = lax.rsqrt(jnp.mean(rows_mine * rows_mine, axis=-1, keepdims=True) + epsilon)
    rows_back, _ = norm_pull(rows_mine, inverse_mine, gain_one, first_grad)
    grad_input = (to_positions(hidden_low) + rows_back).astype(BF16)[:, None]
    output = to_positions(final).astype(BF16)[:, None]

    if tuned:
        small = jnp.concatenate(
            [router_total, second_total[:, None], first_total[:, None]], axis=1
        )
        small = jnp.pad(small, ((0, 0), (0, 128 - small.shape[1]))).astype(BF16)
        grad_query, grad_key, grad_value, grad_out, small_sum, diag_all = reduce_dense(
            qkv_total.astype(BF16), out_total.astype(BF16), small, diagonals, own_width
        )
        grad_router = small_sum[:, :experts]
        grad_second = small_sum[:, experts]
        grad_first = small_sum[:, experts + 1]
        diag_all = diag_all.reshape((head_count, -1))
    else:
        sums = plain_sums(
            qkv_total, out_total, router_total, first_total, second_total, own_width
        )
        grad_query, grad_key, grad_value, grad_out, grad_router, grad_first, grad_second = sums
        diag_all = lax.all_gather(
            lax.psum(diagonals, ("dp", "experts")), "context", axis=0, tiled=True
        )
    offsets = jnp.concatenate([diag_all[:, :1], diag_all[:, : seq : -1]], axis=1)
    grad_table = jnp.einsum(
        "hs,sb->bh", offsets, bucket_hot.astype(F32), precision=lax.Precision.HIGHEST
    )
    return (
        output,
        grad_input,
        grad_query,
        grad_key,
        grad_value,
        grad_out,
        grad_router,
        grad_first,
        grad_second,
        grad_table,
        grad_gate[None],
        grad_up[None],
        grad_down[None],
    )


def solution(mesh):
    tokens = P(None, ("dp", "experts"), "context", None)
    sequences = P(None, ("dp", "experts"))
    rows = P(("dp", "context", "experts"), None)
    gains = P(("dp", "context", "experts"))
    experts = P("experts", ("dp", "context"), None)
    placed = (
        (tokens, tokens, P(None, ("dp", "experts"), None), sequences, tokens, P())
        + (rows,) * 5
        + (gains, gains, P())
        + (experts,) * 3
    )
    return jax.shard_map(
        body,
        mesh=mesh,
        in_specs=placed,
        out_specs=(tokens, tokens) + (rows,) * 5 + (gains, gains, P()) + (experts,) * 3,
        check_vma=False,
    )
```

```python
import functools

import jax
import jax.numpy as jnp
from jax import lax
from jax.experimental import pallas as pl
from jax.experimental.pallas import tpu as pltpu
from jax.sharding import PartitionSpec as P

epsilon = 1e-06
masked_score = -1e30
ALL = ("dp", "context", "experts")
F32 = jnp.float32
BF16 = jnp.bfloat16


def dot_f32(spec, left, right):
    return jnp.einsum(spec, left, right, preferred_element_type=F32)


def swap(value, axis, offset):
    size = lax.axis_size(axis)
    return lax.ppermute(value, axis, [(i, i ^ offset) for i in range(size)])


def reorder(pieces, index):
    pieces = list(pieces)
    bit = 1
    while bit < len(pieces):
        flag = (index // bit) % 2 == 1
        pieces = [jnp.where(flag, pieces[j ^ bit], pieces[j]) for j in range(len(pieces))]
        bit *= 2
    return pieces


def reorder_lanes(value, blocks, index):
    return jnp.concatenate(reorder(jnp.split(value, blocks, axis=-1), index), axis=-1)


def toeplitz_bias(line, size):
    rows = jnp.broadcast_to(line, (size, 2 * size))
    return pltpu.roll(rows, 0, 1, stride=1, stride_axis=0)[:, :size]


def masked_scores(query, key, line, length, scale):
    size = query.shape[0]
    scores = lax.dot_general(query, key, (((1,), (1,)), ((), ())), preferred_element_type=F32)
    scores = scores * scale + toeplitz_bias(line, size)
    row_id = lax.broadcasted_iota(jnp.int32, (size, size), 0)
    col_id = lax.broadcasted_iota(jnp.int32, (size, size), 1)
    allowed = (row_id >= col_id) & (col_id < length)
    return jnp.where(allowed, scores, masked_score)


def soft(scores):
    top_score = jnp.max(scores, axis=-1, keepdims=True)
    raised = jnp.exp(scores - top_score)
    return raised / jnp.sum(raised, axis=-1, keepdims=True)


def attend_kernel(heads, head_size, length_ref, line_ref, qkv_ref, mixed_ref):
    scale = head_size ** (-0.5)
    width = heads * head_size
    length = length_ref[pl.program_id(0)]
    for head in range(heads):
        query = qkv_ref[0, :, head * head_size : (head + 1) * head_size]
        key = qkv_ref[0, :, width + head * head_size : width + (head + 1) * head_size]
        value = qkv_ref[0, :, 2 * width + head * head_size : 2 * width + (head + 1) * head_size]
        scores = masked_scores(query, key, line_ref[head : head + 1, :], length, scale)
        probs = soft(scores).astype(BF16)
        mixed = jnp.dot(probs, value, preferred_element_type=F32)
        mixed_ref[0, :, head * head_size : (head + 1) * head_size] = mixed.astype(BF16)


def attend(qkv, lines, lengths, heads):
    micro, seq, width = qkv.shape
    width = width // 3
    head_size = width // heads
    return pl.pallas_call(
        functools.partial(attend_kernel, heads, head_size),
        grid=(micro,),
        out_shape=jax.ShapeDtypeStruct((micro, seq, width), BF16),
        in_specs=[
            pl.BlockSpec(memory_space=pltpu.SMEM),
            pl.BlockSpec(lines.shape, lambda i: (0, 0)),
            pl.BlockSpec((1, seq, 3 * width), lambda i: (i, 0, 0)),
        ],
        out_specs=pl.BlockSpec((1, seq, width), lambda i: (i, 0, 0)),
        compiler_params=pltpu.CompilerParams(vmem_limit_bytes=32 * 2**20),
    )(lengths, lines, qkv)


def diagonal_sums(grad):
    size = grad.shape[0]
    wide = jnp.concatenate([grad, jnp.zeros_like(grad)], axis=1)
    rows = size
    while rows > 1:
        rows //= 2
        lower = pltpu.roll(wide[rows:], 2 * size - rows, 1)
        wide = wide[:rows] + lower
    return wide


def attend_back_kernel(
    heads, head_size, length_ref, line_ref, qkv_ref, grad_ref, out_ref, diag_ref
):
    scale = head_size ** (-0.5)
    width = heads * head_size
    length = length_ref[pl.program_id(0)]

    @pl.when(pl.program_id(0) == 0)
    def _():
        diag_ref[...] = jnp.zeros_like(diag_ref)

    for head in range(heads):
        at = [
            slice(part * width + head * head_size, part * width + (head + 1) * head_size)
            for part in range(3)
        ]
        query, key, value = (qkv_ref[0, :, part] for part in at)
        grad = grad_ref[0, :, at[0]]
        scores = masked_scores(query, key, line_ref[head : head + 1, :], length, scale)
        probs = soft(scores)
        prob_grad = lax.dot_general(
            grad, value, (((1,), (1,)), ((), ())), preferred_element_type=F32
        )
        delta = jnp.sum(probs * prob_grad, axis=-1, keepdims=True)
        score_grad = (probs * (prob_grad - delta)).astype(BF16)
        diag_ref[head : head + 1, :] += diagonal_sums(score_grad.astype(F32))
        query_grad = jnp.dot(score_grad, key, preferred_element_type=F32) * scale
        key_grad = (
            lax.dot_general(
                score_grad, query, (((0,), (0,)), ((), ())), preferred_element_type=F32
            )
            * scale
        )
        value_grad = lax.dot_general(
            probs.astype(BF16), grad, (((0,), (0,)), ((), ())), preferred_element_type=F32
        )
        out_ref[0, :, at[0]] = query_grad.astype(BF16)
        out_ref[0, :, at[1]] = key_grad.astype(BF16)
        out_ref[0, :, at[2]] = value_grad.astype(BF16)


def attend_back(qkv, grad, lines, lengths, heads):
    micro, seq, width = grad.shape
    head_size = width // heads
    return pl.pallas_call(
        functools.partial(attend_back_kernel, heads, head_size),
        grid=(micro,),
        out_shape=(
            jax.ShapeDtypeStruct(qkv.shape, BF16),
            jax.ShapeDtypeStruct(lines.shape, F32),
        ),
        in_specs=[
            pl.BlockSpec(memory_space=pltpu.SMEM),
            pl.BlockSpec(lines.shape, lambda i: (0, 0)),
            pl.BlockSpec((1, seq, 3 * width), lambda i: (i, 0, 0)),
            pl.BlockSpec((1, seq, width), lambda i: (i, 0, 0)),
        ],
        out_specs=(
            pl.BlockSpec((1, seq, 3 * width), lambda i: (i, 0, 0)),
            pl.BlockSpec(lines.shape, lambda i: (0, 0)),
        ),
        compiler_params=pltpu.CompilerParams(vmem_limit_bytes=32 * 2**20),
    )(lengths, lines, qkv, grad)


def halve(value, axis, bit, flag):
    kept = jnp.where(flag, value[1], value[0])
    sent = jnp.where(flag, value[0], value[1]).astype(BF16)
    return kept + swap(sent, axis, bit).astype(F32)


def scatter_sum(value, dp_index, expert_index):
    dp_count, ctx_count, expert_count = value.shape[:3]
    rest = value.shape[3:]
    count, bit = dp_count, 1
    while count > 1:
        shaped = value.reshape((count // 2, 2, -1))
        value = halve(jnp.moveaxis(shaped, 1, 0), "dp", bit, (dp_index // bit) % 2 == 1)
        count //= 2
        bit *= 2
    value = value.reshape((ctx_count, expert_count) + rest)
    count, bit = expert_count, 1
    while count > 1:
        shaped = value.reshape((ctx_count, count // 2, 2) + rest)
        value = halve(jnp.moveaxis(shaped, 2, 0), "experts", bit, (expert_index // bit) % 2 == 1)
        count //= 2
        bit *= 2
    return value.reshape((ctx_count,) + rest)


MESH = pl.DeviceIdType.MESH


def flip(index, bit):
    return index + bit - 2 * bit * ((index // bit) % 2)


def greet(targets):
    barrier = pltpu.get_barrier_semaphore()
    for target in targets:
        pl.semaphore_signal(barrier, inc=1, device_id=target, device_id_type=MESH)
    pl.semaphore_wait(barrier, len(targets))


def remote(source, place, sends, receives, target):
    return pltpu.make_async_remote_copy(
        src_ref=source,
        dst_ref=place,
        send_sem=sends,
        recv_sem=receives,
        device_id=target,
        device_id_type=MESH,
    )


def reduce_kernel(
    own_width,
    qkv_ref,
    out_ref,
    small_ref,
    diag_ref,
    query_out,
    key_out,
    value_out,
    out_out,
    small_out,
    diag_out,
    *scratch,
):
    dp, ctx, exp = (lax.axis_index(name) for name in ALL)
    high, low = dp // 2, dp % 2
    z_high, z_low = exp // 2, exp % 2
    peers = [
        (flip(dp, 1), ctx, exp),
        (flip(dp, 2), ctx, exp),
        (dp, ctx, flip(exp, 1)),
        (dp, ctx, flip(exp, 2)),
        (dp, 1 - ctx, exp),
    ]
    chunks = []
    for c in range(3):
        chunks.append((qkv_ref, c * own_width, own_width))
    width = out_ref.shape[-1]
    for c in range(width // own_width):
        chunks.append((out_ref, c * own_width, own_width))
    chunks.append((small_ref, 0, small_ref.shape[-1]))
    count = len(chunks)
    per = 9
    bufs = [scratch[i * per : (i + 1) * per] for i in range(count)]
    diag_buf, sends, receives, diag_sends, diag_receives = scratch[count * per :]
    greet(peers)

    flying = []

    def launch(i, stage, source, place):
        copy = remote(source, place, sends.at[i, stage], receives.at[i, stage], peers[stage])
        copy.start()
        flying.append(copy)
        return copy

    copies = {}
    for i, (ref, start, size) in enumerate(chunks):
        copies[i, 0] = launch(
            i, 0, ref.at[:, 1 - low, :, start : start + size], bufs[i][0]
        )
    diag_buf[0] = diag_ref[...]
    diag_copies = []

    def diag_step(stage):
        if stage:
            diag_copies[stage - 1].wait_recv()
        if stage and stage < 5:
            diag_buf[2 * stage] = diag_buf[2 * stage - 2] + diag_buf[2 * stage - 1]
        if stage < 5:
            copy = remote(
                diag_buf.at[2 * stage],
                diag_buf.at[2 * stage + 1],
                diag_sends.at[stage],
                diag_receives.at[stage],
                peers[stage],
            )
            copy.start()
            diag_copies.append(copy)
            flying.append(copy)

    def advance(i, stage):
        ref, start, size = chunks[i]
        recv_a, send_b, recv_b, send_c, recv_c, send_d, recv_d, send_e, recv_e = bufs[i]
        copies[i, stage].wait_recv()
        if stage == 0:
            send_b[...] = (
                ref[1 - high, low, :, start : start + size].astype(F32)
                + recv_a[1 - high].astype(F32)
            ).astype(BF16)
            copies[i, 1] = launch(i, 1, send_b, recv_b)
        elif stage == 1:
            total = (
                ref[high, low, :, start : start + size].astype(F32)
                + recv_a[high].astype(F32)
                + recv_b[...].astype(F32)
            ).astype(BF16)
            send_c[...] = total.reshape(send_c.shape)
            copies[i, 2] = launch(i, 2, send_c.at[:, :, 1 - z_low], recv_c)
        elif stage == 2:
            send_d[...] = (
                send_c[:, :, z_low].astype(F32) + recv_c[...].astype(F32)
            ).astype(BF16)
            copies[i, 3] = launch(i, 3, send_d.at[:, 1 - z_high], recv_d)
        elif stage == 3:
            send_e[...] = (send_d[:, z_high].astype(F32) + recv_d[...].astype(F32)).astype(BF16)
            copies[i, 4] = launch(i, 4, send_e.at[1 - ctx], recv_e)
        else:
            mine, other = send_e[ctx].astype(F32), recv_e[...].astype(F32)
            if i < 3:
                place = (query_out, key_out, value_out)[i]
                place[:, pl.ds(pl.multiple_of(ctx * size, 128), size)] = mine
                place[:, pl.ds(pl.multiple_of((1 - ctx) * size, 128), size)] = other
            elif ref is out_ref:
                out_out[:, start : start + size] = mine + other
            else:
                small_out[...] = mine + other

    for step in range(count + 4):
        if step < 6:
            diag_step(step)
        for stage in range(4, -1, -1):
            if 0 <= step - stage < count:
                advance(step - stage, stage)
    diag_out[ctx] = diag_buf[8]
    diag_out[1 - ctx] = diag_buf[9]
    for copy in flying:
        copy.wait_send()


def reduce_dense(qkv_total, out_total, small, diagonals, own_width):
    rows, width = out_total.shape
    dp_count, ctx_count, expert_count = (lax.axis_size(name) for name in ALL)
    per_row = rows // (dp_count * ctx_count * expert_count)
    shaped = lambda v: v.reshape((2, 2, rows // 4, v.shape[-1]))
    sizes = [own_width] * (3 + width // own_width) + [small.shape[-1]]
    scratch = []
    quarter = rows // 4
    for size in sizes:
        scratch += [
            pltpu.VMEM((2, quarter, size), BF16),
            pltpu.VMEM((quarter, size), BF16),
            pltpu.VMEM((quarter, size), BF16),
            pltpu.VMEM((2, 2, 2, per_row, size), BF16),
            pltpu.VMEM((2, 2, per_row, size), BF16),
            pltpu.VMEM((2, 2, per_row, size), BF16),
            pltpu.VMEM((2, per_row, size), BF16),
            pltpu.VMEM((2, per_row, size), BF16),
            pltpu.VMEM((per_row, size), BF16),
        ]
    scratch += [
        pltpu.VMEM((10,) + diagonals.shape, F32),
        pltpu.SemaphoreType.DMA((len(sizes), 5)),
        pltpu.SemaphoreType.DMA((len(sizes), 5)),
        pltpu.SemaphoreType.DMA((5,)),
        pltpu.SemaphoreType.DMA((5,)),
    ]
    whole = pl.BlockSpec(memory_space=pltpu.VMEM)
    return pl.pallas_call(
        functools.partial(reduce_kernel, own_width),
        out_shape=tuple(jax.ShapeDtypeStruct((per_row, width), F32) for _ in range(4))
        + (
            jax.ShapeDtypeStruct((per_row, small.shape[-1]), F32),
            jax.ShapeDtypeStruct((2,) + diagonals.shape, F32),
        ),
        in_specs=[whole] * 4,
        out_specs=(whole,) * 6,
        scratch_shapes=scratch,
        compiler_params=pltpu.CompilerParams(
            collective_id=0, has_side_effects=True, vmem_limit_bytes=48 * 2**20
        ),
    )(shaped(qkv_total), shaped(out_total), shaped(small), diagonals)


def plain_sums(qkv_total, out_total, router_total, first_total, second_total, own_width):
    width, experts = router_total.shape
    dp_count, ctx_count, expert_count = (lax.axis_size(name) for name in ALL)
    dp_index, ctx_index, expert_index = (lax.axis_index(name) for name in ALL)
    owners = (dp_count, ctx_count, expert_count, -1)
    out_pack = jnp.concatenate([out_total, router_total, second_total[:, None]], axis=1)
    out_pack = jnp.pad(out_pack, ((0, 0), (0, width + 128 - out_pack.shape[1])))
    out_pack = scatter_sum(
        out_pack.reshape(owners + (out_pack.shape[1],)), dp_index, expert_index
    )
    qkv_pack = jnp.pad(
        jnp.concatenate([qkv_total, first_total[:, None]], axis=1), ((0, 0), (0, 127))
    )
    qkv_pack = scatter_sum(
        qkv_pack.reshape(owners + (qkv_pack.shape[1],)), dp_index, expert_index
    )

    def across(value):
        parts = reorder([value[c] for c in range(ctx_count)], ctx_index)
        return [parts[0]] + [
            swap(parts[k].astype(BF16), "context", k).astype(F32) for k in range(1, ctx_count)
        ]

    out_sum = sum(across(out_pack))
    qkv_parts = across(qkv_pack)
    grad_first = sum(part[:, 3 * own_width] for part in qkv_parts)
    qkv_parts = reorder(qkv_parts, ctx_index)
    grads = tuple(
        jnp.concatenate(
            [part[:, i * own_width : (i + 1) * own_width] for part in qkv_parts], axis=1
        )
        for i in range(3)
    )
    return grads + (
        out_sum[:, :width],
        out_sum[:, width : width + experts],
        grad_first,
        out_sum[:, width + experts],
    )


def norm_pull(features, inverse, gain, grad):
    lifted = gain * grad
    mean_part = jnp.mean(lifted * features, axis=-1, keepdims=True)
    back = inverse * lifted - features * (inverse * inverse * inverse) * mean_part
    gain_grad = jnp.sum(grad * features * inverse, axis=(0, 1))
    return back, gain_grad


def gelu_parts(pre):
    root = 0.7978845608028654
    cubic = 0.044715
    square = pre * pre
    wave = jnp.tanh(root * (pre + cubic * pre * square))
    value = 0.5 * pre * (1.0 + wave)
    slope = 0.5 * (1.0 + wave) + 0.5 * pre * (1.0 - wave * wave) * root * (
        1.0 + 3.0 * cubic * square
    )
    return value, slope


def down_routes(dp_count, ctx_count, expert_count, core, ctx_offset):
    pairs = []
    for dp in range(dp_count):
        for ctx in range(ctx_count):
            for expert in range(expert_count):
                high, low = dp // 2, dp % 2
                to_high = high if low == core else high ^ 1
                target = ((to_high * 2 + high) * ctx_count + (ctx ^ ctx_offset)) * expert_count
                pairs.append(((dp * ctx_count + ctx) * expert_count + expert, target + expert))
    return pairs


def plain_body(
    activations,
    cotangent,
    dealing,
    lengths,
    routes,
    buckets,
    w_query,
    w_key,
    w_value,
    w_out,
    w_router,
    norm_first,
    norm_second,
    bias_table,
    w_gate,
    w_up,
    w_down,
):
    micro, _, rows_dev, width = activations.shape
    seq = dealing.shape[2]
    bucket_count, head_count = bias_table.shape
    dp_count, ctx_count, expert_count = (lax.axis_size(name) for name in ALL)
    dp_index, ctx_index, expert_index = (lax.axis_index(name) for name in ALL)
    high, low = dp_index // 2, dp_index % 2
    heads = head_count // ctx_count
    head_size = width // head_count
    own_width = heads * head_size
    experts = w_router.shape[1]
    top_count = routes.shape[3]
    capacity = (5 * rows_dev * top_count + 4 * experts - 1) // (4 * experts)
    slots = -(-capacity // 16) * 16
    ff = w_gate.shape[2]
    half_ff = ff // 2
    weight_rows = w_query.shape[0]
    plane = dp_count * ctx_count
    plane_index = dp_index * ctx_count + ctx_index
    act = activations[:, 0]
    cot = cotangent[:, 0]
    deal = dealing[:, 0]
    length = lengths[:, 0]
    route = routes[:, 0]

    extras = jnp.concatenate(
        [w_router, norm_first[:, None], norm_second[:, None]], axis=1
    )
    extras = jnp.pad(extras, ((0, 0), (0, 128 - extras.shape[1])))
    column_parts = [
        jnp.split(weight, ctx_count, axis=1) for weight in (w_query, w_key, w_value)
    ]
    packs = [
        jnp.concatenate([part[c] for part in column_parts] + [extras], axis=1)
        for c in range(ctx_count)
    ]
    packs = reorder(packs, ctx_index)
    packs = [packs[0]] + [swap(packs[k], "context", k) for k in range(1, ctx_count)]
    packs = jnp.stack(reorder(packs, ctx_index))
    dense = lax.all_gather(packs, ("dp", "experts"), axis=0, tiled=False)
    dense = dense.reshape((dp_count, expert_count) + packs.shape)
    dense = jnp.transpose(dense, (0, 2, 1, 3, 4)).reshape(width, -1)
    qkv_w = dense[:, : 3 * own_width]
    router_w = dense[:, 3 * own_width : 3 * own_width + experts]
    gain_one = dense[:, 3 * own_width + experts].astype(F32)
    gain_two = dense[:, 3 * own_width + experts + 1].astype(F32)
    out_w = lax.all_gather(w_out, ALL, axis=0, tiled=True)

    gate_up = [
        jnp.concatenate([w_gate[0, :, h * half_ff : (h + 1) * half_ff], w_up[0, :, h * half_ff : (h + 1) * half_ff]], axis=1)
        for h in range(2)
    ]
    halves = reorder(gate_up, low)
    gate_blocks = []
    for j in range(plane):
        dp_offset, ctx_offset = j // ctx_count, j % ctx_count
        piece = halves[dp_offset % 2]
        if dp_offset:
            piece = swap(piece, "dp", dp_offset)
        if ctx_offset:
            piece = swap(piece, "context", ctx_offset) if not dp_offset else piece
        gate_blocks.append(piece)
    for j in range(plane):
        dp_offset, ctx_offset = j // ctx_count, j % ctx_count
        if dp_offset and ctx_offset:
            gate_blocks[j] = swap(gate_blocks[dp_offset * ctx_count], "context", ctx_offset)
    gate_up_w = jnp.concatenate(gate_blocks, axis=0)
    down_w = jnp.zeros((half_ff, width), BF16)
    down_rows = w_down.shape[1]
    for ctx_offset in range(ctx_count):
        for core in range(2):
            pairs = down_routes(dp_count, ctx_count, expert_count, core, ctx_offset)
            piece = lax.ppermute(w_down[0], ALL, pairs)
            from_core = jnp.where(low == high, core, 1 - core)
            place = (from_core * ctx_count + (ctx_index ^ ctx_offset)) * down_rows
            down_w = lax.dynamic_update_slice(down_w, piece, (place, 0))

    act_all = jnp.concatenate(
        reorder([act] + [swap(act, "context", k) for k in range(1, ctx_count)], ctx_index), axis=1
    )
    cot_all = jnp.concatenate(
        reorder([cot] + [swap(cot, "context", k) for k in range(1, ctx_count)], ctx_index), axis=1
    )
    position_ids = jnp.arange(seq, dtype=jnp.int32)
    slot_blocks = [
        lax.dynamic_slice_in_dim(deal, (ctx_index ^ k) * rows_dev, rows_dev, axis=1)
        for k in range(ctx_count)
    ]
    hot = [
        (block[:, :, None] == position_ids[None, None, :]).astype(BF16) for block in slot_blocks
    ]
    my_positions = ctx_index * rows_dev + jnp.arange(rows_dev, dtype=jnp.int32)
    hot_mine = [
        (block[:, :, None] == my_positions[None, None, :]).astype(BF16) for block in slot_blocks
    ]
    live = slot_blocks[0] < length[:, None]
    live_rows = live.astype(F32)[:, :, None]
    bucket_hot = (buckets[:, None] == jnp.arange(bucket_count)[None, :]).astype(BF16)
    own_table = lax.dynamic_slice_in_dim(bias_table, ctx_index * heads, heads, axis=1)
    lookup = dot_f32("sb,bh->hs", bucket_hot, own_table)
    lines = jnp.concatenate(
        [lookup[:, :1], jnp.zeros((heads, seq), F32), lookup[:, :0:-1]], axis=1
    )

    rows_all = act_all.astype(F32)
    inverse_one = lax.rsqrt(jnp.mean(rows_all * rows_all, axis=-1, keepdims=True) + epsilon)
    normed = (rows_all * inverse_one * gain_one).astype(BF16)
    qkv = dot_f32("mpd,dw->mpw", normed, qkv_w).astype(BF16)
    mixed_own = attend(qkv, lines, length, heads)
    mixed_parts = [
        dot_f32("msp,mpw->msw", hot[k], mixed_own).astype(BF16) for k in range(ctx_count)
    ]
    mixed_parts = [mixed_parts[0]] + [
        swap(mixed_parts[k], "context", k) for k in range(1, ctx_count)
    ]
    mixed = jnp.concatenate(reorder(mixed_parts, ctx_index), axis=-1)

    rows_in = dot_f32("msp,mpd->msd", hot[0], act_all)
    cot_rows = dot_f32("msp,mpd->msd", hot[0], cot_all)
    branch = dot_f32("msi,io->mso", mixed, out_w)
    hidden = rows_in + branch * live_rows
    inverse_two = lax.rsqrt(jnp.mean(hidden * hidden, axis=-1, keepdims=True) + epsilon)
    normed_two = (hidden * inverse_two * gain_two).astype(BF16)
    logits = dot_f32("msd,de->mse", normed_two, router_w)
    route_hot = (route[..., None] == jnp.arange(experts)).astype(F32)
    chosen = jnp.sum(route_hot * logits[:, :, None, :], axis=3)
    gate_probs = jax.nn.softmax(chosen, axis=-1)

    flat_hot = (route_hot * live_rows[..., None]).reshape(micro, rows_dev * top_count, experts)
    pair_ids = jnp.arange(rows_dev * top_count)
    before = (pair_ids[:, None] > pair_ids[None, :]).astype(BF16)
    earlier = dot_f32("ab,mbe->mae", before, flat_hot.astype(BF16))
    rank = jnp.sum(earlier * flat_hot, axis=2).astype(jnp.int32).reshape(route.shape)
    kept = live[:, :, None] & (rank < capacity)
    target = jnp.where(kept, (route ^ expert_index) * slots + rank, -1)
    place_ids = jnp.arange(experts * slots, dtype=jnp.int32)
    pick = [
        (target[:, None, :, j] == place_ids[None, :, None]) for j in range(top_count)
    ]
    pick_any = functools.reduce(jnp.logical_or, pick).astype(BF16)
    pick_bf = [p.astype(BF16) for p in pick]
    prob_rows = sum(
        jnp.sum(jnp.where(pick[j], gate_probs[:, None, :, j], 0.0), axis=2)
        for j in range(top_count)
    )

    def by_expert(value):
        shaped = value.reshape((micro, experts, slots) + value.shape[2:])
        return jnp.moveaxis(shaped, 1, 0)

    def exchange(value):
        parts = [value[0]] + [swap(value[k], "experts", k) for k in range(1, expert_count)]
        return jnp.stack(parts)

    normed_rel = reorder_lanes(normed_two, plane, plane_index)
    sent_rows = by_expert(dot_f32("mrs,msd->mrd", pick_any, normed_rel).astype(BF16))
    sent_up = by_expert(
        dot_f32("mrs,msd->mrd", pick_any, cot_rows.astype(BF16)).astype(BF16)
    )
    row_count = expert_count * micro * slots
    own_x = exchange(sent_rows).reshape(row_count, width)
    own_u = exchange(sent_up).reshape(row_count, width)
    own_p = exchange(by_expert(prob_rows)).reshape(row_count, 1)
    own_g = (own_p * own_u.astype(F32)).astype(BF16)

    def core_swap(value):
        blocks = jnp.split(value, plane, axis=-1)
        return jnp.concatenate([blocks[j ^ ctx_count] for j in range(plane)], axis=-1)

    all_x = jnp.concatenate([own_x, core_swap(swap(own_x, "dp", 1))], axis=0)
    all_g = jnp.concatenate([own_g, swap(own_g, "dp", 1)], axis=0)

    pre_up = dot_f32("rd,df->rf", all_x, gate_up_w)
    gelu_value, gelu_slope = gelu_parts(pre_up[:, :half_ff])
    up_part = pre_up[:, half_ff:]
    activated = (gelu_value * up_part).astype(BF16)
    act_grad = dot_f32("rd,fd->rf", all_g, down_w)
    pre_grad = (act_grad * up_part * gelu_slope).astype(BF16)
    up_grad = (act_grad * gelu_value).astype(BF16)
    both_grad = jnp.concatenate([pre_grad, up_grad], axis=1)
    back_part = dot_f32("rf,df->rd", both_grad, gate_up_w)
    out_part = dot_f32("rf,fd->rd", activated, down_w)
    out_own = (
        out_part[:row_count] + swap(out_part[row_count:].astype(BF16), "dp", 1).astype(F32)
    ).astype(BF16)
    back_own = (
        back_part[:row_count]
        + swap(core_swap(back_part[row_count:].astype(BF16)), "dp", 1).astype(F32)
    ).astype(BF16)
    gate_rows = jnp.sum(own_u.astype(F32) * out_own.astype(F32), axis=-1)

    def to_source(value):
        parts = value.reshape((expert_count, micro, slots) + value.shape[1:])
        parts = exchange(parts)
        return jnp.moveaxis(parts, 0, 1).reshape((micro, experts * slots) + value.shape[1:])

    back_rows = to_source(back_own)
    gate_back = to_source(gate_rows)
    out_rows = to_source(out_own)

    gate_up_total = dot_f32("rd,rf->df", all_x, both_grad)
    down_total = dot_f32("rf,rd->fd", activated, all_g)

    gate_up_sums = [0.0, 0.0]
    for j in range(plane):
        dp_offset, ctx_offset = j // ctx_count, j % ctx_count
        block = gate_up_total[j * (width // plane) : (j + 1) * (width // plane)].astype(BF16)
        pairs = [
            (
                (d * ctx_count + c) * expert_count + e,
                ((d ^ dp_offset) * ctx_count + (c ^ ctx_offset)) * expert_count + e,
            )
            for d in range(dp_count)
            for c in range(ctx_count)
            for e in range(expert_count)
        ]
        if j:
            block = lax.ppermute(block, ALL, pairs)
        gate_up_sums[dp_offset % 2] = gate_up_sums[dp_offset % 2] + block.astype(F32)
    first_half, second_half = reorder(gate_up_sums, low)
    grad_gate = jnp.concatenate([first_half[:, :half_ff], second_half[:, :half_ff]], axis=1)
    grad_up = jnp.concatenate([first_half[:, half_ff:], second_half[:, half_ff:]], axis=1)
    grad_down = 0.0
    for ctx_offset in range(ctx_count):
        for core in range(2):
            pairs = down_routes(dp_count, ctx_count, expert_count, core, ctx_offset)
            from_core = jnp.where(low == high, core, 1 - core)
            place = (from_core * ctx_count + (ctx_index ^ ctx_offset)) * down_rows
            piece = lax.dynamic_slice_in_dim(down_total, place, down_rows, axis=0).astype(BF16)
            arrived = lax.ppermute(piece, ALL, [(b, a) for a, b in pairs])
            grad_down = grad_down + arrived.astype(F32)

    pair_out = [dot_f32("mrs,mrd->msd", pick_bf[j], out_rows) for j in range(top_count)]
    final = hidden + sum(gate_probs[:, :, j, None] * pair_out[j] for j in range(top_count))
    final = final.astype(BF16)
    gate_grad = jnp.stack(
        [
            jnp.sum(jnp.where(pick[j], gate_back[:, :, None], 0.0), axis=1)
            for j in range(top_count)
        ],
        axis=-1,
    )
    chosen_grad = gate_probs * (
        gate_grad - jnp.sum(gate_probs * gate_grad, axis=-1, keepdims=True)
    )
    logit_grad = jnp.sum(route_hot * chosen_grad[..., None], axis=2).astype(BF16)
    normed_grad = reorder_lanes(
        dot_f32("mrs,mrd->msd", pick_any, back_rows), plane, plane_index
    ) + dot_f32("mse,de->msd", logit_grad, router_w)
    router_total = dot_f32("msd,mse->de", normed_two, logit_grad)
    hidden_norm_grad, second_total = norm_pull(hidden, inverse_two, gain_two, normed_grad)
    hidden_grad = cot_rows + hidden_norm_grad
    branch_grad = (hidden_grad * live_rows).astype(BF16)
    hidden_low = hidden_grad.astype(BF16)
    out_total = dot_f32("msi,mso->io", mixed, branch_grad)
    mixed_grad = dot_f32("mso,io->msi", branch_grad, out_w).astype(BF16)
    grad_parts = reorder(jnp.split(mixed_grad, ctx_count, axis=-1), ctx_index)
    grad_parts = [grad_parts[0]] + [
        swap(grad_parts[k], "context", k) for k in range(1, ctx_count)
    ]
    mixed_back = sum(
        dot_f32("msp,msw->mpw", hot[k], grad_parts[k]) for k in range(ctx_count)
    ).astype(BF16)
    qkv_grad, diagonals = attend_back(qkv, mixed_back, lines, length, heads)
    qkv_total = dot_f32("mpd,mpw->dw", normed, qkv_grad)
    first_part = dot_f32("mpw,dw->mpd", qkv_grad, qkv_w)
    first_total = jnp.sum(first_part * rows_all * inverse_one, axis=(0, 1))
    blocks = [
        lax.dynamic_slice_in_dim(first_part, (ctx_index ^ k) * rows_dev, rows_dev, axis=1)
        for k in range(ctx_count)
    ]
    first_grad = blocks[0] + sum(
        swap(blocks[k].astype(BF16), "context", k).astype(F32) for k in range(1, ctx_count)
    )

    def to_positions(value):
        parts = [value] + [swap(value, "context", k) for k in range(1, ctx_count)]
        return sum(dot_f32("msp,msd->mpd", hot_mine[k], parts[k]) for k in range(ctx_count))

    rows_mine = act.astype(F32)
    inverse_mine = lax.rsqrt(jnp.mean(rows_mine * rows_mine, axis=-1, keepdims=True) + epsilon)
    rows_back, _ = norm_pull(rows_mine, inverse_mine, gain_one, first_grad)
    grad_input = (to_positions(hidden_low) + rows_back).astype(BF16)[:, None]
    output = to_positions(final).astype(BF16)[:, None]

    sums = plain_sums(
        qkv_total, out_total, router_total, first_total, second_total, own_width
    )
    grad_query, grad_key, grad_value, grad_out, grad_router, grad_first, grad_second = sums
    diag_all = lax.all_gather(
        lax.psum(diagonals, ("dp", "experts")), "context", axis=0, tiled=True
    )
    offsets = jnp.concatenate([diag_all[:, :1], diag_all[:, : seq : -1]], axis=1)
    grad_table = jnp.einsum(
        "hs,sb->bh", offsets, bucket_hot.astype(F32), precision=lax.Precision.HIGHEST
    )
    return (
        output,
        grad_input,
        grad_query,
        grad_key,
        grad_value,
        grad_out,
        grad_router,
        grad_first,
        grad_second,
        grad_table,
        grad_gate[None],
        grad_up[None],
        grad_down[None],
    )


class Wires:
    def __init__(self, sends, receives, homes):
        self.sends, self.receives, self.homes = sends, receives, homes
        self.used, self.used_home = 0, 0

    def take(self):
        self.used += 1
        return self.used - 1

    def copy(self, source, place, peer, index):
        return remote(source, place, self.sends.at[index], self.receives.at[index], peer)

    def home(self, source, place):
        copy = pltpu.make_async_copy(source, place, self.homes.at[self.used_home])
        self.used_home += 1
        return copy


class Spread:
    def __init__(self, wires, buf, ctx_axis):
        self.wires, self.buf = wires, buf
        dp, ctx, exp = (lax.axis_index(name) for name in ALL)
        self.high, self.low, self.exp = dp // 2, dp % 2, exp
        self.last = lax.axis_size("experts") - 1
        self.core_peer = (flip(dp, 1), ctx, exp)
        self.x_peer = (flip(dp, 2), ctx, exp)
        self.up_peer = (dp, ctx, jnp.minimum(exp + 1, self.last))
        self.down_peer = (dp, ctx, jnp.maximum(exp - 1, 0))
        self.labels = [(0, 0)] + [(h, d) for h in range(1, self.last + 1) for d in (1, -1)]
        self.z_wire, self.x_wire, self.own_wire, self.far_wire = (
            {label: wires.take() for label in self.labels} for _ in range(4)
        )

    def block(self, label):
        hop, way = label
        return jnp.clip(self.exp - hop * way, 0, self.last) if hop else self.exp

    def when(self, label):
        hop, way = label
        if hop == 0:
            return lambda f: f()
        here = self.exp - hop * way
        return pl.when((here >= 0) & (here <= self.last))

    def can_send(self, label, act):
        hop, way = label
        held = self.exp - (hop - 1) * way
        ahead = self.exp + way
        pl.when((held >= 0) & (held <= self.last) & (ahead >= 0) & (ahead <= self.last))(act)

    def z_copy(self, label):
        hop, way = label
        held = jnp.clip(self.exp - (hop - 1) * way, 0, self.last)
        part = self.buf.at[self.high, self.low, :, held]
        peer = self.up_peer if way == 1 else self.down_peer
        return self.wires.copy(part, part, peer, self.z_wire[label])

    def part_copy(self, label, high, wire, peer):
        part = self.buf.at[high, self.low, :, self.block(label)]
        return self.wires.copy(part, part, peer, wire[label])

    def x_copy(self, label):
        return self.part_copy(label, self.high, self.x_wire, self.x_peer)

    def own_copy(self, label):
        return self.part_copy(label, self.high, self.own_wire, self.core_peer)

    def far_copy(self, label):
        return self.part_copy(label, 1 - self.high, self.far_wire, self.core_peer)

    def spread(self, label):
        self.x_copy(label).start()
        self.own_copy(label).start()

    def begin(self):
        for way in (1, -1):
            self.can_send((1, way), lambda way=way: self.z_copy((1, way)).start())
        self.spread((0, 0))

    def hop(self, hop):
        for way in (1, -1):
            label = (hop, way)

            @self.when(label)
            def _(label=label):
                part = self.buf.at[self.high, self.low, :, self.block(label)]
                self.wires.copy(part, part, self.up_peer, self.z_wire[label]).wait_recv()

            if hop < self.last:
                nxt = (hop + 1, way)
                self.can_send(nxt, lambda nxt=nxt: self.z_copy(nxt).start())

            @self.when(label)
            def _(label=label):
                self.spread(label)

        for label in self.labels:
            if label[0] == hop - 1:
                self.pass_far(label)

    def pass_far(self, label):
        @self.when(label)
        def _():
            self.x_copy(label).wait_recv()
            self.far_copy(label).start()

    def end(self):
        for label in self.labels:
            if label[0] == self.last:
                self.pass_far(label)
        for label in self.labels:

            @self.when(label)
            def _(label=label):
                self.own_copy(label).wait_recv()
                self.far_copy(label).wait_recv()

    def drain(self):
        for label in self.labels:
            if label[0]:
                self.can_send(label, lambda label=label: self.z_copy(label).wait_send())

            @self.when(label)
            def _(label=label):
                self.x_copy(label).wait_send()
                self.own_copy(label).wait_send()
                self.far_copy(label).wait_send()


def front_kernel(
    sizes,
    act_ref,
    cot_ref,
    deal_ref,
    length_ref,
    route_ref,
    line_ref,
    query_ref,
    key_ref,
    value_ref,
    out_ref,
    extra_ref,
    gate_ref,
    up_ref,
    down_ref,
    dense,
    out_w,
    act_all,
    normed_ref,
    qkv_ref,
    mixed,
    hidden_ref,
    logit_ref,
    cot_rows_ref,
    all_x,
    all_u,
    all_p,
    gate_up,
    down,
    cot_all,
    mixed_own,
    mixed_sent,
    sent_x,
    sent_u,
    sent_p,
    sends,
    receives,
    homes,
):
    heads, head_size, experts, capacity, slots = sizes
    micro, rows_dev, width = act_ref.shape
    own_width = heads * head_size
    half = gate_ref.shape[1] // 2
    dp, ctx, exp = (lax.axis_index(name) for name in ALL)
    high, low = dp // 2, dp % 2
    block = dp * 2 + ctx
    core_peer, x_peer, x_core = ((flip(dp, 1), ctx, exp), (flip(dp, 2), ctx, exp), (3 - dp, ctx, exp))
    x_core = (flip(flip(dp, 2), 1), ctx, exp)
    y_peer, y_core = (dp, 1 - ctx, exp), (flip(dp, 1), 1 - ctx, exp)
    z_peers = [None] + [(dp, ctx, flip(exp, 1)), (dp, ctx, flip(exp, 2)), (dp, ctx, 3 - exp)]
    z_index = [exp, flip(exp, 1), flip(exp, 2), 3 - exp]
    greet([core_peer, x_peer, x_core, y_peer, y_core] + z_peers[1:])
    wires = Wires(sends, receives, homes)
    drains = []
    home_copies = []

    def send(source, place, peer):
        copy = wires.copy(source, place, peer, wires.take())
        copy.start()
        drains.append(copy)
        return copy

    def multiple(index, size):
        return pl.ds(pl.multiple_of(index * size, size), size)

    mine, other = multiple(ctx, own_width), multiple(1 - ctx, own_width)
    first = []
    for i, ref in enumerate((query_ref, key_ref, value_ref)):
        place = dense.at[high, low, ctx, exp, :, i * own_width : (i + 1) * own_width]
        first.append(send(ref.at[:, other], place, y_peer))
    first.append(send(extra_ref, dense.at[high, low, ctx, exp, :, 3 * own_width :], y_peer))
    out_first = send(out_ref, out_w.at[high, low, ctx, exp], y_peer)
    here = multiple(ctx, rows_dev)
    act_first = send(act_ref, act_all.at[:, here], y_peer)
    for i, ref in enumerate((query_ref, key_ref, value_ref)):
        dense[high, low, ctx, exp, :, i * own_width : (i + 1) * own_width] = ref[:, mine]
    dense[high, low, ctx, exp, :, 3 * own_width :] = extra_ref[...]
    out_w[high, low, ctx, exp] = out_ref[...]
    act_all[:, here, :] = act_ref[...]
    cot_all[:, here, :] = cot_ref[...]

    spread = Spread(wires, dense, 2)
    spread_out = Spread(wires, out_w, 2)
    for copy in first:
        copy.wait_recv()
    spread.begin()
    cot_first = send(cot_ref, cot_all.at[:, here], y_peer)

    def gate_sends(core, peer):
        cols = multiple(core, half)
        return [
            send(gate_ref.at[:, cols], gate_up.at[block, :, 0:half], peer),
            send(up_ref.at[:, cols], gate_up.at[block, :, half:], peer),
        ]

    for ref, start in ((gate_ref, 0), (up_ref, half)):
        copy = wires.home(ref.at[:, multiple(low, half)], gate_up.at[block, :, start : start + half])
        copy.start()
        home_copies.append(copy)

    spread.hop(1)
    from_core = gate_sends(1 - low, core_peer)
    from_x = gate_sends(low, x_peer)
    from_y = gate_sends(low, y_peer)
    from_x_core = gate_sends(1 - low, x_core)
    from_y_core = gate_sends(1 - low, y_core)

    own_down = low * 2 + ctx
    home_down = wires.home(down_ref, down.at[own_down])
    down_wire = {name: wires.take() for name in ("core", "x", "xc", "y", "yc", "rx", "ry")}
    at_home = low == high

    def down_copy(name, peer, source=None):
        source = down_ref if source is None else source
        return wires.copy(source, down.at[own_down], peer, down_wire[name])

    down_sends = [
        ("core", core_peer, False),
        ("x", x_peer, True),
        ("xc", x_core, False),
        ("y", y_peer, True),
        ("yc", y_core, False),
    ]

    def down_start():
        @pl.when(at_home)
        def _():
            home_down.start()

        for name, peer, straight in down_sends:
            pl.when(at_home == straight)(lambda name=name, peer=peer: down_copy(name, peer).start())

    lane = lax.broadcasted_iota(jnp.int32, (rows_dev, 128), 1)
    lane_f = lane.astype(F32)
    row_id = lax.broadcasted_iota(jnp.int32, (rows_dev, rows_dev), 0)
    col_id = lax.broadcasted_iota(jnp.int32, (rows_dev, rows_dev), 1)
    before = (row_id > col_id).astype(BF16)
    seq = deal_ref.shape[1]
    seq_lane = lax.broadcasted_iota(jnp.int32, (rows_dev, seq), 1)

    def hot(m, k):
        index = ctx if k == 0 else 1 - ctx
        return (deal_ref[m, multiple(index, rows_dev), :] == seq_lane).astype(BF16)

    def live_slots(m):
        return deal_ref[m, here, :] < length_ref[m]

    def ranks(m):
        live = live_slots(m)
        hots = [(route_ref[m, :, j : j + 1] == lane) for j in range(2)]
        used = jnp.where((hots[0] | hots[1]) & live, 1.0, 0.0).astype(BF16)
        earlier = jnp.dot(before, used, preferred_element_type=F32)
        found = []
        for j in range(2):
            rank = jnp.sum(jnp.where(hots[j], earlier, 0.0), axis=1, keepdims=True)
            found.append(jnp.where(live & (rank < capacity), rank, -1.0))
        return found

    def picks(m, k, rank):
        return [
            (route_ref[m, :, j : j + 1] == z_index[k]) & (rank[j] == lane_f) for j in range(2)
        ]

    def as_rows(pick, value):
        chosen = lax.dot_general(
            pick, value, (((0,), (0,)), ((), ())), preferred_element_type=F32
        )
        return chosen[:slots].astype(BF16)

    spread.hop(2)
    rank_of = [ranks(m) for m in range(micro)]
    act_first.wait_recv()
    spread.hop(3)
    cot_first.wait_recv()
    pick_of = {}
    for m in range(micro):
        hot_mine = hot(m, 0)
        cot_rows = jnp.dot(hot_mine, cot_all[m], preferred_element_type=F32).astype(BF16)
        cot_rows_ref[m] = cot_rows
        for k in range(experts):
            pick = picks(m, k, rank_of[m])
            pick_any = jnp.where(pick[0] | pick[1], 1.0, 0.0).astype(BF16)
            rows = as_rows(pick_any, cot_rows)
            if k == 0:
                all_u[0, 0, m] = rows
            else:
                sent_u[k - 1, m] = rows
    out_first.wait_recv()
    spread.end()
    spread_out.begin()

    extras = dense[:, :, :, :, :, 3 * own_width :].reshape(width, 128).astype(F32)
    turned = extras.T
    gain_one, gain_two = turned[experts : experts + 1], turned[experts + 1 : experts + 2]
    for m in range(micro):
        rows = act_all[m].astype(F32)
        inverse = lax.rsqrt(jnp.mean(rows * rows, axis=-1, keepdims=True) + epsilon)
        normed_ref[m] = (rows * inverse * gain_one).astype(BF16)
    for i in range(3):
        weight = dense[:, :, :, :, :, i * own_width : (i + 1) * own_width].reshape(width, own_width)
        for m in range(micro):
            qkv_ref[m, :, i * own_width : (i + 1) * own_width] = jnp.dot(
                normed_ref[m], weight, preferred_element_type=F32
            ).astype(BF16)
    spread_out.hop(1)
    down_start()

    scale = head_size ** (-0.5)
    mixed_first = []
    u_first, u_core = {}, []
    for m in range(micro):
        length = length_ref[m]
        for head in range(heads):
            at = [
                slice(part * own_width + head * head_size, part * own_width + (head + 1) * head_size)
                for part in range(3)
            ]
            scores = masked_scores(
                qkv_ref[m, :, at[0]], qkv_ref[m, :, at[1]], line_ref[head : head + 1, :], length, scale
            )
            probs = soft(scores).astype(BF16)
            mixed_own[:, at[0]] = jnp.dot(
                probs, qkv_ref[m, :, at[2]], preferred_element_type=F32
            ).astype(BF16)
        own = mixed_own[...]
        mixed_sent[m] = jnp.dot(hot(m, 1), own, preferred_element_type=F32).astype(BF16)
        mixed_first.append(send(mixed_sent.at[m], mixed.at[m, :, mine], y_peer))
        mixed[m, :, mine] = jnp.dot(hot(m, 0), own, preferred_element_type=F32).astype(BF16)
        spread_out.hop(2 + m)
        for k in range(1, experts):
            u_first[k, m] = send(sent_u.at[k - 1, m], all_u.at[0, k, m], z_peers[k])
        u_core.append(send(all_u.at[0, 0, m], all_u.at[1, 0, m], core_peer))
    spread_out.end()

    for copy in from_x:
        copy.wait_recv()
    x_block = flip(dp, 2) * 2 + ctx
    relay_y = send(gate_up.at[x_block], gate_up.at[x_block], y_peer)
    for copy in from_y_core:
        copy.wait_recv()
    y_block = flip(dp, 1) * 2 + 1 - ctx
    relay_x = send(gate_up.at[y_block], gate_up.at[y_block], x_peer)

    router_w = dense[:, :, :, :, :, 3 * own_width :].reshape(width, 128)
    x_first, p_first, core_copies = {}, {}, []
    for m in range(micro):
        mixed_first[m].wait_recv()
        branch = jnp.dot(
            mixed[m], out_w[...].reshape(width, width), preferred_element_type=F32
        )
        rows_in = jnp.dot(hot(m, 0), act_all[m], preferred_element_type=F32)
        live = live_slots(m)
        hidden = rows_in + jnp.where(live, branch, 0.0)
        hidden_ref[m] = hidden
        inverse = lax.rsqrt(jnp.mean(hidden * hidden, axis=-1, keepdims=True) + epsilon)
        normed_two = (hidden * inverse * gain_two).astype(BF16)
        logits = jnp.dot(normed_two, router_w, preferred_element_type=F32)
        logit_ref[m] = logits
        chosen = [
            jnp.sum(jnp.where(route_ref[m, :, j : j + 1] == lane, logits, 0.0), axis=1, keepdims=True)
            for j in range(2)
        ]
        top = jnp.maximum(chosen[0], chosen[1])
        raised = [jnp.exp(c - top) for c in chosen]
        total = raised[0] + raised[1]
        gates = [r / total for r in raised]
        for k in range(experts):
            pick = picks(m, k, rank_of[m])
            pick_any = jnp.where(pick[0] | pick[1], 1.0, 0.0).astype(BF16)
            rows = as_rows(pick_any, normed_two)
            weights = jnp.sum(
                jnp.where(pick[0], gates[0], 0.0) + jnp.where(pick[1], gates[1], 0.0),
                axis=0,
                keepdims=True,
            )
            weights = jnp.broadcast_to(weights, (8, 128))
            if k == 0:
                all_x[0, 0, m] = rows
                all_p[0, 0, m] = weights
                core_copies.append(send(all_x.at[0, 0, m], all_x.at[1, 0, m], core_peer))
                core_copies.append(send(all_p.at[0, 0, m], all_p.at[1, 0, m], core_peer))
            else:
                sent_x[k - 1, m] = rows
                sent_p[k - 1, m] = weights
                x_first[k, m] = send(sent_x.at[k - 1, m], all_x.at[0, k, m], z_peers[k])
                p_first[k, m] = send(sent_p.at[k - 1, m], all_p.at[0, k, m], z_peers[k])

    away = jnp.logical_not(at_home)
    rx_place = low * 2 + 1 - ctx
    ry_place = (1 - low) * 2 + ctx

    @pl.when(at_home)
    def _():
        down_copy("y", y_peer).wait_recv()
        wires.copy(down.at[rx_place], down.at[rx_place], x_peer, down_wire["rx"]).start()

    @pl.when(away)
    def _():
        down_copy("xc", x_core).wait_recv()
        wires.copy(down.at[ry_place], down.at[ry_place], y_peer, down_wire["ry"]).start()

    for m in range(micro):
        for k in range(1, experts):
            u_first[k, m].wait_recv()
            u_core.append(send(all_u.at[0, k, m], all_u.at[1, k, m], core_peer))
    for m in range(micro):
        for k in range(1, experts):
            x_first[k, m].wait_recv()
            core_copies.append(send(all_x.at[0, k, m], all_x.at[1, k, m], core_peer))
            p_first[k, m].wait_recv()
            core_copies.append(send(all_p.at[0, k, m], all_p.at[1, k, m], core_peer))

    for copy in from_core + from_y + from_x_core + [relay_x, relay_y] + u_core + core_copies:
        copy.wait_recv()

    @pl.when(at_home)
    def _():
        for name in ("core", "yc"):
            down_copy(name, core_peer).wait_recv()
        home_down.wait()
        down_copy("rx", x_peer).wait_send()

    @pl.when(away)
    def _():
        for name in ("x", "rx", "ry"):
            down_copy(name, core_peer).wait_recv()
        down_copy("ry", y_peer).wait_send()

    for name, peer, straight in down_sends:
        pl.when(at_home == straight)(lambda name=name, peer=peer: down_copy(name, peer).wait_send())
    for copy in home_copies:
        copy.wait()
    for copy in drains:
        copy.wait_send()
    spread.drain()
    spread_out.drain()


def front(sizes, act, cot, deal, length, route, lines, weights, extras, w_gate, w_up, w_down):
    heads, head_size, experts, capacity, slots = sizes
    micro, rows_dev, width = act.shape
    own_width = heads * head_size
    per_row = weights[0].shape[0]
    seq = deal.shape[1]
    half = w_gate.shape[1] // 2
    in_vmem, in_hbm = pl.BlockSpec(memory_space=pltpu.VMEM), pl.BlockSpec(memory_space=pltpu.HBM)
    wide = 3 * own_width + 128
    outs = [
        ((2, 2, 2, 4, per_row, wide), BF16),
        ((2, 2, 2, 4, per_row, width), BF16),
        ((micro, seq, width), BF16),
        ((micro, seq, width), BF16),
        ((micro, seq, 3 * own_width), BF16),
        ((micro, rows_dev, width), BF16),
        ((micro, rows_dev, width), F32),
        ((micro, rows_dev, 128), F32),
        ((micro, rows_dev, width), BF16),
        ((2, experts, micro, slots, width), BF16),
        ((2, experts, micro, slots, width), BF16),
        ((2, experts, micro, 8, 128), F32),
        ((8,) + (w_gate.shape[0], 2 * half), BF16),
        ((4,) + w_down.shape, BF16),
    ]
    return pl.pallas_call(
        functools.partial(front_kernel, sizes),
        out_shape=tuple(jax.ShapeDtypeStruct(*out) for out in outs),
        in_specs=[in_vmem] * 3 + [pl.BlockSpec(memory_space=pltpu.SMEM)] + [in_vmem] * 7 + [in_hbm] * 3,
        out_specs=(in_vmem,) * 12 + (in_hbm,) * 2,
        scratch_shapes=[
            pltpu.VMEM((micro, seq, width), BF16),
            pltpu.VMEM((seq, own_width), BF16),
            pltpu.VMEM((micro, rows_dev, own_width), BF16),
            pltpu.VMEM((experts - 1, micro, slots, width), BF16),
            pltpu.VMEM((experts - 1, micro, slots, width), BF16),
            pltpu.VMEM((experts - 1, micro, 8, 128), F32),
            pltpu.SemaphoreType.DMA((160,)),
            pltpu.SemaphoreType.DMA((160,)),
            pltpu.SemaphoreType.DMA((4,)),
        ],
        compiler_params=pltpu.CompilerParams(
            collective_id=1, has_side_effects=True, vmem_limit_bytes=56 * 2**20
        ),
    )(act, cot, deal[:, :, None], length, route, lines, *weights, extras, w_gate, w_up, w_down)


def tuned_body(
    activations,
    cotangent,
    dealing,
    lengths,
    routes,
    buckets,
    w_query,
    w_key,
    w_value,
    w_out,
    w_router,
    norm_first,
    norm_second,
    bias_table,
    w_gate,
    w_up,
    w_down,
):
    micro, _, rows_dev, width = activations.shape
    seq = dealing.shape[2]
    bucket_count, head_count = bias_table.shape
    dp_count, ctx_count, expert_count = (lax.axis_size(name) for name in ALL)
    dp_index, ctx_index, expert_index = (lax.axis_index(name) for name in ALL)
    high, low = dp_index // 2, dp_index % 2
    heads = head_count // ctx_count
    head_size = width // head_count
    own_width = heads * head_size
    experts = w_router.shape[1]
    top_count = routes.shape[3]
    capacity = (5 * rows_dev * top_count + 4 * experts - 1) // (4 * experts)
    slots = -(-capacity // 16) * 16
    half_ff = w_gate.shape[2] // 2
    down_rows = w_down.shape[1]
    plane = dp_count * ctx_count
    plane_index = dp_index * ctx_count + ctx_index
    act = activations[:, 0]
    cot = cotangent[:, 0]
    deal = dealing[:, 0]
    length = lengths[:, 0]
    route = routes[:, 0]
    extras = jnp.concatenate([w_router, norm_first[:, None], norm_second[:, None]], axis=1)
    extras = jnp.pad(extras, ((0, 0), (0, 128 - extras.shape[1])))
    bucket_hot = (buckets[:, None] == jnp.arange(bucket_count)[None, :]).astype(BF16)
    own_table = lax.dynamic_slice_in_dim(bias_table, ctx_index * heads, heads, axis=1)
    lookup = dot_f32("sb,bh->hs", bucket_hot, own_table)
    lines = jnp.concatenate(
        [lookup[:, :1], jnp.zeros((heads, seq), F32), lookup[:, :0:-1]], axis=1
    )
    (
        dense,
        out_w,
        act_all,
        normed,
        qkv,
        mixed,
        hidden,
        logits,
        cot_low,
        all_x,
        all_u,
        all_p,
        gate_up_w,
        down_w,
    ) = front(
        (heads, head_size, experts, capacity, slots),
        act,
        cot,
        deal,
        length,
        route,
        lines,
        (w_query, w_key, w_value, w_out),
        extras,
        w_gate[0],
        w_up[0],
        w_down[0],
    )
    dense = dense.reshape(width, -1)
    qkv_w = dense[:, : 3 * own_width]
    router_w = dense[:, 3 * own_width : 3 * own_width + experts]
    gain_one = dense[:, 3 * own_width + experts].astype(F32)
    gain_two = dense[:, 3 * own_width + experts + 1].astype(F32)
    out_w = out_w.reshape(width, width)
    gate_up_w = gate_up_w.reshape(width, 2 * half_ff)
    down_w = down_w.reshape(half_ff, width)
    row_count = experts * micro * slots

    all_x = all_x.reshape(2 * row_count, width)
    own_u = all_u[0].reshape(row_count, width)
    all_p = all_p[..., 0, :slots].reshape(2 * row_count, 1)
    all_g = (all_p * all_u.reshape(2 * row_count, width).astype(F32)).astype(BF16)
    pre_up = dot_f32("rd,df->rf", all_x, gate_up_w)
    gelu_value, gelu_slope = gelu_parts(pre_up[:, :half_ff])
    up_part = pre_up[:, half_ff:]
    activated = (gelu_value * up_part).astype(BF16)
    act_grad = dot_f32("rd,fd->rf", all_g, down_w)
    pre_grad = (act_grad * up_part * gelu_slope).astype(BF16)
    up_grad = (act_grad * gelu_value).astype(BF16)
    both_grad = jnp.concatenate([pre_grad, up_grad], axis=1)
    back_part = dot_f32("rf,df->rd", both_grad, gate_up_w)
    out_part = dot_f32("rf,fd->rd", activated, down_w)
    out_own = (
        out_part[:row_count] + swap(out_part[row_count:].astype(BF16), "dp", 1).astype(F32)
    ).astype(BF16)
    back_own = (
        back_part[:row_count] + swap(back_part[row_count:].astype(BF16), "dp", 1).astype(F32)
    ).astype(BF16)
    gate_rows = jnp.sum(own_u.astype(F32) * out_own.astype(F32), axis=-1)

    def to_source(value):
        parts = value.reshape((expert_count, micro, slots) + value.shape[1:])
        parts = [parts[0]] + [swap(parts[k], "experts", k) for k in range(1, expert_count)]
        parts = jnp.stack(parts)
        return jnp.moveaxis(parts, 0, 1).reshape((micro, experts * slots) + value.shape[1:])

    back_rows = to_source(back_own)
    gate_back = to_source(gate_rows)
    out_rows = to_source(out_own)
    gate_up_total = dot_f32("rd,rf->df", all_x, both_grad).astype(BF16)
    down_total = dot_f32("rf,rd->fd", activated, all_g).astype(BF16)

    gate_up_sums = [0.0, 0.0]
    for j in range(plane):
        dp_offset, ctx_offset = j // ctx_count, j % ctx_count
        block = lax.dynamic_slice_in_dim(
            gate_up_total, (plane_index ^ j) * (width // plane), width // plane, axis=0
        )
        pairs = [
            (
                (d * ctx_count + c) * expert_count + e,
                ((d ^ dp_offset) * ctx_count + (c ^ ctx_offset)) * expert_count + e,
            )
            for d in range(dp_count)
            for c in range(ctx_count)
            for e in range(expert_count)
        ]
        if j:
            block = lax.ppermute(block, ALL, pairs)
        gate_up_sums[dp_offset % 2] = gate_up_sums[dp_offset % 2] + block.astype(F32)
    first_half, second_half = reorder(gate_up_sums, low)
    grad_gate = jnp.concatenate([first_half[:, :half_ff], second_half[:, :half_ff]], axis=1)
    grad_up = jnp.concatenate([first_half[:, half_ff:], second_half[:, half_ff:]], axis=1)
    grad_down = 0.0
    for ctx_offset in range(ctx_count):
        for core in range(2):
            pairs = down_routes(dp_count, ctx_count, expert_count, core, ctx_offset)
            from_core = jnp.where(low == high, core, 1 - core)
            place = (from_core * ctx_count + (ctx_index ^ ctx_offset)) * down_rows
            piece = lax.dynamic_slice_in_dim(down_total, place, down_rows, axis=0)
            arrived = lax.ppermute(piece, ALL, [(b, a) for a, b in pairs])
            grad_down = grad_down + arrived.astype(F32)

    position_ids = jnp.arange(seq, dtype=jnp.int32)
    slot_blocks = [
        lax.dynamic_slice_in_dim(deal, (ctx_index ^ k) * rows_dev, rows_dev, axis=1)
        for k in range(ctx_count)
    ]
    hot = [
        (block[:, :, None] == position_ids[None, None, :]).astype(BF16) for block in slot_blocks
    ]
    my_positions = ctx_index * rows_dev + jnp.arange(rows_dev, dtype=jnp.int32)
    hot_mine = [
        (block[:, :, None] == my_positions[None, None, :]).astype(BF16) for block in slot_blocks
    ]
    live = slot_blocks[0] < length[:, None]
    live_rows = live.astype(F32)[:, :, None]
    route_hot = (route[..., None] == jnp.arange(experts)).astype(F32)
    chosen = jnp.sum(route_hot * logits[:, :, None, :experts], axis=3)
    gate_probs = jax.nn.softmax(chosen, axis=-1)
    flat_hot = (route_hot * live_rows[..., None]).reshape(micro, rows_dev * top_count, experts)
    pair_ids = jnp.arange(rows_dev * top_count)
    before = (pair_ids[:, None] > pair_ids[None, :]).astype(BF16)
    earlier = dot_f32("ab,mbe->mae", before, flat_hot.astype(BF16))
    rank = jnp.sum(earlier * flat_hot, axis=2).astype(jnp.int32).reshape(route.shape)
    kept = live[:, :, None] & (rank < capacity)
    target = jnp.where(kept, (route ^ expert_index) * slots + rank, -1)
    place_ids = jnp.arange(experts * slots, dtype=jnp.int32)
    pick = [(target[:, None, :, j] == place_ids[None, :, None]) for j in range(top_count)]
    pick_any = functools.reduce(jnp.logical_or, pick).astype(BF16)
    pick_bf = [p.astype(BF16) for p in pick]

    cot_rows = cot_low.astype(F32)
    inverse_two = lax.rsqrt(jnp.mean(hidden * hidden, axis=-1, keepdims=True) + epsilon)
    normed_two = (hidden * inverse_two * gain_two).astype(BF16)
    pair_out = [dot_f32("mrs,mrd->msd", pick_bf[j], out_rows) for j in range(top_count)]
    final = hidden + sum(gate_probs[:, :, j, None] * pair_out[j] for j in range(top_count))
    final = final.astype(BF16)
    gate_grad = jnp.stack(
        [
            jnp.sum(jnp.where(pick[j], gate_back[:, :, None], 0.0), axis=1)
            for j in range(top_count)
        ],
        axis=-1,
    )
    chosen_grad = gate_probs * (
        gate_grad - jnp.sum(gate_probs * gate_grad, axis=-1, keepdims=True)
    )
    logit_grad = jnp.sum(route_hot * chosen_grad[..., None], axis=2).astype(BF16)
    normed_grad = dot_f32("mrs,mrd->msd", pick_any, back_rows) + dot_f32(
        "mse,de->msd", logit_grad, router_w
    )
    router_total = dot_f32("msd,mse->de", normed_two, logit_grad)
    hidden_norm_grad, second_total = norm_pull(hidden, inverse_two, gain_two, normed_grad)
    hidden_grad = cot_rows + hidden_norm_grad
    branch_grad = (hidden_grad * live_rows).astype(BF16)
    hidden_low = hidden_grad.astype(BF16)
    out_total = dot_f32("msi,mso->io", mixed, branch_grad)
    mixed_grad = dot_f32("mso,io->msi", branch_grad, out_w).astype(BF16)
    grad_parts = reorder(jnp.split(mixed_grad, ctx_count, axis=-1), ctx_index)
    grad_parts = [grad_parts[0]] + [
        swap(grad_parts[k], "context", k) for k in range(1, ctx_count)
    ]
    mixed_back = sum(
        dot_f32("msp,msw->mpw", hot[k], grad_parts[k]) for k in range(ctx_count)
    ).astype(BF16)
    qkv_grad, diagonals = attend_back(qkv, mixed_back, lines, length, heads)
    qkv_total = dot_f32("mpd,mpw->dw", normed, qkv_grad)
    first_part = dot_f32("mpw,dw->mpd", qkv_grad, qkv_w)
    rows_all = act_all.astype(F32)
    inverse_one = lax.rsqrt(jnp.mean(rows_all * rows_all, axis=-1, keepdims=True) + epsilon)
    first_total = jnp.sum(first_part * rows_all * inverse_one, axis=(0, 1))
    blocks = [
        lax.dynamic_slice_in_dim(first_part, (ctx_index ^ k) * rows_dev, rows_dev, axis=1)
        for k in range(ctx_count)
    ]
    first_grad = blocks[0] + sum(
        swap(blocks[k].astype(BF16), "context", k).astype(F32) for k in range(1, ctx_count)
    )

    def to_positions(value):
        parts = [value] + [swap(value, "context", k) for k in range(1, ctx_count)]
        return sum(dot_f32("msp,msd->mpd", hot_mine[k], parts[k]) for k in range(ctx_count))

    rows_mine = act.astype(F32)
    inverse_mine = lax.rsqrt(jnp.mean(rows_mine * rows_mine, axis=-1, keepdims=True) + epsilon)
    rows_back, _ = norm_pull(rows_mine, inverse_mine, gain_one, first_grad)
    grad_input = (to_positions(hidden_low) + rows_back).astype(BF16)[:, None]
    output = to_positions(final).astype(BF16)[:, None]

    small = jnp.concatenate([router_total, second_total[:, None], first_total[:, None]], axis=1)
    small = jnp.pad(small, ((0, 0), (0, 128 - small.shape[1]))).astype(BF16)
    grad_query, grad_key, grad_value, grad_out, small_sum, diag_all = reduce_dense(
        qkv_total.astype(BF16), out_total.astype(BF16), small, diagonals, own_width
    )
    diag_all = diag_all.reshape((head_count, -1))
    offsets = jnp.concatenate([diag_all[:, :1], diag_all[:, : seq : -1]], axis=1)
    grad_table = jnp.einsum(
        "hs,sb->bh", offsets, bucket_hot.astype(F32), precision=lax.Precision.HIGHEST
    )
    return (
        output,
        grad_input,
        grad_query,
        grad_key,
        grad_value,
        grad_out,
        small_sum[:, :experts],
        small_sum[:, experts + 1],
        small_sum[:, experts],
        grad_table,
        grad_gate[None],
        grad_up[None],
        grad_down[None],
    )


def body(*arguments):
    counts = tuple(lax.axis_size(name) for name in ALL)
    activations, w_query, bias_table, w_gate = (arguments[i] for i in (0, 6, 13, 14))
    own_width = activations.shape[3] // counts[1]
    fits = (
        counts == (4, 2, 4)
        and w_gate.shape[0] == 1
        and w_query.shape[0] % 16 == 0
        and own_width % 128 == 0
        and bias_table.shape[1] % counts[1] == 0
        and arguments[4].shape[3] == 2
    )
    return (tuned_body if fits else plain_body)(*arguments)


def solution(mesh):
    tokens = P(None, ("dp", "experts"), "context", None)
    sequences = P(None, ("dp", "experts"))
    rows = P(("dp", "context", "experts"), None)
    gains = P(("dp", "context", "experts"))
    experts = P("experts", ("dp", "context"), None)
    placed = (
        (tokens, tokens, P(None, ("dp", "experts"), None), sequences, tokens, P())
        + (rows,) * 5
        + (gains, gains, P())
        + (experts,) * 3
    )
    return jax.shard_map(
        body,
        mesh=mesh,
        in_specs=placed,
        out_specs=(tokens, tokens) + (rows,) * 5 + (gains, gains, P()) + (experts,) * 3,
        check_vma=False,
    )
```

```python
import functools

import jax
import jax.numpy as jnp
from jax import lax
from jax.experimental import pallas as pl
from jax.experimental.pallas import tpu as pltpu
from jax.sharding import PartitionSpec as P

epsilon = 1e-06
masked_score = -1e30
ALL = ("dp", "context", "experts")
F32 = jnp.float32
BF16 = jnp.bfloat16


def dot_f32(spec, left, right):
    return jnp.einsum(spec, left, right, preferred_element_type=F32)


def swap(value, axis, offset):
    size = lax.axis_size(axis)
    return lax.ppermute(value, axis, [(i, i ^ offset) for i in range(size)])


def reorder(pieces, index):
    pieces = list(pieces)
    bit = 1
    while bit < len(pieces):
        flag = (index // bit) % 2 == 1
        pieces = [jnp.where(flag, pieces[j ^ bit], pieces[j]) for j in range(len(pieces))]
        bit *= 2
    return pieces


def reorder_lanes(value, blocks, index):
    return jnp.concatenate(reorder(jnp.split(value, blocks, axis=-1), index), axis=-1)


def toeplitz_bias(line, size):
    rows = jnp.broadcast_to(line, (size, 2 * size))
    return pltpu.roll(rows, 0, 1, stride=1, stride_axis=0)[:, :size]


def masked_scores(query, key, line, length, scale):
    size = query.shape[0]
    scores = lax.dot_general(query, key, (((1,), (1,)), ((), ())), preferred_element_type=F32)
    scores = scores * scale + toeplitz_bias(line, size)
    row_id = lax.broadcasted_iota(jnp.int32, (size, size), 0)
    col_id = lax.broadcasted_iota(jnp.int32, (size, size), 1)
    allowed = (row_id >= col_id) & (col_id < length)
    return jnp.where(allowed, scores, masked_score)


def soft(scores):
    top_score = jnp.max(scores, axis=-1, keepdims=True)
    raised = jnp.exp(scores - top_score)
    return raised / jnp.sum(raised, axis=-1, keepdims=True)


def attend_kernel(heads, head_size, length_ref, line_ref, qkv_ref, mixed_ref):
    scale = head_size ** (-0.5)
    width = heads * head_size
    length = length_ref[pl.program_id(0)]
    for head in range(heads):
        query = qkv_ref[0, :, head * head_size : (head + 1) * head_size]
        key = qkv_ref[0, :, width + head * head_size : width + (head + 1) * head_size]
        value = qkv_ref[0, :, 2 * width + head * head_size : 2 * width + (head + 1) * head_size]
        scores = masked_scores(query, key, line_ref[head : head + 1, :], length, scale)
        probs = soft(scores).astype(BF16)
        mixed = jnp.dot(probs, value, preferred_element_type=F32)
        mixed_ref[0, :, head * head_size : (head + 1) * head_size] = mixed.astype(BF16)


def attend(qkv, lines, lengths, heads):
    micro, seq, width = qkv.shape
    width = width // 3
    head_size = width // heads
    return pl.pallas_call(
        functools.partial(attend_kernel, heads, head_size),
        grid=(micro,),
        out_shape=jax.ShapeDtypeStruct((micro, seq, width), BF16),
        in_specs=[
            pl.BlockSpec(memory_space=pltpu.SMEM),
            pl.BlockSpec(lines.shape, lambda i: (0, 0)),
            pl.BlockSpec((1, seq, 3 * width), lambda i: (i, 0, 0)),
        ],
        out_specs=pl.BlockSpec((1, seq, width), lambda i: (i, 0, 0)),
        compiler_params=pltpu.CompilerParams(vmem_limit_bytes=32 * 2**20),
    )(lengths, lines, qkv)


def diagonal_sums(grad):
    size = grad.shape[0]
    wide = jnp.concatenate([grad, jnp.zeros_like(grad)], axis=1)
    rows = size
    while rows > 1:
        rows //= 2
        lower = pltpu.roll(wide[rows:], 2 * size - rows, 1)
        wide = wide[:rows] + lower
    return wide


def attend_back_kernel(
    heads, head_size, length_ref, line_ref, qkv_ref, grad_ref, out_ref, diag_ref
):
    scale = head_size ** (-0.5)
    width = heads * head_size
    length = length_ref[pl.program_id(0)]

    @pl.when(pl.program_id(0) == 0)
    def _():
        diag_ref[...] = jnp.zeros_like(diag_ref)

    for head in range(heads):
        at = [
            slice(part * width + head * head_size, part * width + (head + 1) * head_size)
            for part in range(3)
        ]
        query, key, value = (qkv_ref[0, :, part] for part in at)
        grad = grad_ref[0, :, at[0]]
        scores = masked_scores(query, key, line_ref[head : head + 1, :], length, scale)
        probs = soft(scores)
        prob_grad = lax.dot_general(
            grad, value, (((1,), (1,)), ((), ())), preferred_element_type=F32
        )
        delta = jnp.sum(probs * prob_grad, axis=-1, keepdims=True)
        score_grad = (probs * (prob_grad - delta)).astype(BF16)
        diag_ref[head : head + 1, :] += diagonal_sums(score_grad.astype(F32))
        query_grad = jnp.dot(score_grad, key, preferred_element_type=F32) * scale
        key_grad = (
            lax.dot_general(
                score_grad, query, (((0,), (0,)), ((), ())), preferred_element_type=F32
            )
            * scale
        )
        value_grad = lax.dot_general(
            probs.astype(BF16), grad, (((0,), (0,)), ((), ())), preferred_element_type=F32
        )
        out_ref[0, :, at[0]] = query_grad.astype(BF16)
        out_ref[0, :, at[1]] = key_grad.astype(BF16)
        out_ref[0, :, at[2]] = value_grad.astype(BF16)


def attend_back(qkv, grad, lines, lengths, heads):
    micro, seq, width = grad.shape
    head_size = width // heads
    return pl.pallas_call(
        functools.partial(attend_back_kernel, heads, head_size),
        grid=(micro,),
        out_shape=(
            jax.ShapeDtypeStruct(qkv.shape, BF16),
            jax.ShapeDtypeStruct(lines.shape, F32),
        ),
        in_specs=[
            pl.BlockSpec(memory_space=pltpu.SMEM),
            pl.BlockSpec(lines.shape, lambda i: (0, 0)),
            pl.BlockSpec((1, seq, 3 * width), lambda i: (i, 0, 0)),
            pl.BlockSpec((1, seq, width), lambda i: (i, 0, 0)),
        ],
        out_specs=(
            pl.BlockSpec((1, seq, 3 * width), lambda i: (i, 0, 0)),
            pl.BlockSpec(lines.shape, lambda i: (0, 0)),
        ),
        compiler_params=pltpu.CompilerParams(vmem_limit_bytes=32 * 2**20),
    )(lengths, lines, qkv, grad)


def halve(value, axis, bit, flag):
    kept = jnp.where(flag, value[1], value[0])
    sent = jnp.where(flag, value[0], value[1]).astype(BF16)
    return kept + swap(sent, axis, bit).astype(F32)


def scatter_sum(value, dp_index, expert_index):
    dp_count, ctx_count, expert_count = value.shape[:3]
    rest = value.shape[3:]
    count, bit = dp_count, 1
    while count > 1:
        shaped = value.reshape((count // 2, 2, -1))
        value = halve(jnp.moveaxis(shaped, 1, 0), "dp", bit, (dp_index // bit) % 2 == 1)
        count //= 2
        bit *= 2
    value = value.reshape((ctx_count, expert_count) + rest)
    count, bit = expert_count, 1
    while count > 1:
        shaped = value.reshape((ctx_count, count // 2, 2) + rest)
        value = halve(jnp.moveaxis(shaped, 2, 0), "experts", bit, (expert_index // bit) % 2 == 1)
        count //= 2
        bit *= 2
    return value.reshape((ctx_count,) + rest)


MESH = pl.DeviceIdType.MESH


def flip(index, bit):
    return index + bit - 2 * bit * ((index // bit) % 2)


def greet(targets):
    barrier = pltpu.get_barrier_semaphore()
    for target in targets:
        pl.semaphore_signal(barrier, inc=1, device_id=target, device_id_type=MESH)
    pl.semaphore_wait(barrier, len(targets))


def remote(source, place, sends, receives, target):
    return pltpu.make_async_remote_copy(
        src_ref=source,
        dst_ref=place,
        send_sem=sends,
        recv_sem=receives,
        device_id=target,
        device_id_type=MESH,
    )


def plain_sums(qkv_total, out_total, router_total, first_total, second_total, own_width):
    width, experts = router_total.shape
    dp_count, ctx_count, expert_count = (lax.axis_size(name) for name in ALL)
    dp_index, ctx_index, expert_index = (lax.axis_index(name) for name in ALL)
    owners = (dp_count, ctx_count, expert_count, -1)
    out_pack = jnp.concatenate([out_total, router_total, second_total[:, None]], axis=1)
    out_pack = jnp.pad(out_pack, ((0, 0), (0, width + 128 - out_pack.shape[1])))
    out_pack = scatter_sum(
        out_pack.reshape(owners + (out_pack.shape[1],)), dp_index, expert_index
    )
    qkv_pack = jnp.pad(
        jnp.concatenate([qkv_total, first_total[:, None]], axis=1), ((0, 0), (0, 127))
    )
    qkv_pack = scatter_sum(
        qkv_pack.reshape(owners + (qkv_pack.shape[1],)), dp_index, expert_index
    )

    def across(value):
        parts = reorder([value[c] for c in range(ctx_count)], ctx_index)
        return [parts[0]] + [
            swap(parts[k].astype(BF16), "context", k).astype(F32) for k in range(1, ctx_count)
        ]

    out_sum = sum(across(out_pack))
    qkv_parts = across(qkv_pack)
    grad_first = sum(part[:, 3 * own_width] for part in qkv_parts)
    qkv_parts = reorder(qkv_parts, ctx_index)
    grads = tuple(
        jnp.concatenate(
            [part[:, i * own_width : (i + 1) * own_width] for part in qkv_parts], axis=1
        )
        for i in range(3)
    )
    return grads + (
        out_sum[:, :width],
        out_sum[:, width : width + experts],
        grad_first,
        out_sum[:, width + experts],
    )


def norm_pull(features, inverse, gain, grad):
    lifted = gain * grad
    mean_part = jnp.mean(lifted * features, axis=-1, keepdims=True)
    back = inverse * lifted - features * (inverse * inverse * inverse) * mean_part
    gain_grad = jnp.sum(grad * features * inverse, axis=(0, 1))
    return back, gain_grad


def gelu_parts(pre):
    root = 0.7978845608028654
    cubic = 0.044715
    square = pre * pre
    wave = jnp.tanh(root * (pre + cubic * pre * square))
    value = 0.5 * pre * (1.0 + wave)
    slope = 0.5 * (1.0 + wave) + 0.5 * pre * (1.0 - wave * wave) * root * (
        1.0 + 3.0 * cubic * square
    )
    return value, slope


def down_routes(dp_count, ctx_count, expert_count, core, ctx_offset):
    pairs = []
    for dp in range(dp_count):
        for ctx in range(ctx_count):
            for expert in range(expert_count):
                high, low = dp // 2, dp % 2
                to_high = high if low == core else high ^ 1
                target = ((to_high * 2 + high) * ctx_count + (ctx ^ ctx_offset)) * expert_count
                pairs.append(((dp * ctx_count + ctx) * expert_count + expert, target + expert))
    return pairs


def plain_body(
    activations,
    cotangent,
    dealing,
    lengths,
    routes,
    buckets,
    w_query,
    w_key,
    w_value,
    w_out,
    w_router,
    norm_first,
    norm_second,
    bias_table,
    w_gate,
    w_up,
    w_down,
):
    micro, _, rows_dev, width = activations.shape
    seq = dealing.shape[2]
    bucket_count, head_count = bias_table.shape
    dp_count, ctx_count, expert_count = (lax.axis_size(name) for name in ALL)
    dp_index, ctx_index, expert_index = (lax.axis_index(name) for name in ALL)
    high, low = dp_index // 2, dp_index % 2
    heads = head_count // ctx_count
    head_size = width // head_count
    own_width = heads * head_size
    experts = w_router.shape[1]
    top_count = routes.shape[3]
    capacity = (5 * rows_dev * top_count + 4 * experts - 1) // (4 * experts)
    slots = -(-capacity // 16) * 16
    ff = w_gate.shape[2]
    half_ff = ff // 2
    weight_rows = w_query.shape[0]
    plane = dp_count * ctx_count
    plane_index = dp_index * ctx_count + ctx_index
    act = activations[:, 0]
    cot = cotangent[:, 0]
    deal = dealing[:, 0]
    length = lengths[:, 0]
    route = routes[:, 0]

    extras = jnp.concatenate(
        [w_router, norm_first[:, None], norm_second[:, None]], axis=1
    )
    extras = jnp.pad(extras, ((0, 0), (0, 128 - extras.shape[1])))
    column_parts = [
        jnp.split(weight, ctx_count, axis=1) for weight in (w_query, w_key, w_value)
    ]
    packs = [
        jnp.concatenate([part[c] for part in column_parts] + [extras], axis=1)
        for c in range(ctx_count)
    ]
    packs = reorder(packs, ctx_index)
    packs = [packs[0]] + [swap(packs[k], "context", k) for k in range(1, ctx_count)]
    packs = jnp.stack(reorder(packs, ctx_index))
    dense = lax.all_gather(packs, ("dp", "experts"), axis=0, tiled=False)
    dense = dense.reshape((dp_count, expert_count) + packs.shape)
    dense = jnp.transpose(dense, (0, 2, 1, 3, 4)).reshape(width, -1)
    qkv_w = dense[:, : 3 * own_width]
    router_w = dense[:, 3 * own_width : 3 * own_width + experts]
    gain_one = dense[:, 3 * own_width + experts].astype(F32)
    gain_two = dense[:, 3 * own_width + experts + 1].astype(F32)
    out_w = lax.all_gather(w_out, ALL, axis=0, tiled=True)

    gate_up = [
        jnp.concatenate([w_gate[0, :, h * half_ff : (h + 1) * half_ff], w_up[0, :, h * half_ff : (h + 1) * half_ff]], axis=1)
        for h in range(2)
    ]
    halves = reorder(gate_up, low)
    gate_blocks = []
    for j in range(plane):
        dp_offset, ctx_offset = j // ctx_count, j % ctx_count
        piece = halves[dp_offset % 2]
        if dp_offset:
            piece = swap(piece, "dp", dp_offset)
        if ctx_offset:
            piece = swap(piece, "context", ctx_offset) if not dp_offset else piece
        gate_blocks.append(piece)
    for j in range(plane):
        dp_offset, ctx_offset = j // ctx_count, j % ctx_count
        if dp_offset and ctx_offset:
            gate_blocks[j] = swap(gate_blocks[dp_offset * ctx_count], "context", ctx_offset)
    gate_up_w = jnp.concatenate(gate_blocks, axis=0)
    down_w = jnp.zeros((half_ff, width), BF16)
    down_rows = w_down.shape[1]
    for ctx_offset in range(ctx_count):
        for core in range(2):
            pairs = down_routes(dp_count, ctx_count, expert_count, core, ctx_offset)
            piece = lax.ppermute(w_down[0], ALL, pairs)
            from_core = jnp.where(low == high, core, 1 - core)
            place = (from_core * ctx_count + (ctx_index ^ ctx_offset)) * down_rows
            down_w = lax.dynamic_update_slice(down_w, piece, (place, 0))

    act_all = jnp.concatenate(
        reorder([act] + [swap(act, "context", k) for k in range(1, ctx_count)], ctx_index), axis=1
    )
    cot_all = jnp.concatenate(
        reorder([cot] + [swap(cot, "context", k) for k in range(1, ctx_count)], ctx_index), axis=1
    )
    position_ids = jnp.arange(seq, dtype=jnp.int32)
    slot_blocks = [
        lax.dynamic_slice_in_dim(deal, (ctx_index ^ k) * rows_dev, rows_dev, axis=1)
        for k in range(ctx_count)
    ]
    hot = [
        (block[:, :, None] == position_ids[None, None, :]).astype(BF16) for block in slot_blocks
    ]
    my_positions = ctx_index * rows_dev + jnp.arange(rows_dev, dtype=jnp.int32)
    hot_mine = [
        (block[:, :, None] == my_positions[None, None, :]).astype(BF16) for block in slot_blocks
    ]
    live = slot_blocks[0] < length[:, None]
    live_rows = live.astype(F32)[:, :, None]
    bucket_hot = (buckets[:, None] == jnp.arange(bucket_count)[None, :]).astype(BF16)
    own_table = lax.dynamic_slice_in_dim(bias_table, ctx_index * heads, heads, axis=1)
    lookup = dot_f32("sb,bh->hs", bucket_hot, own_table)
    lines = jnp.concatenate(
        [lookup[:, :1], jnp.zeros((heads, seq), F32), lookup[:, :0:-1]], axis=1
    )

    rows_all = act_all.astype(F32)
    inverse_one = lax.rsqrt(jnp.mean(rows_all * rows_all, axis=-1, keepdims=True) + epsilon)
    normed = (rows_all * inverse_one * gain_one).astype(BF16)
    qkv = dot_f32("mpd,dw->mpw", normed, qkv_w).astype(BF16)
    mixed_own = attend(qkv, lines, length, heads)
    mixed_parts = [
        dot_f32("msp,mpw->msw", hot[k], mixed_own).astype(BF16) for k in range(ctx_count)
    ]
    mixed_parts = [mixed_parts[0]] + [
        swap(mixed_parts[k], "context", k) for k in range(1, ctx_count)
    ]
    mixed = jnp.concatenate(reorder(mixed_parts, ctx_index), axis=-1)

    rows_in = dot_f32("msp,mpd->msd", hot[0], act_all)
    cot_rows = dot_f32("msp,mpd->msd", hot[0], cot_all)
    branch = dot_f32("msi,io->mso", mixed, out_w)
    hidden = rows_in + branch * live_rows
    inverse_two = lax.rsqrt(jnp.mean(hidden * hidden, axis=-1, keepdims=True) + epsilon)
    normed_two = (hidden * inverse_two * gain_two).astype(BF16)
    logits = dot_f32("msd,de->mse", normed_two, router_w)
    route_hot = (route[..., None] == jnp.arange(experts)).astype(F32)
    chosen = jnp.sum(route_hot * logits[:, :, None, :], axis=3)
    gate_probs = jax.nn.softmax(chosen, axis=-1)

    flat_hot = (route_hot * live_rows[..., None]).reshape(micro, rows_dev * top_count, experts)
    pair_ids = jnp.arange(rows_dev * top_count)
    before = (pair_ids[:, None] > pair_ids[None, :]).astype(BF16)
    earlier = dot_f32("ab,mbe->mae", before, flat_hot.astype(BF16))
    rank = jnp.sum(earlier * flat_hot, axis=2).astype(jnp.int32).reshape(route.shape)
    kept = live[:, :, None] & (rank < capacity)
    target = jnp.where(kept, (route ^ expert_index) * slots + rank, -1)
    place_ids = jnp.arange(experts * slots, dtype=jnp.int32)
    pick = [
        (target[:, None, :, j] == place_ids[None, :, None]) for j in range(top_count)
    ]
    pick_any = functools.reduce(jnp.logical_or, pick).astype(BF16)
    pick_bf = [p.astype(BF16) for p in pick]
    prob_rows = sum(
        jnp.sum(jnp.where(pick[j], gate_probs[:, None, :, j], 0.0), axis=2)
        for j in range(top_count)
    )

    def by_expert(value):
        shaped = value.reshape((micro, experts, slots) + value.shape[2:])
        return jnp.moveaxis(shaped, 1, 0)

    def exchange(value):
        parts = [value[0]] + [swap(value[k], "experts", k) for k in range(1, expert_count)]
        return jnp.stack(parts)

    normed_rel = reorder_lanes(normed_two, plane, plane_index)
    sent_rows = by_expert(dot_f32("mrs,msd->mrd", pick_any, normed_rel).astype(BF16))
    sent_up = by_expert(
        dot_f32("mrs,msd->mrd", pick_any, cot_rows.astype(BF16)).astype(BF16)
    )
    row_count = expert_count * micro * slots
    own_x = exchange(sent_rows).reshape(row_count, width)
    own_u = exchange(sent_up).reshape(row_count, width)
    own_p = exchange(by_expert(prob_rows)).reshape(row_count, 1)
    own_g = (own_p * own_u.astype(F32)).astype(BF16)

    def core_swap(value):
        blocks = jnp.split(value, plane, axis=-1)
        return jnp.concatenate([blocks[j ^ ctx_count] for j in range(plane)], axis=-1)

    all_x = jnp.concatenate([own_x, core_swap(swap(own_x, "dp", 1))], axis=0)
    all_g = jnp.concatenate([own_g, swap(own_g, "dp", 1)], axis=0)

    pre_up = dot_f32("rd,df->rf", all_x, gate_up_w)
    gelu_value, gelu_slope = gelu_parts(pre_up[:, :half_ff])
    up_part = pre_up[:, half_ff:]
    activated = (gelu_value * up_part).astype(BF16)
    act_grad = dot_f32("rd,fd->rf", all_g, down_w)
    pre_grad = (act_grad * up_part * gelu_slope).astype(BF16)
    up_grad = (act_grad * gelu_value).astype(BF16)
    both_grad = jnp.concatenate([pre_grad, up_grad], axis=1)
    back_part = dot_f32("rf,df->rd", both_grad, gate_up_w)
    out_part = dot_f32("rf,fd->rd", activated, down_w)
    out_own = (
        out_part[:row_count] + swap(out_part[row_count:].astype(BF16), "dp", 1).astype(F32)
    ).astype(BF16)
    back_own = (
        back_part[:row_count]
        + swap(core_swap(back_part[row_count:].astype(BF16)), "dp", 1).astype(F32)
    ).astype(BF16)
    gate_rows = jnp.sum(own_u.astype(F32) * out_own.astype(F32), axis=-1)

    def to_source(value):
        parts = value.reshape((expert_count, micro, slots) + value.shape[1:])
        parts = exchange(parts)
        return jnp.moveaxis(parts, 0, 1).reshape((micro, experts * slots) + value.shape[1:])

    back_rows = to_source(back_own)
    gate_back = to_source(gate_rows)
    out_rows = to_source(out_own)

    gate_up_total = dot_f32("rd,rf->df", all_x, both_grad)
    down_total = dot_f32("rf,rd->fd", activated, all_g)

    gate_up_sums = [0.0, 0.0]
    for j in range(plane):
        dp_offset, ctx_offset = j // ctx_count, j % ctx_count
        block = gate_up_total[j * (width // plane) : (j + 1) * (width // plane)].astype(BF16)
        pairs = [
            (
                (d * ctx_count + c) * expert_count + e,
                ((d ^ dp_offset) * ctx_count + (c ^ ctx_offset)) * expert_count + e,
            )
            for d in range(dp_count)
            for c in range(ctx_count)
            for e in range(expert_count)
        ]
        if j:
            block = lax.ppermute(block, ALL, pairs)
        gate_up_sums[dp_offset % 2] = gate_up_sums[dp_offset % 2] + block.astype(F32)
    first_half, second_half = reorder(gate_up_sums, low)
    grad_gate = jnp.concatenate([first_half[:, :half_ff], second_half[:, :half_ff]], axis=1)
    grad_up = jnp.concatenate([first_half[:, half_ff:], second_half[:, half_ff:]], axis=1)
    grad_down = 0.0
    for ctx_offset in range(ctx_count):
        for core in range(2):
            pairs = down_routes(dp_count, ctx_count, expert_count, core, ctx_offset)
            from_core = jnp.where(low == high, core, 1 - core)
            place = (from_core * ctx_count + (ctx_index ^ ctx_offset)) * down_rows
            piece = lax.dynamic_slice_in_dim(down_total, place, down_rows, axis=0).astype(BF16)
            arrived = lax.ppermute(piece, ALL, [(b, a) for a, b in pairs])
            grad_down = grad_down + arrived.astype(F32)

    pair_out = [dot_f32("mrs,mrd->msd", pick_bf[j], out_rows) for j in range(top_count)]
    final = hidden + sum(gate_probs[:, :, j, None] * pair_out[j] for j in range(top_count))
    final = final.astype(BF16)
    gate_grad = jnp.stack(
        [
            jnp.sum(jnp.where(pick[j], gate_back[:, :, None], 0.0), axis=1)
            for j in range(top_count)
        ],
        axis=-1,
    )
    chosen_grad = gate_probs * (
        gate_grad - jnp.sum(gate_probs * gate_grad, axis=-1, keepdims=True)
    )
    logit_grad = jnp.sum(route_hot * chosen_grad[..., None], axis=2).astype(BF16)
    normed_grad = reorder_lanes(
        dot_f32("mrs,mrd->msd", pick_any, back_rows), plane, plane_index
    ) + dot_f32("mse,de->msd", logit_grad, router_w)
    router_total = dot_f32("msd,mse->de", normed_two, logit_grad)
    hidden_norm_grad, second_total = norm_pull(hidden, inverse_two, gain_two, normed_grad)
    hidden_grad = cot_rows + hidden_norm_grad
    branch_grad = (hidden_grad * live_rows).astype(BF16)
    hidden_low = hidden_grad.astype(BF16)
    out_total = dot_f32("msi,mso->io", mixed, branch_grad)
    mixed_grad = dot_f32("mso,io->msi", branch_grad, out_w).astype(BF16)
    grad_parts = reorder(jnp.split(mixed_grad, ctx_count, axis=-1), ctx_index)
    grad_parts = [grad_parts[0]] + [
        swap(grad_parts[k], "context", k) for k in range(1, ctx_count)
    ]
    mixed_back = sum(
        dot_f32("msp,msw->mpw", hot[k], grad_parts[k]) for k in range(ctx_count)
    ).astype(BF16)
    qkv_grad, diagonals = attend_back(qkv, mixed_back, lines, length, heads)
    qkv_total = dot_f32("mpd,mpw->dw", normed, qkv_grad)
    first_part = dot_f32("mpw,dw->mpd", qkv_grad, qkv_w)
    first_total = jnp.sum(first_part * rows_all * inverse_one, axis=(0, 1))
    blocks = [
        lax.dynamic_slice_in_dim(first_part, (ctx_index ^ k) * rows_dev, rows_dev, axis=1)
        for k in range(ctx_count)
    ]
    first_grad = blocks[0] + sum(
        swap(blocks[k].astype(BF16), "context", k).astype(F32) for k in range(1, ctx_count)
    )

    def to_positions(value):
        parts = [value] + [swap(value, "context", k) for k in range(1, ctx_count)]
        return sum(dot_f32("msp,msd->mpd", hot_mine[k], parts[k]) for k in range(ctx_count))

    rows_mine = act.astype(F32)
    inverse_mine = lax.rsqrt(jnp.mean(rows_mine * rows_mine, axis=-1, keepdims=True) + epsilon)
    rows_back, _ = norm_pull(rows_mine, inverse_mine, gain_one, first_grad)
    grad_input = (to_positions(hidden_low) + rows_back).astype(BF16)[:, None]
    output = to_positions(final).astype(BF16)[:, None]

    sums = plain_sums(
        qkv_total, out_total, router_total, first_total, second_total, own_width
    )
    grad_query, grad_key, grad_value, grad_out, grad_router, grad_first, grad_second = sums
    diag_all = lax.all_gather(
        lax.psum(diagonals, ("dp", "experts")), "context", axis=0, tiled=True
    )
    offsets = jnp.concatenate([diag_all[:, :1], diag_all[:, : seq : -1]], axis=1)
    grad_table = jnp.einsum(
        "hs,sb->bh", offsets, bucket_hot.astype(F32), precision=lax.Precision.HIGHEST
    )
    return (
        output,
        grad_input,
        grad_query,
        grad_key,
        grad_value,
        grad_out,
        grad_router,
        grad_first,
        grad_second,
        grad_table,
        grad_gate[None],
        grad_up[None],
        grad_down[None],
    )


class Wires:
    def __init__(self, sends, receives, homes):
        self.sends, self.receives, self.homes = sends, receives, homes
        self.used, self.used_home = 0, 0

    def take(self):
        self.used += 1
        return self.used - 1

    def copy(self, source, place, peer, index):
        return remote(source, place, self.sends.at[index], self.receives.at[index], peer)

    def home(self, source, place):
        copy = pltpu.make_async_copy(source, place, self.homes.at[self.used_home])
        self.used_home += 1
        return copy


class Spread:
    def __init__(self, wires, buf, ctx_axis):
        self.wires, self.buf = wires, buf
        dp, ctx, exp = (lax.axis_index(name) for name in ALL)
        self.high, self.low, self.exp = dp // 2, dp % 2, exp
        self.last = lax.axis_size("experts") - 1
        self.core_peer = (flip(dp, 1), ctx, exp)
        self.x_peer = (flip(dp, 2), ctx, exp)
        self.up_peer = (dp, ctx, jnp.minimum(exp + 1, self.last))
        self.down_peer = (dp, ctx, jnp.maximum(exp - 1, 0))
        self.labels = [(0, 0)] + [(h, d) for h in range(1, self.last + 1) for d in (1, -1)]
        self.z_wire, self.x_wire, self.own_wire, self.far_wire = (
            {label: wires.take() for label in self.labels} for _ in range(4)
        )

    def block(self, label):
        hop, way = label
        return jnp.clip(self.exp - hop * way, 0, self.last) if hop else self.exp

    def when(self, label):
        hop, way = label
        if hop == 0:
            return lambda f: f()
        here = self.exp - hop * way
        return pl.when((here >= 0) & (here <= self.last))

    def can_send(self, label, act):
        hop, way = label
        held = self.exp - (hop - 1) * way
        ahead = self.exp + way
        pl.when((held >= 0) & (held <= self.last) & (ahead >= 0) & (ahead <= self.last))(act)

    def z_copy(self, label):
        hop, way = label
        held = jnp.clip(self.exp - (hop - 1) * way, 0, self.last)
        part = self.buf.at[self.high, self.low, :, held]
        peer = self.up_peer if way == 1 else self.down_peer
        return self.wires.copy(part, part, peer, self.z_wire[label])

    def part_copy(self, label, high, wire, peer):
        part = self.buf.at[high, self.low, :, self.block(label)]
        return self.wires.copy(part, part, peer, wire[label])

    def x_copy(self, label):
        return self.part_copy(label, self.high, self.x_wire, self.x_peer)

    def own_copy(self, label):
        return self.part_copy(label, self.high, self.own_wire, self.core_peer)

    def far_copy(self, label):
        return self.part_copy(label, 1 - self.high, self.far_wire, self.core_peer)

    def spread(self, label):
        self.x_copy(label).start()
        self.own_copy(label).start()

    def begin(self):
        for way in (1, -1):
            self.can_send((1, way), lambda way=way: self.z_copy((1, way)).start())
        self.spread((0, 0))

    def hop(self, hop):
        for way in (1, -1):
            label = (hop, way)

            @self.when(label)
            def _(label=label):
                part = self.buf.at[self.high, self.low, :, self.block(label)]
                self.wires.copy(part, part, self.up_peer, self.z_wire[label]).wait_recv()

            if hop < self.last:
                nxt = (hop + 1, way)
                self.can_send(nxt, lambda nxt=nxt: self.z_copy(nxt).start())

            @self.when(label)
            def _(label=label):
                self.spread(label)

        for label in self.labels:
            if label[0] == hop - 1:
                self.pass_far(label)

    def pass_far(self, label):
        @self.when(label)
        def _():
            self.x_copy(label).wait_recv()
            self.far_copy(label).start()

    def end(self):
        for label in self.labels:
            if label[0] == self.last:
                self.pass_far(label)
        for label in self.labels:

            @self.when(label)
            def _(label=label):
                self.own_copy(label).wait_recv()
                self.far_copy(label).wait_recv()

    def drain(self):
        for label in self.labels:
            if label[0]:
                self.can_send(label, lambda label=label: self.z_copy(label).wait_send())

            @self.when(label)
            def _(label=label):
                self.x_copy(label).wait_send()
                self.own_copy(label).wait_send()
                self.far_copy(label).wait_send()


def front_kernel(
    sizes,
    act_ref,
    cot_ref,
    deal_ref,
    length_ref,
    route_ref,
    line_ref,
    query_ref,
    key_ref,
    value_ref,
    out_ref,
    extra_ref,
    gate_ref,
    up_ref,
    down_ref,
    dense,
    out_w,
    act_all,
    normed_ref,
    qkv_ref,
    mixed,
    hidden_ref,
    logit_ref,
    cot_rows_ref,
    all_x,
    all_u,
    all_p,
    gate_up,
    down,
    cot_all,
    mixed_own,
    mixed_sent,
    sent_x,
    sent_u,
    sent_p,
    sends,
    receives,
    homes,
):
    heads, head_size, experts, capacity, slots = sizes
    micro, rows_dev, width = act_ref.shape
    own_width = heads * head_size
    half = gate_ref.shape[1] // 2
    dp, ctx, exp = (lax.axis_index(name) for name in ALL)
    high, low = dp // 2, dp % 2
    block = dp * 2 + ctx
    core_peer, x_peer, x_core = ((flip(dp, 1), ctx, exp), (flip(dp, 2), ctx, exp), (3 - dp, ctx, exp))
    x_core = (flip(flip(dp, 2), 1), ctx, exp)
    y_peer, y_core = (dp, 1 - ctx, exp), (flip(dp, 1), 1 - ctx, exp)
    z_peers = [None] + [(dp, ctx, flip(exp, 1)), (dp, ctx, flip(exp, 2)), (dp, ctx, 3 - exp)]
    z_index = [exp, flip(exp, 1), flip(exp, 2), 3 - exp]
    greet([core_peer, x_peer, x_core, y_peer, y_core] + z_peers[1:])
    wires = Wires(sends, receives, homes)
    drains = []
    home_copies = []

    def send(source, place, peer):
        copy = wires.copy(source, place, peer, wires.take())
        copy.start()
        drains.append(copy)
        return copy

    def multiple(index, size):
        return pl.ds(pl.multiple_of(index * size, size), size)

    mine, other = multiple(ctx, own_width), multiple(1 - ctx, own_width)
    first = []
    for i, ref in enumerate((query_ref, key_ref, value_ref)):
        place = dense.at[high, low, ctx, exp, :, i * own_width : (i + 1) * own_width]
        first.append(send(ref.at[:, other], place, y_peer))
    first.append(send(extra_ref, dense.at[high, low, ctx, exp, :, 3 * own_width :], y_peer))
    out_first = send(out_ref, out_w.at[high, low, ctx, exp], y_peer)
    here = multiple(ctx, rows_dev)
    act_first = send(act_ref, act_all.at[:, here], y_peer)
    for i, ref in enumerate((query_ref, key_ref, value_ref)):
        dense[high, low, ctx, exp, :, i * own_width : (i + 1) * own_width] = ref[:, mine]
    dense[high, low, ctx, exp, :, 3 * own_width :] = extra_ref[...]
    out_w[high, low, ctx, exp] = out_ref[...]
    act_all[:, here, :] = act_ref[...]
    cot_all[:, here, :] = cot_ref[...]

    spread = Spread(wires, dense, 2)
    spread_out = Spread(wires, out_w, 2)
    for copy in first:
        copy.wait_recv()
    spread.begin()
    cot_first = send(cot_ref, cot_all.at[:, here], y_peer)

    def gate_sends(core, peer):
        cols = multiple(core, half)
        return [
            send(gate_ref.at[:, cols], gate_up.at[block, :, 0:half], peer),
            send(up_ref.at[:, cols], gate_up.at[block, :, half:], peer),
        ]

    for ref, start in ((gate_ref, 0), (up_ref, half)):
        copy = wires.home(ref.at[:, multiple(low, half)], gate_up.at[block, :, start : start + half])
        copy.start()
        home_copies.append(copy)

    spread.hop(1)
    from_core = gate_sends(1 - low, core_peer)
    from_x = gate_sends(low, x_peer)
    from_y = gate_sends(low, y_peer)
    from_x_core = gate_sends(1 - low, x_core)
    from_y_core = gate_sends(1 - low, y_core)

    own_down = low * 2 + ctx
    home_down = wires.home(down_ref, down.at[own_down])
    down_wire = {name: wires.take() for name in ("core", "x", "xc", "y", "yc", "rx", "ry")}
    at_home = low == high

    def down_copy(name, peer, source=None):
        source = down_ref if source is None else source
        return wires.copy(source, down.at[own_down], peer, down_wire[name])

    down_sends = [
        ("core", core_peer, False),
        ("x", x_peer, True),
        ("xc", x_core, False),
        ("y", y_peer, True),
        ("yc", y_core, False),
    ]

    def down_start():
        @pl.when(at_home)
        def _():
            home_down.start()

        for name, peer, straight in down_sends:
            pl.when(at_home == straight)(lambda name=name, peer=peer: down_copy(name, peer).start())

    lane = lax.broadcasted_iota(jnp.int32, (rows_dev, 128), 1)
    lane_f = lane.astype(F32)
    row_id = lax.broadcasted_iota(jnp.int32, (rows_dev, rows_dev), 0)
    col_id = lax.broadcasted_iota(jnp.int32, (rows_dev, rows_dev), 1)
    before = (row_id > col_id).astype(BF16)
    seq = deal_ref.shape[1]
    seq_lane = lax.broadcasted_iota(jnp.int32, (rows_dev, seq), 1)

    def hot(m, k):
        index = ctx if k == 0 else 1 - ctx
        return (deal_ref[m, multiple(index, rows_dev), :] == seq_lane).astype(BF16)

    def live_slots(m):
        return deal_ref[m, here, :] < length_ref[m]

    def ranks(m):
        live = live_slots(m)
        hots = [(route_ref[m, :, j : j + 1] == lane) for j in range(2)]
        used = jnp.where((hots[0] | hots[1]) & live, 1.0, 0.0).astype(BF16)
        earlier = jnp.dot(before, used, preferred_element_type=F32)
        found = []
        for j in range(2):
            rank = jnp.sum(jnp.where(hots[j], earlier, 0.0), axis=1, keepdims=True)
            found.append(jnp.where(live & (rank < capacity), rank, -1.0))
        return found

    def picks(m, k, rank):
        return [
            (route_ref[m, :, j : j + 1] == z_index[k]) & (rank[j] == lane_f) for j in range(2)
        ]

    def as_rows(pick, value):
        chosen = lax.dot_general(
            pick, value, (((0,), (0,)), ((), ())), preferred_element_type=F32
        )
        return chosen[:slots].astype(BF16)

    spread.hop(2)
    rank_of = [ranks(m) for m in range(micro)]
    act_first.wait_recv()
    spread.hop(3)
    cot_first.wait_recv()
    pick_of = {}
    for m in range(micro):
        hot_mine = hot(m, 0)
        cot_rows = jnp.dot(hot_mine, cot_all[m], preferred_element_type=F32).astype(BF16)
        cot_rows_ref[m] = cot_rows
        for k in range(experts):
            pick = picks(m, k, rank_of[m])
            pick_any = jnp.where(pick[0] | pick[1], 1.0, 0.0).astype(BF16)
            rows = as_rows(pick_any, cot_rows)
            if k == 0:
                all_u[0, 0, m] = rows
            else:
                sent_u[k - 1, m] = rows
    out_first.wait_recv()
    spread.end()
    spread_out.begin()

    extras = dense[:, :, :, :, :, 3 * own_width :].reshape(width, 128).astype(F32)
    turned = extras.T
    gain_one, gain_two = turned[experts : experts + 1], turned[experts + 1 : experts + 2]
    for m in range(micro):
        rows = act_all[m].astype(F32)
        inverse = lax.rsqrt(jnp.mean(rows * rows, axis=-1, keepdims=True) + epsilon)
        normed_ref[m] = (rows * inverse * gain_one).astype(BF16)
    for i in range(3):
        weight = dense[:, :, :, :, :, i * own_width : (i + 1) * own_width].reshape(width, own_width)
        for m in range(micro):
            qkv_ref[m, :, i * own_width : (i + 1) * own_width] = jnp.dot(
                normed_ref[m], weight, preferred_element_type=F32
            ).astype(BF16)
    spread_out.hop(1)
    down_start()

    scale = head_size ** (-0.5)
    mixed_first = []
    u_first, u_core = {}, []
    for m in range(micro):
        length = length_ref[m]
        for head in range(heads):
            at = [
                slice(part * own_width + head * head_size, part * own_width + (head + 1) * head_size)
                for part in range(3)
            ]
            scores = masked_scores(
                qkv_ref[m, :, at[0]], qkv_ref[m, :, at[1]], line_ref[head : head + 1, :], length, scale
            )
            probs = soft(scores).astype(BF16)
            mixed_own[:, at[0]] = jnp.dot(
                probs, qkv_ref[m, :, at[2]], preferred_element_type=F32
            ).astype(BF16)
        own = mixed_own[...]
        mixed_sent[m] = jnp.dot(hot(m, 1), own, preferred_element_type=F32).astype(BF16)
        mixed_first.append(send(mixed_sent.at[m], mixed.at[m, :, mine], y_peer))
        mixed[m, :, mine] = jnp.dot(hot(m, 0), own, preferred_element_type=F32).astype(BF16)
        spread_out.hop(2 + m)
        for k in range(1, experts):
            u_first[k, m] = send(sent_u.at[k - 1, m], all_u.at[0, k, m], z_peers[k])
        u_core.append(send(all_u.at[0, 0, m], all_u.at[1, 0, m], core_peer))
    spread_out.end()

    for copy in from_x:
        copy.wait_recv()
    x_block = flip(dp, 2) * 2 + ctx
    relay_y = send(gate_up.at[x_block], gate_up.at[x_block], y_peer)
    for copy in from_y_core:
        copy.wait_recv()
    y_block = flip(dp, 1) * 2 + 1 - ctx
    relay_x = send(gate_up.at[y_block], gate_up.at[y_block], x_peer)

    router_w = dense[:, :, :, :, :, 3 * own_width :].reshape(width, 128)
    x_first, p_first, core_copies = {}, {}, []
    for m in range(micro):
        mixed_first[m].wait_recv()
        branch = jnp.dot(
            mixed[m], out_w[...].reshape(width, width), preferred_element_type=F32
        )
        rows_in = jnp.dot(hot(m, 0), act_all[m], preferred_element_type=F32)
        live = live_slots(m)
        hidden = rows_in + jnp.where(live, branch, 0.0)
        hidden_ref[m] = hidden
        inverse = lax.rsqrt(jnp.mean(hidden * hidden, axis=-1, keepdims=True) + epsilon)
        normed_two = (hidden * inverse * gain_two).astype(BF16)
        logits = jnp.dot(normed_two, router_w, preferred_element_type=F32)
        logit_ref[m] = logits
        chosen = [
            jnp.sum(jnp.where(route_ref[m, :, j : j + 1] == lane, logits, 0.0), axis=1, keepdims=True)
            for j in range(2)
        ]
        top = jnp.maximum(chosen[0], chosen[1])
        raised = [jnp.exp(c - top) for c in chosen]
        total = raised[0] + raised[1]
        gates = [r / total for r in raised]
        for k in range(experts):
            pick = picks(m, k, rank_of[m])
            pick_any = jnp.where(pick[0] | pick[1], 1.0, 0.0).astype(BF16)
            rows = as_rows(pick_any, normed_two)
            weights = jnp.sum(
                jnp.where(pick[0], gates[0], 0.0) + jnp.where(pick[1], gates[1], 0.0),
                axis=0,
                keepdims=True,
            )
            weights = jnp.broadcast_to(weights, (8, 128))
            if k == 0:
                all_x[0, 0, m] = rows
                all_p[0, 0, m] = weights
                core_copies.append(send(all_x.at[0, 0, m], all_x.at[1, 0, m], core_peer))
                core_copies.append(send(all_p.at[0, 0, m], all_p.at[1, 0, m], core_peer))
            else:
                sent_x[k - 1, m] = rows
                sent_p[k - 1, m] = weights
                x_first[k, m] = send(sent_x.at[k - 1, m], all_x.at[0, k, m], z_peers[k])
                p_first[k, m] = send(sent_p.at[k - 1, m], all_p.at[0, k, m], z_peers[k])

    away = jnp.logical_not(at_home)
    rx_place = low * 2 + 1 - ctx
    ry_place = (1 - low) * 2 + ctx

    @pl.when(at_home)
    def _():
        down_copy("y", y_peer).wait_recv()
        wires.copy(down.at[rx_place], down.at[rx_place], x_peer, down_wire["rx"]).start()

    @pl.when(away)
    def _():
        down_copy("xc", x_core).wait_recv()
        wires.copy(down.at[ry_place], down.at[ry_place], y_peer, down_wire["ry"]).start()

    for m in range(micro):
        for k in range(1, experts):
            u_first[k, m].wait_recv()
            u_core.append(send(all_u.at[0, k, m], all_u.at[1, k, m], core_peer))
    for m in range(micro):
        for k in range(1, experts):
            x_first[k, m].wait_recv()
            core_copies.append(send(all_x.at[0, k, m], all_x.at[1, k, m], core_peer))
            p_first[k, m].wait_recv()
            core_copies.append(send(all_p.at[0, k, m], all_p.at[1, k, m], core_peer))

    for copy in from_core + from_y + from_x_core + [relay_x, relay_y] + u_core + core_copies:
        copy.wait_recv()

    @pl.when(at_home)
    def _():
        for name in ("core", "yc"):
            down_copy(name, core_peer).wait_recv()
        home_down.wait()
        down_copy("rx", x_peer).wait_send()

    @pl.when(away)
    def _():
        for name in ("x", "rx", "ry"):
            down_copy(name, core_peer).wait_recv()
        down_copy("ry", y_peer).wait_send()

    for name, peer, straight in down_sends:
        pl.when(at_home == straight)(lambda name=name, peer=peer: down_copy(name, peer).wait_send())
    for copy in home_copies:
        copy.wait()
    for copy in drains:
        copy.wait_send()
    spread.drain()
    spread_out.drain()


def front(sizes, act, cot, deal, length, route, lines, weights, extras, w_gate, w_up, w_down):
    heads, head_size, experts, capacity, slots = sizes
    micro, rows_dev, width = act.shape
    own_width = heads * head_size
    per_row = weights[0].shape[0]
    seq = deal.shape[1]
    half = w_gate.shape[1] // 2
    in_vmem, in_hbm = pl.BlockSpec(memory_space=pltpu.VMEM), pl.BlockSpec(memory_space=pltpu.HBM)
    wide = 3 * own_width + 128
    outs = [
        ((2, 2, 2, 4, per_row, wide), BF16),
        ((2, 2, 2, 4, per_row, width), BF16),
        ((micro, seq, width), BF16),
        ((micro, seq, width), BF16),
        ((micro, seq, 3 * own_width), BF16),
        ((micro, rows_dev, width), BF16),
        ((micro, rows_dev, width), F32),
        ((micro, rows_dev, 128), F32),
        ((micro, rows_dev, width), BF16),
        ((2, experts, micro, slots, width), BF16),
        ((2, experts, micro, slots, width), BF16),
        ((2, experts, micro, 8, 128), F32),
        ((8,) + (w_gate.shape[0], 2 * half), BF16),
        ((4,) + w_down.shape, BF16),
    ]
    return pl.pallas_call(
        functools.partial(front_kernel, sizes),
        out_shape=tuple(jax.ShapeDtypeStruct(*out) for out in outs),
        in_specs=[in_vmem] * 3 + [pl.BlockSpec(memory_space=pltpu.SMEM)] + [in_vmem] * 7 + [in_hbm] * 3,
        out_specs=(in_vmem,) * 12 + (in_hbm,) * 2,
        scratch_shapes=[
            pltpu.VMEM((micro, seq, width), BF16),
            pltpu.VMEM((seq, own_width), BF16),
            pltpu.VMEM((micro, rows_dev, own_width), BF16),
            pltpu.VMEM((experts - 1, micro, slots, width), BF16),
            pltpu.VMEM((experts - 1, micro, slots, width), BF16),
            pltpu.VMEM((experts - 1, micro, 8, 128), F32),
            pltpu.SemaphoreType.DMA((160,)),
            pltpu.SemaphoreType.DMA((160,)),
            pltpu.SemaphoreType.DMA((4,)),
        ],
        compiler_params=pltpu.CompilerParams(
            collective_id=1, has_side_effects=True, vmem_limit_bytes=56 * 2**20
        ),
    )(act, cot, deal[:, :, None], length, route, lines, *weights, extras, w_gate, w_up, w_down)


class Plan:
    def __init__(self, deal_ref, length_ref, route_ref, rows_dev, capacity):
        self.deal, self.length, self.route = deal_ref, length_ref, route_ref
        self.rows, self.capacity = rows_dev, capacity
        self.ctx, exp = lax.axis_index("context"), lax.axis_index("experts")
        self.z_index = [exp, flip(exp, 1), flip(exp, 2), 3 - exp]
        self.lane = lax.broadcasted_iota(jnp.int32, (rows_dev, 128), 1)
        self.lane_f = self.lane.astype(F32)

    def at(self, k):
        index = self.ctx if k == 0 else 1 - self.ctx
        return pl.ds(pl.multiple_of(index * self.rows, self.rows), self.rows)

    def hot(self, m, k):
        seq = self.deal.shape[1]
        lane = lax.broadcasted_iota(jnp.int32, (self.rows, seq), 1)
        return (self.deal[m, self.at(k), :] == lane).astype(BF16)

    def hot_mine(self, m, k):
        lane = lax.broadcasted_iota(jnp.int32, (self.rows, self.rows), 1) + self.ctx * self.rows
        return (self.deal[m, self.at(k), :] == lane).astype(BF16)

    def live(self, m):
        return self.deal[m, self.at(0), :] < self.length[m]

    def named(self, m, j):
        return self.route[m, :, j : j + 1]

    def ranks(self, m):
        row_id = lax.broadcasted_iota(jnp.int32, (self.rows, self.rows), 0)
        col_id = lax.broadcasted_iota(jnp.int32, (self.rows, self.rows), 1)
        before = (row_id > col_id).astype(BF16)
        live = self.live(m)
        hots = [self.named(m, j) == self.lane for j in range(2)]
        used = jnp.where((hots[0] | hots[1]) & live, 1.0, 0.0).astype(BF16)
        earlier = jnp.dot(before, used, preferred_element_type=F32)
        found = []
        for j in range(2):
            rank = jnp.sum(jnp.where(hots[j], earlier, 0.0), axis=1, keepdims=True)
            found.append(jnp.where(live & (rank < self.capacity), rank, -1.0))
        return found

    def picks(self, m, k, rank):
        return [
            (self.named(m, j) == self.z_index[k]) & (rank[j] == self.lane_f) for j in range(2)
        ]

    def places(self, m, rank, experts, slots):
        lane = lax.broadcasted_iota(jnp.int32, (self.rows, experts * slots), 1).astype(F32)
        picks = []
        for j in range(2):
            place = rank[j]
            for k in range(1, experts):
                place = place + jnp.where(self.named(m, j) == self.z_index[k], 1.0 * k * slots, 0.0)
            place = jnp.where(rank[j] < 0, -1.0, place)
            picks.append(jnp.where(place == lane, 1.0, 0.0).astype(BF16))
        return picks

    def gates(self, m, logits):
        chosen = [
            jnp.sum(jnp.where(self.named(m, j) == self.lane, logits, 0.0), axis=1, keepdims=True)
            for j in range(2)
        ]
        top = jnp.maximum(chosen[0], chosen[1])
        raised = [jnp.exp(c - top) for c in chosen]
        total = raised[0] + raised[1]
        return [r / total for r in raised]


def dot_rows(left, right):
    return lax.dot_general(left, right, (((0,), (0,)), ((), ())), preferred_element_type=F32)


def dot_lanes(left, right):
    return lax.dot_general(left, right, (((1,), (1,)), ((), ())), preferred_element_type=F32)


STAGES = {"x": 0, "zl": 3, "zh": 2, "y": 1}


class Reduce:
    def __init__(self, wires, source, columns, order, bufs, peers, indices, finish):
        self.wires, self.source, self.columns = wires, source, columns
        self.order, self.bufs, self.peers, self.indices = order, bufs, peers, indices
        self.finish = finish
        self.flying, self.step = [], 0

    def launch(self, source, place, name):
        copy = self.wires.copy(source, place, self.peers[name], self.wires.take())
        copy.start()
        self.flying.append(copy)

    def begin(self):
        low = self.indices["core"]
        self.launch(self.source.at[:, 1 - low, :, self.columns], self.bufs[0], "core")

    def advance(self):
        if self.step > len(self.order):
            return False
        low = self.indices["core"]
        self.flying[-1].wait_recv()
        if self.step == 0:
            total = self.source[:, low, :, self.columns].astype(F32) + self.bufs[0][...].astype(F32)
            self.bufs[1][...] = total.astype(BF16).reshape(self.bufs[1].shape)
        else:
            kept = self.bufs[2 * self.step - 1]
            arrived = self.bufs[2 * self.step][...].astype(F32)
            mine = kept[self.cut(self.order[self.step - 1], True)].astype(F32)
            if self.step == len(self.order):
                self.finish(mine, arrived)
                self.step += 1
                return False
            self.bufs[2 * self.step + 1][...] = (mine + arrived).astype(BF16)
        name = self.order[self.step]
        kept = self.bufs[2 * self.step + 1]
        self.launch(kept.at[self.cut(name, False)], self.bufs[2 * self.step + 2], name)
        self.step += 1
        return True

    def cut(self, name, own):
        gone = set(self.order[: self.order.index(name)])
        axis = sum(1 for n, place in STAGES.items() if place < STAGES[name] and n not in gone)
        index = self.indices[name] if own else 1 - self.indices[name]
        return (slice(None),) * axis + (index,)


def reduce_buffers(order, rows, per_row, size):
    left = {"x", "zl", "zh", "y"}
    shapes = [(2, rows // 4, size)]
    for name in order:
        shapes.append((2,) * len(left) + (per_row, size))
        left.discard(name)
        shapes.append((2,) * len(left) + (per_row, size))
    return [pltpu.VMEM(shape, BF16) for shape in shapes]


ORDERS = [("x", "zl", "zh", "y")] * 3 + [("zl", "zh", "x", "y")] * 2 + [("x", "zl", "zh", "y")]


def back_kernel(
    sizes,
    back_ref,
    outp_ref,
    u_ref,
    hidden_ref,
    logit_ref,
    cot_rows_ref,
    mixed,
    qkv_ref,
    normed_ref,
    act_all,
    act_ref,
    dense,
    out_w,
    deal_ref,
    length_ref,
    route_ref,
    line_ref,
    gate_total,
    down_total,
    output_ref,
    grad_input_ref,
    query_out,
    key_out,
    value_out,
    out_out,
    small_out,
    diag_out,
    gate_in,
    down_in,
    back_got,
    out_got,
    sent_back,
    sent_out,
    sent_gate,
    ret_back,
    ret_out,
    ret_gate,
    final_all,
    hidden_all,
    mixed_got,
    grad_sent,
    first_sent,
    first_got,
    first_own,
    grad_own,
    qkv_grad,
    qkv_total,
    out_total,
    out_low,
    small_f,
    small_low,
    diag_buf,
    *rest,
):
    heads, head_size, experts, capacity, slots = sizes
    chunk_bufs, (sends, receives, homes) = rest[:-3], rest[-3:]
    micro, rows_dev, width = hidden_ref.shape
    seq = deal_ref.shape[1]
    own_width = heads * head_size
    dp, ctx, exp = (lax.axis_index(name) for name in ALL)
    high, low = dp // 2, dp % 2
    other_core, other_x, both = flip(dp, 1), flip(dp, 2), flip(flip(dp, 1), 2)
    core_peer, x_peer, x_core = (other_core, ctx, exp), (other_x, ctx, exp), (both, ctx, exp)
    y_peer, y_core = (dp, 1 - ctx, exp), (other_core, 1 - ctx, exp)
    far_peer, far_core = (other_x, 1 - ctx, exp), (both, 1 - ctx, exp)
    z_peers = [None] + [(dp, ctx, flip(exp, 1)), (dp, ctx, flip(exp, 2)), (dp, ctx, 3 - exp)]
    greet([core_peer, x_peer, x_core, y_peer, y_core, far_peer, far_core] + z_peers[1:])
    wires = Wires(sends, receives, homes)
    drains = []

    def send(source, place, peer):
        copy = wires.copy(source, place, peer, wires.take())
        copy.start()
        drains.append(copy)
        return copy

    plan = Plan(deal_ref, length_ref, route_ref, rows_dev, capacity)
    mine = pl.ds(pl.multiple_of(ctx * own_width, own_width), own_width)
    other = pl.ds(pl.multiple_of((1 - ctx) * own_width, own_width), own_width)

    back_core = [send(back_ref.at[1, :, m], back_got.at[m], core_peer) for m in range(micro)]
    out_core = [send(outp_ref.at[1, :, m], out_got.at[m], core_peer) for m in range(micro)]

    bulk = []
    home_copies = []
    block = dp * 2 + ctx
    own_copy = wires.home(gate_total.at[block], gate_in.at[0])
    own_copy.start()
    home_copies.append(own_copy)
    at_home = low == high
    away = jnp.logical_not(at_home)
    down_wire = [wires.take() for _ in range(8)]
    home_down = wires.home(down_total.at[low * 2 + ctx], down_in.at[0])
    down_sends = [
        (None, False, low * 2 + ctx, 0),
        (core_peer, False, (1 - low) * 2 + ctx, 0),
        (y_peer, False, low * 2 + 1 - ctx, 1),
        (y_core, False, (1 - low) * 2 + 1 - ctx, 1),
        (x_peer, True, low * 2 + ctx, 2),
        (x_core, True, (1 - low) * 2 + ctx, 2),
        (far_peer, True, low * 2 + 1 - ctx, 3),
        (far_core, True, (1 - low) * 2 + 1 - ctx, 3),
    ]

    def down_copy(i):
        peer, _, place, slot = down_sends[i]
        return wires.copy(down_total.at[place], down_in.at[slot], peer or core_peer, down_wire[i])

    def start_bulk():
        for j, (target_dp, target_ctx, peer) in enumerate(
            [
                (other_core, ctx, core_peer),
                (other_x, ctx, x_peer),
                (dp, 1 - ctx, y_peer),
                (both, ctx, x_core),
                (other_core, 1 - ctx, y_core),
                (other_x, 1 - ctx, far_peer),
                (both, 1 - ctx, far_core),
            ]
        ):
            bulk.append(send(gate_total.at[target_dp * 2 + target_ctx], gate_in.at[j + 1], peer))
        for i, (peer, is_away, _, _) in enumerate(down_sends):
            start = home_down.start if peer is None else down_copy(i).start
            pl.when(away if is_away else at_home)(start)

    ret_first = {}
    for m in range(micro):
        back_core[m].wait_recv()
        for k in range(experts):
            rows = (
                back_ref[0, k, m].astype(F32) + back_got[m, k].astype(F32)
            ).astype(BF16)
            if k == 0:
                ret_back[m, 0] = rows
            else:
                sent_back[m, k - 1] = rows
                ret_first["back", m, k] = send(sent_back.at[m, k - 1], ret_back.at[m, k], z_peers[k])
        out_core[m].wait_recv()
        ones = jnp.ones((8, width), F32)
        for k in range(experts):
            rows = (
                outp_ref[0, k, m].astype(F32) + out_got[m, k].astype(F32)
            ).astype(BF16)
            worth = lax.dot_general(
                ones,
                rows.astype(F32) * u_ref[k, m].astype(F32),
                (((1,), (1,)), ((), ())),
                precision=lax.Precision.HIGHEST,
                preferred_element_type=F32,
            )
            if k == 0:
                ret_out[m, 0] = rows
                ret_gate[m, 0, :, :slots] = worth
            else:
                sent_out[m, k - 1] = rows
                sent_gate[m, k - 1, :, :slots] = worth
                ret_first["gate", m, k] = send(sent_gate.at[m, k - 1], ret_gate.at[m, k], z_peers[k])
    start_bulk()
    for m in range(micro):
        for k in range(1, experts):
            ret_first["out", m, k] = send(sent_out.at[m, k - 1], ret_out.at[m, k], z_peers[k])

    extras = dense[:, :, :, :, :, 3 * own_width :].reshape(width, 128)
    turned = extras.astype(F32).T
    gain_one, gain_two = turned[experts : experts + 1], turned[experts + 1 : experts + 2]
    lanes = lax.broadcasted_iota(jnp.int32, (width, 128), 1)
    rank_of = [plan.ranks(m) for m in range(micro)]
    gate_of = [plan.gates(m, logit_ref[m]) for m in range(micro)]
    mixed_first, hidden_first = [], []
    second = jnp.zeros((1, width), F32)
    out_matrix = out_w[...].reshape(width, width)
    here = plan.at(0)
    for m in range(micro):
        for k in range(1, experts):
            ret_first["back", m, k].wait_recv()
            ret_first["gate", m, k].wait_recv()
        worths = []
        for j in range(2):
            worth = jnp.zeros((rows_dev, 1), F32)
            for k in range(experts):
                pick = plan.picks(m, k, rank_of[m])[j]
                worth = worth + jnp.sum(
                    jnp.where(pick, ret_gate[m, k, 0:1, :], 0.0), axis=1, keepdims=True
                )
            worths.append(worth)
        gates = gate_of[m]
        mean_worth = gates[0] * worths[0] + gates[1] * worths[1]
        logit_grad = sum(
            jnp.where(plan.named(m, j) == plan.lane, gates[j] * (worths[j] - mean_worth), 0.0)
            for j in range(2)
        ).astype(BF16)
        places = plan.places(m, rank_of[m], experts, slots)
        normed_grad = jnp.dot(
            places[0] + places[1],
            ret_back[m].reshape(experts * slots, width),
            preferred_element_type=F32,
        ) + dot_lanes(logit_grad, extras)
        hidden = hidden_ref[m]
        inverse = lax.rsqrt(jnp.mean(hidden * hidden, axis=-1, keepdims=True) + epsilon)
        scaled = hidden * inverse
        normed_two = (scaled * gain_two).astype(BF16)
        router = dot_rows(normed_two, logit_grad)
        small_f[...] = router if m == 0 else small_f[...] + router
        second = second + jnp.sum(normed_grad * scaled, axis=0, keepdims=True)
        lifted = gain_two * normed_grad
        mean_part = jnp.mean(lifted * hidden, axis=-1, keepdims=True)
        hidden_grad = (
            cot_rows_ref[m].astype(F32)
            + inverse * lifted
            - hidden * (inverse * inverse * inverse) * mean_part
        )
        hidden_all[m, 0] = hidden_grad.astype(BF16)
        branch_grad = jnp.where(plan.live(m), hidden_grad, 0.0).astype(BF16)
        mixed_grad = dot_lanes(branch_grad, out_matrix).astype(BF16)
        grad_sent[m] = mixed_grad
        mixed_first.append(send(grad_sent.at[m, :, other], mixed_got.at[m], y_peer))
        out_part = dot_rows(mixed[m], branch_grad)
        if m == 0:
            out_total[...] = out_part
        else:
            out_low[...] = (out_total[...] + out_part).astype(BF16).reshape(out_low.shape)
    for m in range(micro):
        hidden_first.append(send(hidden_all.at[m, 0], hidden_all.at[m, 1], y_peer))

    indices = {"core": low, "x": high, "y": ctx, "zl": exp % 2, "zh": exp // 2}
    peers = {"core": core_peer, "x": x_peer, "y": y_peer, "zl": z_peers[1], "zh": z_peers[2]}

    def finish_qkv(place):
        def store(kept, arrived):
            place[:, mine] = kept
            place[:, other] = arrived

        return store

    def finish_out(start):
        def store(kept, arrived):
            out_out[:, start : start + own_width] = kept + arrived

        return store

    def finish_small(kept, arrived):
        small_out[...] = kept + arrived

    chunks = []
    at = 0
    for i, order in enumerate(ORDERS):
        bufs = chunk_bufs[at : at + 9]
        at += 9
        if i < 3:
            source, start = qkv_total, i * own_width
            finish = finish_qkv((query_out, key_out, value_out)[i])
        elif i < 5:
            source, start = out_low, (i - 3) * own_width
            finish = finish_out(start)
        else:
            source, start, finish = small_low, 0, finish_small
        size = bufs[0].shape[-1]
        chunks.append(
            Reduce(wires, source, slice(start, start + size), order, bufs, peers, indices, finish)
        )
    chunks[3].begin()
    chunks[4].begin()

    scale = head_size ** (-0.5)
    for m in range(micro):
        mixed_first[m].wait_recv()
        grad_own[...] = (
            dot_rows(plan.hot(m, 0), grad_sent[m, :, mine]) + dot_rows(plan.hot(m, 1), mixed_got[m])
        ).astype(BF16)
        length = length_ref[m]
        for head in range(heads):
            cols = [
                slice(part * own_width + head * head_size, part * own_width + (head + 1) * head_size)
                for part in range(3)
            ]
            query, key, value = (qkv_ref[m, :, part] for part in cols)
            grad = grad_own[:, cols[0]]
            scores = masked_scores(query, key, line_ref[head : head + 1, :], length, scale)
            probs = soft(scores)
            prob_grad = dot_lanes(grad, value)
            delta = jnp.sum(probs * prob_grad, axis=-1, keepdims=True)
            score_grad = (probs * (prob_grad - delta)).astype(BF16)
            diagonal = diagonal_sums(score_grad.astype(F32))
            if m:
                diagonal = diagonal + diag_buf[0, head : head + 1, :]
            diag_buf[0, head : head + 1, :] = diagonal
            qkv_grad[m, :, cols[0]] = (
                jnp.dot(score_grad, key, preferred_element_type=F32) * scale
            ).astype(BF16)
            qkv_grad[m, :, cols[1]] = (dot_rows(score_grad, query) * scale).astype(BF16)
            qkv_grad[m, :, cols[2]] = dot_rows(probs.astype(BF16), grad).astype(BF16)
            if head % 4 == 3:
                for i in (3, 4):
                    chunks[i].advance()
    for i in range(3):
        cols = slice(i * own_width, (i + 1) * own_width)
        total = dot_rows(normed_ref[0], qkv_grad[0, :, cols]) + dot_rows(
            normed_ref[1], qkv_grad[1, :, cols]
        )
        qkv_total[:, :, :, cols] = total.astype(BF16).reshape(2, 2, width // 4, own_width)
        chunks[i].begin()

    diag_peers = [core_peer, x_peer, z_peers[1], z_peers[2], y_peer]
    diag_copies = []

    def diag_step(stage):
        if stage:
            diag_copies[stage - 1].wait_recv()
        if 0 < stage < 5:
            diag_buf[2 * stage] = diag_buf[2 * stage - 2] + diag_buf[2 * stage - 1]
        if stage < 5:
            diag_copies.append(
                send(diag_buf.at[2 * stage], diag_buf.at[2 * stage + 1], diag_peers[stage])
            )

    diag_step(0)
    first_total = jnp.zeros((1, width), F32)
    first_first = []
    for m in range(micro):
        part = jnp.zeros((seq, width), F32)
        for i in range(3):
            cols = slice(i * own_width, (i + 1) * own_width)
            part = part + dot_lanes(
                qkv_grad[m, :, cols], dense[:, :, :, :, :, cols].reshape(width, own_width)
            )
        rows = act_all[m].astype(F32)
        inverse = lax.rsqrt(jnp.mean(rows * rows, axis=-1, keepdims=True) + epsilon)
        first_total = first_total + jnp.sum(part * rows * inverse, axis=0, keepdims=True)
        first_own[...] = part
        first_sent[m] = first_own[plan.at(1), :].astype(BF16)
        first_got[m, 0] = first_own[here, :].astype(BF16)
        first_first.append(send(first_sent.at[m], first_got.at[m, 1], y_peer))
        chunks[m].advance()
        diag_step(1 + m)
    columns = jnp.where(
        lanes == experts,
        jnp.broadcast_to(second, (128, width)).T,
        jnp.where(
            lanes == experts + 1, jnp.broadcast_to(first_total, (128, width)).T, small_f[...]
        ),
    )
    small_low[...] = columns.astype(BF16).reshape(small_low.shape)
    chunks[5].begin()
    chunks[2].advance()
    chunks[0].advance()

    final_first = []
    for m in range(micro):
        for k in range(1, experts):
            ret_first["out", m, k].wait_recv()
        places = plan.places(m, rank_of[m], experts, slots)
        rows = ret_out[m].reshape(experts * slots, width)
        final = hidden_ref[m]
        for j in range(2):
            final = final + gate_of[m][j] * jnp.dot(places[j], rows, preferred_element_type=F32)
        final_all[m, 0] = final.astype(BF16)
        final_first.append(send(final_all.at[m, 0], final_all.at[m, 1], y_peer))
        if m == 0:
            chunks[1].advance()
            chunks[3].advance()
            diag_step(3)
    chunks[5].advance()
    chunks[2].advance()
    chunks[0].advance()
    chunks[4].advance()
    diag_step(4)
    chunks[1].advance()
    chunks[5].advance()

    for m in range(micro):
        hidden_first[m].wait_recv()
        first_first[m].wait_recv()
        first = first_got[m, 0].astype(F32) + first_got[m, 1].astype(F32)
        rows = act_ref[m].astype(F32)
        inverse = lax.rsqrt(jnp.mean(rows * rows, axis=-1, keepdims=True) + epsilon)
        lifted = gain_one * first
        mean_part = jnp.mean(lifted * rows, axis=-1, keepdims=True)
        back = inverse * lifted - rows * (inverse * inverse * inverse) * mean_part
        moved = sum(dot_rows(plan.hot_mine(m, k), hidden_all[m, k]) for k in range(2))
        grad_input_ref[m] = (moved + back).astype(BF16)
        if m == 0:
            chunks[0].advance()
            chunks[2].advance()
            chunks[1].advance()
    for m in range(micro):
        final_first[m].wait_recv()
        moved = sum(dot_rows(plan.hot_mine(m, k), final_all[m, k]) for k in range(2))
        output_ref[m] = moved.astype(BF16)
    busy = True
    while busy:
        busy = False
        for i in (0, 1, 2, 3, 4, 5):
            if chunks[i].step <= len(chunks[i].order):
                chunks[i].advance()
                busy = True
    diag_step(5)
    diag_out[ctx] = diag_buf[8]
    diag_out[1 - ctx] = diag_buf[9]

    for copy in bulk:
        copy.wait_recv()
    for i, (peer, is_away, _, _) in enumerate(down_sends):
        if peer is None:
            pl.when(at_home)(home_down.wait)
            continue
        pl.when(away if is_away else at_home)(lambda i=i: down_copy(i).wait_send())
    @pl.when(at_home)
    def _():
        for i in (2, 4 , 6):
            down_copy(i).wait_recv()

    @pl.when(away)
    def _():
        for i in (1, 3, 5, 7):
            down_copy(i).wait_recv()

    for copy in home_copies:
        copy.wait()
    for chunk in chunks:
        for copy in chunk.flying:
            copy.wait_send()
    for copy in drains:
        copy.wait_send()


def back(sizes, values, gate_total, down_total):
    heads, head_size, experts, capacity, slots = sizes
    hidden, dense, qkv, lines = values[3], values[11], values[7], values[16]
    micro, rows_dev, width = hidden.shape
    seq = qkv.shape[1]
    own_width = heads * head_size
    per_row = dense.shape[4]
    in_vmem, in_hbm = pl.BlockSpec(memory_space=pltpu.VMEM), pl.BlockSpec(memory_space=pltpu.HBM)
    smem = pl.BlockSpec(memory_space=pltpu.SMEM)
    outs = (
        [((micro, rows_dev, width), BF16)] * 2
        + [((per_row, width), F32)] * 4
        + [((per_row, 128), F32), ((2,) + lines.shape, F32)]
        + [(gate_total.shape, BF16), (down_total.shape, BF16)]
    )
    rows = (micro, experts, slots, width)
    sent = (micro, experts - 1, slots, width)
    scratch = [
        pltpu.VMEM(rows, BF16),
        pltpu.VMEM(rows, BF16),
        pltpu.VMEM(sent, BF16),
        pltpu.VMEM(sent, BF16),
        pltpu.VMEM((micro, experts - 1, 8, 128), F32),
        pltpu.VMEM(rows, BF16),
        pltpu.VMEM(rows, BF16),
        pltpu.VMEM((micro, experts, 8, 128), F32),
        pltpu.VMEM((micro, 2, rows_dev, width), BF16),
        pltpu.VMEM((micro, 2, rows_dev, width), BF16),
        pltpu.VMEM((micro, rows_dev, own_width), BF16),
        pltpu.VMEM((micro, rows_dev, width), BF16),
        pltpu.VMEM((micro, rows_dev, width), BF16),
        pltpu.VMEM((micro, 2, rows_dev, width), BF16),
        pltpu.VMEM((seq, width), F32),
        pltpu.VMEM((seq, own_width), BF16),
        pltpu.VMEM((micro, seq, 3 * own_width), BF16),
        pltpu.VMEM((2, 2, width // 4, 3 * own_width), BF16),
        pltpu.VMEM((width, width), F32),
        pltpu.VMEM((2, 2, width // 4, width), BF16),
        pltpu.VMEM((width, 128), F32),
        pltpu.VMEM((2, 2, width // 4, 128), BF16),
        pltpu.VMEM((10,) + lines.shape, F32),
    ]
    chunk_sizes = [own_width] * 5 + [128]
    for order, size in zip(ORDERS, chunk_sizes):
        scratch += reduce_buffers(order, width, per_row, size)
    scratch += [
        pltpu.SemaphoreType.DMA((160,)),
        pltpu.SemaphoreType.DMA((160,)),
        pltpu.SemaphoreType.DMA((4,)),
    ]
    return pl.pallas_call(
        functools.partial(back_kernel, sizes),
        out_shape=tuple(jax.ShapeDtypeStruct(*out) for out in outs),
        in_specs=[in_vmem] * 14 + [smem] + [in_vmem] * 2 + [in_hbm] * 2,
        out_specs=(in_vmem,) * 8 + (in_hbm,) * 2,
        scratch_shapes=scratch,
        compiler_params=pltpu.CompilerParams(
            collective_id=2, has_side_effects=True, vmem_limit_bytes=60 * 2**20
        ),
    )(*values, gate_total, down_total)


def tuned_body(
    activations,
    cotangent,
    dealing,
    lengths,
    routes,
    buckets,
    w_query,
    w_key,
    w_value,
    w_out,
    w_router,
    norm_first,
    norm_second,
    bias_table,
    w_gate,
    w_up,
    w_down,
):
    micro, _, rows_dev, width = activations.shape
    seq = dealing.shape[2]
    bucket_count, head_count = bias_table.shape
    dp_count, ctx_count, expert_count = (lax.axis_size(name) for name in ALL)
    dp_index, ctx_index, expert_index = (lax.axis_index(name) for name in ALL)
    high, low = dp_index // 2, dp_index % 2
    heads = head_count // ctx_count
    head_size = width // head_count
    own_width = heads * head_size
    experts = w_router.shape[1]
    top_count = routes.shape[3]
    capacity = (5 * rows_dev * top_count + 4 * experts - 1) // (4 * experts)
    slots = -(-capacity // 16) * 16
    half_ff = w_gate.shape[2] // 2
    down_rows = w_down.shape[1]
    plane = dp_count * ctx_count
    plane_index = dp_index * ctx_count + ctx_index
    act = activations[:, 0]
    cot = cotangent[:, 0]
    deal = dealing[:, 0]
    length = lengths[:, 0]
    route = routes[:, 0]
    sizes = (heads, head_size, experts, capacity, slots)
    extras = jnp.concatenate([w_router, norm_first[:, None], norm_second[:, None]], axis=1)
    extras = jnp.pad(extras, ((0, 0), (0, 128 - extras.shape[1])))
    bucket_hot = (buckets[:, None] == jnp.arange(bucket_count)[None, :]).astype(BF16)
    own_table = lax.dynamic_slice_in_dim(bias_table, ctx_index * heads, heads, axis=1)
    lookup = dot_f32("sb,bh->hs", bucket_hot, own_table)
    lines = jnp.concatenate(
        [lookup[:, :1], jnp.zeros((heads, seq), F32), lookup[:, :0:-1]], axis=1
    )
    (
        dense,
        out_w,
        act_all,
        normed,
        qkv,
        mixed,
        hidden,
        logits,
        cot_low,
        all_x,
        all_u,
        all_p,
        gate_up_w,
        down_w,
    ) = front(
        sizes,
        act,
        cot,
        deal,
        length,
        route,
        lines,
        (w_query, w_key, w_value, w_out),
        extras,
        w_gate[0],
        w_up[0],
        w_down[0],
    )
    gate_up_w = gate_up_w.reshape(width, 2 * half_ff)
    down_w = down_w.reshape(half_ff, width)
    row_count = experts * micro * slots

    all_x = all_x.reshape(2 * row_count, width)
    all_p = all_p[..., 0, :slots].reshape(2 * row_count, 1)
    all_g = (all_p * all_u.reshape(2 * row_count, width).astype(F32)).astype(BF16)
    pre_up = dot_f32("rd,df->rf", all_x, gate_up_w)
    gelu_value, gelu_slope = gelu_parts(pre_up[:, :half_ff])
    up_part = pre_up[:, half_ff:]
    activated = (gelu_value * up_part).astype(BF16)
    act_grad = dot_f32("rd,fd->rf", all_g, down_w)
    pre_grad = (act_grad * up_part * gelu_slope).astype(BF16)
    up_grad = (act_grad * gelu_value).astype(BF16)
    both_grad = jnp.concatenate([pre_grad, up_grad], axis=1)
    parts_shape = (2, experts, micro, slots, width)
    back_part = dot_f32("rf,df->rd", both_grad, gate_up_w).astype(BF16).reshape(parts_shape)
    out_part = dot_f32("rf,fd->rd", activated, down_w).astype(BF16).reshape(parts_shape)
    gate_up_total = dot_f32("rd,rf->df", all_x, both_grad).astype(BF16)
    down_total = dot_f32("rf,rd->fd", activated, all_g).astype(BF16)
    (
        output,
        grad_input,
        grad_query,
        grad_key,
        grad_value,
        grad_out,
        small_sum,
        diag_all,
        gate_in,
        down_in,
    ) = back(
        sizes,
        (
            back_part,
            out_part,
            all_u[0],
            hidden,
            logits,
            cot_low,
            mixed,
            qkv,
            normed,
            act_all,
            act,
            dense,
            out_w,
            deal[:, :, None],
            length,
            route,
            lines,
        ),
        gate_up_total.reshape(plane, width // plane, 2 * half_ff),
        down_total.reshape(-1, w_down.shape[1], width),
    )
    same = sum(gate_in[j].astype(F32) for j in (0, 2, 3, 6))
    far = sum(gate_in[j].astype(F32) for j in (1, 4, 5, 7))
    first_half, second_half = reorder([same, far], low)
    grad_gate = jnp.concatenate([first_half[:, :half_ff], second_half[:, :half_ff]], axis=1)
    grad_up = jnp.concatenate([first_half[:, half_ff:], second_half[:, half_ff:]], axis=1)
    grad_down = sum(down_in[j].astype(F32) for j in range(down_in.shape[0]))
    diag_all = diag_all.reshape((head_count, -1))
    offsets = jnp.concatenate([diag_all[:, :1], diag_all[:, : seq : -1]], axis=1)
    grad_table = jnp.einsum(
        "hs,sb->bh", offsets, bucket_hot.astype(F32), precision=lax.Precision.HIGHEST
    )
    return (
        output[:, None],
        grad_input[:, None],
        grad_query,
        grad_key,
        grad_value,
        grad_out,
        small_sum[:, :experts],
        small_sum[:, experts + 1],
        small_sum[:, experts],
        grad_table,
        grad_gate[None],
        grad_up[None],
        grad_down[None],
    )


def body(*arguments):
    counts = tuple(lax.axis_size(name) for name in ALL)
    activations, w_query, bias_table, w_gate = (arguments[i] for i in (0, 6, 13, 14))
    own_width = activations.shape[3] // counts[1]
    fits = (
        counts == (4, 2, 4)
        and w_gate.shape[0] == 1
        and w_query.shape[0] % 16 == 0
        and own_width % 128 == 0
        and bias_table.shape[1] % counts[1] == 0
        and arguments[4].shape[3] == 2
    )
    return (tuned_body if fits else plain_body)(*arguments)


def solution(mesh):
    tokens = P(None, ("dp", "experts"), "context", None)
    sequences = P(None, ("dp", "experts"))
    rows = P(("dp", "context", "experts"), None)
    gains = P(("dp", "context", "experts"))
    experts = P("experts", ("dp", "context"), None)
    placed = (
        (tokens, tokens, P(None, ("dp", "experts"), None), sequences, tokens, P())
        + (rows,) * 5
        + (gains, gains, P())
        + (experts,) * 3
    )
    return jax.shard_map(
        body,
        mesh=mesh,
        in_specs=placed,
        out_specs=(tokens, tokens) + (rows,) * 5 + (gains, gains, P()) + (experts,) * 3,
        check_vma=False,
    )
```

```python
import functools

import jax
import jax.numpy as jnp
from jax import lax
from jax.experimental import pallas as pl
from jax.experimental.pallas import tpu as pltpu
from jax.sharding import PartitionSpec as P

epsilon = 1e-06
masked_score = -1e30
ALL = ("dp", "context", "experts")
F32 = jnp.float32
BF16 = jnp.bfloat16


def dot_f32(spec, left, right):
    return jnp.einsum(spec, left, right, preferred_element_type=F32)


def swap(value, axis, offset):
    size = lax.axis_size(axis)
    return lax.ppermute(value, axis, [(i, i ^ offset) for i in range(size)])


def reorder(pieces, index):
    pieces = list(pieces)
    bit = 1
    while bit < len(pieces):
        flag = (index // bit) % 2 == 1
        pieces = [jnp.where(flag, pieces[j ^ bit], pieces[j]) for j in range(len(pieces))]
        bit *= 2
    return pieces


def reorder_lanes(value, blocks, index):
    return jnp.concatenate(reorder(jnp.split(value, blocks, axis=-1), index), axis=-1)


def toeplitz_bias(line, size):
    rows = jnp.broadcast_to(line, (size, 2 * size))
    return pltpu.roll(rows, 0, 1, stride=1, stride_axis=0)[:, :size]


def masked_scores(query, key, line, length, scale):
    size = query.shape[0]
    scores = lax.dot_general(query, key, (((1,), (1,)), ((), ())), preferred_element_type=F32)
    scores = scores * scale + toeplitz_bias(line, size)
    row_id = lax.broadcasted_iota(jnp.int32, (size, size), 0)
    col_id = lax.broadcasted_iota(jnp.int32, (size, size), 1)
    allowed = (row_id >= col_id) & (col_id < length)
    return jnp.where(allowed, scores, masked_score)


def soft(scores):
    top_score = jnp.max(scores, axis=-1, keepdims=True)
    raised = jnp.exp(scores - top_score)
    return raised / jnp.sum(raised, axis=-1, keepdims=True)


def attend_kernel(heads, head_size, length_ref, line_ref, qkv_ref, mixed_ref):
    scale = head_size ** (-0.5)
    width = heads * head_size
    length = length_ref[pl.program_id(0)]
    for head in range(heads):
        query = qkv_ref[0, :, head * head_size : (head + 1) * head_size]
        key = qkv_ref[0, :, width + head * head_size : width + (head + 1) * head_size]
        value = qkv_ref[0, :, 2 * width + head * head_size : 2 * width + (head + 1) * head_size]
        scores = masked_scores(query, key, line_ref[head : head + 1, :], length, scale)
        probs = soft(scores).astype(BF16)
        mixed = jnp.dot(probs, value, preferred_element_type=F32)
        mixed_ref[0, :, head * head_size : (head + 1) * head_size] = mixed.astype(BF16)


def attend(qkv, lines, lengths, heads):
    micro, seq, width = qkv.shape
    width = width // 3
    head_size = width // heads
    return pl.pallas_call(
        functools.partial(attend_kernel, heads, head_size),
        grid=(micro,),
        out_shape=jax.ShapeDtypeStruct((micro, seq, width), BF16),
        in_specs=[
            pl.BlockSpec(memory_space=pltpu.SMEM),
            pl.BlockSpec(lines.shape, lambda i: (0, 0)),
            pl.BlockSpec((1, seq, 3 * width), lambda i: (i, 0, 0)),
        ],
        out_specs=pl.BlockSpec((1, seq, width), lambda i: (i, 0, 0)),
        compiler_params=pltpu.CompilerParams(vmem_limit_bytes=32 * 2**20),
    )(lengths, lines, qkv)


def diagonal_sums(grad):
    size = grad.shape[0]
    wide = jnp.concatenate([grad, jnp.zeros_like(grad)], axis=1)
    rows = size
    while rows > 1:
        rows //= 2
        lower = pltpu.roll(wide[rows:], 2 * size - rows, 1)
        wide = wide[:rows] + lower
    return wide


def attend_back_kernel(
    heads, head_size, length_ref, line_ref, qkv_ref, grad_ref, out_ref, diag_ref
):
    scale = head_size ** (-0.5)
    width = heads * head_size
    length = length_ref[pl.program_id(0)]

    @pl.when(pl.program_id(0) == 0)
    def _():
        diag_ref[...] = jnp.zeros_like(diag_ref)

    for head in range(heads):
        at = [
            slice(part * width + head * head_size, part * width + (head + 1) * head_size)
            for part in range(3)
        ]
        query, key, value = (qkv_ref[0, :, part] for part in at)
        grad = grad_ref[0, :, at[0]]
        scores = masked_scores(query, key, line_ref[head : head + 1, :], length, scale)
        probs = soft(scores)
        prob_grad = lax.dot_general(
            grad, value, (((1,), (1,)), ((), ())), preferred_element_type=F32
        )
        delta = jnp.sum(probs * prob_grad, axis=-1, keepdims=True)
        score_grad = (probs * (prob_grad - delta)).astype(BF16)
        diag_ref[head : head + 1, :] += diagonal_sums(score_grad.astype(F32))
        query_grad = jnp.dot(score_grad, key, preferred_element_type=F32) * scale
        key_grad = (
            lax.dot_general(
                score_grad, query, (((0,), (0,)), ((), ())), preferred_element_type=F32
            )
            * scale
        )
        value_grad = lax.dot_general(
            probs.astype(BF16), grad, (((0,), (0,)), ((), ())), preferred_element_type=F32
        )
        out_ref[0, :, at[0]] = query_grad.astype(BF16)
        out_ref[0, :, at[1]] = key_grad.astype(BF16)
        out_ref[0, :, at[2]] = value_grad.astype(BF16)


def attend_back(qkv, grad, lines, lengths, heads):
    micro, seq, width = grad.shape
    head_size = width // heads
    return pl.pallas_call(
        functools.partial(attend_back_kernel, heads, head_size),
        grid=(micro,),
        out_shape=(
            jax.ShapeDtypeStruct(qkv.shape, BF16),
            jax.ShapeDtypeStruct(lines.shape, F32),
        ),
        in_specs=[
            pl.BlockSpec(memory_space=pltpu.SMEM),
            pl.BlockSpec(lines.shape, lambda i: (0, 0)),
            pl.BlockSpec((1, seq, 3 * width), lambda i: (i, 0, 0)),
            pl.BlockSpec((1, seq, width), lambda i: (i, 0, 0)),
        ],
        out_specs=(
            pl.BlockSpec((1, seq, 3 * width), lambda i: (i, 0, 0)),
            pl.BlockSpec(lines.shape, lambda i: (0, 0)),
        ),
        compiler_params=pltpu.CompilerParams(vmem_limit_bytes=32 * 2**20),
    )(lengths, lines, qkv, grad)


def halve(value, axis, bit, flag):
    kept = jnp.where(flag, value[1], value[0])
    sent = jnp.where(flag, value[0], value[1]).astype(BF16)
    return kept + swap(sent, axis, bit).astype(F32)


def scatter_sum(value, dp_index, expert_index):
    dp_count, ctx_count, expert_count = value.shape[:3]
    rest = value.shape[3:]
    count, bit = dp_count, 1
    while count > 1:
        shaped = value.reshape((count // 2, 2, -1))
        value = halve(jnp.moveaxis(shaped, 1, 0), "dp", bit, (dp_index // bit) % 2 == 1)
        count //= 2
        bit *= 2
    value = value.reshape((ctx_count, expert_count) + rest)
    count, bit = expert_count, 1
    while count > 1:
        shaped = value.reshape((ctx_count, count // 2, 2) + rest)
        value = halve(jnp.moveaxis(shaped, 2, 0), "experts", bit, (expert_index // bit) % 2 == 1)
        count //= 2
        bit *= 2
    return value.reshape((ctx_count,) + rest)


MESH = pl.DeviceIdType.MESH


def flip(index, bit):
    return index + bit - 2 * bit * ((index // bit) % 2)


def greet(targets):
    barrier = pltpu.get_barrier_semaphore()
    for target in targets:
        pl.semaphore_signal(barrier, inc=1, device_id=target, device_id_type=MESH)
    pl.semaphore_wait(barrier, len(targets))


def remote(source, place, sends, receives, target):
    return pltpu.make_async_remote_copy(
        src_ref=source,
        dst_ref=place,
        send_sem=sends,
        recv_sem=receives,
        device_id=target,
        device_id_type=MESH,
    )


def plain_sums(qkv_total, out_total, router_total, first_total, second_total, own_width):
    width, experts = router_total.shape
    dp_count, ctx_count, expert_count = (lax.axis_size(name) for name in ALL)
    dp_index, ctx_index, expert_index = (lax.axis_index(name) for name in ALL)
    owners = (dp_count, ctx_count, expert_count, -1)
    out_pack = jnp.concatenate([out_total, router_total, second_total[:, None]], axis=1)
    out_pack = jnp.pad(out_pack, ((0, 0), (0, width + 128 - out_pack.shape[1])))
    out_pack = scatter_sum(
        out_pack.reshape(owners + (out_pack.shape[1],)), dp_index, expert_index
    )
    qkv_pack = jnp.pad(
        jnp.concatenate([qkv_total, first_total[:, None]], axis=1), ((0, 0), (0, 127))
    )
    qkv_pack = scatter_sum(
        qkv_pack.reshape(owners + (qkv_pack.shape[1],)), dp_index, expert_index
    )

    def across(value):
        parts = reorder([value[c] for c in range(ctx_count)], ctx_index)
        return [parts[0]] + [
            swap(parts[k].astype(BF16), "context", k).astype(F32) for k in range(1, ctx_count)
        ]

    out_sum = sum(across(out_pack))
    qkv_parts = across(qkv_pack)
    grad_first = sum(part[:, 3 * own_width] for part in qkv_parts)
    qkv_parts = reorder(qkv_parts, ctx_index)
    grads = tuple(
        jnp.concatenate(
            [part[:, i * own_width : (i + 1) * own_width] for part in qkv_parts], axis=1
        )
        for i in range(3)
    )
    return grads + (
        out_sum[:, :width],
        out_sum[:, width : width + experts],
        grad_first,
        out_sum[:, width + experts],
    )


def norm_pull(features, inverse, gain, grad):
    lifted = gain * grad
    mean_part = jnp.mean(lifted * features, axis=-1, keepdims=True)
    back = inverse * lifted - features * (inverse * inverse * inverse) * mean_part
    gain_grad = jnp.sum(grad * features * inverse, axis=(0, 1))
    return back, gain_grad


def gelu_parts(pre):
    root = 0.7978845608028654
    cubic = 0.044715
    square = pre * pre
    wave = jnp.tanh(root * (pre + cubic * pre * square))
    value = 0.5 * pre * (1.0 + wave)
    slope = 0.5 * (1.0 + wave) + 0.5 * pre * (1.0 - wave * wave) * root * (
        1.0 + 3.0 * cubic * square
    )
    return value, slope


def down_routes(dp_count, ctx_count, expert_count, core, ctx_offset):
    pairs = []
    for dp in range(dp_count):
        for ctx in range(ctx_count):
            for expert in range(expert_count):
                high, low = dp // 2, dp % 2
                to_high = high if low == core else high ^ 1
                target = ((to_high * 2 + high) * ctx_count + (ctx ^ ctx_offset)) * expert_count
                pairs.append(((dp * ctx_count + ctx) * expert_count + expert, target + expert))
    return pairs


def plain_body(
    activations,
    cotangent,
    dealing,
    lengths,
    routes,
    buckets,
    w_query,
    w_key,
    w_value,
    w_out,
    w_router,
    norm_first,
    norm_second,
    bias_table,
    w_gate,
    w_up,
    w_down,
):
    micro, _, rows_dev, width = activations.shape
    seq = dealing.shape[2]
    bucket_count, head_count = bias_table.shape
    dp_count, ctx_count, expert_count = (lax.axis_size(name) for name in ALL)
    dp_index, ctx_index, expert_index = (lax.axis_index(name) for name in ALL)
    high, low = dp_index // 2, dp_index % 2
    heads = head_count // ctx_count
    head_size = width // head_count
    own_width = heads * head_size
    experts = w_router.shape[1]
    top_count = routes.shape[3]
    capacity = (5 * rows_dev * top_count + 4 * experts - 1) // (4 * experts)
    slots = -(-capacity // 16) * 16
    ff = w_gate.shape[2]
    half_ff = ff // 2
    weight_rows = w_query.shape[0]
    plane = dp_count * ctx_count
    plane_index = dp_index * ctx_count + ctx_index
    act = activations[:, 0]
    cot = cotangent[:, 0]
    deal = dealing[:, 0]
    length = lengths[:, 0]
    route = routes[:, 0]

    extras = jnp.concatenate(
        [w_router, norm_first[:, None], norm_second[:, None]], axis=1
    )
    extras = jnp.pad(extras, ((0, 0), (0, 128 - extras.shape[1])))
    column_parts = [
        jnp.split(weight, ctx_count, axis=1) for weight in (w_query, w_key, w_value)
    ]
    packs = [
        jnp.concatenate([part[c] for part in column_parts] + [extras], axis=1)
        for c in range(ctx_count)
    ]
    packs = reorder(packs, ctx_index)
    packs = [packs[0]] + [swap(packs[k], "context", k) for k in range(1, ctx_count)]
    packs = jnp.stack(reorder(packs, ctx_index))
    dense = lax.all_gather(packs, ("dp", "experts"), axis=0, tiled=False)
    dense = dense.reshape((dp_count, expert_count) + packs.shape)
    dense = jnp.transpose(dense, (0, 2, 1, 3, 4)).reshape(width, -1)
    qkv_w = dense[:, : 3 * own_width]
    router_w = dense[:, 3 * own_width : 3 * own_width + experts]
    gain_one = dense[:, 3 * own_width + experts].astype(F32)
    gain_two = dense[:, 3 * own_width + experts + 1].astype(F32)
    out_w = lax.all_gather(w_out, ALL, axis=0, tiled=True)

    gate_up = [
        jnp.concatenate([w_gate[0, :, h * half_ff : (h + 1) * half_ff], w_up[0, :, h * half_ff : (h + 1) * half_ff]], axis=1)
        for h in range(2)
    ]
    halves = reorder(gate_up, low)
    gate_blocks = []
    for j in range(plane):
        dp_offset, ctx_offset = j // ctx_count, j % ctx_count
        piece = halves[dp_offset % 2]
        if dp_offset:
            piece = swap(piece, "dp", dp_offset)
        if ctx_offset:
            piece = swap(piece, "context", ctx_offset) if not dp_offset else piece
        gate_blocks.append(piece)
    for j in range(plane):
        dp_offset, ctx_offset = j // ctx_count, j % ctx_count
        if dp_offset and ctx_offset:
            gate_blocks[j] = swap(gate_blocks[dp_offset * ctx_count], "context", ctx_offset)
    gate_up_w = jnp.concatenate(gate_blocks, axis=0)
    down_w = jnp.zeros((half_ff, width), BF16)
    down_rows = w_down.shape[1]
    for ctx_offset in range(ctx_count):
        for core in range(2):
            pairs = down_routes(dp_count, ctx_count, expert_count, core, ctx_offset)
            piece = lax.ppermute(w_down[0], ALL, pairs)
            from_core = jnp.where(low == high, core, 1 - core)
            place = (from_core * ctx_count + (ctx_index ^ ctx_offset)) * down_rows
            down_w = lax.dynamic_update_slice(down_w, piece, (place, 0))

    act_all = jnp.concatenate(
        reorder([act] + [swap(act, "context", k) for k in range(1, ctx_count)], ctx_index), axis=1
    )
    cot_all = jnp.concatenate(
        reorder([cot] + [swap(cot, "context", k) for k in range(1, ctx_count)], ctx_index), axis=1
    )
    position_ids = jnp.arange(seq, dtype=jnp.int32)
    slot_blocks = [
        lax.dynamic_slice_in_dim(deal, (ctx_index ^ k) * rows_dev, rows_dev, axis=1)
        for k in range(ctx_count)
    ]
    hot = [
        (block[:, :, None] == position_ids[None, None, :]).astype(BF16) for block in slot_blocks
    ]
    my_positions = ctx_index * rows_dev + jnp.arange(rows_dev, dtype=jnp.int32)
    hot_mine = [
        (block[:, :, None] == my_positions[None, None, :]).astype(BF16) for block in slot_blocks
    ]
    live = slot_blocks[0] < length[:, None]
    live_rows = live.astype(F32)[:, :, None]
    bucket_hot = (buckets[:, None] == jnp.arange(bucket_count)[None, :]).astype(BF16)
    own_table = lax.dynamic_slice_in_dim(bias_table, ctx_index * heads, heads, axis=1)
    lookup = dot_f32("sb,bh->hs", bucket_hot, own_table)
    lines = jnp.concatenate(
        [lookup[:, :1], jnp.zeros((heads, seq), F32), lookup[:, :0:-1]], axis=1
    )

    rows_all = act_all.astype(F32)
    inverse_one = lax.rsqrt(jnp.mean(rows_all * rows_all, axis=-1, keepdims=True) + epsilon)
    normed = (rows_all * inverse_one * gain_one).astype(BF16)
    qkv = dot_f32("mpd,dw->mpw", normed, qkv_w).astype(BF16)
    mixed_own = attend(qkv, lines, length, heads)
    mixed_parts = [
        dot_f32("msp,mpw->msw", hot[k], mixed_own).astype(BF16) for k in range(ctx_count)
    ]
    mixed_parts = [mixed_parts[0]] + [
        swap(mixed_parts[k], "context", k) for k in range(1, ctx_count)
    ]
    mixed = jnp.concatenate(reorder(mixed_parts, ctx_index), axis=-1)

    rows_in = dot_f32("msp,mpd->msd", hot[0], act_all)
    cot_rows = dot_f32("msp,mpd->msd", hot[0], cot_all)
    branch = dot_f32("msi,io->mso", mixed, out_w)
    hidden = rows_in + branch * live_rows
    inverse_two = lax.rsqrt(jnp.mean(hidden * hidden, axis=-1, keepdims=True) + epsilon)
    normed_two = (hidden * inverse_two * gain_two).astype(BF16)
    logits = dot_f32("msd,de->mse", normed_two, router_w)
    route_hot = (route[..., None] == jnp.arange(experts)).astype(F32)
    chosen = jnp.sum(route_hot * logits[:, :, None, :], axis=3)
    gate_probs = jax.nn.softmax(chosen, axis=-1)

    flat_hot = (route_hot * live_rows[..., None]).reshape(micro, rows_dev * top_count, experts)
    pair_ids = jnp.arange(rows_dev * top_count)
    before = (pair_ids[:, None] > pair_ids[None, :]).astype(BF16)
    earlier = dot_f32("ab,mbe->mae", before, flat_hot.astype(BF16))
    rank = jnp.sum(earlier * flat_hot, axis=2).astype(jnp.int32).reshape(route.shape)
    kept = live[:, :, None] & (rank < capacity)
    target = jnp.where(kept, (route ^ expert_index) * slots + rank, -1)
    place_ids = jnp.arange(experts * slots, dtype=jnp.int32)
    pick = [
        (target[:, None, :, j] == place_ids[None, :, None]) for j in range(top_count)
    ]
    pick_any = functools.reduce(jnp.logical_or, pick).astype(BF16)
    pick_bf = [p.astype(BF16) for p in pick]
    prob_rows = sum(
        jnp.sum(jnp.where(pick[j], gate_probs[:, None, :, j], 0.0), axis=2)
        for j in range(top_count)
    )

    def by_expert(value):
        shaped = value.reshape((micro, experts, slots) + value.shape[2:])
        return jnp.moveaxis(shaped, 1, 0)

    def exchange(value):
        parts = [value[0]] + [swap(value[k], "experts", k) for k in range(1, expert_count)]
        return jnp.stack(parts)

    normed_rel = reorder_lanes(normed_two, plane, plane_index)
    sent_rows = by_expert(dot_f32("mrs,msd->mrd", pick_any, normed_rel).astype(BF16))
    sent_up = by_expert(
        dot_f32("mrs,msd->mrd", pick_any, cot_rows.astype(BF16)).astype(BF16)
    )
    row_count = expert_count * micro * slots
    own_x = exchange(sent_rows).reshape(row_count, width)
    own_u = exchange(sent_up).reshape(row_count, width)
    own_p = exchange(by_expert(prob_rows)).reshape(row_count, 1)
    own_g = (own_p * own_u.astype(F32)).astype(BF16)

    def core_swap(value):
        blocks = jnp.split(value, plane, axis=-1)
        return jnp.concatenate([blocks[j ^ ctx_count] for j in range(plane)], axis=-1)

    all_x = jnp.concatenate([own_x, core_swap(swap(own_x, "dp", 1))], axis=0)
    all_g = jnp.concatenate([own_g, swap(own_g, "dp", 1)], axis=0)

    pre_up = dot_f32("rd,df->rf", all_x, gate_up_w)
    gelu_value, gelu_slope = gelu_parts(pre_up[:, :half_ff])
    up_part = pre_up[:, half_ff:]
    activated = (gelu_value * up_part).astype(BF16)
    act_grad = dot_f32("rd,fd->rf", all_g, down_w)
    pre_grad = (act_grad * up_part * gelu_slope).astype(BF16)
    up_grad = (act_grad * gelu_value).astype(BF16)
    both_grad = jnp.concatenate([pre_grad, up_grad], axis=1)
    back_part = dot_f32("rf,df->rd", both_grad, gate_up_w)
    out_part = dot_f32("rf,fd->rd", activated, down_w)
    out_own = (
        out_part[:row_count] + swap(out_part[row_count:].astype(BF16), "dp", 1).astype(F32)
    ).astype(BF16)
    back_own = (
        back_part[:row_count]
        + swap(core_swap(back_part[row_count:].astype(BF16)), "dp", 1).astype(F32)
    ).astype(BF16)
    gate_rows = jnp.sum(own_u.astype(F32) * out_own.astype(F32), axis=-1)

    def to_source(value):
        parts = value.reshape((expert_count, micro, slots) + value.shape[1:])
        parts = exchange(parts)
        return jnp.moveaxis(parts, 0, 1).reshape((micro, experts * slots) + value.shape[1:])

    back_rows = to_source(back_own)
    gate_back = to_source(gate_rows)
    out_rows = to_source(out_own)

    gate_up_total = dot_f32("rd,rf->df", all_x, both_grad)
    down_total = dot_f32("rf,rd->fd", activated, all_g)

    gate_up_sums = [0.0, 0.0]
    for j in range(plane):
        dp_offset, ctx_offset = j // ctx_count, j % ctx_count
        block = gate_up_total[j * (width // plane) : (j + 1) * (width // plane)].astype(BF16)
        pairs = [
            (
                (d * ctx_count + c) * expert_count + e,
                ((d ^ dp_offset) * ctx_count + (c ^ ctx_offset)) * expert_count + e,
            )
            for d in range(dp_count)
            for c in range(ctx_count)
            for e in range(expert_count)
        ]
        if j:
            block = lax.ppermute(block, ALL, pairs)
        gate_up_sums[dp_offset % 2] = gate_up_sums[dp_offset % 2] + block.astype(F32)
    first_half, second_half = reorder(gate_up_sums, low)
    grad_gate = jnp.concatenate([first_half[:, :half_ff], second_half[:, :half_ff]], axis=1)
    grad_up = jnp.concatenate([first_half[:, half_ff:], second_half[:, half_ff:]], axis=1)
    grad_down = 0.0
    for ctx_offset in range(ctx_count):
        for core in range(2):
            pairs = down_routes(dp_count, ctx_count, expert_count, core, ctx_offset)
            from_core = jnp.where(low == high, core, 1 - core)
            place = (from_core * ctx_count + (ctx_index ^ ctx_offset)) * down_rows
            piece = lax.dynamic_slice_in_dim(down_total, place, down_rows, axis=0).astype(BF16)
            arrived = lax.ppermute(piece, ALL, [(b, a) for a, b in pairs])
            grad_down = grad_down + arrived.astype(F32)

    pair_out = [dot_f32("mrs,mrd->msd", pick_bf[j], out_rows) for j in range(top_count)]
    final = hidden + sum(gate_probs[:, :, j, None] * pair_out[j] for j in range(top_count))
    final = final.astype(BF16)
    gate_grad = jnp.stack(
        [
            jnp.sum(jnp.where(pick[j], gate_back[:, :, None], 0.0), axis=1)
            for j in range(top_count)
        ],
        axis=-1,
    )
    chosen_grad = gate_probs * (
        gate_grad - jnp.sum(gate_probs * gate_grad, axis=-1, keepdims=True)
    )
    logit_grad = jnp.sum(route_hot * chosen_grad[..., None], axis=2).astype(BF16)
    normed_grad = reorder_lanes(
        dot_f32("mrs,mrd->msd", pick_any, back_rows), plane, plane_index
    ) + dot_f32("mse,de->msd", logit_grad, router_w)
    router_total = dot_f32("msd,mse->de", normed_two, logit_grad)
    hidden_norm_grad, second_total = norm_pull(hidden, inverse_two, gain_two, normed_grad)
    hidden_grad = cot_rows + hidden_norm_grad
    branch_grad = (hidden_grad * live_rows).astype(BF16)
    hidden_low = hidden_grad.astype(BF16)
    out_total = dot_f32("msi,mso->io", mixed, branch_grad)
    mixed_grad = dot_f32("mso,io->msi", branch_grad, out_w).astype(BF16)
    grad_parts = reorder(jnp.split(mixed_grad, ctx_count, axis=-1), ctx_index)
    grad_parts = [grad_parts[0]] + [
        swap(grad_parts[k], "context", k) for k in range(1, ctx_count)
    ]
    mixed_back = sum(
        dot_f32("msp,msw->mpw", hot[k], grad_parts[k]) for k in range(ctx_count)
    ).astype(BF16)
    qkv_grad, diagonals = attend_back(qkv, mixed_back, lines, length, heads)
    qkv_total = dot_f32("mpd,mpw->dw", normed, qkv_grad)
    first_part = dot_f32("mpw,dw->mpd", qkv_grad, qkv_w)
    first_total = jnp.sum(first_part * rows_all * inverse_one, axis=(0, 1))
    blocks = [
        lax.dynamic_slice_in_dim(first_part, (ctx_index ^ k) * rows_dev, rows_dev, axis=1)
        for k in range(ctx_count)
    ]
    first_grad = blocks[0] + sum(
        swap(blocks[k].astype(BF16), "context", k).astype(F32) for k in range(1, ctx_count)
    )

    def to_positions(value):
        parts = [value] + [swap(value, "context", k) for k in range(1, ctx_count)]
        return sum(dot_f32("msp,msd->mpd", hot_mine[k], parts[k]) for k in range(ctx_count))

    rows_mine = act.astype(F32)
    inverse_mine = lax.rsqrt(jnp.mean(rows_mine * rows_mine, axis=-1, keepdims=True) + epsilon)
    rows_back, _ = norm_pull(rows_mine, inverse_mine, gain_one, first_grad)
    grad_input = (to_positions(hidden_low) + rows_back).astype(BF16)[:, None]
    output = to_positions(final).astype(BF16)[:, None]

    sums = plain_sums(
        qkv_total, out_total, router_total, first_total, second_total, own_width
    )
    grad_query, grad_key, grad_value, grad_out, grad_router, grad_first, grad_second = sums
    diag_all = lax.all_gather(
        lax.psum(diagonals, ("dp", "experts")), "context", axis=0, tiled=True
    )
    offsets = jnp.concatenate([diag_all[:, :1], diag_all[:, : seq : -1]], axis=1)
    grad_table = jnp.einsum(
        "hs,sb->bh", offsets, bucket_hot.astype(F32), precision=lax.Precision.HIGHEST
    )
    return (
        output,
        grad_input,
        grad_query,
        grad_key,
        grad_value,
        grad_out,
        grad_router,
        grad_first,
        grad_second,
        grad_table,
        grad_gate[None],
        grad_up[None],
        grad_down[None],
    )


class Wires:
    def __init__(self, sends, receives, homes):
        self.sends, self.receives, self.homes = sends, receives, homes
        self.used, self.used_home = 0, 0

    def take(self):
        self.used += 1
        return self.used - 1

    def copy(self, source, place, peer, index):
        return remote(source, place, self.sends.at[index], self.receives.at[index], peer)

    def home(self, source, place):
        copy = pltpu.make_async_copy(source, place, self.homes.at[self.used_home])
        self.used_home += 1
        return copy


class Spread:
    def __init__(self, wires, buf, ctx_axis):
        self.wires, self.buf = wires, buf
        dp, ctx, exp = (lax.axis_index(name) for name in ALL)
        self.high, self.low, self.exp = dp // 2, dp % 2, exp
        self.last = lax.axis_size("experts") - 1
        self.core_peer = (flip(dp, 1), ctx, exp)
        self.x_peer = (flip(dp, 2), ctx, exp)
        self.up_peer = (dp, ctx, jnp.minimum(exp + 1, self.last))
        self.down_peer = (dp, ctx, jnp.maximum(exp - 1, 0))
        self.labels = [(0, 0)] + [(h, d) for h in range(1, self.last + 1) for d in (1, -1)]
        self.z_wire, self.x_wire, self.own_wire, self.far_wire = (
            {label: wires.take() for label in self.labels} for _ in range(4)
        )

    def block(self, label):
        hop, way = label
        return jnp.clip(self.exp - hop * way, 0, self.last) if hop else self.exp

    def when(self, label):
        hop, way = label
        if hop == 0:
            return lambda f: f()
        here = self.exp - hop * way
        return pl.when((here >= 0) & (here <= self.last))

    def can_send(self, label, act):
        hop, way = label
        held = self.exp - (hop - 1) * way
        ahead = self.exp + way
        pl.when((held >= 0) & (held <= self.last) & (ahead >= 0) & (ahead <= self.last))(act)

    def z_copy(self, label):
        hop, way = label
        held = jnp.clip(self.exp - (hop - 1) * way, 0, self.last)
        part = self.buf.at[self.high, self.low, :, held]
        peer = self.up_peer if way == 1 else self.down_peer
        return self.wires.copy(part, part, peer, self.z_wire[label])

    def part_copy(self, label, high, wire, peer):
        part = self.buf.at[high, self.low, :, self.block(label)]
        return self.wires.copy(part, part, peer, wire[label])

    def x_copy(self, label):
        return self.part_copy(label, self.high, self.x_wire, self.x_peer)

    def own_copy(self, label):
        return self.part_copy(label, self.high, self.own_wire, self.core_peer)

    def far_copy(self, label):
        return self.part_copy(label, 1 - self.high, self.far_wire, self.core_peer)

    def spread(self, label):
        self.x_copy(label).start()
        self.own_copy(label).start()

    def begin(self):
        for way in (1, -1):
            self.can_send((1, way), lambda way=way: self.z_copy((1, way)).start())
        self.spread((0, 0))

    def hop(self, hop):
        for way in (1, -1):
            label = (hop, way)

            @self.when(label)
            def _(label=label):
                part = self.buf.at[self.high, self.low, :, self.block(label)]
                self.wires.copy(part, part, self.up_peer, self.z_wire[label]).wait_recv()

            if hop < self.last:
                nxt = (hop + 1, way)
                self.can_send(nxt, lambda nxt=nxt: self.z_copy(nxt).start())

            @self.when(label)
            def _(label=label):
                self.spread(label)

        for label in self.labels:
            if label[0] == hop - 1:
                self.pass_far(label)

    def pass_far(self, label):
        @self.when(label)
        def _():
            self.x_copy(label).wait_recv()
            self.far_copy(label).start()

    def end(self):
        for label in self.labels:
            if label[0] == self.last:
                self.pass_far(label)
        for label in self.labels:

            @self.when(label)
            def _(label=label):
                self.own_copy(label).wait_recv()
                self.far_copy(label).wait_recv()

    def drain(self):
        for label in self.labels:
            if label[0]:
                self.can_send(label, lambda label=label: self.z_copy(label).wait_send())

            @self.when(label)
            def _(label=label):
                self.x_copy(label).wait_send()
                self.own_copy(label).wait_send()
                self.far_copy(label).wait_send()


def front_kernel(
    sizes,
    act_ref,
    cot_ref,
    deal_ref,
    length_ref,
    route_ref,
    line_ref,
    query_ref,
    key_ref,
    value_ref,
    out_ref,
    extra_ref,
    gate_ref,
    up_ref,
    down_ref,
    hidden_ref,
    logit_ref,
    mixed,
    cot_rows_ref,
    dense_save,
    out_save,
    act_save,
    normed_save,
    qkv_save,
    x_save,
    u_save,
    g_save,
    gate_save,
    down_save,
    both_save,
    activated_save,
    dense,
    out_w,
    act_all,
    normed_ref,
    qkv_ref,
    all_x,
    all_u,
    all_p,
    all_g,
    gate_up,
    down,
    both,
    activated,
    cot_all,
    mixed_own,
    mixed_sent,
    sent_x,
    sent_u,
    sent_p,
    sends,
    receives,
    homes,
):
    heads, head_size, experts, capacity, slots = sizes
    micro, rows_dev, width = act_ref.shape
    own_width = heads * head_size
    half = gate_ref.shape[1] // 2
    dp, ctx, exp = (lax.axis_index(name) for name in ALL)
    high, low = dp // 2, dp % 2
    block = dp * 2 + ctx
    core_peer, x_peer, x_core = ((flip(dp, 1), ctx, exp), (flip(dp, 2), ctx, exp), (3 - dp, ctx, exp))
    x_core = (flip(flip(dp, 2), 1), ctx, exp)
    y_peer, y_core = (dp, 1 - ctx, exp), (flip(dp, 1), 1 - ctx, exp)
    z_peers = [None] + [(dp, ctx, flip(exp, 1)), (dp, ctx, flip(exp, 2)), (dp, ctx, 3 - exp)]
    z_index = [exp, flip(exp, 1), flip(exp, 2), 3 - exp]
    greet([core_peer, x_peer, x_core, y_peer, y_core] + z_peers[1:])
    wires = Wires(sends, receives, homes)
    drains = []
    home_copies = []

    def send(source, place, peer):
        copy = wires.copy(source, place, peer, wires.take())
        copy.start()
        drains.append(copy)
        return copy

    def multiple(index, size):
        return pl.ds(pl.multiple_of(index * size, size), size)

    def save(source, place):
        copy = wires.home(source, place)
        copy.start()
        home_copies.append(copy)

    mine, other = multiple(ctx, own_width), multiple(1 - ctx, own_width)
    first = []
    for i, ref in enumerate((query_ref, key_ref, value_ref)):
        place = dense.at[high, low, ctx, exp, :, i * own_width : (i + 1) * own_width]
        first.append(send(ref.at[:, other], place, y_peer))
    first.append(send(extra_ref, dense.at[high, low, ctx, exp, :, 3 * own_width :], y_peer))
    out_first = send(out_ref, out_w.at[high, low, ctx, exp], y_peer)
    here = multiple(ctx, rows_dev)
    act_first = send(act_ref, act_all.at[:, here], y_peer)
    def gate_sends(core, peer):
        cols = multiple(core, half)
        return [
            send(gate_ref.at[:, cols], gate_up.at[block, :, 0:half], peer),
            send(up_ref.at[:, cols], gate_up.at[block, :, half:], peer),
        ]

    own_gate = []
    for ref, start in ((gate_ref, 0), (up_ref, half)):
        copy = wires.home(ref.at[:, multiple(low, half)], gate_up.at[block, :, start : start + half])
        copy.start()
        own_gate.append(copy)

    for i, ref in enumerate((query_ref, key_ref, value_ref)):
        dense[high, low, ctx, exp, :, i * own_width : (i + 1) * own_width] = ref[:, mine]
    dense[high, low, ctx, exp, :, 3 * own_width :] = extra_ref[...]
    out_w[high, low, ctx, exp] = out_ref[...]
    act_all[:, here, :] = act_ref[...]
    cot_all[:, here, :] = cot_ref[...]

    spread = Spread(wires, dense, 2)
    spread_out = Spread(wires, out_w, 2)
    for copy in first:
        copy.wait_recv()
    spread.begin()
    cot_first = send(cot_ref, cot_all.at[:, here], y_peer)
    from_y_core = gate_sends(1 - low, y_core)
    from_y = gate_sends(low, y_peer)
    from_core = gate_sends(1 - low, core_peer)

    spread.hop(1)

    own_down = low * 2 + ctx
    home_down = wires.home(down_ref, down.at[own_down])
    down_wire = {name: wires.take() for name in ("core", "x", "xc", "y", "yc", "rx", "ry")}
    at_home = low == high

    def down_copy(name, peer, source=None):
        source = down_ref if source is None else source
        return wires.copy(source, down.at[own_down], peer, down_wire[name])

    down_sends = [
        ("core", core_peer, False),
        ("x", x_peer, True),
        ("xc", x_core, False),
        ("y", y_peer, True),
        ("yc", y_core, False),
    ]

    def down_start():
        @pl.when(at_home)
        def _():
            home_down.start()

        for name, peer, straight in down_sends:
            pl.when(at_home == straight)(lambda name=name, peer=peer: down_copy(name, peer).start())

    lane = lax.broadcasted_iota(jnp.int32, (rows_dev, 128), 1)
    lane_f = lane.astype(F32)
    row_id = lax.broadcasted_iota(jnp.int32, (rows_dev, rows_dev), 0)
    col_id = lax.broadcasted_iota(jnp.int32, (rows_dev, rows_dev), 1)
    before = (row_id > col_id).astype(BF16)
    seq = deal_ref.shape[1]
    seq_lane = lax.broadcasted_iota(jnp.int32, (rows_dev, seq), 1)

    def hot(m, k):
        index = ctx if k == 0 else 1 - ctx
        return (deal_ref[m, multiple(index, rows_dev), :] == seq_lane).astype(BF16)

    def live_slots(m):
        return deal_ref[m, here, :] < length_ref[m]

    def ranks(m):
        live = live_slots(m)
        hots = [(route_ref[m, :, j : j + 1] == lane) for j in range(2)]
        used = jnp.where((hots[0] | hots[1]) & live, 1.0, 0.0).astype(BF16)
        earlier = jnp.dot(before, used, preferred_element_type=F32)
        found = []
        for j in range(2):
            rank = jnp.sum(jnp.where(hots[j], earlier, 0.0), axis=1, keepdims=True)
            found.append(jnp.where(live & (rank < capacity), rank, -1.0))
        return found

    def picks(m, k, rank):
        return [
            (route_ref[m, :, j : j + 1] == z_index[k]) & (rank[j] == lane_f) for j in range(2)
        ]

    def as_rows(pick, value):
        chosen = lax.dot_general(
            pick, value, (((0,), (0,)), ((), ())), preferred_element_type=F32
        )
        return chosen[:slots].astype(BF16)

    spread.hop(2)
    rank_of = [ranks(m) for m in range(micro)]
    act_first.wait_recv()
    spread.hop(3)
    cot_first.wait_recv()
    pick_of = {}
    for m in range(micro):
        hot_mine = hot(m, 0)
        cot_rows = jnp.dot(hot_mine, cot_all[m], preferred_element_type=F32).astype(BF16)
        cot_rows_ref[m] = cot_rows
        for k in range(experts):
            pick = picks(m, k, rank_of[m])
            pick_any = jnp.where(pick[0] | pick[1], 1.0, 0.0).astype(BF16)
            rows = as_rows(pick_any, cot_rows)
            if k == 0:
                all_u[0, 0, m] = rows
            else:
                sent_u[k - 1, m] = rows
    out_first.wait_recv()
    spread.end()
    from_x = gate_sends(low, x_peer)
    from_x_core = gate_sends(1 - low, x_core)
    spread_out.begin()
    save(dense, dense_save)
    save(act_all, act_save)
    u_first, u_core = {}, []

    def send_u(m):
        for k in range(1, experts):
            u_first[k, m] = send(sent_u.at[k - 1, m], all_u.at[0, k, m], z_peers[k])
        u_core.append(send(all_u.at[0, 0, m], all_u.at[1, 0, m], core_peer))

    def pass_u(m):
        for k in range(1, experts):
            u_first[k, m].wait_recv()
            u_core.append(send(all_u.at[0, k, m], all_u.at[1, k, m], core_peer))

    send_u(0)

    extras = dense[:, :, :, :, :, 3 * own_width :].reshape(width, 128).astype(F32)
    turned = extras.T
    gain_one, gain_two = turned[experts : experts + 1], turned[experts + 1 : experts + 2]
    for m in range(micro):
        rows = act_all[m].astype(F32)
        inverse = lax.rsqrt(jnp.mean(rows * rows, axis=-1, keepdims=True) + epsilon)
        normed_ref[m] = (rows * inverse * gain_one).astype(BF16)
    for i in range(3):
        weight = dense[:, :, :, :, :, i * own_width : (i + 1) * own_width].reshape(width, own_width)
        for m in range(micro):
            qkv_ref[m, :, i * own_width : (i + 1) * own_width] = jnp.dot(
                normed_ref[m], weight, preferred_element_type=F32
            ).astype(BF16)
    spread_out.hop(1)

    scale = head_size ** (-0.5)
    mixed_first = []
    save(normed_ref, normed_save)
    save(qkv_ref, qkv_save)
    for m in range(micro):
        length = length_ref[m]
        for head in range(heads):
            at = [
                slice(part * own_width + head * head_size, part * own_width + (head + 1) * head_size)
                for part in range(3)
            ]
            scores = masked_scores(
                qkv_ref[m, :, at[0]], qkv_ref[m, :, at[1]], line_ref[head : head + 1, :], length, scale
            )
            probs = soft(scores).astype(BF16)
            mixed_own[:, at[0]] = jnp.dot(
                probs, qkv_ref[m, :, at[2]], preferred_element_type=F32
            ).astype(BF16)
        own = mixed_own[...]
        mixed_sent[m] = jnp.dot(hot(m, 1), own, preferred_element_type=F32).astype(BF16)
        mixed_first.append(send(mixed_sent.at[m], mixed.at[m, :, mine], y_peer))
        mixed[m, :, mine] = jnp.dot(hot(m, 0), own, preferred_element_type=F32).astype(BF16)
        spread_out.hop(2 + m)
    spread_out.end()

    router_w = dense[:, :, :, :, :, 3 * own_width :].reshape(width, 128)
    x_first, p_first, x_core_copy, core_copies = {}, {}, {}, []
    for m in range(micro):
        mixed_first[m].wait_recv()
        branch = jnp.dot(
            mixed[m], out_w[...].reshape(width, width), preferred_element_type=F32
        )
        rows_in = jnp.dot(hot(m, 0), act_all[m], preferred_element_type=F32)
        live = live_slots(m)
        hidden = rows_in + jnp.where(live, branch, 0.0)
        hidden_ref[m] = hidden
        inverse = lax.rsqrt(jnp.mean(hidden * hidden, axis=-1, keepdims=True) + epsilon)
        normed_two = (hidden * inverse * gain_two).astype(BF16)
        logits = jnp.dot(normed_two, router_w, preferred_element_type=F32)
        logit_ref[m] = logits
        chosen = [
            jnp.sum(jnp.where(route_ref[m, :, j : j + 1] == lane, logits, 0.0), axis=1, keepdims=True)
            for j in range(2)
        ]
        top = jnp.maximum(chosen[0], chosen[1])
        raised = [jnp.exp(c - top) for c in chosen]
        total = raised[0] + raised[1]
        gates = [r / total for r in raised]
        for k in range(experts):
            pick = picks(m, k, rank_of[m])
            pick_any = jnp.where(pick[0] | pick[1], 1.0, 0.0).astype(BF16)
            rows = as_rows(pick_any, normed_two)
            weights = jnp.sum(
                jnp.where(pick[0], gates[0], 0.0) + jnp.where(pick[1], gates[1], 0.0),
                axis=0,
                keepdims=True,
            )
            weights = jnp.broadcast_to(weights, (8, 128))
            if k == 0:
                all_x[0, 0, m] = rows
                all_p[0, 0, m] = weights
                x_core_copy[0, m] = send(all_x.at[0, 0, m], all_x.at[1, 0, m], core_peer)
                core_copies.append(send(all_p.at[0, 0, m], all_p.at[1, 0, m], core_peer))
            else:
                sent_x[k - 1, m] = rows
                sent_p[k - 1, m] = weights
                x_first[k, m] = send(sent_x.at[k - 1, m], all_x.at[0, k, m], z_peers[k])
                p_first[k, m] = send(sent_p.at[k - 1, m], all_p.at[0, k, m], z_peers[k])

    for m in range(1, micro):
        send_u(m)
    save(out_w, out_save)
    for copy in from_x:
        copy.wait_recv()
    x_block = flip(dp, 2) * 2 + ctx
    relay_y = send(gate_up.at[x_block], gate_up.at[x_block], y_peer)
    for copy in from_y_core:
        copy.wait_recv()
    y_block = flip(dp, 1) * 2 + 1 - ctx
    relay_x = send(gate_up.at[y_block], gate_up.at[y_block], x_peer)

    down_start()
    pass_u(0)

    def pass_rows(k):
        for m in range(micro):
            x_first[k, m].wait_recv()
            x_core_copy[k, m] = send(all_x.at[0, k, m], all_x.at[1, k, m], core_peer)
            p_first[k, m].wait_recv()
            core_copies.append(send(all_p.at[0, k, m], all_p.at[1, k, m], core_peer))

    def hidden_units(k):
        for m in range(micro):
            x_core_copy[k, m].wait_recv()
        count = 2 * micro * slots
        shape = (2, micro, slots)

        def tile(start, size):
            rows = all_x[:, k].reshape(count, width)
            gate_w = gate_up[:, :, pl.ds(start, size)].reshape(width, size)
            up_w = gate_up[:, :, pl.ds(half + start, size)].reshape(width, size)
            pre = jnp.dot(rows, gate_w, preferred_element_type=F32)
            up_part = jnp.dot(rows, up_w, preferred_element_type=F32)
            value, slope = gelu_parts(pre)
            activated[:, k, :, :, pl.ds(start, size)] = (
                (value * up_part).astype(BF16).reshape(shape + (size,))
            )
            both[:, k, :, :, pl.ds(start, size)] = (
                (up_part * slope).astype(BF16).reshape(shape + (size,))
            )
            both[:, k, :, :, pl.ds(half + start, size)] = value.astype(BF16).reshape(shape + (size,))

        wide = half // 256

        def step(i, carry):
            tile(pl.multiple_of(i * 256, 256), 256)
            return carry

        lax.fori_loop(0, wide, step, 0)
        if half % 256:
            tile(wide * 256, half - wide * 256)

    for k in (1, 2):
        pass_rows(k)
    for copy in from_core + from_y + from_x_core + [relay_x, relay_y]:
        copy.wait_recv()
    for copy in own_gate:
        copy.wait()
    save(gate_up, gate_save)
    hidden_units(0)
    hidden_units(1)
    away = jnp.logical_not(at_home)
    rx_place = low * 2 + 1 - ctx
    ry_place = (1 - low) * 2 + ctx

    @pl.when(at_home)
    def _():
        down_copy("y", y_peer).wait_recv()
        wires.copy(down.at[rx_place], down.at[rx_place], x_peer, down_wire["rx"]).start()

    @pl.when(away)
    def _():
        down_copy("xc", x_core).wait_recv()
        wires.copy(down.at[ry_place], down.at[ry_place], y_peer, down_wire["ry"]).start()

    pass_rows(3)
    hidden_units(2)
    hidden_units(3)
    save(both, both_save)
    save(activated, activated_save)
    save(all_x, x_save)
    for m in range(1, micro):
        pass_u(m)
    for copy in u_core + core_copies:
        copy.wait_recv()
    save(all_u.at[0], u_save)
    for part in range(2):
        for k in range(experts):
            for m in range(micro):
                column = jnp.broadcast_to(all_p[part, k, m, 0:1, :], (128, 128)).T[:slots, 0:1]
                all_g[part, k, m] = (column * all_u[part, k, m].astype(F32)).astype(BF16)
    save(all_g, g_save)

    @pl.when(at_home)
    def _():
        for name in ("core", "yc"):
            down_copy(name, core_peer).wait_recv()
        home_down.wait()
        down_copy("rx", x_peer).wait_send()

    @pl.when(away)
    def _():
        for name in ("x", "rx", "ry"):
            down_copy(name, core_peer).wait_recv()
        down_copy("ry", y_peer).wait_send()

    save(down, down_save)
    for name, peer, straight in down_sends:
        pl.when(at_home == straight)(lambda name=name, peer=peer: down_copy(name, peer).wait_send())
    for copy in home_copies:
        copy.wait()
    for copy in drains:
        copy.wait_send()
    spread.drain()
    spread_out.drain()


def front(sizes, act, cot, deal, length, route, lines, weights, extras, w_gate, w_up, w_down):
    heads, head_size, experts, capacity, slots = sizes
    micro, rows_dev, width = act.shape
    own_width = heads * head_size
    per_row = weights[0].shape[0]
    seq = deal.shape[1]
    half = w_gate.shape[1] // 2
    in_vmem, in_hbm = pl.BlockSpec(memory_space=pltpu.VMEM), pl.BlockSpec(memory_space=pltpu.HBM)
    wide = 3 * own_width + 128
    rows = (2, experts, micro, slots)
    outs = [
        ((micro, rows_dev, width), F32),
        ((micro, rows_dev, 128), F32),
        ((micro, rows_dev, width), BF16),
        ((micro, rows_dev, width), BF16),
    ]
    saved = [
        ((2, 2, 2, 4, per_row, wide), BF16),
        ((2, 2, 2, 4, per_row, width), BF16),
        ((micro, seq, width), BF16),
        ((micro, seq, width), BF16),
        ((micro, seq, 3 * own_width), BF16),
        (rows + (width,), BF16),
        (rows[1:] + (width,), BF16),
        (rows + (width,), BF16),
        ((8,) + (w_gate.shape[0], 2 * half), BF16),
        ((4,) + w_down.shape, BF16),
        (rows + (2 * half,), BF16),
        (rows + (half,), BF16),
    ]
    held = (
        saved[:6]
        + [(rows + (width,), BF16), ((2, experts, micro, 8, 128), F32)]
        + saved[7:]
    )
    return pl.pallas_call(
        functools.partial(front_kernel, sizes),
        out_shape=tuple(jax.ShapeDtypeStruct(*out) for out in outs + saved),
        in_specs=[in_vmem] * 3 + [pl.BlockSpec(memory_space=pltpu.SMEM)] + [in_vmem] * 7 + [in_hbm] * 3,
        out_specs=(in_vmem,) * len(outs) + (in_hbm,) * len(saved),
        scratch_shapes=[pltpu.VMEM(*shape) for shape in held]
        + [
            pltpu.VMEM((micro, seq, width), BF16),
            pltpu.VMEM((seq, own_width), BF16),
            pltpu.VMEM((micro, rows_dev, own_width), BF16),
            pltpu.VMEM((experts - 1, micro, slots, width), BF16),
            pltpu.VMEM((experts - 1, micro, slots, width), BF16),
            pltpu.VMEM((experts - 1, micro, 8, 128), F32),
            pltpu.SemaphoreType.DMA((160,)),
            pltpu.SemaphoreType.DMA((160,)),
            pltpu.SemaphoreType.DMA((24,)),
        ],
        compiler_params=pltpu.CompilerParams(
            collective_id=1, has_side_effects=True, vmem_limit_bytes=60 * 2**20
        ),
    )(act, cot, deal[:, :, None], length, route, lines, *weights, extras, w_gate, w_up, w_down)


class Plan:
    def __init__(self, deal_ref, length_ref, route_ref, rows_dev, capacity):
        self.deal, self.length, self.route = deal_ref, length_ref, route_ref
        self.rows, self.capacity = rows_dev, capacity
        self.ctx, exp = lax.axis_index("context"), lax.axis_index("experts")
        self.z_index = [exp, flip(exp, 1), flip(exp, 2), 3 - exp]
        self.lane = lax.broadcasted_iota(jnp.int32, (rows_dev, 128), 1)
        self.lane_f = self.lane.astype(F32)

    def at(self, k):
        index = self.ctx if k == 0 else 1 - self.ctx
        return pl.ds(pl.multiple_of(index * self.rows, self.rows), self.rows)

    def hot(self, m, k):
        seq = self.deal.shape[1]
        lane = lax.broadcasted_iota(jnp.int32, (self.rows, seq), 1)
        return (self.deal[m, self.at(k), :] == lane).astype(BF16)

    def hot_mine(self, m, k):
        lane = lax.broadcasted_iota(jnp.int32, (self.rows, self.rows), 1) + self.ctx * self.rows
        return (self.deal[m, self.at(k), :] == lane).astype(BF16)

    def live(self, m):
        return self.deal[m, self.at(0), :] < self.length[m]

    def named(self, m, j):
        return self.route[m, :, j : j + 1]

    def ranks(self, m):
        row_id = lax.broadcasted_iota(jnp.int32, (self.rows, self.rows), 0)
        col_id = lax.broadcasted_iota(jnp.int32, (self.rows, self.rows), 1)
        before = (row_id > col_id).astype(BF16)
        live = self.live(m)
        hots = [self.named(m, j) == self.lane for j in range(2)]
        used = jnp.where((hots[0] | hots[1]) & live, 1.0, 0.0).astype(BF16)
        earlier = jnp.dot(before, used, preferred_element_type=F32)
        found = []
        for j in range(2):
            rank = jnp.sum(jnp.where(hots[j], earlier, 0.0), axis=1, keepdims=True)
            found.append(jnp.where(live & (rank < self.capacity), rank, -1.0))
        return found

    def picks(self, m, k, rank):
        return [
            (self.named(m, j) == self.z_index[k]) & (rank[j] == self.lane_f) for j in range(2)
        ]

    def places(self, m, rank, experts, slots):
        lane = lax.broadcasted_iota(jnp.int32, (self.rows, experts * slots), 1).astype(F32)
        picks = []
        for j in range(2):
            place = rank[j]
            for k in range(1, experts):
                place = place + jnp.where(self.named(m, j) == self.z_index[k], 1.0 * k * slots, 0.0)
            place = jnp.where(rank[j] < 0, -1.0, place)
            picks.append(jnp.where(place == lane, 1.0, 0.0).astype(BF16))
        return picks

    def gates(self, m, logits):
        chosen = [
            jnp.sum(jnp.where(self.named(m, j) == self.lane, logits, 0.0), axis=1, keepdims=True)
            for j in range(2)
        ]
        top = jnp.maximum(chosen[0], chosen[1])
        raised = [jnp.exp(c - top) for c in chosen]
        total = raised[0] + raised[1]
        return [r / total for r in raised]


def dot_rows(left, right):
    return lax.dot_general(left, right, (((0,), (0,)), ((), ())), preferred_element_type=F32)


def dot_lanes(left, right):
    return lax.dot_general(left, right, (((1,), (1,)), ((), ())), preferred_element_type=F32)


STAGES = {"x": 0, "zl": 3, "zh": 2, "y": 1}


class Reduce:
    def __init__(self, wires, source, columns, order, bufs, peers, indices, finish):
        self.wires, self.source, self.columns = wires, source, columns
        self.order, self.bufs, self.peers, self.indices = order, bufs, peers, indices
        self.finish = finish
        self.flying, self.step = [], 0

    def launch(self, source, place, name):
        copy = self.wires.copy(source, place, self.peers[name], self.wires.take())
        copy.start()
        self.flying.append(copy)

    def begin(self):
        low = self.indices["core"]
        self.launch(self.source.at[:, 1 - low, :, self.columns], self.bufs[0], "core")

    def advance(self):
        if self.step > len(self.order):
            return False
        low = self.indices["core"]
        self.flying[-1].wait_recv()
        if self.step == 0:
            total = self.source[:, low, :, self.columns].astype(F32) + self.bufs[0][...].astype(F32)
            self.bufs[1][...] = total.astype(BF16).reshape(self.bufs[1].shape)
        else:
            kept = self.bufs[2 * self.step - 1]
            arrived = self.bufs[2 * self.step][...].astype(F32)
            mine = kept[self.cut(self.order[self.step - 1], True)].astype(F32)
            if self.step == len(self.order):
                self.finish(mine, arrived)
                self.step += 1
                return False
            self.bufs[2 * self.step + 1][...] = (mine + arrived).astype(BF16)
        name = self.order[self.step]
        kept = self.bufs[2 * self.step + 1]
        self.launch(kept.at[self.cut(name, False)], self.bufs[2 * self.step + 2], name)
        self.step += 1
        return True

    def cut(self, name, own):
        gone = set(self.order[: self.order.index(name)])
        axis = sum(1 for n, place in STAGES.items() if place < STAGES[name] and n not in gone)
        index = self.indices[name] if own else 1 - self.indices[name]
        return (slice(None),) * axis + (index,)


def reduce_buffers(order, rows, per_row, size):
    left = {"x", "zl", "zh", "y"}
    shapes = [(2, rows // 4, size)]
    for name in order:
        shapes.append((2,) * len(left) + (per_row, size))
        left.discard(name)
        shapes.append((2,) * len(left) + (per_row, size))
    return [pltpu.VMEM(shape, BF16) for shape in shapes]


ORDERS = [("x", "zl", "zh", "y")] * 3 + [("zl", "zh", "x", "y")] * 2 + [("x", "zl", "zh", "y")]


def back_kernel(
    sizes,
    back_ref,
    outp_ref,
    u_ref,
    hidden_ref,
    logit_ref,
    cot_rows_ref,
    mixed,
    qkv_ref,
    normed_ref,
    act_all,
    act_ref,
    dense,
    out_w,
    deal_ref,
    length_ref,
    route_ref,
    line_ref,
    gate_total,
    down_total,
    output_ref,
    grad_input_ref,
    query_out,
    key_out,
    value_out,
    out_out,
    small_out,
    diag_out,
    gate_in,
    down_in,
    back_got,
    out_got,
    sent_back,
    sent_out,
    sent_gate,
    ret_back,
    ret_out,
    ret_gate,
    final_all,
    hidden_all,
    mixed_got,
    grad_sent,
    first_sent,
    first_got,
    first_own,
    grad_own,
    qkv_grad,
    qkv_total,
    out_total,
    out_low,
    small_f,
    small_low,
    diag_buf,
    *rest,
):
    heads, head_size, experts, capacity, slots = sizes
    chunk_bufs, (sends, receives, homes) = rest[:-3], rest[-3:]
    micro, rows_dev, width = hidden_ref.shape
    seq = deal_ref.shape[1]
    own_width = heads * head_size
    dp, ctx, exp = (lax.axis_index(name) for name in ALL)
    high, low = dp // 2, dp % 2
    other_core, other_x, both = flip(dp, 1), flip(dp, 2), flip(flip(dp, 1), 2)
    core_peer, x_peer, x_core = (other_core, ctx, exp), (other_x, ctx, exp), (both, ctx, exp)
    y_peer, y_core = (dp, 1 - ctx, exp), (other_core, 1 - ctx, exp)
    far_peer, far_core = (other_x, 1 - ctx, exp), (both, 1 - ctx, exp)
    z_peers = [None] + [(dp, ctx, flip(exp, 1)), (dp, ctx, flip(exp, 2)), (dp, ctx, 3 - exp)]
    greet([core_peer, x_peer, x_core, y_peer, y_core, far_peer, far_core] + z_peers[1:])
    wires = Wires(sends, receives, homes)
    drains = []

    def send(source, place, peer):
        copy = wires.copy(source, place, peer, wires.take())
        copy.start()
        drains.append(copy)
        return copy

    plan = Plan(deal_ref, length_ref, route_ref, rows_dev, capacity)
    mine = pl.ds(pl.multiple_of(ctx * own_width, own_width), own_width)
    other = pl.ds(pl.multiple_of((1 - ctx) * own_width, own_width), own_width)

    back_core = [send(back_ref.at[1, :, m], back_got.at[m], core_peer) for m in range(micro)]
    out_core = [send(outp_ref.at[1, :, m], out_got.at[m], core_peer) for m in range(micro)]

    bulk = []
    home_copies = []
    block = dp * 2 + ctx
    own_copy = wires.home(gate_total.at[block], gate_in.at[0])
    own_copy.start()
    home_copies.append(own_copy)
    at_home = low == high
    away = jnp.logical_not(at_home)
    down_wire = [wires.take() for _ in range(8)]
    home_down = wires.home(down_total.at[low * 2 + ctx], down_in.at[0])
    down_sends = [
        (None, False, low * 2 + ctx, 0),
        (core_peer, False, (1 - low) * 2 + ctx, 0),
        (y_peer, False, low * 2 + 1 - ctx, 1),
        (y_core, False, (1 - low) * 2 + 1 - ctx, 1),
        (x_peer, True, low * 2 + ctx, 2),
        (x_core, True, (1 - low) * 2 + ctx, 2),
        (far_peer, True, low * 2 + 1 - ctx, 3),
        (far_core, True, (1 - low) * 2 + 1 - ctx, 3),
    ]

    def down_copy(i):
        peer, _, place, slot = down_sends[i]
        return wires.copy(down_total.at[place], down_in.at[slot], peer or core_peer, down_wire[i])

    def start_bulk():
        for j, (target_dp, target_ctx, peer) in enumerate(
            [
                (other_core, ctx, core_peer),
                (other_x, ctx, x_peer),
                (dp, 1 - ctx, y_peer),
                (both, ctx, x_core),
                (other_core, 1 - ctx, y_core),
                (other_x, 1 - ctx, far_peer),
                (both, 1 - ctx, far_core),
            ]
        ):
            bulk.append(send(gate_total.at[target_dp * 2 + target_ctx], gate_in.at[j + 1], peer))
        for i, (peer, is_away, _, _) in enumerate(down_sends):
            start = home_down.start if peer is None else down_copy(i).start
            pl.when(away if is_away else at_home)(start)

    ret_first = {}
    for m in range(micro):
        back_core[m].wait_recv()
        for k in range(experts):
            rows = (
                back_ref[0, k, m].astype(F32) + back_got[m, k].astype(F32)
            ).astype(BF16)
            if k == 0:
                ret_back[m, 0] = rows
            else:
                sent_back[m, k - 1] = rows
                ret_first["back", m, k] = send(sent_back.at[m, k - 1], ret_back.at[m, k], z_peers[k])
        out_core[m].wait_recv()
        ones = jnp.ones((8, width), F32)
        for k in range(experts):
            rows = (
                outp_ref[0, k, m].astype(F32) + out_got[m, k].astype(F32)
            ).astype(BF16)
            worth = lax.dot_general(
                ones,
                rows.astype(F32) * u_ref[k, m].astype(F32),
                (((1,), (1,)), ((), ())),
                precision=lax.Precision.HIGHEST,
                preferred_element_type=F32,
            )
            if k == 0:
                ret_out[m, 0] = rows
                ret_gate[m, 0, :, :slots] = worth
            else:
                sent_out[m, k - 1] = rows
                sent_gate[m, k - 1, :, :slots] = worth
                ret_first["gate", m, k] = send(sent_gate.at[m, k - 1], ret_gate.at[m, k], z_peers[k])
    start_bulk()
    for m in range(micro):
        for k in range(1, experts):
            ret_first["out", m, k] = send(sent_out.at[m, k - 1], ret_out.at[m, k], z_peers[k])

    extras = dense[:, :, :, :, :, 3 * own_width :].reshape(width, 128)
    turned = extras.astype(F32).T
    gain_one, gain_two = turned[experts : experts + 1], turned[experts + 1 : experts + 2]
    lanes = lax.broadcasted_iota(jnp.int32, (width, 128), 1)
    rank_of = [plan.ranks(m) for m in range(micro)]
    gate_of = [plan.gates(m, logit_ref[m]) for m in range(micro)]
    mixed_first, hidden_first = [], []
    second = jnp.zeros((1, width), F32)
    out_matrix = out_w[...].reshape(width, width)
    here = plan.at(0)
    for m in range(micro):
        for k in range(1, experts):
            ret_first["back", m, k].wait_recv()
            ret_first["gate", m, k].wait_recv()
        worths = []
        for j in range(2):
            worth = jnp.zeros((rows_dev, 1), F32)
            for k in range(experts):
                pick = plan.picks(m, k, rank_of[m])[j]
                worth = worth + jnp.sum(
                    jnp.where(pick, ret_gate[m, k, 0:1, :], 0.0), axis=1, keepdims=True
                )
            worths.append(worth)
        gates = gate_of[m]
        mean_worth = gates[0] * worths[0] + gates[1] * worths[1]
        logit_grad = sum(
            jnp.where(plan.named(m, j) == plan.lane, gates[j] * (worths[j] - mean_worth), 0.0)
            for j in range(2)
        ).astype(BF16)
        places = plan.places(m, rank_of[m], experts, slots)
        normed_grad = jnp.dot(
            places[0] + places[1],
            ret_back[m].reshape(experts * slots, width),
            preferred_element_type=F32,
        ) + dot_lanes(logit_grad, extras)
        hidden = hidden_ref[m]
        inverse = lax.rsqrt(jnp.mean(hidden * hidden, axis=-1, keepdims=True) + epsilon)
        scaled = hidden * inverse
        normed_two = (scaled * gain_two).astype(BF16)
        router = dot_rows(normed_two, logit_grad)
        small_f[...] = router if m == 0 else small_f[...] + router
        second = second + jnp.sum(normed_grad * scaled, axis=0, keepdims=True)
        lifted = gain_two * normed_grad
        mean_part = jnp.mean(lifted * hidden, axis=-1, keepdims=True)
        hidden_grad = (
            cot_rows_ref[m].astype(F32)
            + inverse * lifted
            - hidden * (inverse * inverse * inverse) * mean_part
        )
        hidden_all[m, 0] = hidden_grad.astype(BF16)
        branch_grad = jnp.where(plan.live(m), hidden_grad, 0.0).astype(BF16)
        mixed_grad = dot_lanes(branch_grad, out_matrix).astype(BF16)
        grad_sent[m] = mixed_grad
        mixed_first.append(send(grad_sent.at[m, :, other], mixed_got.at[m], y_peer))
        out_part = dot_rows(mixed[m], branch_grad)
        if m == 0:
            out_total[...] = out_part
        else:
            out_low[...] = (out_total[...] + out_part).astype(BF16).reshape(out_low.shape)
    for m in range(micro):
        hidden_first.append(send(hidden_all.at[m, 0], hidden_all.at[m, 1], y_peer))

    indices = {"core": low, "x": high, "y": ctx, "zl": exp % 2, "zh": exp // 2}
    peers = {"core": core_peer, "x": x_peer, "y": y_peer, "zl": z_peers[1], "zh": z_peers[2]}

    def finish_qkv(place):
        def store(kept, arrived):
            place[:, mine] = kept
            place[:, other] = arrived

        return store

    def finish_out(start):
        def store(kept, arrived):
            out_out[:, start : start + own_width] = kept + arrived

        return store

    def finish_small(kept, arrived):
        small_out[...] = kept + arrived

    chunks = []
    at = 0
    for i, order in enumerate(ORDERS):
        bufs = chunk_bufs[at : at + 9]
        at += 9
        if i < 3:
            source, start = qkv_total, i * own_width
            finish = finish_qkv((query_out, key_out, value_out)[i])
        elif i < 5:
            source, start = out_low, (i - 3) * own_width
            finish = finish_out(start)
        else:
            source, start, finish = small_low, 0, finish_small
        size = bufs[0].shape[-1]
        chunks.append(
            Reduce(wires, source, slice(start, start + size), order, bufs, peers, indices, finish)
        )
    chunks[3].begin()
    chunks[4].begin()

    scale = head_size ** (-0.5)
    for m in range(micro):
        mixed_first[m].wait_recv()
        grad_own[...] = (
            dot_rows(plan.hot(m, 0), grad_sent[m, :, mine]) + dot_rows(plan.hot(m, 1), mixed_got[m])
        ).astype(BF16)
        length = length_ref[m]
        for head in range(heads):
            cols = [
                slice(part * own_width + head * head_size, part * own_width + (head + 1) * head_size)
                for part in range(3)
            ]
            query, key, value = (qkv_ref[m, :, part] for part in cols)
            grad = grad_own[:, cols[0]]
            scores = masked_scores(query, key, line_ref[head : head + 1, :], length, scale)
            probs = soft(scores)
            prob_grad = dot_lanes(grad, value)
            delta = jnp.sum(probs * prob_grad, axis=-1, keepdims=True)
            score_grad = (probs * (prob_grad - delta)).astype(BF16)
            diagonal = diagonal_sums(score_grad.astype(F32))
            if m:
                diagonal = diagonal + diag_buf[0, head : head + 1, :]
            diag_buf[0, head : head + 1, :] = diagonal
            qkv_grad[m, :, cols[0]] = (
                jnp.dot(score_grad, key, preferred_element_type=F32) * scale
            ).astype(BF16)
            qkv_grad[m, :, cols[1]] = (dot_rows(score_grad, query) * scale).astype(BF16)
            qkv_grad[m, :, cols[2]] = dot_rows(probs.astype(BF16), grad).astype(BF16)
            if head % 4 == 3:
                for i in (3, 4):
                    chunks[i].advance()
    for i in range(3):
        cols = slice(i * own_width, (i + 1) * own_width)
        total = dot_rows(normed_ref[0], qkv_grad[0, :, cols]) + dot_rows(
            normed_ref[1], qkv_grad[1, :, cols]
        )
        qkv_total[:, :, :, cols] = total.astype(BF16).reshape(2, 2, width // 4, own_width)
        chunks[i].begin()

    diag_peers = [core_peer, x_peer, z_peers[1], z_peers[2], y_peer]
    diag_copies = []

    def diag_step(stage):
        if stage:
            diag_copies[stage - 1].wait_recv()
        if 0 < stage < 5:
            diag_buf[2 * stage] = diag_buf[2 * stage - 2] + diag_buf[2 * stage - 1]
        if stage < 5:
            diag_copies.append(
                send(diag_buf.at[2 * stage], diag_buf.at[2 * stage + 1], diag_peers[stage])
            )

    diag_step(0)
    first_total = jnp.zeros((1, width), F32)
    first_first = []
    for m in range(micro):
        part = jnp.zeros((seq, width), F32)
        for i in range(3):
            cols = slice(i * own_width, (i + 1) * own_width)
            part = part + dot_lanes(
                qkv_grad[m, :, cols], dense[:, :, :, :, :, cols].reshape(width, own_width)
            )
        rows = act_all[m].astype(F32)
        inverse = lax.rsqrt(jnp.mean(rows * rows, axis=-1, keepdims=True) + epsilon)
        first_total = first_total + jnp.sum(part * rows * inverse, axis=0, keepdims=True)
        first_own[...] = part
        first_sent[m] = first_own[plan.at(1), :].astype(BF16)
        first_got[m, 0] = first_own[here, :].astype(BF16)
        first_first.append(send(first_sent.at[m], first_got.at[m, 1], y_peer))
        chunks[m].advance()
        diag_step(1 + m)
    columns = jnp.where(
        lanes == experts,
        jnp.broadcast_to(second, (128, width)).T,
        jnp.where(
            lanes == experts + 1, jnp.broadcast_to(first_total, (128, width)).T, small_f[...]
        ),
    )
    small_low[...] = columns.astype(BF16).reshape(small_low.shape)
    chunks[5].begin()
    chunks[2].advance()
    chunks[0].advance()

    final_first = []
    for m in range(micro):
        for k in range(1, experts):
            ret_first["out", m, k].wait_recv()
        places = plan.places(m, rank_of[m], experts, slots)
        rows = ret_out[m].reshape(experts * slots, width)
        final = hidden_ref[m]
        for j in range(2):
            final = final + gate_of[m][j] * jnp.dot(places[j], rows, preferred_element_type=F32)
        final_all[m, 0] = final.astype(BF16)
        final_first.append(send(final_all.at[m, 0], final_all.at[m, 1], y_peer))
        if m == 0:
            chunks[1].advance()
            chunks[3].advance()
            diag_step(3)
    chunks[5].advance()
    chunks[2].advance()
    chunks[0].advance()
    chunks[4].advance()
    diag_step(4)
    chunks[1].advance()
    chunks[5].advance()

    for m in range(micro):
        hidden_first[m].wait_recv()
        first_first[m].wait_recv()
        first = first_got[m, 0].astype(F32) + first_got[m, 1].astype(F32)
        rows = act_ref[m].astype(F32)
        inverse = lax.rsqrt(jnp.mean(rows * rows, axis=-1, keepdims=True) + epsilon)
        lifted = gain_one * first
        mean_part = jnp.mean(lifted * rows, axis=-1, keepdims=True)
        back = inverse * lifted - rows * (inverse * inverse * inverse) * mean_part
        moved = sum(dot_rows(plan.hot_mine(m, k), hidden_all[m, k]) for k in range(2))
        grad_input_ref[m] = (moved + back).astype(BF16)
        if m == 0:
            chunks[0].advance()
            chunks[2].advance()
            chunks[1].advance()
    for m in range(micro):
        final_first[m].wait_recv()
        moved = sum(dot_rows(plan.hot_mine(m, k), final_all[m, k]) for k in range(2))
        output_ref[m] = moved.astype(BF16)
    busy = True
    while busy:
        busy = False
        for i in (0, 1, 2, 3, 4, 5):
            if chunks[i].step <= len(chunks[i].order):
                chunks[i].advance()
                busy = True
    diag_step(5)
    diag_out[ctx] = diag_buf[8]
    diag_out[1 - ctx] = diag_buf[9]

    for copy in bulk:
        copy.wait_recv()
    for i, (peer, is_away, _, _) in enumerate(down_sends):
        if peer is None:
            pl.when(at_home)(home_down.wait)
            continue
        pl.when(away if is_away else at_home)(lambda i=i: down_copy(i).wait_send())
    @pl.when(at_home)
    def _():
        for i in (2, 4 , 6):
            down_copy(i).wait_recv()

    @pl.when(away)
    def _():
        for i in (1, 3, 5, 7):
            down_copy(i).wait_recv()

    for copy in home_copies:
        copy.wait()
    for chunk in chunks:
        for copy in chunk.flying:
            copy.wait_send()
    for copy in drains:
        copy.wait_send()


def back(sizes, values, gate_total, down_total):
    heads, head_size, experts, capacity, slots = sizes
    hidden, dense, qkv, lines = values[3], values[11], values[7], values[16]
    micro, rows_dev, width = hidden.shape
    seq = qkv.shape[1]
    own_width = heads * head_size
    per_row = dense.shape[4]
    in_vmem, in_hbm = pl.BlockSpec(memory_space=pltpu.VMEM), pl.BlockSpec(memory_space=pltpu.HBM)
    smem = pl.BlockSpec(memory_space=pltpu.SMEM)
    outs = (
        [((micro, rows_dev, width), BF16)] * 2
        + [((per_row, width), F32)] * 4
        + [((per_row, 128), F32), ((2,) + lines.shape, F32)]
        + [(gate_total.shape, BF16), (down_total.shape, BF16)]
    )
    rows = (micro, experts, slots, width)
    sent = (micro, experts - 1, slots, width)
    scratch = [
        pltpu.VMEM(rows, BF16),
        pltpu.VMEM(rows, BF16),
        pltpu.VMEM(sent, BF16),
        pltpu.VMEM(sent, BF16),
        pltpu.VMEM((micro, experts - 1, 8, 128), F32),
        pltpu.VMEM(rows, BF16),
        pltpu.VMEM(rows, BF16),
        pltpu.VMEM((micro, experts, 8, 128), F32),
        pltpu.VMEM((micro, 2, rows_dev, width), BF16),
        pltpu.VMEM((micro, 2, rows_dev, width), BF16),
        pltpu.VMEM((micro, rows_dev, own_width), BF16),
        pltpu.VMEM((micro, rows_dev, width), BF16),
        pltpu.VMEM((micro, rows_dev, width), BF16),
        pltpu.VMEM((micro, 2, rows_dev, width), BF16),
        pltpu.VMEM((seq, width), F32),
        pltpu.VMEM((seq, own_width), BF16),
        pltpu.VMEM((micro, seq, 3 * own_width), BF16),
        pltpu.VMEM((2, 2, width // 4, 3 * own_width), BF16),
        pltpu.VMEM((width, width), F32),
        pltpu.VMEM((2, 2, width // 4, width), BF16),
        pltpu.VMEM((width, 128), F32),
        pltpu.VMEM((2, 2, width // 4, 128), BF16),
        pltpu.VMEM((10,) + lines.shape, F32),
    ]
    chunk_sizes = [own_width] * 5 + [128]
    for order, size in zip(ORDERS, chunk_sizes):
        scratch += reduce_buffers(order, width, per_row, size)
    scratch += [
        pltpu.SemaphoreType.DMA((160,)),
        pltpu.SemaphoreType.DMA((160,)),
        pltpu.SemaphoreType.DMA((4,)),
    ]
    return pl.pallas_call(
        functools.partial(back_kernel, sizes),
        out_shape=tuple(jax.ShapeDtypeStruct(*out) for out in outs),
        in_specs=[in_vmem] * 14 + [smem] + [in_vmem] * 2 + [in_hbm] * 2,
        out_specs=(in_vmem,) * 8 + (in_hbm,) * 2,
        scratch_shapes=scratch,
        compiler_params=pltpu.CompilerParams(
            collective_id=2, has_side_effects=True, vmem_limit_bytes=60 * 2**20
        ),
    )(*values, gate_total, down_total)


def tuned_body(
    activations,
    cotangent,
    dealing,
    lengths,
    routes,
    buckets,
    w_query,
    w_key,
    w_value,
    w_out,
    w_router,
    norm_first,
    norm_second,
    bias_table,
    w_gate,
    w_up,
    w_down,
):
    micro, _, rows_dev, width = activations.shape
    seq = dealing.shape[2]
    bucket_count, head_count = bias_table.shape
    dp_count, ctx_count, expert_count = (lax.axis_size(name) for name in ALL)
    dp_index, ctx_index, expert_index = (lax.axis_index(name) for name in ALL)
    high, low = dp_index // 2, dp_index % 2
    heads = head_count // ctx_count
    head_size = width // head_count
    own_width = heads * head_size
    experts = w_router.shape[1]
    top_count = routes.shape[3]
    capacity = (5 * rows_dev * top_count + 4 * experts - 1) // (4 * experts)
    slots = -(-capacity // 16) * 16
    half_ff = w_gate.shape[2] // 2
    down_rows = w_down.shape[1]
    plane = dp_count * ctx_count
    plane_index = dp_index * ctx_count + ctx_index
    act = activations[:, 0]
    cot = cotangent[:, 0]
    deal = dealing[:, 0]
    length = lengths[:, 0]
    route = routes[:, 0]
    sizes = (heads, head_size, experts, capacity, slots)
    extras = jnp.concatenate([w_router, norm_first[:, None], norm_second[:, None]], axis=1)
    extras = jnp.pad(extras, ((0, 0), (0, 128 - extras.shape[1])))
    bucket_hot = (buckets[:, None] == jnp.arange(bucket_count)[None, :]).astype(BF16)
    own_table = lax.dynamic_slice_in_dim(bias_table, ctx_index * heads, heads, axis=1)
    lookup = dot_f32("sb,bh->hs", bucket_hot, own_table)
    lines = jnp.concatenate(
        [lookup[:, :1], jnp.zeros((heads, seq), F32), lookup[:, :0:-1]], axis=1
    )
    (
        hidden,
        logits,
        mixed,
        cot_low,
        dense,
        out_w,
        act_all,
        normed,
        qkv,
        all_x,
        own_u,
        all_g,
        gate_up_w,
        down_w,
        both,
        activated,
    ) = front(
        sizes,
        act,
        cot,
        deal,
        length,
        route,
        lines,
        (w_query, w_key, w_value, w_out),
        extras,
        w_gate[0],
        w_up[0],
        w_down[0],
    )
    gate_up_w = gate_up_w.reshape(width, 2 * half_ff)
    down_w = down_w.reshape(half_ff, width)
    row_count = experts * micro * slots

    all_x = all_x.reshape(2 * row_count, width)
    all_g = all_g.reshape(2 * row_count, width)
    both = both.reshape(2 * row_count, 2 * half_ff)
    activated = activated.reshape(2 * row_count, half_ff)
    act_grad = dot_f32("rd,fd->rf", all_g, down_w)
    both_grad = (jnp.concatenate([act_grad, act_grad], axis=1) * both.astype(F32)).astype(BF16)
    parts_shape = (2, experts, micro, slots, width)
    back_part = dot_f32("rf,df->rd", both_grad, gate_up_w).astype(BF16).reshape(parts_shape)
    out_part = dot_f32("rf,fd->rd", activated, down_w).astype(BF16).reshape(parts_shape)
    gate_up_total = dot_f32("rd,rf->df", all_x, both_grad).astype(BF16)
    down_total = dot_f32("rf,rd->fd", activated, all_g).astype(BF16)
    (
        output,
        grad_input,
        grad_query,
        grad_key,
        grad_value,
        grad_out,
        small_sum,
        diag_all,
        gate_in,
        down_in,
    ) = back(
        sizes,
        (
            back_part,
            out_part,
            own_u,
            hidden,
            logits,
            cot_low,
            mixed,
            qkv,
            normed,
            act_all,
            act,
            dense,
            out_w,
            deal[:, :, None],
            length,
            route,
            lines,
        ),
        gate_up_total.reshape(plane, width // plane, 2 * half_ff),
        down_total.reshape(-1, w_down.shape[1], width),
    )
    same = sum(gate_in[j].astype(F32) for j in (0, 2, 3, 6))
    far = sum(gate_in[j].astype(F32) for j in (1, 4, 5, 7))
    first_half, second_half = reorder([same, far], low)
    grad_gate = jnp.concatenate([first_half[:, :half_ff], second_half[:, :half_ff]], axis=1)
    grad_up = jnp.concatenate([first_half[:, half_ff:], second_half[:, half_ff:]], axis=1)
    grad_down = sum(down_in[j].astype(F32) for j in range(down_in.shape[0]))
    diag_all = diag_all.reshape((head_count, -1))
    offsets = jnp.concatenate([diag_all[:, :1], diag_all[:, : seq : -1]], axis=1)
    grad_table = jnp.einsum(
        "hs,sb->bh", offsets, bucket_hot.astype(F32), precision=lax.Precision.HIGHEST
    )
    return (
        output[:, None],
        grad_input[:, None],
        grad_query,
        grad_key,
        grad_value,
        grad_out,
        small_sum[:, :experts],
        small_sum[:, experts + 1],
        small_sum[:, experts],
        grad_table,
        grad_gate[None],
        grad_up[None],
        grad_down[None],
    )


def body(*arguments):
    counts = tuple(lax.axis_size(name) for name in ALL)
    activations, w_query, bias_table, w_gate = (arguments[i] for i in (0, 6, 13, 14))
    own_width = activations.shape[3] // counts[1]
    fits = (
        counts == (4, 2, 4)
        and w_gate.shape[0] == 1
        and w_query.shape[0] % 16 == 0
        and own_width % 128 == 0
        and bias_table.shape[1] % counts[1] == 0
        and arguments[4].shape[3] == 2
    )
    return (tuned_body if fits else plain_body)(*arguments)


def solution(mesh):
    tokens = P(None, ("dp", "experts"), "context", None)
    sequences = P(None, ("dp", "experts"))
    rows = P(("dp", "context", "experts"), None)
    gains = P(("dp", "context", "experts"))
    experts = P("experts", ("dp", "context"), None)
    placed = (
        (tokens, tokens, P(None, ("dp", "experts"), None), sequences, tokens, P())
        + (rows,) * 5
        + (gains, gains, P())
        + (experts,) * 3
    )
    return jax.shard_map(
        body,
        mesh=mesh,
        in_specs=placed,
        out_specs=(tokens, tokens) + (rows,) * 5 + (gains, gains, P()) + (experts,) * 3,
        check_vma=False,
    )
```

```python
import functools

import jax
import jax.numpy as jnp
from jax import lax
from jax.experimental import pallas as pl
from jax.experimental.pallas import tpu as pltpu
from jax.sharding import PartitionSpec as P

epsilon = 1e-06
masked_score = -1e30
ALL = ("dp", "context", "experts")
F32 = jnp.float32
BF16 = jnp.bfloat16


def dot_f32(spec, left, right):
    return jnp.einsum(spec, left, right, preferred_element_type=F32)


def swap(value, axis, offset):
    size = lax.axis_size(axis)
    return lax.ppermute(value, axis, [(i, i ^ offset) for i in range(size)])


def reorder(pieces, index):
    pieces = list(pieces)
    bit = 1
    while bit < len(pieces):
        flag = (index // bit) % 2 == 1
        pieces = [jnp.where(flag, pieces[j ^ bit], pieces[j]) for j in range(len(pieces))]
        bit *= 2
    return pieces


def reorder_lanes(value, blocks, index):
    return jnp.concatenate(reorder(jnp.split(value, blocks, axis=-1), index), axis=-1)


def toeplitz_bias(line, size):
    rows = jnp.broadcast_to(line, (size, 2 * size))
    return pltpu.roll(rows, 0, 1, stride=1, stride_axis=0)[:, :size]


def masked_scores(query, key, line, length, scale):
    size = query.shape[0]
    scores = lax.dot_general(query, key, (((1,), (1,)), ((), ())), preferred_element_type=F32)
    scores = scores * scale + toeplitz_bias(line, size)
    row_id = lax.broadcasted_iota(jnp.int32, (size, size), 0)
    col_id = lax.broadcasted_iota(jnp.int32, (size, size), 1)
    allowed = (row_id >= col_id) & (col_id < length)
    return jnp.where(allowed, scores, masked_score)


def soft(scores):
    top_score = jnp.max(scores, axis=-1, keepdims=True)
    raised = jnp.exp(scores - top_score)
    return raised / jnp.sum(raised, axis=-1, keepdims=True)


def attend_kernel(heads, head_size, length_ref, line_ref, qkv_ref, mixed_ref):
    scale = head_size ** (-0.5)
    width = heads * head_size
    length = length_ref[pl.program_id(0)]
    for head in range(heads):
        query = qkv_ref[0, :, head * head_size : (head + 1) * head_size]
        key = qkv_ref[0, :, width + head * head_size : width + (head + 1) * head_size]
        value = qkv_ref[0, :, 2 * width + head * head_size : 2 * width + (head + 1) * head_size]
        scores = masked_scores(query, key, line_ref[head : head + 1, :], length, scale)
        probs = soft(scores).astype(BF16)
        mixed = jnp.dot(probs, value, preferred_element_type=F32)
        mixed_ref[0, :, head * head_size : (head + 1) * head_size] = mixed.astype(BF16)


def attend(qkv, lines, lengths, heads):
    micro, seq, width = qkv.shape
    width = width // 3
    head_size = width // heads
    return pl.pallas_call(
        functools.partial(attend_kernel, heads, head_size),
        grid=(micro,),
        out_shape=jax.ShapeDtypeStruct((micro, seq, width), BF16),
        in_specs=[
            pl.BlockSpec(memory_space=pltpu.SMEM),
            pl.BlockSpec(lines.shape, lambda i: (0, 0)),
            pl.BlockSpec((1, seq, 3 * width), lambda i: (i, 0, 0)),
        ],
        out_specs=pl.BlockSpec((1, seq, width), lambda i: (i, 0, 0)),
        compiler_params=pltpu.CompilerParams(vmem_limit_bytes=32 * 2**20),
    )(lengths, lines, qkv)


def diagonal_sums(grad):
    size = grad.shape[0]
    wide = jnp.concatenate([grad, jnp.zeros_like(grad)], axis=1)
    rows = size
    while rows > 1:
        rows //= 2
        lower = pltpu.roll(wide[rows:], 2 * size - rows, 1)
        wide = wide[:rows] + lower
    return wide


def attend_back_kernel(
    heads, head_size, length_ref, line_ref, qkv_ref, grad_ref, out_ref, diag_ref
):
    scale = head_size ** (-0.5)
    width = heads * head_size
    length = length_ref[pl.program_id(0)]

    @pl.when(pl.program_id(0) == 0)
    def _():
        diag_ref[...] = jnp.zeros_like(diag_ref)

    for head in range(heads):
        at = [
            slice(part * width + head * head_size, part * width + (head + 1) * head_size)
            for part in range(3)
        ]
        query, key, value = (qkv_ref[0, :, part] for part in at)
        grad = grad_ref[0, :, at[0]]
        scores = masked_scores(query, key, line_ref[head : head + 1, :], length, scale)
        probs = soft(scores)
        prob_grad = lax.dot_general(
            grad, value, (((1,), (1,)), ((), ())), preferred_element_type=F32
        )
        delta = jnp.sum(probs * prob_grad, axis=-1, keepdims=True)
        score_grad = (probs * (prob_grad - delta)).astype(BF16)
        diag_ref[head : head + 1, :] += diagonal_sums(score_grad.astype(F32))
        query_grad = jnp.dot(score_grad, key, preferred_element_type=F32) * scale
        key_grad = (
            lax.dot_general(
                score_grad, query, (((0,), (0,)), ((), ())), preferred_element_type=F32
            )
            * scale
        )
        value_grad = lax.dot_general(
            probs.astype(BF16), grad, (((0,), (0,)), ((), ())), preferred_element_type=F32
        )
        out_ref[0, :, at[0]] = query_grad.astype(BF16)
        out_ref[0, :, at[1]] = key_grad.astype(BF16)
        out_ref[0, :, at[2]] = value_grad.astype(BF16)


def attend_back(qkv, grad, lines, lengths, heads):
    micro, seq, width = grad.shape
    head_size = width // heads
    return pl.pallas_call(
        functools.partial(attend_back_kernel, heads, head_size),
        grid=(micro,),
        out_shape=(
            jax.ShapeDtypeStruct(qkv.shape, BF16),
            jax.ShapeDtypeStruct(lines.shape, F32),
        ),
        in_specs=[
            pl.BlockSpec(memory_space=pltpu.SMEM),
            pl.BlockSpec(lines.shape, lambda i: (0, 0)),
            pl.BlockSpec((1, seq, 3 * width), lambda i: (i, 0, 0)),
            pl.BlockSpec((1, seq, width), lambda i: (i, 0, 0)),
        ],
        out_specs=(
            pl.BlockSpec((1, seq, 3 * width), lambda i: (i, 0, 0)),
            pl.BlockSpec(lines.shape, lambda i: (0, 0)),
        ),
        compiler_params=pltpu.CompilerParams(vmem_limit_bytes=32 * 2**20),
    )(lengths, lines, qkv, grad)


def halve(value, axis, bit, flag):
    kept = jnp.where(flag, value[1], value[0])
    sent = jnp.where(flag, value[0], value[1]).astype(BF16)
    return kept + swap(sent, axis, bit).astype(F32)


def scatter_sum(value, dp_index, expert_index):
    dp_count, ctx_count, expert_count = value.shape[:3]
    rest = value.shape[3:]
    count, bit = dp_count, 1
    while count > 1:
        shaped = value.reshape((count // 2, 2, -1))
        value = halve(jnp.moveaxis(shaped, 1, 0), "dp", bit, (dp_index // bit) % 2 == 1)
        count //= 2
        bit *= 2
    value = value.reshape((ctx_count, expert_count) + rest)
    count, bit = expert_count, 1
    while count > 1:
        shaped = value.reshape((ctx_count, count // 2, 2) + rest)
        value = halve(jnp.moveaxis(shaped, 2, 0), "experts", bit, (expert_index // bit) % 2 == 1)
        count //= 2
        bit *= 2
    return value.reshape((ctx_count,) + rest)


MESH = pl.DeviceIdType.MESH


def flip(index, bit):
    return index + bit - 2 * bit * ((index // bit) % 2)


def greet(targets):
    barrier = pltpu.get_barrier_semaphore()
    for target in targets:
        pl.semaphore_signal(barrier, inc=1, device_id=target, device_id_type=MESH)
    pl.semaphore_wait(barrier, len(targets))


def remote(source, place, sends, receives, target):
    return pltpu.make_async_remote_copy(
        src_ref=source,
        dst_ref=place,
        send_sem=sends,
        recv_sem=receives,
        device_id=target,
        device_id_type=MESH,
    )


def plain_sums(qkv_total, out_total, router_total, first_total, second_total, own_width):
    width, experts = router_total.shape
    dp_count, ctx_count, expert_count = (lax.axis_size(name) for name in ALL)
    dp_index, ctx_index, expert_index = (lax.axis_index(name) for name in ALL)
    owners = (dp_count, ctx_count, expert_count, -1)
    out_pack = jnp.concatenate([out_total, router_total, second_total[:, None]], axis=1)
    out_pack = jnp.pad(out_pack, ((0, 0), (0, width + 128 - out_pack.shape[1])))
    out_pack = scatter_sum(
        out_pack.reshape(owners + (out_pack.shape[1],)), dp_index, expert_index
    )
    qkv_pack = jnp.pad(
        jnp.concatenate([qkv_total, first_total[:, None]], axis=1), ((0, 0), (0, 127))
    )
    qkv_pack = scatter_sum(
        qkv_pack.reshape(owners + (qkv_pack.shape[1],)), dp_index, expert_index
    )

    def across(value):
        parts = reorder([value[c] for c in range(ctx_count)], ctx_index)
        return [parts[0]] + [
            swap(parts[k].astype(BF16), "context", k).astype(F32) for k in range(1, ctx_count)
        ]

    out_sum = sum(across(out_pack))
    qkv_parts = across(qkv_pack)
    grad_first = sum(part[:, 3 * own_width] for part in qkv_parts)
    qkv_parts = reorder(qkv_parts, ctx_index)
    grads = tuple(
        jnp.concatenate(
            [part[:, i * own_width : (i + 1) * own_width] for part in qkv_parts], axis=1
        )
        for i in range(3)
    )
    return grads + (
        out_sum[:, :width],
        out_sum[:, width : width + experts],
        grad_first,
        out_sum[:, width + experts],
    )


def norm_pull(features, inverse, gain, grad):
    lifted = gain * grad
    mean_part = jnp.mean(lifted * features, axis=-1, keepdims=True)
    back = inverse * lifted - features * (inverse * inverse * inverse) * mean_part
    gain_grad = jnp.sum(grad * features * inverse, axis=(0, 1))
    return back, gain_grad


def gelu_parts(pre):
    root = 0.7978845608028654
    cubic = 0.044715
    square = pre * pre
    wave = jnp.tanh(root * (pre + cubic * pre * square))
    value = 0.5 * pre * (1.0 + wave)
    slope = 0.5 * (1.0 + wave) + 0.5 * pre * (1.0 - wave * wave) * root * (
        1.0 + 3.0 * cubic * square
    )
    return value, slope


def down_routes(dp_count, ctx_count, expert_count, core, ctx_offset):
    pairs = []
    for dp in range(dp_count):
        for ctx in range(ctx_count):
            for expert in range(expert_count):
                high, low = dp // 2, dp % 2
                to_high = high if low == core else high ^ 1
                target = ((to_high * 2 + high) * ctx_count + (ctx ^ ctx_offset)) * expert_count
                pairs.append(((dp * ctx_count + ctx) * expert_count + expert, target + expert))
    return pairs


def plain_body(
    activations,
    cotangent,
    dealing,
    lengths,
    routes,
    buckets,
    w_query,
    w_key,
    w_value,
    w_out,
    w_router,
    norm_first,
    norm_second,
    bias_table,
    w_gate,
    w_up,
    w_down,
):
    micro, _, rows_dev, width = activations.shape
    seq = dealing.shape[2]
    bucket_count, head_count = bias_table.shape
    dp_count, ctx_count, expert_count = (lax.axis_size(name) for name in ALL)
    dp_index, ctx_index, expert_index = (lax.axis_index(name) for name in ALL)
    high, low = dp_index // 2, dp_index % 2
    heads = head_count // ctx_count
    head_size = width // head_count
    own_width = heads * head_size
    experts = w_router.shape[1]
    top_count = routes.shape[3]
    capacity = (5 * rows_dev * top_count + 4 * experts - 1) // (4 * experts)
    slots = -(-capacity // 16) * 16
    ff = w_gate.shape[2]
    half_ff = ff // 2
    weight_rows = w_query.shape[0]
    plane = dp_count * ctx_count
    plane_index = dp_index * ctx_count + ctx_index
    act = activations[:, 0]
    cot = cotangent[:, 0]
    deal = dealing[:, 0]
    length = lengths[:, 0]
    route = routes[:, 0]

    extras = jnp.concatenate(
        [w_router, norm_first[:, None], norm_second[:, None]], axis=1
    )
    extras = jnp.pad(extras, ((0, 0), (0, 128 - extras.shape[1])))
    column_parts = [
        jnp.split(weight, ctx_count, axis=1) for weight in (w_query, w_key, w_value)
    ]
    packs = [
        jnp.concatenate([part[c] for part in column_parts] + [extras], axis=1)
        for c in range(ctx_count)
    ]
    packs = reorder(packs, ctx_index)
    packs = [packs[0]] + [swap(packs[k], "context", k) for k in range(1, ctx_count)]
    packs = jnp.stack(reorder(packs, ctx_index))
    dense = lax.all_gather(packs, ("dp", "experts"), axis=0, tiled=False)
    dense = dense.reshape((dp_count, expert_count) + packs.shape)
    dense = jnp.transpose(dense, (0, 2, 1, 3, 4)).reshape(width, -1)
    qkv_w = dense[:, : 3 * own_width]
    router_w = dense[:, 3 * own_width : 3 * own_width + experts]
    gain_one = dense[:, 3 * own_width + experts].astype(F32)
    gain_two = dense[:, 3 * own_width + experts + 1].astype(F32)
    out_w = lax.all_gather(w_out, ALL, axis=0, tiled=True)

    gate_up = [
        jnp.concatenate([w_gate[0, :, h * half_ff : (h + 1) * half_ff], w_up[0, :, h * half_ff : (h + 1) * half_ff]], axis=1)
        for h in range(2)
    ]
    halves = reorder(gate_up, low)
    gate_blocks = []
    for j in range(plane):
        dp_offset, ctx_offset = j // ctx_count, j % ctx_count
        piece = halves[dp_offset % 2]
        if dp_offset:
            piece = swap(piece, "dp", dp_offset)
        if ctx_offset:
            piece = swap(piece, "context", ctx_offset) if not dp_offset else piece
        gate_blocks.append(piece)
    for j in range(plane):
        dp_offset, ctx_offset = j // ctx_count, j % ctx_count
        if dp_offset and ctx_offset:
            gate_blocks[j] = swap(gate_blocks[dp_offset * ctx_count], "context", ctx_offset)
    gate_up_w = jnp.concatenate(gate_blocks, axis=0)
    down_w = jnp.zeros((half_ff, width), BF16)
    down_rows = w_down.shape[1]
    for ctx_offset in range(ctx_count):
        for core in range(2):
            pairs = down_routes(dp_count, ctx_count, expert_count, core, ctx_offset)
            piece = lax.ppermute(w_down[0], ALL, pairs)
            from_core = jnp.where(low == high, core, 1 - core)
            place = (from_core * ctx_count + (ctx_index ^ ctx_offset)) * down_rows
            down_w = lax.dynamic_update_slice(down_w, piece, (place, 0))

    act_all = jnp.concatenate(
        reorder([act] + [swap(act, "context", k) for k in range(1, ctx_count)], ctx_index), axis=1
    )
    cot_all = jnp.concatenate(
        reorder([cot] + [swap(cot, "context", k) for k in range(1, ctx_count)], ctx_index), axis=1
    )
    position_ids = jnp.arange(seq, dtype=jnp.int32)
    slot_blocks = [
        lax.dynamic_slice_in_dim(deal, (ctx_index ^ k) * rows_dev, rows_dev, axis=1)
        for k in range(ctx_count)
    ]
    hot = [
        (block[:, :, None] == position_ids[None, None, :]).astype(BF16) for block in slot_blocks
    ]
    my_positions = ctx_index * rows_dev + jnp.arange(rows_dev, dtype=jnp.int32)
    hot_mine = [
        (block[:, :, None] == my_positions[None, None, :]).astype(BF16) for block in slot_blocks
    ]
    live = slot_blocks[0] < length[:, None]
    live_rows = live.astype(F32)[:, :, None]
    bucket_hot = (buckets[:, None] == jnp.arange(bucket_count)[None, :]).astype(BF16)
    own_table = lax.dynamic_slice_in_dim(bias_table, ctx_index * heads, heads, axis=1)
    lookup = dot_f32("sb,bh->hs", bucket_hot, own_table)
    lines = jnp.concatenate(
        [lookup[:, :1], jnp.zeros((heads, seq), F32), lookup[:, :0:-1]], axis=1
    )

    rows_all = act_all.astype(F32)
    inverse_one = lax.rsqrt(jnp.mean(rows_all * rows_all, axis=-1, keepdims=True) + epsilon)
    normed = (rows_all * inverse_one * gain_one).astype(BF16)
    qkv = dot_f32("mpd,dw->mpw", normed, qkv_w).astype(BF16)
    mixed_own = attend(qkv, lines, length, heads)
    mixed_parts = [
        dot_f32("msp,mpw->msw", hot[k], mixed_own).astype(BF16) for k in range(ctx_count)
    ]
    mixed_parts = [mixed_parts[0]] + [
        swap(mixed_parts[k], "context", k) for k in range(1, ctx_count)
    ]
    mixed = jnp.concatenate(reorder(mixed_parts, ctx_index), axis=-1)

    rows_in = dot_f32("msp,mpd->msd", hot[0], act_all)
    cot_rows = dot_f32("msp,mpd->msd", hot[0], cot_all)
    branch = dot_f32("msi,io->mso", mixed, out_w)
    hidden = rows_in + branch * live_rows
    inverse_two = lax.rsqrt(jnp.mean(hidden * hidden, axis=-1, keepdims=True) + epsilon)
    normed_two = (hidden * inverse_two * gain_two).astype(BF16)
    logits = dot_f32("msd,de->mse", normed_two, router_w)
    route_hot = (route[..., None] == jnp.arange(experts)).astype(F32)
    chosen = jnp.sum(route_hot * logits[:, :, None, :], axis=3)
    gate_probs = jax.nn.softmax(chosen, axis=-1)

    flat_hot = (route_hot * live_rows[..., None]).reshape(micro, rows_dev * top_count, experts)
    pair_ids = jnp.arange(rows_dev * top_count)
    before = (pair_ids[:, None] > pair_ids[None, :]).astype(BF16)
    earlier = dot_f32("ab,mbe->mae", before, flat_hot.astype(BF16))
    rank = jnp.sum(earlier * flat_hot, axis=2).astype(jnp.int32).reshape(route.shape)
    kept = live[:, :, None] & (rank < capacity)
    target = jnp.where(kept, (route ^ expert_index) * slots + rank, -1)
    place_ids = jnp.arange(experts * slots, dtype=jnp.int32)
    pick = [
        (target[:, None, :, j] == place_ids[None, :, None]) for j in range(top_count)
    ]
    pick_any = functools.reduce(jnp.logical_or, pick).astype(BF16)
    pick_bf = [p.astype(BF16) for p in pick]
    prob_rows = sum(
        jnp.sum(jnp.where(pick[j], gate_probs[:, None, :, j], 0.0), axis=2)
        for j in range(top_count)
    )

    def by_expert(value):
        shaped = value.reshape((micro, experts, slots) + value.shape[2:])
        return jnp.moveaxis(shaped, 1, 0)

    def exchange(value):
        parts = [value[0]] + [swap(value[k], "experts", k) for k in range(1, expert_count)]
        return jnp.stack(parts)

    normed_rel = reorder_lanes(normed_two, plane, plane_index)
    sent_rows = by_expert(dot_f32("mrs,msd->mrd", pick_any, normed_rel).astype(BF16))
    sent_up = by_expert(
        dot_f32("mrs,msd->mrd", pick_any, cot_rows.astype(BF16)).astype(BF16)
    )
    row_count = expert_count * micro * slots
    own_x = exchange(sent_rows).reshape(row_count, width)
    own_u = exchange(sent_up).reshape(row_count, width)
    own_p = exchange(by_expert(prob_rows)).reshape(row_count, 1)
    own_g = (own_p * own_u.astype(F32)).astype(BF16)

    def core_swap(value):
        blocks = jnp.split(value, plane, axis=-1)
        return jnp.concatenate([blocks[j ^ ctx_count] for j in range(plane)], axis=-1)

    all_x = jnp.concatenate([own_x, core_swap(swap(own_x, "dp", 1))], axis=0)
    all_g = jnp.concatenate([own_g, swap(own_g, "dp", 1)], axis=0)

    pre_up = dot_f32("rd,df->rf", all_x, gate_up_w)
    gelu_value, gelu_slope = gelu_parts(pre_up[:, :half_ff])
    up_part = pre_up[:, half_ff:]
    activated = (gelu_value * up_part).astype(BF16)
    act_grad = dot_f32("rd,fd->rf", all_g, down_w)
    pre_grad = (act_grad * up_part * gelu_slope).astype(BF16)
    up_grad = (act_grad * gelu_value).astype(BF16)
    both_grad = jnp.concatenate([pre_grad, up_grad], axis=1)
    back_part = dot_f32("rf,df->rd", both_grad, gate_up_w)
    out_part = dot_f32("rf,fd->rd", activated, down_w)
    out_own = (
        out_part[:row_count] + swap(out_part[row_count:].astype(BF16), "dp", 1).astype(F32)
    ).astype(BF16)
    back_own = (
        back_part[:row_count]
        + swap(core_swap(back_part[row_count:].astype(BF16)), "dp", 1).astype(F32)
    ).astype(BF16)
    gate_rows = jnp.sum(own_u.astype(F32) * out_own.astype(F32), axis=-1)

    def to_source(value):
        parts = value.reshape((expert_count, micro, slots) + value.shape[1:])
        parts = exchange(parts)
        return jnp.moveaxis(parts, 0, 1).reshape((micro, experts * slots) + value.shape[1:])

    back_rows = to_source(back_own)
    gate_back = to_source(gate_rows)
    out_rows = to_source(out_own)

    gate_up_total = dot_f32("rd,rf->df", all_x, both_grad)
    down_total = dot_f32("rf,rd->fd", activated, all_g)

    gate_up_sums = [0.0, 0.0]
    for j in range(plane):
        dp_offset, ctx_offset = j // ctx_count, j % ctx_count
        block = gate_up_total[j * (width // plane) : (j + 1) * (width // plane)].astype(BF16)
        pairs = [
            (
                (d * ctx_count + c) * expert_count + e,
                ((d ^ dp_offset) * ctx_count + (c ^ ctx_offset)) * expert_count + e,
            )
            for d in range(dp_count)
            for c in range(ctx_count)
            for e in range(expert_count)
        ]
        if j:
            block = lax.ppermute(block, ALL, pairs)
        gate_up_sums[dp_offset % 2] = gate_up_sums[dp_offset % 2] + block.astype(F32)
    first_half, second_half = reorder(gate_up_sums, low)
    grad_gate = jnp.concatenate([first_half[:, :half_ff], second_half[:, :half_ff]], axis=1)
    grad_up = jnp.concatenate([first_half[:, half_ff:], second_half[:, half_ff:]], axis=1)
    grad_down = 0.0
    for ctx_offset in range(ctx_count):
        for core in range(2):
            pairs = down_routes(dp_count, ctx_count, expert_count, core, ctx_offset)
            from_core = jnp.where(low == high, core, 1 - core)
            place = (from_core * ctx_count + (ctx_index ^ ctx_offset)) * down_rows
            piece = lax.dynamic_slice_in_dim(down_total, place, down_rows, axis=0).astype(BF16)
            arrived = lax.ppermute(piece, ALL, [(b, a) for a, b in pairs])
            grad_down = grad_down + arrived.astype(F32)

    pair_out = [dot_f32("mrs,mrd->msd", pick_bf[j], out_rows) for j in range(top_count)]
    final = hidden + sum(gate_probs[:, :, j, None] * pair_out[j] for j in range(top_count))
    final = final.astype(BF16)
    gate_grad = jnp.stack(
        [
            jnp.sum(jnp.where(pick[j], gate_back[:, :, None], 0.0), axis=1)
            for j in range(top_count)
        ],
        axis=-1,
    )
    chosen_grad = gate_probs * (
        gate_grad - jnp.sum(gate_probs * gate_grad, axis=-1, keepdims=True)
    )
    logit_grad = jnp.sum(route_hot * chosen_grad[..., None], axis=2).astype(BF16)
    normed_grad = reorder_lanes(
        dot_f32("mrs,mrd->msd", pick_any, back_rows), plane, plane_index
    ) + dot_f32("mse,de->msd", logit_grad, router_w)
    router_total = dot_f32("msd,mse->de", normed_two, logit_grad)
    hidden_norm_grad, second_total = norm_pull(hidden, inverse_two, gain_two, normed_grad)
    hidden_grad = cot_rows + hidden_norm_grad
    branch_grad = (hidden_grad * live_rows).astype(BF16)
    hidden_low = hidden_grad.astype(BF16)
    out_total = dot_f32("msi,mso->io", mixed, branch_grad)
    mixed_grad = dot_f32("mso,io->msi", branch_grad, out_w).astype(BF16)
    grad_parts = reorder(jnp.split(mixed_grad, ctx_count, axis=-1), ctx_index)
    grad_parts = [grad_parts[0]] + [
        swap(grad_parts[k], "context", k) for k in range(1, ctx_count)
    ]
    mixed_back = sum(
        dot_f32("msp,msw->mpw", hot[k], grad_parts[k]) for k in range(ctx_count)
    ).astype(BF16)
    qkv_grad, diagonals = attend_back(qkv, mixed_back, lines, length, heads)
    qkv_total = dot_f32("mpd,mpw->dw", normed, qkv_grad)
    first_part = dot_f32("mpw,dw->mpd", qkv_grad, qkv_w)
    first_total = jnp.sum(first_part * rows_all * inverse_one, axis=(0, 1))
    blocks = [
        lax.dynamic_slice_in_dim(first_part, (ctx_index ^ k) * rows_dev, rows_dev, axis=1)
        for k in range(ctx_count)
    ]
    first_grad = blocks[0] + sum(
        swap(blocks[k].astype(BF16), "context", k).astype(F32) for k in range(1, ctx_count)
    )

    def to_positions(value):
        parts = [value] + [swap(value, "context", k) for k in range(1, ctx_count)]
        return sum(dot_f32("msp,msd->mpd", hot_mine[k], parts[k]) for k in range(ctx_count))

    rows_mine = act.astype(F32)
    inverse_mine = lax.rsqrt(jnp.mean(rows_mine * rows_mine, axis=-1, keepdims=True) + epsilon)
    rows_back, _ = norm_pull(rows_mine, inverse_mine, gain_one, first_grad)
    grad_input = (to_positions(hidden_low) + rows_back).astype(BF16)[:, None]
    output = to_positions(final).astype(BF16)[:, None]

    sums = plain_sums(
        qkv_total, out_total, router_total, first_total, second_total, own_width
    )
    grad_query, grad_key, grad_value, grad_out, grad_router, grad_first, grad_second = sums
    diag_all = lax.all_gather(
        lax.psum(diagonals, ("dp", "experts")), "context", axis=0, tiled=True
    )
    offsets = jnp.concatenate([diag_all[:, :1], diag_all[:, : seq : -1]], axis=1)
    grad_table = jnp.einsum(
        "hs,sb->bh", offsets, bucket_hot.astype(F32), precision=lax.Precision.HIGHEST
    )
    return (
        output,
        grad_input,
        grad_query,
        grad_key,
        grad_value,
        grad_out,
        grad_router,
        grad_first,
        grad_second,
        grad_table,
        grad_gate[None],
        grad_up[None],
        grad_down[None],
    )


class Wires:
    def __init__(self, sends, receives, homes):
        self.sends, self.receives, self.homes = sends, receives, homes
        self.used, self.used_home = 0, 0

    def take(self):
        self.used += 1
        return self.used - 1

    def copy(self, source, place, peer, index):
        return remote(source, place, self.sends.at[index], self.receives.at[index], peer)

    def home(self, source, place):
        copy = pltpu.make_async_copy(source, place, self.homes.at[self.used_home])
        self.used_home += 1
        return copy


class Spread:
    def __init__(self, wires, buf, ctx_axis):
        self.wires, self.buf = wires, buf
        dp, ctx, exp = (lax.axis_index(name) for name in ALL)
        self.high, self.low, self.exp = dp // 2, dp % 2, exp
        self.last = lax.axis_size("experts") - 1
        self.core_peer = (flip(dp, 1), ctx, exp)
        self.x_peer = (flip(dp, 2), ctx, exp)
        self.up_peer = (dp, ctx, jnp.minimum(exp + 1, self.last))
        self.down_peer = (dp, ctx, jnp.maximum(exp - 1, 0))
        self.labels = [(0, 0)] + [(h, d) for h in range(1, self.last + 1) for d in (1, -1)]
        self.z_wire, self.x_wire, self.own_wire, self.far_wire = (
            {label: wires.take() for label in self.labels} for _ in range(4)
        )

    def block(self, label):
        hop, way = label
        return jnp.clip(self.exp - hop * way, 0, self.last) if hop else self.exp

    def when(self, label):
        hop, way = label
        if hop == 0:
            return lambda f: f()
        here = self.exp - hop * way
        return pl.when((here >= 0) & (here <= self.last))

    def can_send(self, label, act):
        hop, way = label
        held = self.exp - (hop - 1) * way
        ahead = self.exp + way
        pl.when((held >= 0) & (held <= self.last) & (ahead >= 0) & (ahead <= self.last))(act)

    def z_copy(self, label):
        hop, way = label
        held = jnp.clip(self.exp - (hop - 1) * way, 0, self.last)
        part = self.buf.at[self.high, self.low, :, held]
        peer = self.up_peer if way == 1 else self.down_peer
        return self.wires.copy(part, part, peer, self.z_wire[label])

    def part_copy(self, label, high, wire, peer):
        part = self.buf.at[high, self.low, :, self.block(label)]
        return self.wires.copy(part, part, peer, wire[label])

    def x_copy(self, label):
        return self.part_copy(label, self.high, self.x_wire, self.x_peer)

    def own_copy(self, label):
        return self.part_copy(label, self.high, self.own_wire, self.core_peer)

    def far_copy(self, label):
        return self.part_copy(label, 1 - self.high, self.far_wire, self.core_peer)

    def spread(self, label):
        self.x_copy(label).start()
        self.own_copy(label).start()

    def begin(self):
        for way in (1, -1):
            self.can_send((1, way), lambda way=way: self.z_copy((1, way)).start())
        self.spread((0, 0))

    def hop(self, hop):
        for way in (1, -1):
            label = (hop, way)

            @self.when(label)
            def _(label=label):
                part = self.buf.at[self.high, self.low, :, self.block(label)]
                self.wires.copy(part, part, self.up_peer, self.z_wire[label]).wait_recv()

            if hop < self.last:
                nxt = (hop + 1, way)
                self.can_send(nxt, lambda nxt=nxt: self.z_copy(nxt).start())

            @self.when(label)
            def _(label=label):
                self.spread(label)

        for label in self.labels:
            if label[0] == hop - 1:
                self.pass_far(label)

    def pass_far(self, label):
        @self.when(label)
        def _():
            self.x_copy(label).wait_recv()
            self.far_copy(label).start()

    def end(self):
        for label in self.labels:
            if label[0] == self.last:
                self.pass_far(label)
        for label in self.labels:

            @self.when(label)
            def _(label=label):
                self.own_copy(label).wait_recv()
                self.far_copy(label).wait_recv()

    def drain(self):
        for label in self.labels:
            if label[0]:
                self.can_send(label, lambda label=label: self.z_copy(label).wait_send())

            @self.when(label)
            def _(label=label):
                self.x_copy(label).wait_send()
                self.own_copy(label).wait_send()
                self.far_copy(label).wait_send()


def front_kernel(
    sizes,
    act_ref,
    cot_ref,
    deal_ref,
    length_ref,
    route_ref,
    line_ref,
    query_ref,
    key_ref,
    value_ref,
    out_ref,
    extra_ref,
    gate_ref,
    up_ref,
    down_ref,
    hidden_ref,
    logit_ref,
    mixed,
    cot_rows_ref,
    dense_save,
    out_save,
    act_save,
    normed_save,
    qkv_save,
    x_save,
    u_save,
    g_save,
    gate_save,
    down_save,
    both_save,
    activated_save,
    dense,
    out_w,
    act_all,
    normed_ref,
    qkv_ref,
    all_x,
    all_u,
    all_p,
    all_g,
    gate_up,
    down,
    both,
    activated,
    cot_all,
    mixed_own,
    mixed_sent,
    sent_x,
    sent_u,
    sent_p,
    sends,
    receives,
    homes,
):
    heads, head_size, experts, capacity, slots = sizes
    micro, rows_dev, width = act_ref.shape
    own_width = heads * head_size
    half = gate_ref.shape[1] // 2
    dp, ctx, exp = (lax.axis_index(name) for name in ALL)
    high, low = dp // 2, dp % 2
    block = dp * 2 + ctx
    core_peer, x_peer, x_core = ((flip(dp, 1), ctx, exp), (flip(dp, 2), ctx, exp), (3 - dp, ctx, exp))
    x_core = (flip(flip(dp, 2), 1), ctx, exp)
    y_peer, y_core = (dp, 1 - ctx, exp), (flip(dp, 1), 1 - ctx, exp)
    z_peers = [None] + [(dp, ctx, flip(exp, 1)), (dp, ctx, flip(exp, 2)), (dp, ctx, 3 - exp)]
    z_index = [exp, flip(exp, 1), flip(exp, 2), 3 - exp]
    greet([core_peer, x_peer, x_core, y_peer, y_core] + z_peers[1:])
    wires = Wires(sends, receives, homes)
    drains = []
    home_copies = []

    def send(source, place, peer):
        copy = wires.copy(source, place, peer, wires.take())
        copy.start()
        drains.append(copy)
        return copy

    def multiple(index, size):
        return pl.ds(pl.multiple_of(index * size, size), size)

    def save(source, place):
        copy = wires.home(source, place)
        copy.start()
        home_copies.append(copy)

    mine, other = multiple(ctx, own_width), multiple(1 - ctx, own_width)
    first = []
    for i, ref in enumerate((query_ref, key_ref, value_ref)):
        place = dense.at[high, low, ctx, exp, :, i * own_width : (i + 1) * own_width]
        first.append(send(ref.at[:, other], place, y_peer))
    first.append(send(extra_ref, dense.at[high, low, ctx, exp, :, 3 * own_width :], y_peer))
    out_first = send(out_ref, out_w.at[high, low, ctx, exp], y_peer)
    here = multiple(ctx, rows_dev)
    act_first = send(act_ref, act_all.at[:, here], y_peer)
    def gate_sends(core, peer):
        cols = multiple(core, half)
        return [
            send(gate_ref.at[:, cols], gate_up.at[block, :, 0:half], peer),
            send(up_ref.at[:, cols], gate_up.at[block, :, half:], peer),
        ]

    own_gate = []
    for ref, start in ((gate_ref, 0), (up_ref, half)):
        copy = wires.home(ref.at[:, multiple(low, half)], gate_up.at[block, :, start : start + half])
        copy.start()
        own_gate.append(copy)

    for i, ref in enumerate((query_ref, key_ref, value_ref)):
        dense[high, low, ctx, exp, :, i * own_width : (i + 1) * own_width] = ref[:, mine]
    dense[high, low, ctx, exp, :, 3 * own_width :] = extra_ref[...]
    out_w[high, low, ctx, exp] = out_ref[...]
    act_all[:, here, :] = act_ref[...]
    cot_all[:, here, :] = cot_ref[...]

    spread = Spread(wires, dense, 2)
    spread_out = Spread(wires, out_w, 2)
    for copy in first:
        copy.wait_recv()
    spread.begin()
    cot_first = send(cot_ref, cot_all.at[:, here], y_peer)
    from_y_core = gate_sends(1 - low, y_core)
    from_y = gate_sends(low, y_peer)
    from_core = gate_sends(1 - low, core_peer)

    spread.hop(1)

    own_down = low * 2 + ctx
    home_down = wires.home(down_ref, down.at[own_down])
    down_wire = {name: wires.take() for name in ("core", "x", "xc", "y", "yc", "rx", "ry")}
    at_home = low == high

    def down_copy(name, peer, source=None):
        source = down_ref if source is None else source
        return wires.copy(source, down.at[own_down], peer, down_wire[name])

    down_sends = [
        ("core", core_peer, False),
        ("x", x_peer, True),
        ("xc", x_core, False),
        ("y", y_peer, True),
        ("yc", y_core, False),
    ]

    def down_start():
        @pl.when(at_home)
        def _():
            home_down.start()

        for name, peer, straight in down_sends:
            pl.when(at_home == straight)(lambda name=name, peer=peer: down_copy(name, peer).start())

    lane = lax.broadcasted_iota(jnp.int32, (rows_dev, 128), 1)
    lane_f = lane.astype(F32)
    row_id = lax.broadcasted_iota(jnp.int32, (rows_dev, rows_dev), 0)
    col_id = lax.broadcasted_iota(jnp.int32, (rows_dev, rows_dev), 1)
    before = (row_id > col_id).astype(BF16)
    seq = deal_ref.shape[1]
    seq_lane = lax.broadcasted_iota(jnp.int32, (rows_dev, seq), 1)

    def hot(m, k):
        index = ctx if k == 0 else 1 - ctx
        return (deal_ref[m, multiple(index, rows_dev), :] == seq_lane).astype(BF16)

    def live_slots(m):
        return deal_ref[m, here, :] < length_ref[m]

    def ranks(m):
        live = live_slots(m)
        hots = [(route_ref[m, :, j : j + 1] == lane) for j in range(2)]
        used = jnp.where((hots[0] | hots[1]) & live, 1.0, 0.0).astype(BF16)
        earlier = jnp.dot(before, used, preferred_element_type=F32)
        found = []
        for j in range(2):
            rank = jnp.sum(jnp.where(hots[j], earlier, 0.0), axis=1, keepdims=True)
            found.append(jnp.where(live & (rank < capacity), rank, -1.0))
        return found

    def picks(m, k, rank):
        return [
            (route_ref[m, :, j : j + 1] == z_index[k]) & (rank[j] == lane_f) for j in range(2)
        ]

    def as_rows(pick, value):
        chosen = lax.dot_general(
            pick, value, (((0,), (0,)), ((), ())), preferred_element_type=F32
        )
        return chosen[:slots].astype(BF16)

    spread.hop(2)
    rank_of = [ranks(m) for m in range(micro)]
    act_first.wait_recv()
    spread.hop(3)
    cot_first.wait_recv()
    pick_of = {}
    for m in range(micro):
        hot_mine = hot(m, 0)
        cot_rows = jnp.dot(hot_mine, cot_all[m], preferred_element_type=F32).astype(BF16)
        cot_rows_ref[m] = cot_rows
        for k in range(experts):
            pick = picks(m, k, rank_of[m])
            pick_any = jnp.where(pick[0] | pick[1], 1.0, 0.0).astype(BF16)
            rows = as_rows(pick_any, cot_rows)
            if k == 0:
                all_u[0, 0, m] = rows
            else:
                sent_u[k - 1, m] = rows
    out_first.wait_recv()
    spread.end()
    from_x = gate_sends(low, x_peer)
    from_x_core = gate_sends(1 - low, x_core)
    spread_out.begin()
    save(dense, dense_save)
    save(act_all, act_save)
    u_first, u_core = {}, []

    def send_u(m):
        for k in range(1, experts):
            u_first[k, m] = send(sent_u.at[k - 1, m], all_u.at[0, k, m], z_peers[k])
        u_core.append(send(all_u.at[0, 0, m], all_u.at[1, 0, m], core_peer))

    def pass_u(m):
        for k in range(1, experts):
            u_first[k, m].wait_recv()
            u_core.append(send(all_u.at[0, k, m], all_u.at[1, k, m], core_peer))

    send_u(0)

    extras = dense[:, :, :, :, :, 3 * own_width :].reshape(width, 128).astype(F32)
    turned = extras.T
    gain_one, gain_two = turned[experts : experts + 1], turned[experts + 1 : experts + 2]
    for m in range(micro):
        rows = act_all[m].astype(F32)
        inverse = lax.rsqrt(jnp.mean(rows * rows, axis=-1, keepdims=True) + epsilon)
        normed_ref[m] = (rows * inverse * gain_one).astype(BF16)
    for i in range(3):
        weight = dense[:, :, :, :, :, i * own_width : (i + 1) * own_width].reshape(width, own_width)
        for m in range(micro):
            qkv_ref[m, :, i * own_width : (i + 1) * own_width] = jnp.dot(
                normed_ref[m], weight, preferred_element_type=F32
            ).astype(BF16)
    spread_out.hop(1)

    scale = head_size ** (-0.5)
    mixed_first = []
    save(normed_ref, normed_save)
    save(qkv_ref, qkv_save)
    for m in range(micro):
        length = length_ref[m]
        for head in range(heads):
            at = [
                slice(part * own_width + head * head_size, part * own_width + (head + 1) * head_size)
                for part in range(3)
            ]
            scores = masked_scores(
                qkv_ref[m, :, at[0]], qkv_ref[m, :, at[1]], line_ref[head : head + 1, :], length, scale
            )
            probs = soft(scores).astype(BF16)
            mixed_own[:, at[0]] = jnp.dot(
                probs, qkv_ref[m, :, at[2]], preferred_element_type=F32
            ).astype(BF16)
        own = mixed_own[...]
        mixed_sent[m] = jnp.dot(hot(m, 1), own, preferred_element_type=F32).astype(BF16)
        mixed_first.append(send(mixed_sent.at[m], mixed.at[m, :, mine], y_peer))
        mixed[m, :, mine] = jnp.dot(hot(m, 0), own, preferred_element_type=F32).astype(BF16)
        spread_out.hop(2 + m)
    spread_out.end()

    router_w = dense[:, :, :, :, :, 3 * own_width :].reshape(width, 128)
    x_first, p_first, x_core_copy, core_copies = {}, {}, {}, []
    for m in range(micro):
        mixed_first[m].wait_recv()
        branch = jnp.dot(
            mixed[m], out_w[...].reshape(width, width), preferred_element_type=F32
        )
        rows_in = jnp.dot(hot(m, 0), act_all[m], preferred_element_type=F32)
        live = live_slots(m)
        hidden = rows_in + jnp.where(live, branch, 0.0)
        hidden_ref[m] = hidden
        inverse = lax.rsqrt(jnp.mean(hidden * hidden, axis=-1, keepdims=True) + epsilon)
        normed_two = (hidden * inverse * gain_two).astype(BF16)
        logits = jnp.dot(normed_two, router_w, preferred_element_type=F32)
        logit_ref[m] = logits
        chosen = [
            jnp.sum(jnp.where(route_ref[m, :, j : j + 1] == lane, logits, 0.0), axis=1, keepdims=True)
            for j in range(2)
        ]
        top = jnp.maximum(chosen[0], chosen[1])
        raised = [jnp.exp(c - top) for c in chosen]
        total = raised[0] + raised[1]
        gates = [r / total for r in raised]
        for k in range(experts):
            pick = picks(m, k, rank_of[m])
            pick_any = jnp.where(pick[0] | pick[1], 1.0, 0.0).astype(BF16)
            rows = as_rows(pick_any, normed_two)
            weights = jnp.sum(
                jnp.where(pick[0], gates[0], 0.0) + jnp.where(pick[1], gates[1], 0.0),
                axis=0,
                keepdims=True,
            )
            weights = jnp.broadcast_to(weights, (8, 128))
            if k == 0:
                all_x[0, 0, m] = rows
                all_p[0, 0, m] = weights
                x_core_copy[0, m] = send(all_x.at[0, 0, m], all_x.at[1, 0, m], core_peer)
                core_copies.append(send(all_p.at[0, 0, m], all_p.at[1, 0, m], core_peer))
            else:
                sent_x[k - 1, m] = rows
                sent_p[k - 1, m] = weights
                x_first[k, m] = send(sent_x.at[k - 1, m], all_x.at[0, k, m], z_peers[k])
                p_first[k, m] = send(sent_p.at[k - 1, m], all_p.at[0, k, m], z_peers[k])

    for m in range(1, micro):
        send_u(m)
    save(out_w, out_save)
    for copy in from_x:
        copy.wait_recv()
    x_block = flip(dp, 2) * 2 + ctx
    relay_y = send(gate_up.at[x_block], gate_up.at[x_block], y_peer)
    for copy in from_y_core:
        copy.wait_recv()
    y_block = flip(dp, 1) * 2 + 1 - ctx
    relay_x = send(gate_up.at[y_block], gate_up.at[y_block], x_peer)

    down_start()
    pass_u(0)

    def pass_rows(k):
        for m in range(micro):
            x_first[k, m].wait_recv()
            x_core_copy[k, m] = send(all_x.at[0, k, m], all_x.at[1, k, m], core_peer)
            p_first[k, m].wait_recv()
            core_copies.append(send(all_p.at[0, k, m], all_p.at[1, k, m], core_peer))

    def hidden_units(k):
        for m in range(micro):
            x_core_copy[k, m].wait_recv()
        count = 2 * micro * slots
        shape = (2, micro, slots)

        def tile(start, size):
            rows = all_x[:, k].reshape(count, width)
            gate_w = gate_up[:, :, pl.ds(start, size)].reshape(width, size)
            up_w = gate_up[:, :, pl.ds(half + start, size)].reshape(width, size)
            pre = jnp.dot(rows, gate_w, preferred_element_type=F32)
            up_part = jnp.dot(rows, up_w, preferred_element_type=F32)
            value, slope = gelu_parts(pre)
            activated[:, k, :, :, pl.ds(start, size)] = (
                (value * up_part).astype(BF16).reshape(shape + (size,))
            )
            both[:, k, :, :, pl.ds(start, size)] = (
                (up_part * slope).astype(BF16).reshape(shape + (size,))
            )
            both[:, k, :, :, pl.ds(half + start, size)] = value.astype(BF16).reshape(shape + (size,))

        wide = half // 256

        def step(i, carry):
            tile(pl.multiple_of(i * 256, 256), 256)
            return carry

        lax.fori_loop(0, wide, step, 0)
        if half % 256:
            tile(wide * 256, half - wide * 256)

    for k in (1, 2):
        pass_rows(k)
    for copy in from_core + from_y + from_x_core + [relay_x, relay_y]:
        copy.wait_recv()
    for copy in own_gate:
        copy.wait()
    save(gate_up, gate_save)
    hidden_units(0)
    hidden_units(1)
    away = jnp.logical_not(at_home)
    rx_place = low * 2 + 1 - ctx
    ry_place = (1 - low) * 2 + ctx

    @pl.when(at_home)
    def _():
        down_copy("y", y_peer).wait_recv()
        wires.copy(down.at[rx_place], down.at[rx_place], x_peer, down_wire["rx"]).start()

    @pl.when(away)
    def _():
        down_copy("xc", x_core).wait_recv()
        wires.copy(down.at[ry_place], down.at[ry_place], y_peer, down_wire["ry"]).start()

    pass_rows(3)
    hidden_units(2)
    hidden_units(3)
    save(both, both_save)
    save(activated, activated_save)
    save(all_x, x_save)
    for m in range(1, micro):
        pass_u(m)
    for copy in u_core + core_copies:
        copy.wait_recv()
    save(all_u.at[0], u_save)
    for part in range(2):
        for k in range(experts):
            for m in range(micro):
                column = jnp.broadcast_to(all_p[part, k, m, 0:1, :], (128, 128)).T[:slots, 0:1]
                all_g[part, k, m] = (column * all_u[part, k, m].astype(F32)).astype(BF16)
    save(all_g, g_save)

    @pl.when(at_home)
    def _():
        for name in ("core", "yc"):
            down_copy(name, core_peer).wait_recv()
        home_down.wait()
        down_copy("rx", x_peer).wait_send()

    @pl.when(away)
    def _():
        for name in ("x", "rx", "ry"):
            down_copy(name, core_peer).wait_recv()
        down_copy("ry", y_peer).wait_send()

    save(down, down_save)
    for name, peer, straight in down_sends:
        pl.when(at_home == straight)(lambda name=name, peer=peer: down_copy(name, peer).wait_send())
    for copy in home_copies:
        copy.wait()
    for copy in drains:
        copy.wait_send()
    spread.drain()
    spread_out.drain()


def front(sizes, act, cot, deal, length, route, lines, weights, extras, w_gate, w_up, w_down):
    heads, head_size, experts, capacity, slots = sizes
    micro, rows_dev, width = act.shape
    own_width = heads * head_size
    per_row = weights[0].shape[0]
    seq = deal.shape[1]
    half = w_gate.shape[1] // 2
    in_vmem, in_hbm = pl.BlockSpec(memory_space=pltpu.VMEM), pl.BlockSpec(memory_space=pltpu.HBM)
    wide = 3 * own_width + 128
    rows = (2, experts, micro, slots)
    outs = [
        ((micro, rows_dev, width), F32),
        ((micro, rows_dev, 128), F32),
        ((micro, rows_dev, width), BF16),
        ((micro, rows_dev, width), BF16),
    ]
    saved = [
        ((2, 2, 2, 4, per_row, wide), BF16),
        ((2, 2, 2, 4, per_row, width), BF16),
        ((micro, seq, width), BF16),
        ((micro, seq, width), BF16),
        ((micro, seq, 3 * own_width), BF16),
        (rows + (width,), BF16),
        (rows[1:] + (width,), BF16),
        (rows + (width,), BF16),
        ((8,) + (w_gate.shape[0], 2 * half), BF16),
        ((4,) + w_down.shape, BF16),
        (rows + (2 * half,), BF16),
        (rows + (half,), BF16),
    ]
    held = (
        saved[:6]
        + [(rows + (width,), BF16), ((2, experts, micro, 8, 128), F32)]
        + saved[7:]
    )
    return pl.pallas_call(
        functools.partial(front_kernel, sizes),
        out_shape=tuple(jax.ShapeDtypeStruct(*out) for out in outs + saved),
        in_specs=[in_vmem] * 3 + [pl.BlockSpec(memory_space=pltpu.SMEM)] + [in_vmem] * 7 + [in_hbm] * 3,
        out_specs=(in_vmem,) * len(outs) + (in_hbm,) * len(saved),
        scratch_shapes=[pltpu.VMEM(*shape) for shape in held]
        + [
            pltpu.VMEM((micro, seq, width), BF16),
            pltpu.VMEM((seq, own_width), BF16),
            pltpu.VMEM((micro, rows_dev, own_width), BF16),
            pltpu.VMEM((experts - 1, micro, slots, width), BF16),
            pltpu.VMEM((experts - 1, micro, slots, width), BF16),
            pltpu.VMEM((experts - 1, micro, 8, 128), F32),
            pltpu.SemaphoreType.DMA((160,)),
            pltpu.SemaphoreType.DMA((160,)),
            pltpu.SemaphoreType.DMA((24,)),
        ],
        compiler_params=pltpu.CompilerParams(
            collective_id=1, has_side_effects=True, vmem_limit_bytes=60 * 2**20
        ),
    )(act, cot, deal[:, :, None], length, route, lines, *weights, extras, w_gate, w_up, w_down)


class Plan:
    def __init__(self, deal_ref, length_ref, route_ref, rows_dev, capacity):
        self.deal, self.length, self.route = deal_ref, length_ref, route_ref
        self.rows, self.capacity = rows_dev, capacity
        self.ctx, exp = lax.axis_index("context"), lax.axis_index("experts")
        self.z_index = [exp, flip(exp, 1), flip(exp, 2), 3 - exp]
        self.lane = lax.broadcasted_iota(jnp.int32, (rows_dev, 128), 1)
        self.lane_f = self.lane.astype(F32)

    def at(self, k):
        index = self.ctx if k == 0 else 1 - self.ctx
        return pl.ds(pl.multiple_of(index * self.rows, self.rows), self.rows)

    def hot(self, m, k):
        seq = self.deal.shape[1]
        lane = lax.broadcasted_iota(jnp.int32, (self.rows, seq), 1)
        return (self.deal[m, self.at(k), :] == lane).astype(BF16)

    def hot_mine(self, m, k):
        lane = lax.broadcasted_iota(jnp.int32, (self.rows, self.rows), 1) + self.ctx * self.rows
        return (self.deal[m, self.at(k), :] == lane).astype(BF16)

    def live(self, m):
        return self.deal[m, self.at(0), :] < self.length[m]

    def named(self, m, j):
        return self.route[m, :, j : j + 1]

    def ranks(self, m):
        row_id = lax.broadcasted_iota(jnp.int32, (self.rows, self.rows), 0)
        col_id = lax.broadcasted_iota(jnp.int32, (self.rows, self.rows), 1)
        before = (row_id > col_id).astype(BF16)
        live = self.live(m)
        hots = [self.named(m, j) == self.lane for j in range(2)]
        used = jnp.where((hots[0] | hots[1]) & live, 1.0, 0.0).astype(BF16)
        earlier = jnp.dot(before, used, preferred_element_type=F32)
        found = []
        for j in range(2):
            rank = jnp.sum(jnp.where(hots[j], earlier, 0.0), axis=1, keepdims=True)
            found.append(jnp.where(live & (rank < self.capacity), rank, -1.0))
        return found

    def picks(self, m, k, rank):
        return [
            (self.named(m, j) == self.z_index[k]) & (rank[j] == self.lane_f) for j in range(2)
        ]

    def places(self, m, rank, experts, slots):
        lane = lax.broadcasted_iota(jnp.int32, (self.rows, experts * slots), 1).astype(F32)
        picks = []
        for j in range(2):
            place = rank[j]
            for k in range(1, experts):
                place = place + jnp.where(self.named(m, j) == self.z_index[k], 1.0 * k * slots, 0.0)
            place = jnp.where(rank[j] < 0, -1.0, place)
            picks.append(jnp.where(place == lane, 1.0, 0.0).astype(BF16))
        return picks

    def gates(self, m, logits):
        chosen = [
            jnp.sum(jnp.where(self.named(m, j) == self.lane, logits, 0.0), axis=1, keepdims=True)
            for j in range(2)
        ]
        top = jnp.maximum(chosen[0], chosen[1])
        raised = [jnp.exp(c - top) for c in chosen]
        total = raised[0] + raised[1]
        return [r / total for r in raised]


def dot_rows(left, right):
    return lax.dot_general(left, right, (((0,), (0,)), ((), ())), preferred_element_type=F32)


def dot_lanes(left, right):
    return lax.dot_general(left, right, (((1,), (1,)), ((), ())), preferred_element_type=F32)


STAGES = {"x": 0, "zl": 3, "zh": 2, "y": 1}


class Reduce:
    def __init__(self, wires, source, columns, order, bufs, peers, indices, finish):
        self.wires, self.source, self.columns = wires, source, columns
        self.order, self.bufs, self.peers, self.indices = order, bufs, peers, indices
        self.finish = finish
        self.flying, self.step = [], 0

    def launch(self, source, place, name):
        copy = self.wires.copy(source, place, self.peers[name], self.wires.take())
        copy.start()
        self.flying.append(copy)

    def begin(self):
        low = self.indices["core"]
        self.launch(self.source.at[:, 1 - low, :, self.columns], self.bufs[0], "core")

    def advance(self):
        if self.step > len(self.order):
            return False
        low = self.indices["core"]
        self.flying[-1].wait_recv()
        if self.step == 0:
            total = self.source[:, low, :, self.columns].astype(F32) + self.bufs[0][...].astype(F32)
            self.bufs[1][...] = total.astype(BF16).reshape(self.bufs[1].shape)
        else:
            kept = self.bufs[2 * self.step - 1]
            arrived = self.bufs[2 * self.step][...].astype(F32)
            mine = kept[self.cut(self.order[self.step - 1], True)].astype(F32)
            if self.step == len(self.order):
                self.finish(mine, arrived)
                self.step += 1
                return False
            self.bufs[2 * self.step + 1][...] = (mine + arrived).astype(BF16)
        name = self.order[self.step]
        kept = self.bufs[2 * self.step + 1]
        self.launch(kept.at[self.cut(name, False)], self.bufs[2 * self.step + 2], name)
        self.step += 1
        return True

    def cut(self, name, own):
        gone = set(self.order[: self.order.index(name)])
        axis = sum(1 for n, place in STAGES.items() if place < STAGES[name] and n not in gone)
        index = self.indices[name] if own else 1 - self.indices[name]
        return (slice(None),) * axis + (index,)


def reduce_buffers(order, rows, per_row, size):
    left = {"x", "zl", "zh", "y"}
    shapes = [(2, rows // 4, size)]
    for name in order:
        shapes.append((2,) * len(left) + (per_row, size))
        left.discard(name)
        shapes.append((2,) * len(left) + (per_row, size))
    return [pltpu.VMEM(shape, BF16) for shape in shapes]


ORDERS = [("x", "zl", "zh", "y")] * 3 + [("zl", "zh", "x", "y")] * 2 + [("x", "zl", "zh", "y")]


def back_kernel(
    sizes,
    hidden_ref,
    logit_ref,
    mixed,
    cot_rows_ref,
    act_ref,
    deal_ref,
    route_ref,
    line_ref,
    length_ref,
    dense_in,
    out_in,
    act_in,
    normed_in,
    qkv_in,
    x_in,
    u_in,
    g_in,
    gate_w_in,
    down_w_in,
    both_in,
    activated_in,
    output_ref,
    grad_input_ref,
    query_out,
    key_out,
    value_out,
    out_out,
    small_out,
    diag_out,
    gate_in,
    down_in,
    gate_w,
    down_w,
    relay_got,
    back_got,
    out_got,
    sent_back,
    sent_out,
    sent_gate,
    ret_back,
    ret_out,
    ret_gate,
    final_all,
    hidden_all,
    mixed_got,
    grad_sent,
    first_sent,
    first_got,
    diag_buf,
    *rest,
):
    heads, head_size, experts, capacity, slots = sizes
    chunk_bufs, (sends, receives, homes) = rest[:-3], rest[-3:]
    micro, rows_dev, width = hidden_ref.shape
    seq = deal_ref.shape[1]
    own_width = heads * head_size
    dp, ctx, exp = (lax.axis_index(name) for name in ALL)
    high, low = dp // 2, dp % 2
    other_core, other_x, both_dp = flip(dp, 1), flip(dp, 2), flip(flip(dp, 1), 2)
    core_peer, x_peer, x_core = (other_core, ctx, exp), (other_x, ctx, exp), (both_dp, ctx, exp)
    y_peer, y_core = (dp, 1 - ctx, exp), (other_core, 1 - ctx, exp)
    far_peer, far_core = (other_x, 1 - ctx, exp), (both_dp, 1 - ctx, exp)
    z_peers = [None] + [(dp, ctx, flip(exp, 1)), (dp, ctx, flip(exp, 2)), (dp, ctx, 3 - exp)]
    greet([core_peer, x_peer, x_core, y_peer, y_core, far_peer, far_core] + z_peers[1:])
    wires = Wires(sends, receives, homes)
    drains = []

    class Sent:
        def __init__(self, like, source, place, peer):
            self.like, self.peer, self.index = like, peer, wires.take()
            wires.copy(source, place, peer, self.index).start()
            drains.append(self)

        def again(self):
            part = self.like()
            return wires.copy(part, part, self.peer, self.index)

        def wait_recv(self):
            self.again().wait_recv()

        def wait_send(self):
            self.again().wait_send()

    def send(source, place, peer, like=None):
        return Sent(like or (lambda: source), source, place, peer)

    def like_rows():
        return ret_back.at[0, 0]

    def like_gate():
        return ret_gate.at[0, 0]

    def like_block():
        return gate_w.at[0]

    plan = Plan(deal_ref, length_ref, route_ref, rows_dev, capacity)
    mine = pl.ds(pl.multiple_of(ctx * own_width, own_width), own_width)
    other = pl.ds(pl.multiple_of((1 - ctx) * own_width, own_width), own_width)

    def load(source, place):
        copy = wires.home(source, place)
        copy.start()
        return copy

    block = dp * 2 + ctx
    at_home = low == high
    away = jnp.logical_not(at_home)
    down_wire = [wires.take() for _ in range(8)]
    down_sends = [
        (None, False, low * 2 + ctx, 0),
        (core_peer, False, (1 - low) * 2 + ctx, 0),
        (y_peer, False, low * 2 + 1 - ctx, 1),
        (y_core, False, (1 - low) * 2 + 1 - ctx, 1),
        (x_peer, True, low * 2 + ctx, 2),
        (x_core, True, (1 - low) * 2 + ctx, 2),
        (far_peer, True, low * 2 + 1 - ctx, 3),
        (far_core, True, (1 - low) * 2 + 1 - ctx, 3),
    ]

    def down_copy(i):
        peer, _, place, slot = down_sends[i]
        return wires.copy(down_w.at[place], down_in.at[slot], peer or core_peer, down_wire[i])

    home_wire = wires.used_home
    wires.used_home += 2

    def home_block():
        return pltpu.make_async_copy(gate_w.at[block], gate_in.at[0], homes.at[home_wire])

    def home_down():
        return pltpu.make_async_copy(
            down_w.at[low * 2 + ctx], down_in.at[0], homes.at[home_wire + 1]
        )

    bulk, relayed = [], []
    ret_first = {}
    both_rows = experts * slots

    def expert_phase(both, rows_x, rows_g, activated, rows_u, back_part, out_part):
        half = activated.shape[-1]
        first = [load(g_in, rows_g), load(down_w_in, down_w)]
        second = [load(both_in, both), load(gate_w_in, gate_w)]
        third = [load(activated_in, activated), load(x_in, rows_x), load(u_in, rows_u)]
        for copy in first + second:
            copy.wait()
        shape = (2, experts, slots)
        count = 2 * experts * slots

        def act_tile(m, start, size):
            rows = rows_g[:, :, m].reshape(count, width)
            weight = down_w[...].reshape(half, width) if size == half else down_flat(start, size)
            grad = dot_lanes(rows, weight)
            for shift in (0, half):
                cols = pl.ds(shift + start, size)
                kept = both[:, :, m, :, cols].reshape(count, size).astype(F32)
                both[:, :, m, :, cols] = (grad * kept).astype(BF16).reshape(shape + (size,))

        def down_flat(start, size):
            per = down_w.shape[1]
            parts = []
            while size:
                index, offset = start // per, start % per
                taken = min(size, per - offset)
                parts.append(down_w[index, offset : offset + taken, :])
                start, size = start + taken, size - taken
            return parts[0] if len(parts) == 1 else jnp.concatenate(parts, axis=0)

        def back_rows(m):
            def step(i, carry):
                rows = both[:, :, m].reshape(count, 2 * half)
                weight = gate_w[pl.ds(i * 2, 2)].reshape(256, 2 * half)
                part = dot_lanes(rows, weight).astype(BF16)
                cols = pl.ds(pl.multiple_of(i * 256, 256), 256)
                back_part[:, :, m, :, cols] = part.reshape(shape + (256,))
                return carry

            lax.fori_loop(0, width // 256, step, 0)

        back_core = []
        for m in range(micro):
            for start in range(0, half, 256):
                act_tile(m, start, min(256, half - start))
            back_rows(m)
            back_core.append(send(back_part.at[1, :, m], back_got.at[m], core_peer))

        def give_back(m):
            back_core[m].wait_recv()
            for k in range(experts):
                rows = (
                    back_part[0, k, m].astype(F32) + back_got[m, k].astype(F32)
                ).astype(BF16)
                if k == 0:
                    ret_back[m, 0] = rows
                else:
                    sent_back[m, k - 1] = rows
                    ret_first["back", m, k] = send(
                        sent_back.at[m, k - 1], ret_back.at[m, k], z_peers[k], like_rows
                    )

        for copy in third:
            copy.wait()
        depth = width // gate_w.shape[0]

        def gate_grad(place):
            cols = pl.ds(pl.multiple_of(place * depth, depth), depth)
            total = jnp.zeros((depth, 2 * half), F32)
            rows = rows_x[:, :, :, :, cols].reshape(micro * count, depth)
            total = dot_rows(rows, both[...].reshape(micro * count, 2 * half))
            gate_w[place] = total.astype(BF16)

        def bulk_send(place, slot, peer):
            bulk.append(send(gate_w.at[place], gate_in.at[slot], peer, like_block))

        far_places = (other_x * 2 + 1 - ctx, both_dp * 2 + 1 - ctx)
        y_places = (dp * 2 + 1 - ctx, other_core * 2 + 1 - ctx)
        for i, place in enumerate(far_places):
            gate_grad(place)
            relayed.append(send(gate_w.at[place], relay_got.at[i], x_peer, like_block))
        give_back(0)
        for place, slot, peer in (
            (other_x * 2 + ctx, 2, x_peer),
            (both_dp * 2 + ctx, 3, x_core),
            (other_core * 2 + ctx, 1, core_peer),
        ):
            gate_grad(place)
            bulk_send(place, slot, peer)
        give_back(1)
        gate_grad(y_places[0])
        gate_grad(y_places[1])
        gate_grad(block)
        home_block().start()

        out_core = []
        for m in range(micro):

            def step(i, carry):
                cols = pl.ds(pl.multiple_of(i * 256, 256), 256)
                rows = activated[:, :, m].reshape(count, half)
                weight = down_w[:, :, cols].reshape(half, 256)
                part = jnp.dot(rows, weight, preferred_element_type=F32).astype(BF16)
                out_part[:, :, m, :, cols] = part.reshape(shape + (256,))
                return carry

            lax.fori_loop(0, width // 256, step, 0)
            out_core.append(send(out_part.at[1, :, m], out_got.at[m], core_peer))

        for i, (place, slot, peer) in enumerate(
            ((y_places[0], 4, y_peer), (y_places[1], 5, y_core))
        ):
            relayed[i].wait_recv()
            gate_w[place] = (gate_w[place].astype(F32) + relay_got[i].astype(F32)).astype(BF16)
            bulk_send(place, slot, peer)

        ones = jnp.ones((8, width), F32)
        for m in range(micro):
            out_core[m].wait_recv()
            for k in range(experts):
                rows = (
                    out_part[0, k, m].astype(F32) + out_got[m, k].astype(F32)
                ).astype(BF16)
                worth = lax.dot_general(
                    ones,
                    rows.astype(F32) * rows_u[k, m].astype(F32),
                    (((1,), (1,)), ((), ())),
                    precision=lax.Precision.HIGHEST,
                    preferred_element_type=F32,
                )
                if k == 0:
                    ret_out[m, 0] = rows
                    ret_gate[m, 0, :, :slots] = worth
                else:
                    sent_out[m, k - 1] = rows
                    sent_gate[m, k - 1, :, :slots] = worth
                    ret_first["gate", m, k] = send(
                        sent_gate.at[m, k - 1], ret_gate.at[m, k], z_peers[k], like_gate
                    )

        totals = {}
        per = down_w.shape[1]
        for start in range(0, half, 128):
            rows = activated[:, :, :, :, start : start + 128].reshape(micro * count, 128)
            total = dot_rows(rows, rows_g[...].reshape(micro * count, width)).astype(BF16)
            done = 0
            while done < 128:
                index, offset = (start + done) // per, (start + done) % per
                taken = min(128 - done, per - offset)
                down_w[index, offset : offset + taken, :] = total[done : done + taken]
                done += taken
        for i, (peer, is_away, _, _) in enumerate(down_sends):
            pl.when(away if is_away else at_home)(
                lambda i=i, peer=peer: (home_down() if peer is None else down_copy(i)).start()
            )
        for m in range(micro):
            for k in range(1, experts):
                ret_first["out", m, k] = send(
                    sent_out.at[m, k - 1], ret_out.at[m, k], z_peers[k], like_rows
                )
        for copy in back_core + out_core:
            copy.wait_send()
        gone = {id(copy) for copy in back_core + out_core}
        drains[:] = [copy for copy in drains if id(copy) not in gone]

    def token_phase(
        dense,
        out_w,
        act_all,
        normed_ref,
        qkv_ref,
        first_own,
        grad_own,
        qkv_grad,
        qkv_total,
        out_low,
        small_f,
        small_low,
        branch_all,
    ):
        loads = [
            load(source, place)
            for source, place in (
                (dense_in, dense),
                (out_in, out_w),
                (qkv_in, qkv_ref),
                (act_in, act_all),
                (normed_in, normed_ref),
            )
        ]
        for copy in loads:
            copy.wait()
        before_tokens = len(drains)
        extras = dense[:, :, :, :, :, 3 * own_width :].reshape(width, 128)
        turned = extras.astype(F32).T
        gain_one, gain_two = turned[experts : experts + 1], turned[experts + 1 : experts + 2]
        lanes = lax.broadcasted_iota(jnp.int32, (width, 128), 1)
        rank_of = [plan.ranks(m) for m in range(micro)]
        gate_of = [plan.gates(m, logit_ref[m]) for m in range(micro)]
        mixed_first, hidden_first = [], []
        second = jnp.zeros((1, width), F32)
        out_matrix = out_w[...].reshape(width, width)
        here = plan.at(0)
        for m in range(micro):
            for k in range(1, experts):
                ret_first["back", m, k].wait_recv()
                ret_first["gate", m, k].wait_recv()
            worths = []
            for j in range(2):
                worth = jnp.zeros((rows_dev, 1), F32)
                for k in range(experts):
                    pick = plan.picks(m, k, rank_of[m])[j]
                    worth = worth + jnp.sum(
                        jnp.where(pick, ret_gate[m, k, 0:1, :], 0.0), axis=1, keepdims=True
                    )
                worths.append(worth)
            gates = gate_of[m]
            mean_worth = gates[0] * worths[0] + gates[1] * worths[1]
            logit_grad = sum(
                jnp.where(plan.named(m, j) == plan.lane, gates[j] * (worths[j] - mean_worth), 0.0)
                for j in range(2)
            ).astype(BF16)
            places = plan.places(m, rank_of[m], experts, slots)
            normed_grad = jnp.dot(
                places[0] + places[1],
                ret_back[m].reshape(experts * slots, width),
                preferred_element_type=F32,
            ) + dot_lanes(logit_grad, extras)
            hidden = hidden_ref[m]
            inverse = lax.rsqrt(jnp.mean(hidden * hidden, axis=-1, keepdims=True) + epsilon)
            scaled = hidden * inverse
            normed_two = (scaled * gain_two).astype(BF16)
            router = dot_rows(normed_two, logit_grad)
            small_f[...] = router if m == 0 else small_f[...] + router
            second = second + jnp.sum(normed_grad * scaled, axis=0, keepdims=True)
            lifted = gain_two * normed_grad
            mean_part = jnp.mean(lifted * hidden, axis=-1, keepdims=True)
            hidden_grad = (
                cot_rows_ref[m].astype(F32)
                + inverse * lifted
                - hidden * (inverse * inverse * inverse) * mean_part
            )
            hidden_all[m, 0] = hidden_grad.astype(BF16)
            branch_grad = jnp.where(plan.live(m), hidden_grad, 0.0).astype(BF16)
            mixed_grad = dot_lanes(branch_grad, out_matrix).astype(BF16)
            grad_sent[m] = mixed_grad
            mixed_first.append(send(grad_sent.at[m, :, other], mixed_got.at[m], y_peer))
            branch_all[m] = branch_grad
        for m in range(micro):
            hidden_first.append(send(hidden_all.at[m, 0], hidden_all.at[m, 1], y_peer))

        out_low[...] = (
            dot_rows(
                mixed[...].reshape(micro * rows_dev, width),
                branch_all[...].reshape(micro * rows_dev, width),
            )
            .astype(BF16)
            .reshape(out_low.shape)
        )

        indices = {"core": low, "x": high, "y": ctx, "zl": exp % 2, "zh": exp // 2}
        peers = {"core": core_peer, "x": x_peer, "y": y_peer, "zl": z_peers[1], "zh": z_peers[2]}

        def finish_qkv(place):
            def store(kept, arrived):
                place[:, mine] = kept
                place[:, other] = arrived

            return store

        def finish_out(start):
            def store(kept, arrived):
                out_out[:, start : start + own_width] = kept + arrived

            return store

        def finish_small(kept, arrived):
            small_out[...] = kept + arrived

        chunks = []
        at = 0
        for i, order in enumerate(ORDERS):
            bufs = chunk_bufs[at : at + 9]
            at += 9
            if i < 3:
                source, start = qkv_total, i * own_width
                finish = finish_qkv((query_out, key_out, value_out)[i])
            elif i < 5:
                source, start = out_low, (i - 3) * own_width
                finish = finish_out(start)
            else:
                source, start, finish = small_low, 0, finish_small
            size = bufs[0].shape[-1]
            chunks.append(
                Reduce(wires, source, slice(start, start + size), order, bufs, peers, indices, finish)
            )
        chunks[3].begin()
        chunks[4].begin()

        scale = head_size ** (-0.5)
        for m in range(micro):
            mixed_first[m].wait_recv()
            grad_own[...] = (
                dot_rows(plan.hot(m, 0), grad_sent[m, :, mine]) + dot_rows(plan.hot(m, 1), mixed_got[m])
            ).astype(BF16)
            length = length_ref[m]
            for head in range(heads):
                cols = [
                    slice(part * own_width + head * head_size, part * own_width + (head + 1) * head_size)
                    for part in range(3)
                ]
                query, key, value = (qkv_ref[m, :, part] for part in cols)
                grad = grad_own[:, cols[0]]
                scores = masked_scores(query, key, line_ref[head : head + 1, :], length, scale)
                probs = soft(scores)
                prob_grad = dot_lanes(grad, value)
                delta = jnp.sum(probs * prob_grad, axis=-1, keepdims=True)
                score_grad = (probs * (prob_grad - delta)).astype(BF16)
                diagonal = diagonal_sums(score_grad.astype(F32))
                if m:
                    diagonal = diagonal + diag_buf[0, head : head + 1, :]
                diag_buf[0, head : head + 1, :] = diagonal
                qkv_grad[m, :, cols[0]] = (
                    jnp.dot(score_grad, key, preferred_element_type=F32) * scale
                ).astype(BF16)
                qkv_grad[m, :, cols[1]] = (dot_rows(score_grad, query) * scale).astype(BF16)
                qkv_grad[m, :, cols[2]] = dot_rows(probs.astype(BF16), grad).astype(BF16)
                if head % 4 == 3:
                    for i in (3, 4):
                        chunks[i].advance()
        for i in range(3):
            cols = slice(i * own_width, (i + 1) * own_width)
            total = dot_rows(normed_ref[0], qkv_grad[0, :, cols]) + dot_rows(
                normed_ref[1], qkv_grad[1, :, cols]
            )
            qkv_total[:, :, :, cols] = total.astype(BF16).reshape(2, 2, width // 4, own_width)
            chunks[i].begin()

        diag_peers = [core_peer, x_peer, z_peers[1], z_peers[2], y_peer]
        diag_copies = []

        def diag_step(stage):
            if stage:
                diag_copies[stage - 1].wait_recv()
            if 0 < stage < 5:
                diag_buf[2 * stage] = diag_buf[2 * stage - 2] + diag_buf[2 * stage - 1]
            if stage < 5:
                diag_copies.append(
                    send(diag_buf.at[2 * stage], diag_buf.at[2 * stage + 1], diag_peers[stage])
                )

        diag_step(0)
        first_total = jnp.zeros((1, width), F32)
        first_first = []
        for m in range(micro):
            part = jnp.zeros((seq, width), F32)
            for i in range(3):
                cols = slice(i * own_width, (i + 1) * own_width)
                part = part + dot_lanes(
                    qkv_grad[m, :, cols], dense[:, :, :, :, :, cols].reshape(width, own_width)
                )
            rows = act_all[m].astype(F32)
            inverse = lax.rsqrt(jnp.mean(rows * rows, axis=-1, keepdims=True) + epsilon)
            first_total = first_total + jnp.sum(part * rows * inverse, axis=0, keepdims=True)
            first_own[...] = part
            first_sent[m] = first_own[plan.at(1), :].astype(BF16)
            first_got[m, 0] = first_own[here, :].astype(BF16)
            first_first.append(send(first_sent.at[m], first_got.at[m, 1], y_peer))
            chunks[m].advance()
            diag_step(1 + m)
        columns = jnp.where(
            lanes == experts,
            jnp.broadcast_to(second, (128, width)).T,
            jnp.where(
                lanes == experts + 1, jnp.broadcast_to(first_total, (128, width)).T, small_f[...]
            ),
        )
        small_low[...] = columns.astype(BF16).reshape(small_low.shape)
        chunks[5].begin()
        chunks[2].advance()
        chunks[0].advance()

        final_first = []
        for m in range(micro):
            for k in range(1, experts):
                ret_first["out", m, k].wait_recv()
            places = plan.places(m, rank_of[m], experts, slots)
            rows = ret_out[m].reshape(experts * slots, width)
            final = hidden_ref[m]
            for j in range(2):
                final = final + gate_of[m][j] * jnp.dot(places[j], rows, preferred_element_type=F32)
            final_all[m, 0] = final.astype(BF16)
            final_first.append(send(final_all.at[m, 0], final_all.at[m, 1], y_peer))
            if m == 0:
                chunks[1].advance()
                chunks[3].advance()
                diag_step(3)
        chunks[5].advance()
        chunks[2].advance()
        chunks[0].advance()
        chunks[4].advance()
        diag_step(4)
        chunks[1].advance()
        chunks[5].advance()

        for m in range(micro):
            hidden_first[m].wait_recv()
            first_first[m].wait_recv()
            first = first_got[m, 0].astype(F32) + first_got[m, 1].astype(F32)
            rows = act_ref[m].astype(F32)
            inverse = lax.rsqrt(jnp.mean(rows * rows, axis=-1, keepdims=True) + epsilon)
            lifted = gain_one * first
            mean_part = jnp.mean(lifted * rows, axis=-1, keepdims=True)
            back = inverse * lifted - rows * (inverse * inverse * inverse) * mean_part
            moved = sum(dot_rows(plan.hot_mine(m, k), hidden_all[m, k]) for k in range(2))
            grad_input_ref[m] = (moved + back).astype(BF16)
            if m == 0:
                chunks[0].advance()
                chunks[2].advance()
                chunks[1].advance()
        for m in range(micro):
            final_first[m].wait_recv()
            moved = sum(dot_rows(plan.hot_mine(m, k), final_all[m, k]) for k in range(2))
            output_ref[m] = moved.astype(BF16)
        busy = True
        while busy:
            busy = False
            for i in (0, 1, 2, 3, 4, 5):
                if chunks[i].step <= len(chunks[i].order):
                    chunks[i].advance()
                    busy = True
        diag_step(5)
        diag_out[ctx] = diag_buf[8]
        diag_out[1 - ctx] = diag_buf[9]
        for chunk in chunks:
            for copy in chunk.flying:
                copy.wait_send()
        for copy in drains[before_tokens:]:
            copy.wait_send()
        del drains[before_tokens:]

    rows_shape = (2, experts, micro, slots)
    half_ff = both_in.shape[-1] // 2
    pl.run_scoped(
        expert_phase,
        pltpu.VMEM(rows_shape + (2 * half_ff,), BF16),
        pltpu.VMEM(rows_shape + (width,), BF16),
        pltpu.VMEM(rows_shape + (width,), BF16),
        pltpu.VMEM(rows_shape + (half_ff,), BF16),
        pltpu.VMEM(rows_shape[1:] + (width,), BF16),
        pltpu.VMEM(rows_shape + (width,), BF16),
        pltpu.VMEM(rows_shape + (width,), BF16),
    )
    pl.run_scoped(
        token_phase,
        pltpu.VMEM(dense_in.shape, BF16),
        pltpu.VMEM(out_in.shape, BF16),
        pltpu.VMEM(act_in.shape, BF16),
        pltpu.VMEM(normed_in.shape, BF16),
        pltpu.VMEM(qkv_in.shape, BF16),
        pltpu.VMEM((seq, width), F32),
        pltpu.VMEM((seq, own_width), BF16),
        pltpu.VMEM((micro, seq, 3 * own_width), BF16),
        pltpu.VMEM((2, 2, width // 4, 3 * own_width), BF16),
        pltpu.VMEM((2, 2, width // 4, width), BF16),
        pltpu.VMEM((width, 128), F32),
        pltpu.VMEM((2, 2, width // 4, 128), BF16),
        pltpu.VMEM((micro, rows_dev, width), BF16),
    )
    for copy in bulk:
        copy.wait_recv()
    for i, (peer, is_away, _, _) in enumerate(down_sends):
        if peer is None:
            pl.when(at_home)(lambda: home_down().wait())
            continue
        pl.when(away if is_away else at_home)(lambda i=i: down_copy(i).wait_send())
    @pl.when(at_home)
    def _():
        for i in (2, 4 , 6):
            down_copy(i).wait_recv()

    @pl.when(away)
    def _():
        for i in (1, 3, 5, 7):
            down_copy(i).wait_recv()

    home_block().wait()
    for copy in drains:
        copy.wait_send()


def back(sizes, values, saved):
    heads, head_size, experts, capacity, slots = sizes
    hidden, lines = values[0], values[7]
    dense, gate_w, down_w = saved[0], saved[8], saved[9]
    micro, rows_dev, width = hidden.shape
    own_width = heads * head_size
    per_row = dense.shape[4]
    in_vmem, in_hbm = pl.BlockSpec(memory_space=pltpu.VMEM), pl.BlockSpec(memory_space=pltpu.HBM)
    smem = pl.BlockSpec(memory_space=pltpu.SMEM)
    outs = (
        [((micro, rows_dev, width), BF16)] * 2
        + [((per_row, width), F32)] * 4
        + [((per_row, 128), F32), ((2,) + lines.shape, F32)]
        + [((6,) + gate_w.shape[1:], BF16), (down_w.shape, BF16)]
    )
    rows = (micro, experts, slots, width)
    sent = (micro, experts - 1, slots, width)
    scratch = [
        pltpu.VMEM(gate_w.shape, BF16),
        pltpu.VMEM(down_w.shape, BF16),
        pltpu.VMEM((2,) + gate_w.shape[1:], BF16),
        pltpu.VMEM(rows, BF16),
        pltpu.VMEM(rows, BF16),
        pltpu.VMEM(sent, BF16),
        pltpu.VMEM(sent, BF16),
        pltpu.VMEM((micro, experts - 1, 8, 128), F32),
        pltpu.VMEM(rows, BF16),
        pltpu.VMEM(rows, BF16),
        pltpu.VMEM((micro, experts, 8, 128), F32),
        pltpu.VMEM((micro, 2, rows_dev, width), BF16),
        pltpu.VMEM((micro, 2, rows_dev, width), BF16),
        pltpu.VMEM((micro, rows_dev, own_width), BF16),
        pltpu.VMEM((micro, rows_dev, width), BF16),
        pltpu.VMEM((micro, rows_dev, width), BF16),
        pltpu.VMEM((micro, 2, rows_dev, width), BF16),
        pltpu.VMEM((10,) + lines.shape, F32),
    ]
    chunk_sizes = [own_width] * 5 + [128]
    for order, size in zip(ORDERS, chunk_sizes):
        scratch += reduce_buffers(order, width, per_row, size)
    scratch += [
        pltpu.SemaphoreType.DMA((160,)),
        pltpu.SemaphoreType.DMA((160,)),
        pltpu.SemaphoreType.DMA((24,)),
    ]
    return pl.pallas_call(
        functools.partial(back_kernel, sizes),
        out_shape=tuple(jax.ShapeDtypeStruct(*out) for out in outs),
        in_specs=[in_vmem] * 8 + [smem] + [in_hbm] * len(saved),
        out_specs=(in_vmem,) * 8 + (in_hbm,) * 2,
        scratch_shapes=scratch,
        compiler_params=pltpu.CompilerParams(
            collective_id=2, has_side_effects=True, vmem_limit_bytes=60 * 2**20
        ),
    )(*values, *saved)


def finish_kernel(
    experts,
    gate_in,
    down_in,
    output_in,
    grad_in,
    query_in,
    key_in,
    value_in,
    out_in,
    small_in,
    diag_in,
    lane_ref,
    gate_out,
    up_out,
    down_out,
    output_out,
    grad_out,
    query_out,
    key_out,
    value_out,
    out_out,
    router_out,
    first_out,
    second_out,
    table_out,
):
    low = lax.axis_index("dp") % 2
    half = gate_out.shape[1] // 2
    own = pl.ds(pl.multiple_of(low * half, half), half)
    other = pl.ds(pl.multiple_of((1 - low) * half, half), half)
    for cols, slots in ((own, (0, 2, 4)), (other, (1, 3, 5))):
        gate_out[:, cols] = sum(gate_in[j, :, :half].astype(F32) for j in slots)
        up_out[:, cols] = sum(gate_in[j, :, half:].astype(F32) for j in slots)
    down_out[...] = sum(down_in[j].astype(F32) for j in range(down_in.shape[0]))

    @pl.when(pl.program_id(0) == 0)
    def _():
        for source, place in (
            (output_in, output_out),
            (grad_in, grad_out),
            (query_in, query_out),
            (key_in, key_out),
            (value_in, value_out),
            (out_in, out_out),
        ):
            place[...] = source[...]
        small = small_in[...]
        router_out[...] = small[:, :experts]
        turned = jnp.concatenate([small] * (128 // small.shape[0]), axis=0).T
        second_out[...] = turned[experts : experts + 1, : small.shape[0]]
        first_out[...] = turned[experts + 1 : experts + 2, : small.shape[0]]
        buckets, lanes = table_out.shape[0], lane_ref.shape[1]
        rows = lax.broadcasted_iota(jnp.int32, (buckets, lanes), 0)
        hot = jnp.where(rows == lane_ref[...], 1.0, 0.0)
        heads = diag_in.shape[0] * diag_in.shape[1]
        table_out[...] = lax.dot_general(
            hot,
            diag_in[...].reshape(heads, lanes),
            (((1,), (1,)), ((), ())),
            precision=lax.Precision.HIGHEST,
            preferred_element_type=F32,
        )


def finish(values, bucket_lanes, experts, table_shape):
    gate_in, down_in, output, grad_input, query, key, value, out, small, diag = values
    steps = 2
    rows, ff = gate_in.shape[1:]
    per_row = small.shape[0]
    fixed = lambda v: pl.BlockSpec(v.shape, lambda i: (0,) * len(v.shape))
    cut = lambda v: pl.BlockSpec(
        (v.shape[0], v.shape[1] // steps, v.shape[2]), lambda i: (0, i, 0)
    )
    outs = [
        jax.ShapeDtypeStruct((rows, ff), F32),
        jax.ShapeDtypeStruct((rows, ff), F32),
        jax.ShapeDtypeStruct(down_in.shape[1:], F32),
    ] + [jax.ShapeDtypeStruct(v.shape, v.dtype) for v in (output, grad_input, query, key, value, out)]
    small_outs = [
        jax.ShapeDtypeStruct((per_row, experts), F32),
        jax.ShapeDtypeStruct((1, per_row), F32),
        jax.ShapeDtypeStruct((1, per_row), F32),
        jax.ShapeDtypeStruct(table_shape, F32),
    ]
    sliced = lambda v: pl.BlockSpec((v.shape[0] // steps, v.shape[1]), lambda i: (i, 0))
    return pl.pallas_call(
        functools.partial(finish_kernel, experts),
        grid=(steps,),
        out_shape=tuple(outs + small_outs),
        in_specs=[cut(gate_in), cut(down_in)] + [fixed(v) for v in values[2:]] + [fixed(bucket_lanes)],
        out_specs=tuple([sliced(v) for v in outs[:3]] + [fixed(v) for v in outs[3:] + small_outs]),
        compiler_params=pltpu.CompilerParams(vmem_limit_bytes=60 * 2**20),
    )(*values, bucket_lanes)


def tuned_body(
    activations,
    cotangent,
    dealing,
    lengths,
    routes,
    buckets,
    w_query,
    w_key,
    w_value,
    w_out,
    w_router,
    norm_first,
    norm_second,
    bias_table,
    w_gate,
    w_up,
    w_down,
):
    micro, _, rows_dev, width = activations.shape
    seq = dealing.shape[2]
    bucket_count, head_count = bias_table.shape
    dp_count, ctx_count, expert_count = (lax.axis_size(name) for name in ALL)
    dp_index, ctx_index, expert_index = (lax.axis_index(name) for name in ALL)
    high, low = dp_index // 2, dp_index % 2
    heads = head_count // ctx_count
    head_size = width // head_count
    own_width = heads * head_size
    experts = w_router.shape[1]
    top_count = routes.shape[3]
    capacity = (5 * rows_dev * top_count + 4 * experts - 1) // (4 * experts)
    slots = -(-capacity // 16) * 16
    half_ff = w_gate.shape[2] // 2
    down_rows = w_down.shape[1]
    plane = dp_count * ctx_count
    plane_index = dp_index * ctx_count + ctx_index
    act = activations[:, 0]
    cot = cotangent[:, 0]
    deal = dealing[:, 0]
    length = lengths[:, 0]
    route = routes[:, 0]
    sizes = (heads, head_size, experts, capacity, slots)
    extras = jnp.concatenate([w_router, norm_first[:, None], norm_second[:, None]], axis=1)
    extras = jnp.pad(extras, ((0, 0), (0, 128 - extras.shape[1])))
    bucket_hot = (buckets[:, None] == jnp.arange(bucket_count)[None, :]).astype(BF16)
    own_table = lax.dynamic_slice_in_dim(bias_table, ctx_index * heads, heads, axis=1)
    lookup = dot_f32("sb,bh->hs", bucket_hot, own_table)
    lines = jnp.concatenate(
        [lookup[:, :1], jnp.zeros((heads, seq), F32), lookup[:, :0:-1]], axis=1
    )
    hidden, logits, mixed, cot_low, *saved = front(
        sizes,
        act,
        cot,
        deal,
        length,
        route,
        lines,
        (w_query, w_key, w_value, w_out),
        extras,
        w_gate[0],
        w_up[0],
        w_down[0],
    )
    (
        output,
        grad_input,
        grad_query,
        grad_key,
        grad_value,
        grad_out,
        small_sum,
        diag_all,
        gate_in,
        down_in,
    ) = back(
        sizes,
        (hidden, logits, mixed, cot_low, act, deal[:, :, None], route, lines, length),
        saved,
    )
    bucket_lanes = jnp.concatenate(
        [buckets[:1], jnp.full((seq,), -1, jnp.int32), buckets[:0:-1]]
    )[None, :]
    (
        grad_gate,
        grad_up,
        grad_down,
        output,
        grad_input,
        grad_query,
        grad_key,
        grad_value,
        grad_out,
        grad_router,
        grad_first,
        grad_second,
        grad_table,
    ) = finish(
        (
            gate_in,
            down_in,
            output,
            grad_input,
            grad_query,
            grad_key,
            grad_value,
            grad_out,
            small_sum,
            diag_all,
        ),
        bucket_lanes,
        experts,
        bias_table.shape,
    )
    return (
        output[:, None],
        grad_input[:, None],
        grad_query,
        grad_key,
        grad_value,
        grad_out,
        grad_router,
        grad_first[0],
        grad_second[0],
        grad_table,
        grad_gate[None],
        grad_up[None],
        grad_down[None],
    )


def body(*arguments):
    counts = tuple(lax.axis_size(name) for name in ALL)
    activations, w_query, bias_table, w_gate = (arguments[i] for i in (0, 6, 13, 14))
    own_width = activations.shape[3] // counts[1]
    fits = (
        counts == (4, 2, 4)
        and w_gate.shape[0] == 1
        and w_query.shape[0] % 16 == 0
        and 128 % w_query.shape[0] == 0
        and own_width % 128 == 0
        and bias_table.shape[1] % counts[1] == 0
        and arguments[4].shape[3] == 2
    )
    return (tuned_body if fits else plain_body)(*arguments)


def solution(mesh):
    tokens = P(None, ("dp", "experts"), "context", None)
    sequences = P(None, ("dp", "experts"))
    rows = P(("dp", "context", "experts"), None)
    gains = P(("dp", "context", "experts"))
    experts = P("experts", ("dp", "context"), None)
    placed = (
        (tokens, tokens, P(None, ("dp", "experts"), None), sequences, tokens, P())
        + (rows,) * 5
        + (gains, gains, P())
        + (experts,) * 3
    )
    return jax.shard_map(
        body,
        mesh=mesh,
        in_specs=placed,
        out_specs=(tokens, tokens) + (rows,) * 5 + (gains, gains, P()) + (experts,) * 3,
        check_vma=False,
    )
```

```python
import functools

import jax
import jax.numpy as jnp
from jax import lax
from jax.experimental import pallas as pl
from jax.experimental.pallas import tpu as pltpu
from jax.sharding import PartitionSpec as P

epsilon = 1e-06
masked_score = -1e30
ALL = ("dp", "context", "experts")
F32 = jnp.float32
BF16 = jnp.bfloat16


def dot_f32(spec, left, right):
    return jnp.einsum(spec, left, right, preferred_element_type=F32)


def swap(value, axis, offset):
    size = lax.axis_size(axis)
    return lax.ppermute(value, axis, [(i, i ^ offset) for i in range(size)])


def reorder(pieces, index):
    pieces = list(pieces)
    bit = 1
    while bit < len(pieces):
        flag = (index // bit) % 2 == 1
        pieces = [jnp.where(flag, pieces[j ^ bit], pieces[j]) for j in range(len(pieces))]
        bit *= 2
    return pieces


def reorder_lanes(value, blocks, index):
    return jnp.concatenate(reorder(jnp.split(value, blocks, axis=-1), index), axis=-1)


def toeplitz_bias(line, size):
    rows = jnp.broadcast_to(line, (size, 2 * size))
    return pltpu.roll(rows, 0, 1, stride=1, stride_axis=0)[:, :size]


def masked_scores(query, key, line, length, scale):
    size = query.shape[0]
    scores = lax.dot_general(query, key, (((1,), (1,)), ((), ())), preferred_element_type=F32)
    scores = scores * scale + toeplitz_bias(line, size)
    row_id = lax.broadcasted_iota(jnp.int32, (size, size), 0)
    col_id = lax.broadcasted_iota(jnp.int32, (size, size), 1)
    allowed = (row_id >= col_id) & (col_id < length)
    return jnp.where(allowed, scores, masked_score)


def soft(scores):
    top_score = jnp.max(scores, axis=-1, keepdims=True)
    raised = jnp.exp(scores - top_score)
    return raised / jnp.sum(raised, axis=-1, keepdims=True)


def attend_kernel(heads, head_size, length_ref, line_ref, qkv_ref, mixed_ref):
    scale = head_size ** (-0.5)
    width = heads * head_size
    length = length_ref[pl.program_id(0)]
    for head in range(heads):
        query = qkv_ref[0, :, head * head_size : (head + 1) * head_size]
        key = qkv_ref[0, :, width + head * head_size : width + (head + 1) * head_size]
        value = qkv_ref[0, :, 2 * width + head * head_size : 2 * width + (head + 1) * head_size]
        scores = masked_scores(query, key, line_ref[head : head + 1, :], length, scale)
        probs = soft(scores).astype(BF16)
        mixed = jnp.dot(probs, value, preferred_element_type=F32)
        mixed_ref[0, :, head * head_size : (head + 1) * head_size] = mixed.astype(BF16)


def attend(qkv, lines, lengths, heads):
    micro, seq, width = qkv.shape
    width = width // 3
    head_size = width // heads
    return pl.pallas_call(
        functools.partial(attend_kernel, heads, head_size),
        grid=(micro,),
        out_shape=jax.ShapeDtypeStruct((micro, seq, width), BF16),
        in_specs=[
            pl.BlockSpec(memory_space=pltpu.SMEM),
            pl.BlockSpec(lines.shape, lambda i: (0, 0)),
            pl.BlockSpec((1, seq, 3 * width), lambda i: (i, 0, 0)),
        ],
        out_specs=pl.BlockSpec((1, seq, width), lambda i: (i, 0, 0)),
        compiler_params=pltpu.CompilerParams(vmem_limit_bytes=32 * 2**20),
    )(lengths, lines, qkv)


def diagonal_sums(grad):
    size = grad.shape[0]
    wide = jnp.concatenate([grad, jnp.zeros_like(grad)], axis=1)
    rows = size
    while rows > 1:
        rows //= 2
        lower = pltpu.roll(wide[rows:], 2 * size - rows, 1)
        wide = wide[:rows] + lower
    return wide


def attend_back_kernel(
    heads, head_size, length_ref, line_ref, qkv_ref, grad_ref, out_ref, diag_ref
):
    scale = head_size ** (-0.5)
    width = heads * head_size
    length = length_ref[pl.program_id(0)]

    @pl.when(pl.program_id(0) == 0)
    def _():
        diag_ref[...] = jnp.zeros_like(diag_ref)

    for head in range(heads):
        at = [
            slice(part * width + head * head_size, part * width + (head + 1) * head_size)
            for part in range(3)
        ]
        query, key, value = (qkv_ref[0, :, part] for part in at)
        grad = grad_ref[0, :, at[0]]
        scores = masked_scores(query, key, line_ref[head : head + 1, :], length, scale)
        probs = soft(scores)
        prob_grad = lax.dot_general(
            grad, value, (((1,), (1,)), ((), ())), preferred_element_type=F32
        )
        delta = jnp.sum(probs * prob_grad, axis=-1, keepdims=True)
        score_grad = (probs * (prob_grad - delta)).astype(BF16)
        diag_ref[head : head + 1, :] += diagonal_sums(score_grad.astype(F32))
        query_grad = jnp.dot(score_grad, key, preferred_element_type=F32) * scale
        key_grad = (
            lax.dot_general(
                score_grad, query, (((0,), (0,)), ((), ())), preferred_element_type=F32
            )
            * scale
        )
        value_grad = lax.dot_general(
            probs.astype(BF16), grad, (((0,), (0,)), ((), ())), preferred_element_type=F32
        )
        out_ref[0, :, at[0]] = query_grad.astype(BF16)
        out_ref[0, :, at[1]] = key_grad.astype(BF16)
        out_ref[0, :, at[2]] = value_grad.astype(BF16)


def attend_back(qkv, grad, lines, lengths, heads):
    micro, seq, width = grad.shape
    head_size = width // heads
    return pl.pallas_call(
        functools.partial(attend_back_kernel, heads, head_size),
        grid=(micro,),
        out_shape=(
            jax.ShapeDtypeStruct(qkv.shape, BF16),
            jax.ShapeDtypeStruct(lines.shape, F32),
        ),
        in_specs=[
            pl.BlockSpec(memory_space=pltpu.SMEM),
            pl.BlockSpec(lines.shape, lambda i: (0, 0)),
            pl.BlockSpec((1, seq, 3 * width), lambda i: (i, 0, 0)),
            pl.BlockSpec((1, seq, width), lambda i: (i, 0, 0)),
        ],
        out_specs=(
            pl.BlockSpec((1, seq, 3 * width), lambda i: (i, 0, 0)),
            pl.BlockSpec(lines.shape, lambda i: (0, 0)),
        ),
        compiler_params=pltpu.CompilerParams(vmem_limit_bytes=32 * 2**20),
    )(lengths, lines, qkv, grad)


def halve(value, axis, bit, flag):
    kept = jnp.where(flag, value[1], value[0])
    sent = jnp.where(flag, value[0], value[1]).astype(BF16)
    return kept + swap(sent, axis, bit).astype(F32)


def scatter_sum(value, dp_index, expert_index):
    dp_count, ctx_count, expert_count = value.shape[:3]
    rest = value.shape[3:]
    count, bit = dp_count, 1
    while count > 1:
        shaped = value.reshape((count // 2, 2, -1))
        value = halve(jnp.moveaxis(shaped, 1, 0), "dp", bit, (dp_index // bit) % 2 == 1)
        count //= 2
        bit *= 2
    value = value.reshape((ctx_count, expert_count) + rest)
    count, bit = expert_count, 1
    while count > 1:
        shaped = value.reshape((ctx_count, count // 2, 2) + rest)
        value = halve(jnp.moveaxis(shaped, 2, 0), "experts", bit, (expert_index // bit) % 2 == 1)
        count //= 2
        bit *= 2
    return value.reshape((ctx_count,) + rest)


MESH = pl.DeviceIdType.MESH


def flip(index, bit):
    return index + bit - 2 * bit * ((index // bit) % 2)


def greet(targets):
    barrier = pltpu.get_barrier_semaphore()
    for target in targets:
        pl.semaphore_signal(barrier, inc=1, device_id=target, device_id_type=MESH)
    pl.semaphore_wait(barrier, len(targets))


def remote(source, place, sends, receives, target):
    return pltpu.make_async_remote_copy(
        src_ref=source,
        dst_ref=place,
        send_sem=sends,
        recv_sem=receives,
        device_id=target,
        device_id_type=MESH,
    )


def plain_sums(qkv_total, out_total, router_total, first_total, second_total, own_width):
    width, experts = router_total.shape
    dp_count, ctx_count, expert_count = (lax.axis_size(name) for name in ALL)
    dp_index, ctx_index, expert_index = (lax.axis_index(name) for name in ALL)
    owners = (dp_count, ctx_count, expert_count, -1)
    out_pack = jnp.concatenate([out_total, router_total, second_total[:, None]], axis=1)
    out_pack = jnp.pad(out_pack, ((0, 0), (0, width + 128 - out_pack.shape[1])))
    out_pack = scatter_sum(
        out_pack.reshape(owners + (out_pack.shape[1],)), dp_index, expert_index
    )
    qkv_pack = jnp.pad(
        jnp.concatenate([qkv_total, first_total[:, None]], axis=1), ((0, 0), (0, 127))
    )
    qkv_pack = scatter_sum(
        qkv_pack.reshape(owners + (qkv_pack.shape[1],)), dp_index, expert_index
    )

    def across(value):
        parts = reorder([value[c] for c in range(ctx_count)], ctx_index)
        return [parts[0]] + [
            swap(parts[k].astype(BF16), "context", k).astype(F32) for k in range(1, ctx_count)
        ]

    out_sum = sum(across(out_pack))
    qkv_parts = across(qkv_pack)
    grad_first = sum(part[:, 3 * own_width] for part in qkv_parts)
    qkv_parts = reorder(qkv_parts, ctx_index)
    grads = tuple(
        jnp.concatenate(
            [part[:, i * own_width : (i + 1) * own_width] for part in qkv_parts], axis=1
        )
        for i in range(3)
    )
    return grads + (
        out_sum[:, :width],
        out_sum[:, width : width + experts],
        grad_first,
        out_sum[:, width + experts],
    )


def norm_pull(features, inverse, gain, grad):
    lifted = gain * grad
    mean_part = jnp.mean(lifted * features, axis=-1, keepdims=True)
    back = inverse * lifted - features * (inverse * inverse * inverse) * mean_part
    gain_grad = jnp.sum(grad * features * inverse, axis=(0, 1))
    return back, gain_grad


def gelu_parts(pre):
    root = 0.7978845608028654
    cubic = 0.044715
    square = pre * pre
    wave = jnp.tanh(root * (pre + cubic * pre * square))
    value = 0.5 * pre * (1.0 + wave)
    slope = 0.5 * (1.0 + wave) + 0.5 * pre * (1.0 - wave * wave) * root * (
        1.0 + 3.0 * cubic * square
    )
    return value, slope


def down_routes(dp_count, ctx_count, expert_count, core, ctx_offset):
    pairs = []
    for dp in range(dp_count):
        for ctx in range(ctx_count):
            for expert in range(expert_count):
                high, low = dp // 2, dp % 2
                to_high = high if low == core else high ^ 1
                target = ((to_high * 2 + high) * ctx_count + (ctx ^ ctx_offset)) * expert_count
                pairs.append(((dp * ctx_count + ctx) * expert_count + expert, target + expert))
    return pairs


def plain_body(
    activations,
    cotangent,
    dealing,
    lengths,
    routes,
    buckets,
    w_query,
    w_key,
    w_value,
    w_out,
    w_router,
    norm_first,
    norm_second,
    bias_table,
    w_gate,
    w_up,
    w_down,
):
    micro, _, rows_dev, width = activations.shape
    seq = dealing.shape[2]
    bucket_count, head_count = bias_table.shape
    dp_count, ctx_count, expert_count = (lax.axis_size(name) for name in ALL)
    dp_index, ctx_index, expert_index = (lax.axis_index(name) for name in ALL)
    high, low = dp_index // 2, dp_index % 2
    heads = head_count // ctx_count
    head_size = width // head_count
    own_width = heads * head_size
    experts = w_router.shape[1]
    top_count = routes.shape[3]
    capacity = (5 * rows_dev * top_count + 4 * experts - 1) // (4 * experts)
    slots = -(-capacity // 16) * 16
    ff = w_gate.shape[2]
    half_ff = ff // 2
    weight_rows = w_query.shape[0]
    plane = dp_count * ctx_count
    plane_index = dp_index * ctx_count + ctx_index
    act = activations[:, 0]
    cot = cotangent[:, 0]
    deal = dealing[:, 0]
    length = lengths[:, 0]
    route = routes[:, 0]

    extras = jnp.concatenate(
        [w_router, norm_first[:, None], norm_second[:, None]], axis=1
    )
    extras = jnp.pad(extras, ((0, 0), (0, 128 - extras.shape[1])))
    column_parts = [
        jnp.split(weight, ctx_count, axis=1) for weight in (w_query, w_key, w_value)
    ]
    packs = [
        jnp.concatenate([part[c] for part in column_parts] + [extras], axis=1)
        for c in range(ctx_count)
    ]
    packs = reorder(packs, ctx_index)
    packs = [packs[0]] + [swap(packs[k], "context", k) for k in range(1, ctx_count)]
    packs = jnp.stack(reorder(packs, ctx_index))
    dense = lax.all_gather(packs, ("dp", "experts"), axis=0, tiled=False)
    dense = dense.reshape((dp_count, expert_count) + packs.shape)
    dense = jnp.transpose(dense, (0, 2, 1, 3, 4)).reshape(width, -1)
    qkv_w = dense[:, : 3 * own_width]
    router_w = dense[:, 3 * own_width : 3 * own_width + experts]
    gain_one = dense[:, 3 * own_width + experts].astype(F32)
    gain_two = dense[:, 3 * own_width + experts + 1].astype(F32)
    out_w = lax.all_gather(w_out, ALL, axis=0, tiled=True)

    gate_up = [
        jnp.concatenate([w_gate[0, :, h * half_ff : (h + 1) * half_ff], w_up[0, :, h * half_ff : (h + 1) * half_ff]], axis=1)
        for h in range(2)
    ]
    halves = reorder(gate_up, low)
    gate_blocks = []
    for j in range(plane):
        dp_offset, ctx_offset = j // ctx_count, j % ctx_count
        piece = halves[dp_offset % 2]
        if dp_offset:
            piece = swap(piece, "dp", dp_offset)
        if ctx_offset:
            piece = swap(piece, "context", ctx_offset) if not dp_offset else piece
        gate_blocks.append(piece)
    for j in range(plane):
        dp_offset, ctx_offset = j // ctx_count, j % ctx_count
        if dp_offset and ctx_offset:
            gate_blocks[j] = swap(gate_blocks[dp_offset * ctx_count], "context", ctx_offset)
    gate_up_w = jnp.concatenate(gate_blocks, axis=0)
    down_w = jnp.zeros((half_ff, width), BF16)
    down_rows = w_down.shape[1]
    for ctx_offset in range(ctx_count):
        for core in range(2):
            pairs = down_routes(dp_count, ctx_count, expert_count, core, ctx_offset)
            piece = lax.ppermute(w_down[0], ALL, pairs)
            from_core = jnp.where(low == high, core, 1 - core)
            place = (from_core * ctx_count + (ctx_index ^ ctx_offset)) * down_rows
            down_w = lax.dynamic_update_slice(down_w, piece, (place, 0))

    act_all = jnp.concatenate(
        reorder([act] + [swap(act, "context", k) for k in range(1, ctx_count)], ctx_index), axis=1
    )
    cot_all = jnp.concatenate(
        reorder([cot] + [swap(cot, "context", k) for k in range(1, ctx_count)], ctx_index), axis=1
    )
    position_ids = jnp.arange(seq, dtype=jnp.int32)
    slot_blocks = [
        lax.dynamic_slice_in_dim(deal, (ctx_index ^ k) * rows_dev, rows_dev, axis=1)
        for k in range(ctx_count)
    ]
    hot = [
        (block[:, :, None] == position_ids[None, None, :]).astype(BF16) for block in slot_blocks
    ]
    my_positions = ctx_index * rows_dev + jnp.arange(rows_dev, dtype=jnp.int32)
    hot_mine = [
        (block[:, :, None] == my_positions[None, None, :]).astype(BF16) for block in slot_blocks
    ]
    live = slot_blocks[0] < length[:, None]
    live_rows = live.astype(F32)[:, :, None]
    bucket_hot = (buckets[:, None] == jnp.arange(bucket_count)[None, :]).astype(BF16)
    own_table = lax.dynamic_slice_in_dim(bias_table, ctx_index * heads, heads, axis=1)
    lookup = dot_f32("sb,bh->hs", bucket_hot, own_table)
    lines = jnp.concatenate(
        [lookup[:, :1], jnp.zeros((heads, seq), F32), lookup[:, :0:-1]], axis=1
    )

    rows_all = act_all.astype(F32)
    inverse_one = lax.rsqrt(jnp.mean(rows_all * rows_all, axis=-1, keepdims=True) + epsilon)
    normed = (rows_all * inverse_one * gain_one).astype(BF16)
    qkv = dot_f32("mpd,dw->mpw", normed, qkv_w).astype(BF16)
    mixed_own = attend(qkv, lines, length, heads)
    mixed_parts = [
        dot_f32("msp,mpw->msw", hot[k], mixed_own).astype(BF16) for k in range(ctx_count)
    ]
    mixed_parts = [mixed_parts[0]] + [
        swap(mixed_parts[k], "context", k) for k in range(1, ctx_count)
    ]
    mixed = jnp.concatenate(reorder(mixed_parts, ctx_index), axis=-1)

    rows_in = dot_f32("msp,mpd->msd", hot[0], act_all)
    cot_rows = dot_f32("msp,mpd->msd", hot[0], cot_all)
    branch = dot_f32("msi,io->mso", mixed, out_w)
    hidden = rows_in + branch * live_rows
    inverse_two = lax.rsqrt(jnp.mean(hidden * hidden, axis=-1, keepdims=True) + epsilon)
    normed_two = (hidden * inverse_two * gain_two).astype(BF16)
    logits = dot_f32("msd,de->mse", normed_two, router_w)
    route_hot = (route[..., None] == jnp.arange(experts)).astype(F32)
    chosen = jnp.sum(route_hot * logits[:, :, None, :], axis=3)
    gate_probs = jax.nn.softmax(chosen, axis=-1)

    flat_hot = (route_hot * live_rows[..., None]).reshape(micro, rows_dev * top_count, experts)
    pair_ids = jnp.arange(rows_dev * top_count)
    before = (pair_ids[:, None] > pair_ids[None, :]).astype(BF16)
    earlier = dot_f32("ab,mbe->mae", before, flat_hot.astype(BF16))
    rank = jnp.sum(earlier * flat_hot, axis=2).astype(jnp.int32).reshape(route.shape)
    kept = live[:, :, None] & (rank < capacity)
    target = jnp.where(kept, (route ^ expert_index) * slots + rank, -1)
    place_ids = jnp.arange(experts * slots, dtype=jnp.int32)
    pick = [
        (target[:, None, :, j] == place_ids[None, :, None]) for j in range(top_count)
    ]
    pick_any = functools.reduce(jnp.logical_or, pick).astype(BF16)
    pick_bf = [p.astype(BF16) for p in pick]
    prob_rows = sum(
        jnp.sum(jnp.where(pick[j], gate_probs[:, None, :, j], 0.0), axis=2)
        for j in range(top_count)
    )

    def by_expert(value):
        shaped = value.reshape((micro, experts, slots) + value.shape[2:])
        return jnp.moveaxis(shaped, 1, 0)

    def exchange(value):
        parts = [value[0]] + [swap(value[k], "experts", k) for k in range(1, expert_count)]
        return jnp.stack(parts)

    normed_rel = reorder_lanes(normed_two, plane, plane_index)
    sent_rows = by_expert(dot_f32("mrs,msd->mrd", pick_any, normed_rel).astype(BF16))
    sent_up = by_expert(
        dot_f32("mrs,msd->mrd", pick_any, cot_rows.astype(BF16)).astype(BF16)
    )
    row_count = expert_count * micro * slots
    own_x = exchange(sent_rows).reshape(row_count, width)
    own_u = exchange(sent_up).reshape(row_count, width)
    own_p = exchange(by_expert(prob_rows)).reshape(row_count, 1)
    own_g = (own_p * own_u.astype(F32)).astype(BF16)

    def core_swap(value):
        blocks = jnp.split(value, plane, axis=-1)
        return jnp.concatenate([blocks[j ^ ctx_count] for j in range(plane)], axis=-1)

    all_x = jnp.concatenate([own_x, core_swap(swap(own_x, "dp", 1))], axis=0)
    all_g = jnp.concatenate([own_g, swap(own_g, "dp", 1)], axis=0)

    pre_up = dot_f32("rd,df->rf", all_x, gate_up_w)
    gelu_value, gelu_slope = gelu_parts(pre_up[:, :half_ff])
    up_part = pre_up[:, half_ff:]
    activated = (gelu_value * up_part).astype(BF16)
    act_grad = dot_f32("rd,fd->rf", all_g, down_w)
    pre_grad = (act_grad * up_part * gelu_slope).astype(BF16)
    up_grad = (act_grad * gelu_value).astype(BF16)
    both_grad = jnp.concatenate([pre_grad, up_grad], axis=1)
    back_part = dot_f32("rf,df->rd", both_grad, gate_up_w)
    out_part = dot_f32("rf,fd->rd", activated, down_w)
    out_own = (
        out_part[:row_count] + swap(out_part[row_count:].astype(BF16), "dp", 1).astype(F32)
    ).astype(BF16)
    back_own = (
        back_part[:row_count]
        + swap(core_swap(back_part[row_count:].astype(BF16)), "dp", 1).astype(F32)
    ).astype(BF16)
    gate_rows = jnp.sum(own_u.astype(F32) * out_own.astype(F32), axis=-1)

    def to_source(value):
        parts = value.reshape((expert_count, micro, slots) + value.shape[1:])
        parts = exchange(parts)
        return jnp.moveaxis(parts, 0, 1).reshape((micro, experts * slots) + value.shape[1:])

    back_rows = to_source(back_own)
    gate_back = to_source(gate_rows)
    out_rows = to_source(out_own)

    gate_up_total = dot_f32("rd,rf->df", all_x, both_grad)
    down_total = dot_f32("rf,rd->fd", activated, all_g)

    gate_up_sums = [0.0, 0.0]
    for j in range(plane):
        dp_offset, ctx_offset = j // ctx_count, j % ctx_count
        block = gate_up_total[j * (width // plane) : (j + 1) * (width // plane)].astype(BF16)
        pairs = [
            (
                (d * ctx_count + c) * expert_count + e,
                ((d ^ dp_offset) * ctx_count + (c ^ ctx_offset)) * expert_count + e,
            )
            for d in range(dp_count)
            for c in range(ctx_count)
            for e in range(expert_count)
        ]
        if j:
            block = lax.ppermute(block, ALL, pairs)
        gate_up_sums[dp_offset % 2] = gate_up_sums[dp_offset % 2] + block.astype(F32)
    first_half, second_half = reorder(gate_up_sums, low)
    grad_gate = jnp.concatenate([first_half[:, :half_ff], second_half[:, :half_ff]], axis=1)
    grad_up = jnp.concatenate([first_half[:, half_ff:], second_half[:, half_ff:]], axis=1)
    grad_down = 0.0
    for ctx_offset in range(ctx_count):
        for core in range(2):
            pairs = down_routes(dp_count, ctx_count, expert_count, core, ctx_offset)
            from_core = jnp.where(low == high, core, 1 - core)
            place = (from_core * ctx_count + (ctx_index ^ ctx_offset)) * down_rows
            piece = lax.dynamic_slice_in_dim(down_total, place, down_rows, axis=0).astype(BF16)
            arrived = lax.ppermute(piece, ALL, [(b, a) for a, b in pairs])
            grad_down = grad_down + arrived.astype(F32)

    pair_out = [dot_f32("mrs,mrd->msd", pick_bf[j], out_rows) for j in range(top_count)]
    final = hidden + sum(gate_probs[:, :, j, None] * pair_out[j] for j in range(top_count))
    final = final.astype(BF16)
    gate_grad = jnp.stack(
        [
            jnp.sum(jnp.where(pick[j], gate_back[:, :, None], 0.0), axis=1)
            for j in range(top_count)
        ],
        axis=-1,
    )
    chosen_grad = gate_probs * (
        gate_grad - jnp.sum(gate_probs * gate_grad, axis=-1, keepdims=True)
    )
    logit_grad = jnp.sum(route_hot * chosen_grad[..., None], axis=2).astype(BF16)
    normed_grad = reorder_lanes(
        dot_f32("mrs,mrd->msd", pick_any, back_rows), plane, plane_index
    ) + dot_f32("mse,de->msd", logit_grad, router_w)
    router_total = dot_f32("msd,mse->de", normed_two, logit_grad)
    hidden_norm_grad, second_total = norm_pull(hidden, inverse_two, gain_two, normed_grad)
    hidden_grad = cot_rows + hidden_norm_grad
    branch_grad = (hidden_grad * live_rows).astype(BF16)
    hidden_low = hidden_grad.astype(BF16)
    out_total = dot_f32("msi,mso->io", mixed, branch_grad)
    mixed_grad = dot_f32("mso,io->msi", branch_grad, out_w).astype(BF16)
    grad_parts = reorder(jnp.split(mixed_grad, ctx_count, axis=-1), ctx_index)
    grad_parts = [grad_parts[0]] + [
        swap(grad_parts[k], "context", k) for k in range(1, ctx_count)
    ]
    mixed_back = sum(
        dot_f32("msp,msw->mpw", hot[k], grad_parts[k]) for k in range(ctx_count)
    ).astype(BF16)
    qkv_grad, diagonals = attend_back(qkv, mixed_back, lines, length, heads)
    qkv_total = dot_f32("mpd,mpw->dw", normed, qkv_grad)
    first_part = dot_f32("mpw,dw->mpd", qkv_grad, qkv_w)
    first_total = jnp.sum(first_part * rows_all * inverse_one, axis=(0, 1))
    blocks = [
        lax.dynamic_slice_in_dim(first_part, (ctx_index ^ k) * rows_dev, rows_dev, axis=1)
        for k in range(ctx_count)
    ]
    first_grad = blocks[0] + sum(
        swap(blocks[k].astype(BF16), "context", k).astype(F32) for k in range(1, ctx_count)
    )

    def to_positions(value):
        parts = [value] + [swap(value, "context", k) for k in range(1, ctx_count)]
        return sum(dot_f32("msp,msd->mpd", hot_mine[k], parts[k]) for k in range(ctx_count))

    rows_mine = act.astype(F32)
    inverse_mine = lax.rsqrt(jnp.mean(rows_mine * rows_mine, axis=-1, keepdims=True) + epsilon)
    rows_back, _ = norm_pull(rows_mine, inverse_mine, gain_one, first_grad)
    grad_input = (to_positions(hidden_low) + rows_back).astype(BF16)[:, None]
    output = to_positions(final).astype(BF16)[:, None]

    sums = plain_sums(
        qkv_total, out_total, router_total, first_total, second_total, own_width
    )
    grad_query, grad_key, grad_value, grad_out, grad_router, grad_first, grad_second = sums
    diag_all = lax.all_gather(
        lax.psum(diagonals, ("dp", "experts")), "context", axis=0, tiled=True
    )
    offsets = jnp.concatenate([diag_all[:, :1], diag_all[:, : seq : -1]], axis=1)
    grad_table = jnp.einsum(
        "hs,sb->bh", offsets, bucket_hot.astype(F32), precision=lax.Precision.HIGHEST
    )
    return (
        output,
        grad_input,
        grad_query,
        grad_key,
        grad_value,
        grad_out,
        grad_router,
        grad_first,
        grad_second,
        grad_table,
        grad_gate[None],
        grad_up[None],
        grad_down[None],
    )


class Wires:
    def __init__(self, sends, receives, homes):
        self.sends, self.receives, self.homes = sends, receives, homes
        self.used, self.used_home = 0, 0

    def take(self):
        self.used += 1
        return self.used - 1

    def copy(self, source, place, peer, index):
        return remote(source, place, self.sends.at[index], self.receives.at[index], peer)

    def home(self, source, place):
        copy = pltpu.make_async_copy(source, place, self.homes.at[self.used_home])
        self.used_home += 1
        return copy


class Spread:
    def __init__(self, wires, buf, ctx_axis):
        self.wires, self.buf = wires, buf
        dp, ctx, exp = (lax.axis_index(name) for name in ALL)
        self.high, self.low, self.exp = dp // 2, dp % 2, exp
        self.last = lax.axis_size("experts") - 1
        self.core_peer = (flip(dp, 1), ctx, exp)
        self.x_peer = (flip(dp, 2), ctx, exp)
        self.up_peer = (dp, ctx, jnp.minimum(exp + 1, self.last))
        self.down_peer = (dp, ctx, jnp.maximum(exp - 1, 0))
        self.labels = [(0, 0)] + [(h, d) for h in range(1, self.last + 1) for d in (1, -1)]
        self.z_wire, self.x_wire, self.own_wire, self.far_wire = (
            {label: wires.take() for label in self.labels} for _ in range(4)
        )

    def block(self, label):
        hop, way = label
        return jnp.clip(self.exp - hop * way, 0, self.last) if hop else self.exp

    def when(self, label):
        hop, way = label
        if hop == 0:
            return lambda f: f()
        here = self.exp - hop * way
        return pl.when((here >= 0) & (here <= self.last))

    def can_send(self, label, act):
        hop, way = label
        held = self.exp - (hop - 1) * way
        ahead = self.exp + way
        pl.when((held >= 0) & (held <= self.last) & (ahead >= 0) & (ahead <= self.last))(act)

    def z_copy(self, label):
        hop, way = label
        held = jnp.clip(self.exp - (hop - 1) * way, 0, self.last)
        part = self.buf.at[self.high, self.low, :, held]
        peer = self.up_peer if way == 1 else self.down_peer
        return self.wires.copy(part, part, peer, self.z_wire[label])

    def part_copy(self, label, high, wire, peer):
        part = self.buf.at[high, self.low, :, self.block(label)]
        return self.wires.copy(part, part, peer, wire[label])

    def x_copy(self, label):
        return self.part_copy(label, self.high, self.x_wire, self.x_peer)

    def own_copy(self, label):
        return self.part_copy(label, self.high, self.own_wire, self.core_peer)

    def far_copy(self, label):
        return self.part_copy(label, 1 - self.high, self.far_wire, self.core_peer)

    def spread(self, label):
        self.x_copy(label).start()
        self.own_copy(label).start()

    def begin(self):
        for way in (1, -1):
            self.can_send((1, way), lambda way=way: self.z_copy((1, way)).start())
        self.spread((0, 0))

    def hop(self, hop):
        for way in (1, -1):
            label = (hop, way)

            @self.when(label)
            def _(label=label):
                part = self.buf.at[self.high, self.low, :, self.block(label)]
                self.wires.copy(part, part, self.up_peer, self.z_wire[label]).wait_recv()

            if hop < self.last:
                nxt = (hop + 1, way)
                self.can_send(nxt, lambda nxt=nxt: self.z_copy(nxt).start())

            @self.when(label)
            def _(label=label):
                self.spread(label)

        for label in self.labels:
            if label[0] == hop - 1:
                self.pass_far(label)

    def pass_far(self, label):
        @self.when(label)
        def _():
            self.x_copy(label).wait_recv()
            self.far_copy(label).start()

    def end(self):
        for label in self.labels:
            if label[0] == self.last:
                self.pass_far(label)
        for label in self.labels:

            @self.when(label)
            def _(label=label):
                self.own_copy(label).wait_recv()
                self.far_copy(label).wait_recv()

    def drain(self):
        for label in self.labels:
            if label[0]:
                self.can_send(label, lambda label=label: self.z_copy(label).wait_send())

            @self.when(label)
            def _(label=label):
                self.x_copy(label).wait_send()
                self.own_copy(label).wait_send()
                self.far_copy(label).wait_send()


def front_kernel(
    sizes,
    act_ref,
    cot_ref,
    deal_lanes,
    length_ref,
    route_lanes,
    bucket_lanes,
    bias_ref,
    query_ref,
    key_ref,
    value_ref,
    out_ref,
    extra_ref,
    gate_ref,
    up_ref,
    down_ref,
    hidden_ref,
    logit_ref,
    mixed,
    cot_rows_ref,
    deal_ref,
    route_ref,
    line_ref,
    dense_save,
    out_save,
    act_save,
    normed_save,
    qkv_save,
    x_save,
    u_save,
    g_save,
    gate_save,
    down_save,
    both_save,
    activated_save,
    dense,
    out_w,
    act_all,
    normed_ref,
    qkv_ref,
    all_x,
    all_u,
    all_p,
    all_g,
    gate_up,
    down,
    both,
    activated,
    cot_all,
    mixed_own,
    mixed_sent,
    sent_x,
    sent_u,
    sent_p,
    line_all,
    sends,
    receives,
    homes,
):
    heads, head_size, experts, capacity, slots = sizes
    micro, rows_dev, width = act_ref.shape
    own_width = heads * head_size
    half = gate_ref.shape[1] // 2
    dp, ctx, exp = (lax.axis_index(name) for name in ALL)
    high, low = dp // 2, dp % 2
    block = dp * 2 + ctx
    core_peer, x_peer, x_core = ((flip(dp, 1), ctx, exp), (flip(dp, 2), ctx, exp), (3 - dp, ctx, exp))
    x_core = (flip(flip(dp, 2), 1), ctx, exp)
    y_peer, y_core = (dp, 1 - ctx, exp), (flip(dp, 1), 1 - ctx, exp)
    z_peers = [None] + [(dp, ctx, flip(exp, 1)), (dp, ctx, flip(exp, 2)), (dp, ctx, 3 - exp)]
    z_index = [exp, flip(exp, 1), flip(exp, 2), 3 - exp]
    greet([core_peer, x_peer, x_core, y_peer, y_core] + z_peers[1:])
    wires = Wires(sends, receives, homes)
    drains = []
    home_copies = []

    def send(source, place, peer):
        copy = wires.copy(source, place, peer, wires.take())
        copy.start()
        drains.append(copy)
        return copy

    def multiple(index, size):
        return pl.ds(pl.multiple_of(index * size, size), size)

    def save(source, place):
        copy = wires.home(source, place)
        copy.start()
        home_copies.append(copy)

    mine, other = multiple(ctx, own_width), multiple(1 - ctx, own_width)
    first = []
    for i, ref in enumerate((query_ref, key_ref, value_ref)):
        place = dense.at[high, low, ctx, exp, :, i * own_width : (i + 1) * own_width]
        first.append(send(ref.at[:, other], place, y_peer))
    first.append(send(extra_ref, dense.at[high, low, ctx, exp, :, 3 * own_width :], y_peer))
    out_first = send(out_ref, out_w.at[high, low, ctx, exp], y_peer)
    here = multiple(ctx, rows_dev)
    act_first = send(act_ref, act_all.at[:, here], y_peer)
    def gate_sends(core, peer):
        cols = multiple(core, half)
        return [
            send(gate_ref.at[:, cols], gate_up.at[block, :, 0:half], peer),
            send(up_ref.at[:, cols], gate_up.at[block, :, half:], peer),
        ]

    own_gate = []
    for ref, start in ((gate_ref, 0), (up_ref, half)):
        copy = wires.home(ref.at[:, multiple(low, half)], gate_up.at[block, :, start : start + half])
        copy.start()
        own_gate.append(copy)

    for i, ref in enumerate((query_ref, key_ref, value_ref)):
        dense[high, low, ctx, exp, :, i * own_width : (i + 1) * own_width] = ref[:, mine]
    dense[high, low, ctx, exp, :, 3 * own_width :] = extra_ref[...]
    out_w[high, low, ctx, exp] = out_ref[...]
    act_all[:, here, :] = act_ref[...]
    cot_all[:, here, :] = cot_ref[...]

    spread = Spread(wires, dense, 2)
    spread_out = Spread(wires, out_w, 2)
    for copy in first:
        copy.wait_recv()
    spread.begin()
    cot_first = send(cot_ref, cot_all.at[:, here], y_peer)
    from_y_core = gate_sends(1 - low, y_core)
    from_y = gate_sends(low, y_peer)
    from_core = gate_sends(1 - low, core_peer)

    spread.hop(1)

    own_down = low * 2 + ctx
    home_down = wires.home(down_ref, down.at[own_down])
    down_wire = {name: wires.take() for name in ("core", "x", "xc", "y", "yc", "rx", "ry")}
    at_home = low == high

    def down_copy(name, peer, source=None):
        source = down_ref if source is None else source
        return wires.copy(source, down.at[own_down], peer, down_wire[name])

    down_sends = [
        ("core", core_peer, False),
        ("x", x_peer, True),
        ("xc", x_core, False),
        ("y", y_peer, True),
        ("yc", y_core, False),
    ]

    def down_start():
        @pl.when(at_home)
        def _():
            home_down.start()

        for name, peer, straight in down_sends:
            pl.when(at_home == straight)(lambda name=name, peer=peer: down_copy(name, peer).start())

    def as_column(line):
        return jnp.broadcast_to(line.astype(F32), (128, line.shape[1])).T[:, 0:1].astype(jnp.int32)

    for m in range(micro):
        deal_ref[m] = as_column(deal_lanes[m : m + 1, :])
        for j in range(2):
            route_ref[m, :, j : j + 1] = as_column(route_lanes[m, j : j + 1, :])
    bucket_rows = lax.broadcasted_iota(
        jnp.int32, (bias_ref.shape[0], bucket_lanes.shape[1]), 0
    )
    bucket_hot = jnp.where(bucket_rows == bucket_lanes[...], 1.0, 0.0).astype(BF16)
    line_all[...] = dot_rows(bias_ref[...], bucket_hot)
    line_ref[...] = line_all[pl.ds(pl.multiple_of(ctx * heads, heads), heads), :]

    lane = lax.broadcasted_iota(jnp.int32, (rows_dev, 128), 1)
    lane_f = lane.astype(F32)
    row_id = lax.broadcasted_iota(jnp.int32, (rows_dev, rows_dev), 0)
    col_id = lax.broadcasted_iota(jnp.int32, (rows_dev, rows_dev), 1)
    before = (row_id > col_id).astype(BF16)
    seq = deal_ref.shape[1]
    seq_lane = lax.broadcasted_iota(jnp.int32, (rows_dev, seq), 1)

    def hot(m, k):
        index = ctx if k == 0 else 1 - ctx
        return (deal_ref[m, multiple(index, rows_dev), :] == seq_lane).astype(BF16)

    def live_slots(m):
        return deal_ref[m, here, :] < length_ref[m]

    def ranks(m):
        live = live_slots(m)
        hots = [(route_ref[m, :, j : j + 1] == lane) for j in range(2)]
        used = jnp.where((hots[0] | hots[1]) & live, 1.0, 0.0).astype(BF16)
        earlier = jnp.dot(before, used, preferred_element_type=F32)
        found = []
        for j in range(2):
            rank = jnp.sum(jnp.where(hots[j], earlier, 0.0), axis=1, keepdims=True)
            found.append(jnp.where(live & (rank < capacity), rank, -1.0))
        return found

    def picks(m, k, rank):
        return [
            (route_ref[m, :, j : j + 1] == z_index[k]) & (rank[j] == lane_f) for j in range(2)
        ]

    def as_rows(pick, value):
        chosen = lax.dot_general(
            pick, value, (((0,), (0,)), ((), ())), preferred_element_type=F32
        )
        return chosen[:slots].astype(BF16)

    spread.hop(2)
    rank_of = [ranks(m) for m in range(micro)]
    act_first.wait_recv()
    spread.hop(3)
    cot_first.wait_recv()
    pick_of = {}
    for m in range(micro):
        hot_mine = hot(m, 0)
        cot_rows = jnp.dot(hot_mine, cot_all[m], preferred_element_type=F32).astype(BF16)
        cot_rows_ref[m] = cot_rows
        for k in range(experts):
            pick = picks(m, k, rank_of[m])
            pick_any = jnp.where(pick[0] | pick[1], 1.0, 0.0).astype(BF16)
            rows = as_rows(pick_any, cot_rows)
            if k == 0:
                all_u[0, 0, m] = rows
            else:
                sent_u[k - 1, m] = rows
    out_first.wait_recv()
    spread.end()
    from_x = gate_sends(low, x_peer)
    from_x_core = gate_sends(1 - low, x_core)
    spread_out.begin()
    save(dense, dense_save)
    save(act_all, act_save)
    u_first, u_core = {}, []

    def send_u(m):
        for k in range(1, experts):
            u_first[k, m] = send(sent_u.at[k - 1, m], all_u.at[0, k, m], z_peers[k])
        u_core.append(send(all_u.at[0, 0, m], all_u.at[1, 0, m], core_peer))

    def pass_u(m):
        for k in range(1, experts):
            u_first[k, m].wait_recv()
            u_core.append(send(all_u.at[0, k, m], all_u.at[1, k, m], core_peer))

    send_u(0)

    extras = dense[:, :, :, :, :, 3 * own_width :].reshape(width, 128).astype(F32)
    turned = extras.T
    gain_one, gain_two = turned[experts : experts + 1], turned[experts + 1 : experts + 2]
    for m in range(micro):
        rows = act_all[m].astype(F32)
        inverse = lax.rsqrt(jnp.mean(rows * rows, axis=-1, keepdims=True) + epsilon)
        normed_ref[m] = (rows * inverse * gain_one).astype(BF16)
    for i in range(3):
        weight = dense[:, :, :, :, :, i * own_width : (i + 1) * own_width].reshape(width, own_width)
        for m in range(micro):
            qkv_ref[m, :, i * own_width : (i + 1) * own_width] = jnp.dot(
                normed_ref[m], weight, preferred_element_type=F32
            ).astype(BF16)
    spread_out.hop(1)

    scale = head_size ** (-0.5)
    mixed_first = []
    save(normed_ref, normed_save)
    save(qkv_ref, qkv_save)
    for m in range(micro):
        length = length_ref[m]
        for head in range(heads):
            at = [
                slice(part * own_width + head * head_size, part * own_width + (head + 1) * head_size)
                for part in range(3)
            ]
            scores = masked_scores(
                qkv_ref[m, :, at[0]], qkv_ref[m, :, at[1]], line_ref[head : head + 1, :], length, scale
            )
            probs = soft(scores).astype(BF16)
            mixed_own[:, at[0]] = jnp.dot(
                probs, qkv_ref[m, :, at[2]], preferred_element_type=F32
            ).astype(BF16)
        own = mixed_own[...]
        mixed_sent[m] = jnp.dot(hot(m, 1), own, preferred_element_type=F32).astype(BF16)
        mixed_first.append(send(mixed_sent.at[m], mixed.at[m, :, mine], y_peer))
        mixed[m, :, mine] = jnp.dot(hot(m, 0), own, preferred_element_type=F32).astype(BF16)
        spread_out.hop(2 + m)
    spread_out.end()

    router_w = dense[:, :, :, :, :, 3 * own_width :].reshape(width, 128)
    x_first, p_first, x_core_copy, core_copies = {}, {}, {}, []
    for m in range(micro):
        mixed_first[m].wait_recv()
        branch = jnp.dot(
            mixed[m], out_w[...].reshape(width, width), preferred_element_type=F32
        )
        rows_in = jnp.dot(hot(m, 0), act_all[m], preferred_element_type=F32)
        live = live_slots(m)
        hidden = rows_in + jnp.where(live, branch, 0.0)
        hidden_ref[m] = hidden
        inverse = lax.rsqrt(jnp.mean(hidden * hidden, axis=-1, keepdims=True) + epsilon)
        normed_two = (hidden * inverse * gain_two).astype(BF16)
        logits = jnp.dot(normed_two, router_w, preferred_element_type=F32)
        logit_ref[m] = logits
        chosen = [
            jnp.sum(jnp.where(route_ref[m, :, j : j + 1] == lane, logits, 0.0), axis=1, keepdims=True)
            for j in range(2)
        ]
        top = jnp.maximum(chosen[0], chosen[1])
        raised = [jnp.exp(c - top) for c in chosen]
        total = raised[0] + raised[1]
        gates = [r / total for r in raised]
        for k in range(experts):
            pick = picks(m, k, rank_of[m])
            pick_any = jnp.where(pick[0] | pick[1], 1.0, 0.0).astype(BF16)
            rows = as_rows(pick_any, normed_two)
            weights = jnp.sum(
                jnp.where(pick[0], gates[0], 0.0) + jnp.where(pick[1], gates[1], 0.0),
                axis=0,
                keepdims=True,
            )
            weights = jnp.broadcast_to(weights, (8, 128))
            if k == 0:
                all_x[0, 0, m] = rows
                all_p[0, 0, m] = weights
                x_core_copy[0, m] = send(all_x.at[0, 0, m], all_x.at[1, 0, m], core_peer)
                core_copies.append(send(all_p.at[0, 0, m], all_p.at[1, 0, m], core_peer))
            else:
                sent_x[k - 1, m] = rows
                sent_p[k - 1, m] = weights
                x_first[k, m] = send(sent_x.at[k - 1, m], all_x.at[0, k, m], z_peers[k])
                p_first[k, m] = send(sent_p.at[k - 1, m], all_p.at[0, k, m], z_peers[k])

    for m in range(1, micro):
        send_u(m)
    save(out_w, out_save)
    for copy in from_x:
        copy.wait_recv()
    x_block = flip(dp, 2) * 2 + ctx
    relay_y = send(gate_up.at[x_block], gate_up.at[x_block], y_peer)
    for copy in from_y_core:
        copy.wait_recv()
    y_block = flip(dp, 1) * 2 + 1 - ctx
    relay_x = send(gate_up.at[y_block], gate_up.at[y_block], x_peer)

    down_start()
    pass_u(0)

    def pass_rows(k):
        for m in range(micro):
            x_first[k, m].wait_recv()
            x_core_copy[k, m] = send(all_x.at[0, k, m], all_x.at[1, k, m], core_peer)
            p_first[k, m].wait_recv()
            core_copies.append(send(all_p.at[0, k, m], all_p.at[1, k, m], core_peer))

    def hidden_units(k):
        for m in range(micro):
            x_core_copy[k, m].wait_recv()
        count = 2 * micro * slots
        shape = (2, micro, slots)

        def tile(start, size):
            rows = all_x[:, k].reshape(count, width)
            gate_w = gate_up[:, :, pl.ds(start, size)].reshape(width, size)
            up_w = gate_up[:, :, pl.ds(half + start, size)].reshape(width, size)
            pre = jnp.dot(rows, gate_w, preferred_element_type=F32)
            up_part = jnp.dot(rows, up_w, preferred_element_type=F32)
            value, slope = gelu_parts(pre)
            activated[:, k, :, :, pl.ds(start, size)] = (
                (value * up_part).astype(BF16).reshape(shape + (size,))
            )
            both[:, k, :, :, pl.ds(start, size)] = (
                (up_part * slope).astype(BF16).reshape(shape + (size,))
            )
            both[:, k, :, :, pl.ds(half + start, size)] = value.astype(BF16).reshape(shape + (size,))

        wide = half // 256

        def step(i, carry):
            tile(pl.multiple_of(i * 256, 256), 256)
            return carry

        lax.fori_loop(0, wide, step, 0)
        if half % 256:
            tile(wide * 256, half - wide * 256)
        save(both.at[:, k], both_save.at[:, k])
        save(activated.at[:, k], activated_save.at[:, k])
        save(all_x.at[:, k], x_save.at[:, k])

    for k in (1, 2):
        pass_rows(k)
    for copy in from_core + from_y + from_x_core + [relay_x, relay_y]:
        copy.wait_recv()
    for copy in own_gate:
        copy.wait()
    save(gate_up, gate_save)
    hidden_units(0)
    hidden_units(1)
    away = jnp.logical_not(at_home)
    rx_place = low * 2 + 1 - ctx
    ry_place = (1 - low) * 2 + ctx

    @pl.when(at_home)
    def _():
        down_copy("y", y_peer).wait_recv()
        wires.copy(down.at[rx_place], down.at[rx_place], x_peer, down_wire["rx"]).start()

    @pl.when(away)
    def _():
        down_copy("xc", x_core).wait_recv()
        wires.copy(down.at[ry_place], down.at[ry_place], y_peer, down_wire["ry"]).start()

    pass_rows(3)
    hidden_units(2)
    hidden_units(3)
    for m in range(1, micro):
        pass_u(m)
    for copy in u_core + core_copies:
        copy.wait_recv()
    save(all_u.at[0], u_save)
    for part in range(2):
        for k in range(experts):
            for m in range(micro):
                column = jnp.broadcast_to(all_p[part, k, m, 0:1, :], (128, 128)).T[:slots, 0:1]
                all_g[part, k, m] = (column * all_u[part, k, m].astype(F32)).astype(BF16)
    save(all_g, g_save)

    @pl.when(at_home)
    def _():
        for name in ("core", "yc"):
            down_copy(name, core_peer).wait_recv()
        home_down.wait()
        down_copy("rx", x_peer).wait_send()

    @pl.when(away)
    def _():
        for name in ("x", "rx", "ry"):
            down_copy(name, core_peer).wait_recv()
        down_copy("ry", y_peer).wait_send()

    save(down, down_save)
    for name, peer, straight in down_sends:
        pl.when(at_home == straight)(lambda name=name, peer=peer: down_copy(name, peer).wait_send())
    for copy in home_copies:
        copy.wait()
    for copy in drains:
        copy.wait_send()
    spread.drain()
    spread_out.drain()


def front(
    sizes, act, cot, deal, length, route, bucket_lanes, table, weights, extras, w_gate, w_up, w_down
):
    heads, head_size, experts, capacity, slots = sizes
    micro, rows_dev, width = act.shape
    own_width = heads * head_size
    per_row = weights[0].shape[0]
    seq = deal.shape[1]
    half = w_gate.shape[1] // 2
    in_vmem, in_hbm = pl.BlockSpec(memory_space=pltpu.VMEM), pl.BlockSpec(memory_space=pltpu.HBM)
    wide = 3 * own_width + 128
    rows = (2, experts, micro, slots)
    outs = [
        ((micro, rows_dev, width), F32),
        ((micro, rows_dev, 128), F32),
        ((micro, rows_dev, width), BF16),
        ((micro, rows_dev, width), BF16),
        ((micro, seq, 1), jnp.int32),
        ((micro, rows_dev, 2), jnp.int32),
        ((heads, 2 * seq), F32),
    ]
    saved = [
        ((2, 2, 2, 4, per_row, wide), BF16),
        ((2, 2, 2, 4, per_row, width), BF16),
        ((micro, seq, width), BF16),
        ((micro, seq, width), BF16),
        ((micro, seq, 3 * own_width), BF16),
        (rows + (width,), BF16),
        (rows[1:] + (width,), BF16),
        (rows + (width,), BF16),
        ((8,) + (w_gate.shape[0], 2 * half), BF16),
        ((4,) + w_down.shape, BF16),
        (rows + (2 * half,), BF16),
        (rows + (half,), BF16),
    ]
    held = (
        saved[:6]
        + [(rows + (width,), BF16), ((2, experts, micro, 8, 128), F32)]
        + saved[7:]
    )
    return pl.pallas_call(
        functools.partial(front_kernel, sizes),
        out_shape=tuple(jax.ShapeDtypeStruct(*out) for out in outs + saved),
        in_specs=[in_vmem] * 3 + [pl.BlockSpec(memory_space=pltpu.SMEM)] + [in_vmem] * 8 + [in_hbm] * 3,
        out_specs=(in_vmem,) * len(outs) + (in_hbm,) * len(saved),
        scratch_shapes=[pltpu.VMEM(*shape) for shape in held]
        + [
            pltpu.VMEM((micro, seq, width), BF16),
            pltpu.VMEM((seq, own_width), BF16),
            pltpu.VMEM((micro, rows_dev, own_width), BF16),
            pltpu.VMEM((experts - 1, micro, slots, width), BF16),
            pltpu.VMEM((experts - 1, micro, slots, width), BF16),
            pltpu.VMEM((experts - 1, micro, 8, 128), F32),
            pltpu.VMEM((table.shape[1], 2 * seq), F32),
            pltpu.SemaphoreType.DMA((160,)),
            pltpu.SemaphoreType.DMA((160,)),
            pltpu.SemaphoreType.DMA((32,)),
        ],
        compiler_params=pltpu.CompilerParams(
            collective_id=1, has_side_effects=True, vmem_limit_bytes=60 * 2**20
        ),
    )(
        act, cot, deal, length, route, bucket_lanes, table, *weights, extras, w_gate, w_up, w_down
    )


class Plan:
    def __init__(self, deal_ref, length_ref, route_ref, rows_dev, capacity):
        self.deal, self.length, self.route = deal_ref, length_ref, route_ref
        self.rows, self.capacity = rows_dev, capacity
        self.ctx, exp = lax.axis_index("context"), lax.axis_index("experts")
        self.z_index = [exp, flip(exp, 1), flip(exp, 2), 3 - exp]
        self.lane = lax.broadcasted_iota(jnp.int32, (rows_dev, 128), 1)
        self.lane_f = self.lane.astype(F32)

    def at(self, k):
        index = self.ctx if k == 0 else 1 - self.ctx
        return pl.ds(pl.multiple_of(index * self.rows, self.rows), self.rows)

    def hot(self, m, k):
        seq = self.deal.shape[1]
        lane = lax.broadcasted_iota(jnp.int32, (self.rows, seq), 1)
        return (self.deal[m, self.at(k), :] == lane).astype(BF16)

    def hot_mine(self, m, k):
        lane = lax.broadcasted_iota(jnp.int32, (self.rows, self.rows), 1) + self.ctx * self.rows
        return (self.deal[m, self.at(k), :] == lane).astype(BF16)

    def live(self, m):
        return self.deal[m, self.at(0), :] < self.length[m]

    def named(self, m, j):
        return self.route[m, :, j : j + 1]

    def ranks(self, m):
        row_id = lax.broadcasted_iota(jnp.int32, (self.rows, self.rows), 0)
        col_id = lax.broadcasted_iota(jnp.int32, (self.rows, self.rows), 1)
        before = (row_id > col_id).astype(BF16)
        live = self.live(m)
        hots = [self.named(m, j) == self.lane for j in range(2)]
        used = jnp.where((hots[0] | hots[1]) & live, 1.0, 0.0).astype(BF16)
        earlier = jnp.dot(before, used, preferred_element_type=F32)
        found = []
        for j in range(2):
            rank = jnp.sum(jnp.where(hots[j], earlier, 0.0), axis=1, keepdims=True)
            found.append(jnp.where(live & (rank < self.capacity), rank, -1.0))
        return found

    def picks(self, m, k, rank):
        return [
            (self.named(m, j) == self.z_index[k]) & (rank[j] == self.lane_f) for j in range(2)
        ]

    def places(self, m, rank, experts, slots):
        lane = lax.broadcasted_iota(jnp.int32, (self.rows, experts * slots), 1).astype(F32)
        picks = []
        for j in range(2):
            place = rank[j]
            for k in range(1, experts):
                place = place + jnp.where(self.named(m, j) == self.z_index[k], 1.0 * k * slots, 0.0)
            place = jnp.where(rank[j] < 0, -1.0, place)
            picks.append(jnp.where(place == lane, 1.0, 0.0).astype(BF16))
        return picks

    def gates(self, m, logits):
        chosen = [
            jnp.sum(jnp.where(self.named(m, j) == self.lane, logits, 0.0), axis=1, keepdims=True)
            for j in range(2)
        ]
        top = jnp.maximum(chosen[0], chosen[1])
        raised = [jnp.exp(c - top) for c in chosen]
        total = raised[0] + raised[1]
        return [r / total for r in raised]


def dot_rows(left, right):
    return lax.dot_general(left, right, (((0,), (0,)), ((), ())), preferred_element_type=F32)


def dot_lanes(left, right):
    return lax.dot_general(left, right, (((1,), (1,)), ((), ())), preferred_element_type=F32)


STAGES = {"x": 0, "zl": 3, "zh": 2, "y": 1}


class Reduce:
    def __init__(self, wires, source, columns, order, bufs, peers, indices, finish):
        self.wires, self.source, self.columns = wires, source, columns
        self.order, self.bufs, self.peers, self.indices = order, bufs, peers, indices
        self.finish = finish
        self.flying, self.step = [], 0

    def launch(self, source, place, name):
        copy = self.wires.copy(source, place, self.peers[name], self.wires.take())
        copy.start()
        self.flying.append(copy)

    def begin(self):
        low = self.indices["core"]
        self.launch(self.source.at[:, 1 - low, :, self.columns], self.bufs[0], "core")

    def advance(self):
        if self.step > len(self.order):
            return False
        low = self.indices["core"]
        self.flying[-1].wait_recv()
        if self.step == 0:
            total = self.source[:, low, :, self.columns].astype(F32) + self.bufs[0][...].astype(F32)
            self.bufs[1][...] = total.astype(BF16).reshape(self.bufs[1].shape)
        else:
            kept = self.bufs[2 * self.step - 1]
            arrived = self.bufs[2 * self.step][...].astype(F32)
            mine = kept[self.cut(self.order[self.step - 1], True)].astype(F32)
            if self.step == len(self.order):
                self.finish(mine, arrived)
                self.step += 1
                return False
            self.bufs[2 * self.step + 1][...] = (mine + arrived).astype(BF16)
        name = self.order[self.step]
        kept = self.bufs[2 * self.step + 1]
        self.launch(kept.at[self.cut(name, False)], self.bufs[2 * self.step + 2], name)
        self.step += 1
        return True

    def cut(self, name, own):
        gone = set(self.order[: self.order.index(name)])
        axis = sum(1 for n, place in STAGES.items() if place < STAGES[name] and n not in gone)
        index = self.indices[name] if own else 1 - self.indices[name]
        return (slice(None),) * axis + (index,)


def reduce_buffers(order, rows, per_row, size):
    left = {"x", "zl", "zh", "y"}
    shapes = [(2, rows // 4, size)]
    for name in order:
        shapes.append((2,) * len(left) + (per_row, size))
        left.discard(name)
        shapes.append((2,) * len(left) + (per_row, size))
    return [pltpu.VMEM(shape, BF16) for shape in shapes]


X_FIRST, Z_FIRST = ("x", "zl", "zh", "y"), ("zl", "zh", "x", "y")
ORDERS = [X_FIRST, Z_FIRST, X_FIRST] * 2 + [Z_FIRST] * 2 + [X_FIRST]


def back_kernel(
    sizes,
    hidden_ref,
    logit_ref,
    mixed,
    cot_rows_ref,
    act_ref,
    deal_ref,
    route_ref,
    line_ref,
    length_ref,
    dense_in,
    out_in,
    act_in,
    normed_in,
    qkv_in,
    x_in,
    u_in,
    g_in,
    gate_w_in,
    down_w_in,
    both_in,
    activated_in,
    output_ref,
    grad_input_ref,
    query_out,
    key_out,
    value_out,
    out_out,
    small_out,
    diag_out,
    gate_in,
    down_in,
    gate_w,
    down_w,
    down_got,
    relay_got,
    back_got,
    out_got,
    sent_back,
    sent_out,
    sent_gate,
    ret_back,
    ret_out,
    ret_gate,
    final_all,
    hidden_all,
    mixed_got,
    grad_sent,
    first_sent,
    first_got,
    diag_buf,
    *rest,
):
    heads, head_size, experts, capacity, slots = sizes
    chunk_bufs, (sends, receives, homes) = rest[:-3], rest[-3:]
    micro, rows_dev, width = hidden_ref.shape
    seq = deal_ref.shape[1]
    own_width = heads * head_size
    dp, ctx, exp = (lax.axis_index(name) for name in ALL)
    high, low = dp // 2, dp % 2
    other_core, other_x, both_dp = flip(dp, 1), flip(dp, 2), flip(flip(dp, 1), 2)
    core_peer, x_peer, x_core = (other_core, ctx, exp), (other_x, ctx, exp), (both_dp, ctx, exp)
    y_peer, y_core = (dp, 1 - ctx, exp), (other_core, 1 - ctx, exp)
    z_peers = [None] + [(dp, ctx, flip(exp, 1)), (dp, ctx, flip(exp, 2)), (dp, ctx, 3 - exp)]
    greet([core_peer, x_peer, x_core, y_peer, y_core] + z_peers[1:])
    wires = Wires(sends, receives, homes)
    drains = []

    class Sent:
        def __init__(self, like, source, place, peer):
            self.like, self.peer, self.index = like, peer, wires.take()
            wires.copy(source, place, peer, self.index).start()
            drains.append(self)

        def again(self):
            part = self.like()
            return wires.copy(part, part, self.peer, self.index)

        def wait_recv(self):
            self.again().wait_recv()

        def wait_send(self):
            self.again().wait_send()

    def send(source, place, peer, like=None):
        return Sent(like or (lambda: source), source, place, peer)

    def like_rows():
        return ret_back.at[0, 0]

    def like_gate():
        return ret_gate.at[0, 0]

    def like_block():
        return gate_w.at[0]

    plan = Plan(deal_ref, length_ref, route_ref, rows_dev, capacity)
    mine = pl.ds(pl.multiple_of(ctx * own_width, own_width), own_width)
    other = pl.ds(pl.multiple_of((1 - ctx) * own_width, own_width), own_width)

    def load(source, place):
        copy = wires.home(source, place)
        copy.start()
        return copy

    block = dp * 2 + ctx
    at_home = low == high
    away = jnp.logical_not(at_home)
    down_wire = [wires.take() for _ in range(8)]
    down_sends = [
        (None, False, low * 2 + ctx, 0),
        (core_peer, False, (1 - low) * 2 + ctx, 0),
        (y_peer, False, low * 2 + 1 - ctx, 1),
        (y_core, False, (1 - low) * 2 + 1 - ctx, 1),
        (x_peer, True, low * 2 + ctx, 2),
        (x_core, True, (1 - low) * 2 + ctx, 2),
        (x_peer, True, low * 2 + 1 - ctx, None),
        (x_peer, True, (1 - low) * 2 + 1 - ctx, None),
    ]

    def down_copy(i):
        peer, _, place, slot = down_sends[i]
        target = down_got.at[i - 6] if slot is None else down_in.at[slot]
        return wires.copy(down_w.at[place], target, peer or core_peer, down_wire[i])

    def down_sums():
        @pl.when(at_home)
        def _():
            for i in range(2):
                down_copy(6 + i).wait_recv()
                place = down_sends[2 + i][2]
                down_w[place] = (
                    down_w[place].astype(F32) + down_got[i].astype(F32)
                ).astype(BF16)
                down_copy(2 + i).start()

    home_wire = wires.used_home
    wires.used_home += 2

    def home_block():
        return pltpu.make_async_copy(gate_w.at[block], gate_in.at[0], homes.at[home_wire])

    def home_down():
        return pltpu.make_async_copy(
            down_w.at[low * 2 + ctx], down_in.at[0], homes.at[home_wire + 1]
        )

    bulk, relayed = [], []
    far_places = (other_x * 2 + 1 - ctx, both_dp * 2 + 1 - ctx)
    y_places = (dp * 2 + 1 - ctx, other_core * 2 + 1 - ctx)
    x_places = (other_x * 2 + ctx, both_dp * 2 + ctx)

    def bulk_send(place, slot, peer):
        bulk.append(send(gate_w.at[place], gate_in.at[slot], peer, like_block))

    def relay_sums():
        for i, (place, slot, peer) in enumerate(
            ((y_places[0], 4, y_peer), (x_places[1], 3, x_core))
        ):
            relayed[i].wait_recv()
            gate_w[place] = (gate_w[place].astype(F32) + relay_got[i].astype(F32)).astype(BF16)
            bulk_send(place, slot, peer)

    def start_down(which):
        for i in which:
            peer, is_away, _, _ = down_sends[i]
            pl.when(away if is_away else at_home)(
                lambda i=i, peer=peer: (home_down() if peer is None else down_copy(i)).start()
            )

    ret_first = {}
    both_rows = experts * slots

    def expert_phase(both, rows_x, rows_g, activated, rows_u, back_part):
        half = activated.shape[-1]
        first = [load(g_in, rows_g), load(down_w_in, down_w)]
        second = [load(both_in.at[:, :, m], both.at[:, :, m]) for m in range(micro)]
        second.append(load(gate_w_in, gate_w))
        third = [load(activated_in, activated), load(x_in, rows_x), load(u_in, rows_u)]
        for copy in first:
            copy.wait()
        shape = (2, experts, slots)
        count = 2 * experts * slots

        def act_tile(m, start, size):
            rows = rows_g[:, :, m].reshape(count, width)
            weight = down_w[...].reshape(half, width) if size == half else down_flat(start, size)
            grad = dot_lanes(rows, weight)
            for shift in (0, half):
                cols = pl.ds(shift + start, size)
                kept = both[:, :, m, :, cols].reshape(count, size).astype(F32)
                both[:, :, m, :, cols] = (grad * kept).astype(BF16).reshape(shape + (size,))

        def down_flat(start, size):
            per = down_w.shape[1]
            parts = []
            while size:
                index, offset = start // per, start % per
                taken = min(size, per - offset)
                parts.append(down_w[index, offset : offset + taken, :])
                start, size = start + taken, size - taken
            return parts[0] if len(parts) == 1 else jnp.concatenate(parts, axis=0)

        def back_rows(m):
            def step(i, carry):
                rows = both[:, :, m].reshape(count, 2 * half)
                weight = gate_w[pl.ds(i * 2, 2)].reshape(256, 2 * half)
                part = dot_lanes(rows, weight).astype(BF16)
                cols = pl.ds(pl.multiple_of(i * 256, 256), 256)
                back_part[:, :, m, :, cols] = part.reshape(shape + (256,))
                return carry

            lax.fori_loop(0, width // 256, step, 0)

        back_core = []
        for m in range(micro):
            second[m].wait()
            for start in range(0, half, 256):
                act_tile(m, start, min(256, half - start))
            if m == 0:
                second[-1].wait()
            back_rows(m)
            back_core.append(send(back_part.at[1, :, m], back_got.at[m], core_peer))

        def give_back(m):
            back_core[m].wait_recv()
            for k in range(experts):
                rows = (
                    back_part[0, k, m].astype(F32) + back_got[m, k].astype(F32)
                ).astype(BF16)
                if k == 0:
                    ret_back[m, 0] = rows
                else:
                    sent_back[m, k - 1] = rows
                    ret_first["back", m, k] = send(
                        sent_back.at[m, k - 1], ret_back.at[m, k], z_peers[k], like_rows
                    )

        for copy in third:
            copy.wait()
        depth = width // gate_w.shape[0]

        def gate_grad(place):
            cols = pl.ds(pl.multiple_of(place * depth, depth), depth)
            total = jnp.zeros((depth, 2 * half), F32)
            rows = rows_x[:, :, :, :, cols].reshape(micro * count, depth)
            total = dot_rows(rows, both[...].reshape(micro * count, 2 * half))
            gate_w[place] = total.astype(BF16)

        for i, (place, peer) in enumerate(zip(far_places, (x_peer, y_peer))):
            gate_grad(place)
            relayed.append(send(gate_w.at[place], relay_got.at[i], peer, like_block))
        give_back(0)
        for place, slot, peer in (
            (x_places[0], 2, x_peer),
            (y_places[1], 5, y_core),
            (other_core * 2 + ctx, 1, core_peer),
        ):
            gate_grad(place)
            bulk_send(place, slot, peer)
        give_back(1)
        gate_grad(y_places[0])
        gate_grad(x_places[1])
        gate_grad(block)
        home_block().start()

        out_part = back_part
        for copy in back_core:
            copy.wait_send()
        out_core = []
        for m in range(micro):

            def step(i, carry):
                cols = pl.ds(pl.multiple_of(i * 256, 256), 256)
                rows = activated[:, :, m].reshape(count, half)
                weight = down_w[:, :, cols].reshape(half, 256)
                part = jnp.dot(rows, weight, preferred_element_type=F32).astype(BF16)
                out_part[:, :, m, :, cols] = part.reshape(shape + (256,))
                return carry

            lax.fori_loop(0, width // 256, step, 0)
            out_core.append(send(out_part.at[1, :, m], out_got.at[m], core_peer))

        ones = jnp.ones((8, width), F32)
        for m in range(micro):
            out_core[m].wait_recv()
            for k in range(experts):
                rows = (
                    out_part[0, k, m].astype(F32) + out_got[m, k].astype(F32)
                ).astype(BF16)
                worth = lax.dot_general(
                    ones,
                    rows.astype(F32) * rows_u[k, m].astype(F32),
                    (((1,), (1,)), ((), ())),
                    precision=lax.Precision.HIGHEST,
                    preferred_element_type=F32,
                )
                if k == 0:
                    ret_out[m, 0] = rows
                    ret_gate[m, 0, :, :slots] = worth
                else:
                    sent_out[m, k - 1] = rows
                    sent_gate[m, k - 1, :, :slots] = worth
                    ret_first["gate", m, k] = send(
                        sent_gate.at[m, k - 1], ret_gate.at[m, k], z_peers[k], like_gate
                    )

        totals = {}
        per = down_w.shape[1]
        for start in range(0, half, 128):
            rows = activated[:, :, :, :, start : start + 128].reshape(micro * count, 128)
            total = dot_rows(rows, rows_g[...].reshape(micro * count, width)).astype(BF16)
            done = 0
            while done < 128:
                index, offset = (start + done) // per, (start + done) % per
                taken = min(128 - done, per - offset)
                down_w[index, offset : offset + taken, :] = total[done : done + taken]
                done += taken
        start_down((0, 1, 6, 7, 4, 5))
        for m in range(micro):
            for k in range(1, experts):
                ret_first["out", m, k] = send(
                    sent_out.at[m, k - 1], ret_out.at[m, k], z_peers[k], like_rows
                )
        for copy in out_core:
            copy.wait_send()
        gone = {id(copy) for copy in back_core + out_core}
        drains[:] = [copy for copy in drains if id(copy) not in gone]

    def token_phase(
        dense,
        out_w,
        act_all,
        normed_ref,
        qkv_ref,
        first_own,
        grad_own,
        qkv_grad,
        qkv_total,
        out_low,
        small_f,
        small_low,
        branch_all,
    ):
        loads = [
            load(source, place)
            for source, place in (
                (dense_in, dense),
                (out_in, out_w),
                (qkv_in, qkv_ref),
                (act_in, act_all),
                (normed_in, normed_ref),
            )
        ]
        for copy in loads:
            copy.wait()
        before_tokens = len(drains)
        extras = dense[:, :, :, :, :, 3 * own_width :].reshape(width, 128)
        turned = extras.astype(F32).T
        gain_one, gain_two = turned[experts : experts + 1], turned[experts + 1 : experts + 2]
        lanes = lax.broadcasted_iota(jnp.int32, (width, 128), 1)
        rank_of = [plan.ranks(m) for m in range(micro)]
        gate_of = [plan.gates(m, logit_ref[m]) for m in range(micro)]
        mixed_first, hidden_first = [], []
        second = jnp.zeros((1, width), F32)
        out_matrix = out_w[...].reshape(width, width)
        here = plan.at(0)
        for m in range(micro):
            for k in range(1, experts):
                ret_first["back", m, k].wait_recv()
                ret_first["gate", m, k].wait_recv()
            worths = []
            for j in range(2):
                worth = jnp.zeros((rows_dev, 1), F32)
                for k in range(experts):
                    pick = plan.picks(m, k, rank_of[m])[j]
                    worth = worth + jnp.sum(
                        jnp.where(pick, ret_gate[m, k, 0:1, :], 0.0), axis=1, keepdims=True
                    )
                worths.append(worth)
            gates = gate_of[m]
            mean_worth = gates[0] * worths[0] + gates[1] * worths[1]
            logit_grad = sum(
                jnp.where(plan.named(m, j) == plan.lane, gates[j] * (worths[j] - mean_worth), 0.0)
                for j in range(2)
            ).astype(BF16)
            places = plan.places(m, rank_of[m], experts, slots)
            normed_grad = jnp.dot(
                places[0] + places[1],
                ret_back[m].reshape(experts * slots, width),
                preferred_element_type=F32,
            ) + dot_lanes(logit_grad, extras)
            hidden = hidden_ref[m]
            inverse = lax.rsqrt(jnp.mean(hidden * hidden, axis=-1, keepdims=True) + epsilon)
            scaled = hidden * inverse
            normed_two = (scaled * gain_two).astype(BF16)
            router = dot_rows(normed_two, logit_grad)
            small_f[...] = router if m == 0 else small_f[...] + router
            second = second + jnp.sum(normed_grad * scaled, axis=0, keepdims=True)
            lifted = gain_two * normed_grad
            mean_part = jnp.mean(lifted * hidden, axis=-1, keepdims=True)
            hidden_grad = (
                cot_rows_ref[m].astype(F32)
                + inverse * lifted
                - hidden * (inverse * inverse * inverse) * mean_part
            )
            hidden_all[m, 0] = hidden_grad.astype(BF16)
            branch_grad = jnp.where(plan.live(m), hidden_grad, 0.0).astype(BF16)
            mixed_grad = dot_lanes(branch_grad, out_matrix).astype(BF16)
            grad_sent[m] = mixed_grad
            mixed_first.append(send(grad_sent.at[m, :, other], mixed_got.at[m], y_peer))
            branch_all[m] = branch_grad
        for m in range(micro):
            hidden_first.append(send(hidden_all.at[m, 0], hidden_all.at[m, 1], y_peer))

        out_low[...] = (
            dot_rows(
                mixed[...].reshape(micro * rows_dev, width),
                branch_all[...].reshape(micro * rows_dev, width),
            )
            .astype(BF16)
            .reshape(out_low.shape)
        )

        relay_sums()
        indices = {"core": low, "x": high, "y": ctx, "zl": exp % 2, "zh": exp // 2}
        peers = {"core": core_peer, "x": x_peer, "y": y_peer, "zl": z_peers[1], "zh": z_peers[2]}

        def finish_qkv(place, start):
            def store(kept, arrived):
                size = own_width // 2
                for index, value in ((ctx, kept), (1 - ctx, arrived)):
                    first = pl.multiple_of(index * own_width + start, size)
                    place[:, pl.ds(first, size)] = value

            return store

        def finish_out(start):
            def store(kept, arrived):
                out_out[:, start : start + own_width] = kept + arrived

            return store

        def finish_small(kept, arrived):
            small_out[...] = kept + arrived

        chunks = []
        at = 0
        for i, order in enumerate(ORDERS):
            bufs = chunk_bufs[at : at + 9]
            at += 9
            if i < 6:
                shift = (i // 3) * (own_width // 2)
                source, start = qkv_total, (i % 3) * own_width + shift
                finish = finish_qkv((query_out, key_out, value_out)[i % 3], shift)
            elif i < 8:
                source, start = out_low, (i - 6) * own_width
                finish = finish_out(start)
            else:
                source, start, finish = small_low, 0, finish_small
            size = bufs[0].shape[-1]
            chunks.append(
                Reduce(wires, source, slice(start, start + size), order, bufs, peers, indices, finish)
            )
        chunks[6].begin()
        chunks[7].begin()

        def advance(*which):
            for i in which:
                chunks[i].advance()

        scale = head_size ** (-0.5)

        def head_back(m, head):
            cols = [
                slice(part * own_width + head * head_size, part * own_width + (head + 1) * head_size)
                for part in range(3)
            ]
            query, key, value = (qkv_ref[m, :, part] for part in cols)
            grad = grad_own[m, :, cols[0]]
            scores = masked_scores(
                query, key, line_ref[head : head + 1, :], length_ref[m], scale
            )
            probs = soft(scores)
            prob_grad = dot_lanes(grad, value)
            delta = jnp.sum(probs * prob_grad, axis=-1, keepdims=True)
            score_grad = (probs * (prob_grad - delta)).astype(BF16)
            diagonal = diagonal_sums(score_grad.astype(F32))
            if m:
                diagonal = diagonal + diag_buf[0, head : head + 1, :]
            diag_buf[0, head : head + 1, :] = diagonal
            qkv_grad[m, :, cols[0]] = (
                jnp.dot(score_grad, key, preferred_element_type=F32) * scale
            ).astype(BF16)
            qkv_grad[m, :, cols[1]] = (dot_rows(score_grad, query) * scale).astype(BF16)
            qkv_grad[m, :, cols[2]] = dot_rows(probs.astype(BF16), grad).astype(BF16)

        for group in range(2):
            for m in range(micro):
                if group == 0:
                    mixed_first[m].wait_recv()
                    grad_own[m] = (
                        dot_rows(plan.hot(m, 0), grad_sent[m, :, mine])
                        + dot_rows(plan.hot(m, 1), mixed_got[m])
                    ).astype(BF16)
                for head in range(group * heads // 2, (group + 1) * heads // 2):
                    head_back(m, head)
                advance(6, 7)
                if group == 1:
                    advance(0, 1, 2)
            for i in range(3):
                start = i * own_width + group * (own_width // 2)
                cols = slice(start, start + own_width // 2)
                total = dot_rows(
                    normed_ref[...].reshape(micro * seq, width),
                    qkv_grad[:, :, cols].reshape(micro * seq, own_width // 2),
                )
                qkv_total[:, :, :, cols] = total.astype(BF16).reshape(
                    2, 2, width // 4, own_width // 2
                )
                chunks[3 * group + i].begin()
            if group == 0:
                down_sums()

        diag_peers = [core_peer, x_peer, z_peers[1], z_peers[2], y_peer]
        diag_copies = []

        def diag_step(stage):
            if stage:
                diag_copies[stage - 1].wait_recv()
            if 0 < stage < 5:
                diag_buf[2 * stage] = diag_buf[2 * stage - 2] + diag_buf[2 * stage - 1]
            if stage < 5:
                diag_copies.append(
                    send(diag_buf.at[2 * stage], diag_buf.at[2 * stage + 1], diag_peers[stage])
                )

        diag_step(0)
        first_total = jnp.zeros((1, width), F32)
        first_first = []
        for m in range(micro):
            part = jnp.zeros((seq, width), F32)
            for i in range(3):
                cols = slice(i * own_width, (i + 1) * own_width)
                part = part + dot_lanes(
                    qkv_grad[m, :, cols], dense[:, :, :, :, :, cols].reshape(width, own_width)
                )
            rows = act_all[m].astype(F32)
            inverse = lax.rsqrt(jnp.mean(rows * rows, axis=-1, keepdims=True) + epsilon)
            first_total = first_total + jnp.sum(part * rows * inverse, axis=0, keepdims=True)
            first_own[...] = part
            first_sent[m] = first_own[plan.at(1), :].astype(BF16)
            first_got[m, 0] = first_own[here, :].astype(BF16)
            first_first.append(send(first_sent.at[m], first_got.at[m, 1], y_peer))
            advance(3, 4, 5)
            diag_step(1 + m)
            advance(0, 1, 2)
        columns = jnp.where(
            lanes == experts,
            jnp.broadcast_to(second, (128, width)).T,
            jnp.where(
                lanes == experts + 1, jnp.broadcast_to(first_total, (128, width)).T, small_f[...]
            ),
        )
        small_low[...] = columns.astype(BF16).reshape(small_low.shape)
        chunks[8].begin()
        advance(3, 4, 5)

        final_first = []
        for m in range(micro):
            for k in range(1, experts):
                ret_first["out", m, k].wait_recv()
            places = plan.places(m, rank_of[m], experts, slots)
            rows = ret_out[m].reshape(experts * slots, width)
            final = hidden_ref[m]
            for j in range(2):
                final = final + gate_of[m][j] * jnp.dot(places[j], rows, preferred_element_type=F32)
            final_all[m, 0] = final.astype(BF16)
            final_first.append(send(final_all.at[m, 0], final_all.at[m, 1], y_peer))
            if m == 0:
                advance(8, 3, 4, 5, 6, 7, 0, 1, 2)
                diag_step(3)
        advance(8)
        diag_step(4)
        advance(3, 4, 5)

        for m in range(micro):
            hidden_first[m].wait_recv()
            first_first[m].wait_recv()
            first = first_got[m, 0].astype(F32) + first_got[m, 1].astype(F32)
            rows = act_ref[m].astype(F32)
            inverse = lax.rsqrt(jnp.mean(rows * rows, axis=-1, keepdims=True) + epsilon)
            lifted = gain_one * first
            mean_part = jnp.mean(lifted * rows, axis=-1, keepdims=True)
            back = inverse * lifted - rows * (inverse * inverse * inverse) * mean_part
            moved = sum(dot_rows(plan.hot_mine(m, k), hidden_all[m, k]) for k in range(2))
            grad_input_ref[m] = (moved + back).astype(BF16)
            if m == 0:
                advance(8)
        for m in range(micro):
            final_first[m].wait_recv()
            moved = sum(dot_rows(plan.hot_mine(m, k), final_all[m, k]) for k in range(2))
            output_ref[m] = moved.astype(BF16)
        busy = True
        while busy:
            busy = False
            for i in range(len(chunks)):
                if chunks[i].step <= len(chunks[i].order):
                    chunks[i].advance()
                    busy = True
        diag_step(5)
        diag_out[ctx] = diag_buf[8]
        diag_out[1 - ctx] = diag_buf[9]
        for chunk in chunks:
            for copy in chunk.flying:
                copy.wait_send()
        for copy in drains[before_tokens:]:
            copy.wait_send()
        del drains[before_tokens:]

    rows_shape = (2, experts, micro, slots)
    half_ff = both_in.shape[-1] // 2
    pl.run_scoped(
        expert_phase,
        pltpu.VMEM(rows_shape + (2 * half_ff,), BF16),
        pltpu.VMEM(rows_shape + (width,), BF16),
        pltpu.VMEM(rows_shape + (width,), BF16),
        pltpu.VMEM(rows_shape + (half_ff,), BF16),
        pltpu.VMEM(rows_shape[1:] + (width,), BF16),
        pltpu.VMEM(rows_shape + (width,), BF16),
    )
    pl.run_scoped(
        token_phase,
        pltpu.VMEM(dense_in.shape, BF16),
        pltpu.VMEM(out_in.shape, BF16),
        pltpu.VMEM(act_in.shape, BF16),
        pltpu.VMEM(normed_in.shape, BF16),
        pltpu.VMEM(qkv_in.shape, BF16),
        pltpu.VMEM((seq, width), F32),
        pltpu.VMEM((micro, seq, own_width), BF16),
        pltpu.VMEM((micro, seq, 3 * own_width), BF16),
        pltpu.VMEM((2, 2, width // 4, 3 * own_width), BF16),
        pltpu.VMEM((2, 2, width // 4, width), BF16),
        pltpu.VMEM((width, 128), F32),
        pltpu.VMEM((2, 2, width // 4, 128), BF16),
        pltpu.VMEM((micro, rows_dev, width), BF16),
    )
    for copy in bulk:
        copy.wait_recv()
    for i, (peer, is_away, _, _) in enumerate(down_sends):
        if peer is None:
            pl.when(at_home)(lambda: home_down().wait())
            continue
        pl.when(away if is_away else at_home)(lambda i=i: down_copy(i).wait_send())
    @pl.when(at_home)
    def _():
        for i in (2, 4):
            down_copy(i).wait_recv()

    @pl.when(away)
    def _():
        for i in (1, 3, 5):
            down_copy(i).wait_recv()

    home_block().wait()
    for copy in drains:
        copy.wait_send()


def back(sizes, values, saved):
    heads, head_size, experts, capacity, slots = sizes
    hidden, lines = values[0], values[7]
    dense, gate_w, down_w = saved[0], saved[8], saved[9]
    micro, rows_dev, width = hidden.shape
    own_width = heads * head_size
    per_row = dense.shape[4]
    in_vmem, in_hbm = pl.BlockSpec(memory_space=pltpu.VMEM), pl.BlockSpec(memory_space=pltpu.HBM)
    smem = pl.BlockSpec(memory_space=pltpu.SMEM)
    outs = (
        [((micro, rows_dev, width), BF16)] * 2
        + [((per_row, width), F32)] * 4
        + [((per_row, 128), F32), ((2,) + lines.shape, F32)]
        + [((6,) + gate_w.shape[1:], BF16), ((3,) + down_w.shape[1:], BF16)]
    )
    rows = (micro, experts, slots, width)
    sent = (micro, experts - 1, slots, width)
    scratch = [
        pltpu.VMEM(gate_w.shape, BF16),
        pltpu.VMEM(down_w.shape, BF16),
        pltpu.VMEM((2,) + down_w.shape[1:], BF16),
        pltpu.VMEM((2,) + gate_w.shape[1:], BF16),
        pltpu.VMEM(rows, BF16),
        pltpu.VMEM(rows, BF16),
        pltpu.VMEM(sent, BF16),
        pltpu.VMEM(sent, BF16),
        pltpu.VMEM((micro, experts - 1, 8, 128), F32),
        pltpu.VMEM(rows, BF16),
        pltpu.VMEM(rows, BF16),
        pltpu.VMEM((micro, experts, 8, 128), F32),
        pltpu.VMEM((micro, 2, rows_dev, width), BF16),
        pltpu.VMEM((micro, 2, rows_dev, width), BF16),
        pltpu.VMEM((micro, rows_dev, own_width), BF16),
        pltpu.VMEM((micro, rows_dev, width), BF16),
        pltpu.VMEM((micro, rows_dev, width), BF16),
        pltpu.VMEM((micro, 2, rows_dev, width), BF16),
        pltpu.VMEM((10,) + lines.shape, F32),
    ]
    chunk_sizes = [own_width // 2] * 6 + [own_width] * 2 + [128]
    for order, size in zip(ORDERS, chunk_sizes):
        scratch += reduce_buffers(order, width, per_row, size)
    scratch += [
        pltpu.SemaphoreType.DMA((192,)),
        pltpu.SemaphoreType.DMA((192,)),
        pltpu.SemaphoreType.DMA((24,)),
    ]
    return pl.pallas_call(
        functools.partial(back_kernel, sizes),
        out_shape=tuple(jax.ShapeDtypeStruct(*out) for out in outs),
        in_specs=[in_vmem] * 8 + [smem] + [in_hbm] * len(saved),
        out_specs=(in_vmem,) * 8 + (in_hbm,) * 2,
        scratch_shapes=scratch,
        compiler_params=pltpu.CompilerParams(
            collective_id=2, has_side_effects=True, vmem_limit_bytes=61 * 2**20
        ),
    )(*values, *saved)


def finish_kernel(
    experts,
    gate_in,
    down_in,
    output_in,
    grad_in,
    query_in,
    key_in,
    value_in,
    out_in,
    small_in,
    diag_in,
    lane_ref,
    gate_out,
    up_out,
    down_out,
    output_out,
    grad_out,
    query_out,
    key_out,
    value_out,
    out_out,
    router_out,
    first_out,
    second_out,
    table_out,
):
    low = lax.axis_index("dp") % 2
    half = gate_out.shape[1] // 2
    own = pl.ds(pl.multiple_of(low * half, half), half)
    other = pl.ds(pl.multiple_of((1 - low) * half, half), half)
    for cols, slots in ((own, (0, 2, 4)), (other, (1, 3, 5))):
        gate_out[:, cols] = sum(gate_in[j, :, :half].astype(F32) for j in slots)
        up_out[:, cols] = sum(gate_in[j, :, half:].astype(F32) for j in slots)
    down_out[...] = sum(down_in[j].astype(F32) for j in range(down_in.shape[0]))

    @pl.when(pl.program_id(0) == 0)
    def _():
        for source, place in (
            (output_in, output_out),
            (grad_in, grad_out),
            (query_in, query_out),
            (key_in, key_out),
            (value_in, value_out),
            (out_in, out_out),
        ):
            place[...] = source[...]
        small = small_in[...]
        router_out[...] = small[:, :experts]
        turned = jnp.concatenate([small] * (128 // small.shape[0]), axis=0).T
        second_out[...] = turned[experts : experts + 1, : small.shape[0]]
        first_out[...] = turned[experts + 1 : experts + 2, : small.shape[0]]
        buckets, lanes = table_out.shape[0], lane_ref.shape[1]
        rows = lax.broadcasted_iota(jnp.int32, (buckets, lanes), 0)
        hot = jnp.where(rows == lane_ref[...], 1.0, 0.0)
        heads = diag_in.shape[0] * diag_in.shape[1]
        table_out[...] = lax.dot_general(
            hot,
            diag_in[...].reshape(heads, lanes),
            (((1,), (1,)), ((), ())),
            precision=lax.Precision.HIGHEST,
            preferred_element_type=F32,
        )


def finish(values, bucket_lanes, experts, table_shape):
    gate_in, down_in, output, grad_input, query, key, value, out, small, diag = values
    steps = 2
    rows, ff = gate_in.shape[1:]
    per_row = small.shape[0]
    fixed = lambda v: pl.BlockSpec(v.shape, lambda i: (0,) * len(v.shape))
    cut = lambda v: pl.BlockSpec(
        (v.shape[0], v.shape[1] // steps, v.shape[2]), lambda i: (0, i, 0)
    )
    outs = [
        jax.ShapeDtypeStruct((rows, ff), F32),
        jax.ShapeDtypeStruct((rows, ff), F32),
        jax.ShapeDtypeStruct(down_in.shape[1:], F32),
    ] + [jax.ShapeDtypeStruct(v.shape, v.dtype) for v in (output, grad_input, query, key, value, out)]
    small_outs = [
        jax.ShapeDtypeStruct((per_row, experts), F32),
        jax.ShapeDtypeStruct((1, per_row), F32),
        jax.ShapeDtypeStruct((1, per_row), F32),
        jax.ShapeDtypeStruct(table_shape, F32),
    ]
    sliced = lambda v: pl.BlockSpec((v.shape[0] // steps, v.shape[1]), lambda i: (i, 0))
    return pl.pallas_call(
        functools.partial(finish_kernel, experts),
        grid=(steps,),
        out_shape=tuple(outs + small_outs),
        in_specs=[cut(gate_in), cut(down_in)] + [fixed(v) for v in values[2:]] + [fixed(bucket_lanes)],
        out_specs=tuple([sliced(v) for v in outs[:3]] + [fixed(v) for v in outs[3:] + small_outs]),
        compiler_params=pltpu.CompilerParams(vmem_limit_bytes=60 * 2**20),
    )(*values, bucket_lanes)


def tuned_body(
    activations,
    cotangent,
    dealing,
    lengths,
    routes,
    buckets,
    w_query,
    w_key,
    w_value,
    w_out,
    w_router,
    norm_first,
    norm_second,
    bias_table,
    w_gate,
    w_up,
    w_down,
):
    micro, _, rows_dev, width = activations.shape
    seq = dealing.shape[2]
    bucket_count, head_count = bias_table.shape
    dp_count, ctx_count, expert_count = (lax.axis_size(name) for name in ALL)
    dp_index, ctx_index, expert_index = (lax.axis_index(name) for name in ALL)
    high, low = dp_index // 2, dp_index % 2
    heads = head_count // ctx_count
    head_size = width // head_count
    own_width = heads * head_size
    experts = w_router.shape[1]
    top_count = routes.shape[3]
    capacity = (5 * rows_dev * top_count + 4 * experts - 1) // (4 * experts)
    slots = -(-capacity // 16) * 16
    half_ff = w_gate.shape[2] // 2
    down_rows = w_down.shape[1]
    plane = dp_count * ctx_count
    plane_index = dp_index * ctx_count + ctx_index
    act = activations[:, 0]
    cot = cotangent[:, 0]
    deal = dealing[:, 0]
    length = lengths[:, 0]
    route = routes[:, 0]
    sizes = (heads, head_size, experts, capacity, slots)
    extras = jnp.concatenate([w_router, norm_first[:, None], norm_second[:, None]], axis=1)
    extras = jnp.pad(extras, ((0, 0), (0, 128 - extras.shape[1])))
    bucket_lanes = jnp.concatenate(
        [buckets[:1], jnp.full((seq,), -1, jnp.int32), buckets[:0:-1]]
    )[None, :]
    hidden, logits, mixed, cot_low, deal_column, route_column, lines, *saved = front(
        sizes,
        act,
        cot,
        deal,
        length,
        jnp.swapaxes(route, 1, 2),
        bucket_lanes,
        bias_table,
        (w_query, w_key, w_value, w_out),
        extras,
        w_gate[0],
        w_up[0],
        w_down[0],
    )
    (
        output,
        grad_input,
        grad_query,
        grad_key,
        grad_value,
        grad_out,
        small_sum,
        diag_all,
        gate_in,
        down_in,
    ) = back(
        sizes,
        (hidden, logits, mixed, cot_low, act, deal_column, route_column, lines, length),
        saved,
    )
    (
        grad_gate,
        grad_up,
        grad_down,
        output,
        grad_input,
        grad_query,
        grad_key,
        grad_value,
        grad_out,
        grad_router,
        grad_first,
        grad_second,
        grad_table,
    ) = finish(
        (
            gate_in,
            down_in,
            output,
            grad_input,
            grad_query,
            grad_key,
            grad_value,
            grad_out,
            small_sum,
            diag_all,
        ),
        bucket_lanes,
        experts,
        bias_table.shape,
    )
    return (
        output[:, None],
        grad_input[:, None],
        grad_query,
        grad_key,
        grad_value,
        grad_out,
        grad_router,
        grad_first[0],
        grad_second[0],
        grad_table,
        grad_gate[None],
        grad_up[None],
        grad_down[None],
    )


def body(*arguments):
    counts = tuple(lax.axis_size(name) for name in ALL)
    activations, w_query, bias_table, w_gate = (arguments[i] for i in (0, 6, 13, 14))
    own_width = activations.shape[3] // counts[1]
    fits = (
        counts == (4, 2, 4)
        and w_gate.shape[0] == 1
        and w_query.shape[0] % 16 == 0
        and 128 % w_query.shape[0] == 0
        and own_width % 128 == 0
        and bias_table.shape[1] % (8 * counts[1]) == 0
        and arguments[2].shape[2] % 128 == 0
        and arguments[4].shape[3] == 2
    )
    return (tuned_body if fits else plain_body)(*arguments)


def solution(mesh):
    tokens = P(None, ("dp", "experts"), "context", None)
    sequences = P(None, ("dp", "experts"))
    rows = P(("dp", "context", "experts"), None)
    gains = P(("dp", "context", "experts"))
    experts = P("experts", ("dp", "context"), None)
    placed = (
        (tokens, tokens, P(None, ("dp", "experts"), None), sequences, tokens, P())
        + (rows,) * 5
        + (gains, gains, P())
        + (experts,) * 3
    )
    return jax.shard_map(
        body,
        mesh=mesh,
        in_specs=placed,
        out_specs=(tokens, tokens) + (rows,) * 5 + (gains, gains, P()) + (experts,) * 3,
        check_vma=False,
    )
```

```python
import functools

import jax
import jax.numpy as jnp
from jax import lax
from jax.experimental import pallas as pl
from jax.experimental.pallas import tpu as pltpu
from jax.sharding import PartitionSpec as P

epsilon = 1e-06
masked_score = -1e30
ALL = ("dp", "context", "experts")
F32 = jnp.float32
BF16 = jnp.bfloat16


def dot_f32(spec, left, right):
    return jnp.einsum(spec, left, right, preferred_element_type=F32)


def swap(value, axis, offset):
    size = lax.axis_size(axis)
    return lax.ppermute(value, axis, [(i, i ^ offset) for i in range(size)])


def reorder(pieces, index):
    pieces = list(pieces)
    bit = 1
    while bit < len(pieces):
        flag = (index // bit) % 2 == 1
        pieces = [jnp.where(flag, pieces[j ^ bit], pieces[j]) for j in range(len(pieces))]
        bit *= 2
    return pieces


def reorder_lanes(value, blocks, index):
    return jnp.concatenate(reorder(jnp.split(value, blocks, axis=-1), index), axis=-1)


def toeplitz_bias(line, size):
    rows = jnp.broadcast_to(line, (size, 2 * size))
    return pltpu.roll(rows, 0, 1, stride=1, stride_axis=0)[:, :size]


def masked_scores(query, key, line, length, scale):
    size = query.shape[0]
    scores = lax.dot_general(query, key, (((1,), (1,)), ((), ())), preferred_element_type=F32)
    scores = scores * scale + toeplitz_bias(line, size)
    row_id = lax.broadcasted_iota(jnp.int32, (size, size), 0)
    col_id = lax.broadcasted_iota(jnp.int32, (size, size), 1)
    allowed = (row_id >= col_id) & (col_id < length)
    return jnp.where(allowed, scores, masked_score)


def soft(scores):
    top_score = jnp.max(scores, axis=-1, keepdims=True)
    raised = jnp.exp(scores - top_score)
    return raised / jnp.sum(raised, axis=-1, keepdims=True)


def attend_kernel(heads, head_size, length_ref, line_ref, qkv_ref, mixed_ref):
    scale = head_size ** (-0.5)
    width = heads * head_size
    length = length_ref[pl.program_id(0)]
    for head in range(heads):
        query = qkv_ref[0, :, head * head_size : (head + 1) * head_size]
        key = qkv_ref[0, :, width + head * head_size : width + (head + 1) * head_size]
        value = qkv_ref[0, :, 2 * width + head * head_size : 2 * width + (head + 1) * head_size]
        scores = masked_scores(query, key, line_ref[head : head + 1, :], length, scale)
        probs = soft(scores).astype(BF16)
        mixed = jnp.dot(probs, value, preferred_element_type=F32)
        mixed_ref[0, :, head * head_size : (head + 1) * head_size] = mixed.astype(BF16)


def attend(qkv, lines, lengths, heads):
    micro, seq, width = qkv.shape
    width = width // 3
    head_size = width // heads
    return pl.pallas_call(
        functools.partial(attend_kernel, heads, head_size),
        grid=(micro,),
        out_shape=jax.ShapeDtypeStruct((micro, seq, width), BF16),
        in_specs=[
            pl.BlockSpec(memory_space=pltpu.SMEM),
            pl.BlockSpec(lines.shape, lambda i: (0, 0)),
            pl.BlockSpec((1, seq, 3 * width), lambda i: (i, 0, 0)),
        ],
        out_specs=pl.BlockSpec((1, seq, width), lambda i: (i, 0, 0)),
        compiler_params=pltpu.CompilerParams(vmem_limit_bytes=32 * 2**20),
    )(lengths, lines, qkv)


def diagonal_sums(grad):
    size = grad.shape[0]
    wide = jnp.concatenate([grad, jnp.zeros_like(grad)], axis=1)
    rows = size
    while rows > 1:
        rows //= 2
        lower = pltpu.roll(wide[rows:], 2 * size - rows, 1)
        wide = wide[:rows] + lower
    return wide


def attend_back_kernel(
    heads, head_size, length_ref, line_ref, qkv_ref, grad_ref, out_ref, diag_ref
):
    scale = head_size ** (-0.5)
    width = heads * head_size
    length = length_ref[pl.program_id(0)]

    @pl.when(pl.program_id(0) == 0)
    def _():
        diag_ref[...] = jnp.zeros_like(diag_ref)

    for head in range(heads):
        at = [
            slice(part * width + head * head_size, part * width + (head + 1) * head_size)
            for part in range(3)
        ]
        query, key, value = (qkv_ref[0, :, part] for part in at)
        grad = grad_ref[0, :, at[0]]
        scores = masked_scores(query, key, line_ref[head : head + 1, :], length, scale)
        probs = soft(scores)
        prob_grad = lax.dot_general(
            grad, value, (((1,), (1,)), ((), ())), preferred_element_type=F32
        )
        delta = jnp.sum(probs * prob_grad, axis=-1, keepdims=True)
        score_grad = (probs * (prob_grad - delta)).astype(BF16)
        diag_ref[head : head + 1, :] += diagonal_sums(score_grad.astype(F32))
        query_grad = jnp.dot(score_grad, key, preferred_element_type=F32) * scale
        key_grad = (
            lax.dot_general(
                score_grad, query, (((0,), (0,)), ((), ())), preferred_element_type=F32
            )
            * scale
        )
        value_grad = lax.dot_general(
            probs.astype(BF16), grad, (((0,), (0,)), ((), ())), preferred_element_type=F32
        )
        out_ref[0, :, at[0]] = query_grad.astype(BF16)
        out_ref[0, :, at[1]] = key_grad.astype(BF16)
        out_ref[0, :, at[2]] = value_grad.astype(BF16)


def attend_back(qkv, grad, lines, lengths, heads):
    micro, seq, width = grad.shape
    head_size = width // heads
    return pl.pallas_call(
        functools.partial(attend_back_kernel, heads, head_size),
        grid=(micro,),
        out_shape=(
            jax.ShapeDtypeStruct(qkv.shape, BF16),
            jax.ShapeDtypeStruct(lines.shape, F32),
        ),
        in_specs=[
            pl.BlockSpec(memory_space=pltpu.SMEM),
            pl.BlockSpec(lines.shape, lambda i: (0, 0)),
            pl.BlockSpec((1, seq, 3 * width), lambda i: (i, 0, 0)),
            pl.BlockSpec((1, seq, width), lambda i: (i, 0, 0)),
        ],
        out_specs=(
            pl.BlockSpec((1, seq, 3 * width), lambda i: (i, 0, 0)),
            pl.BlockSpec(lines.shape, lambda i: (0, 0)),
        ),
        compiler_params=pltpu.CompilerParams(vmem_limit_bytes=32 * 2**20),
    )(lengths, lines, qkv, grad)


def halve(value, axis, bit, flag):
    kept = jnp.where(flag, value[1], value[0])
    sent = jnp.where(flag, value[0], value[1]).astype(BF16)
    return kept + swap(sent, axis, bit).astype(F32)


def scatter_sum(value, dp_index, expert_index):
    dp_count, ctx_count, expert_count = value.shape[:3]
    rest = value.shape[3:]
    count, bit = dp_count, 1
    while count > 1:
        shaped = value.reshape((count // 2, 2, -1))
        value = halve(jnp.moveaxis(shaped, 1, 0), "dp", bit, (dp_index // bit) % 2 == 1)
        count //= 2
        bit *= 2
    value = value.reshape((ctx_count, expert_count) + rest)
    count, bit = expert_count, 1
    while count > 1:
        shaped = value.reshape((ctx_count, count // 2, 2) + rest)
        value = halve(jnp.moveaxis(shaped, 2, 0), "experts", bit, (expert_index // bit) % 2 == 1)
        count //= 2
        bit *= 2
    return value.reshape((ctx_count,) + rest)


MESH = pl.DeviceIdType.MESH


def flip(index, bit):
    return index + bit - 2 * bit * ((index // bit) % 2)


def greet(targets):
    barrier = pltpu.get_barrier_semaphore()
    for target in targets:
        pl.semaphore_signal(barrier, inc=1, device_id=target, device_id_type=MESH)
    pl.semaphore_wait(barrier, len(targets))


def remote(source, place, sends, receives, target):
    return pltpu.make_async_remote_copy(
        src_ref=source,
        dst_ref=place,
        send_sem=sends,
        recv_sem=receives,
        device_id=target,
        device_id_type=MESH,
    )


def plain_sums(qkv_total, out_total, router_total, first_total, second_total, own_width):
    width, experts = router_total.shape
    dp_count, ctx_count, expert_count = (lax.axis_size(name) for name in ALL)
    dp_index, ctx_index, expert_index = (lax.axis_index(name) for name in ALL)
    owners = (dp_count, ctx_count, expert_count, -1)
    out_pack = jnp.concatenate([out_total, router_total, second_total[:, None]], axis=1)
    out_pack = jnp.pad(out_pack, ((0, 0), (0, width + 128 - out_pack.shape[1])))
    out_pack = scatter_sum(
        out_pack.reshape(owners + (out_pack.shape[1],)), dp_index, expert_index
    )
    qkv_pack = jnp.pad(
        jnp.concatenate([qkv_total, first_total[:, None]], axis=1), ((0, 0), (0, 127))
    )
    qkv_pack = scatter_sum(
        qkv_pack.reshape(owners + (qkv_pack.shape[1],)), dp_index, expert_index
    )

    def across(value):
        parts = reorder([value[c] for c in range(ctx_count)], ctx_index)
        return [parts[0]] + [
            swap(parts[k].astype(BF16), "context", k).astype(F32) for k in range(1, ctx_count)
        ]

    out_sum = sum(across(out_pack))
    qkv_parts = across(qkv_pack)
    grad_first = sum(part[:, 3 * own_width] for part in qkv_parts)
    qkv_parts = reorder(qkv_parts, ctx_index)
    grads = tuple(
        jnp.concatenate(
            [part[:, i * own_width : (i + 1) * own_width] for part in qkv_parts], axis=1
        )
        for i in range(3)
    )
    return grads + (
        out_sum[:, :width],
        out_sum[:, width : width + experts],
        grad_first,
        out_sum[:, width + experts],
    )


def norm_pull(features, inverse, gain, grad):
    lifted = gain * grad
    mean_part = jnp.mean(lifted * features, axis=-1, keepdims=True)
    back = inverse * lifted - features * (inverse * inverse * inverse) * mean_part
    gain_grad = jnp.sum(grad * features * inverse, axis=(0, 1))
    return back, gain_grad


def gelu_parts(pre):
    root = 0.7978845608028654
    cubic = 0.044715
    square = pre * pre
    wave = jnp.tanh(root * (pre + cubic * pre * square))
    value = 0.5 * pre * (1.0 + wave)
    slope = 0.5 * (1.0 + wave) + 0.5 * pre * (1.0 - wave * wave) * root * (
        1.0 + 3.0 * cubic * square
    )
    return value, slope


def down_routes(dp_count, ctx_count, expert_count, core, ctx_offset):
    pairs = []
    for dp in range(dp_count):
        for ctx in range(ctx_count):
            for expert in range(expert_count):
                high, low = dp // 2, dp % 2
                to_high = high if low == core else high ^ 1
                target = ((to_high * 2 + high) * ctx_count + (ctx ^ ctx_offset)) * expert_count
                pairs.append(((dp * ctx_count + ctx) * expert_count + expert, target + expert))
    return pairs


def plain_body(
    activations,
    cotangent,
    dealing,
    lengths,
    routes,
    buckets,
    w_query,
    w_key,
    w_value,
    w_out,
    w_router,
    norm_first,
    norm_second,
    bias_table,
    w_gate,
    w_up,
    w_down,
):
    micro, _, rows_dev, width = activations.shape
    seq = dealing.shape[2]
    bucket_count, head_count = bias_table.shape
    dp_count, ctx_count, expert_count = (lax.axis_size(name) for name in ALL)
    dp_index, ctx_index, expert_index = (lax.axis_index(name) for name in ALL)
    high, low = dp_index // 2, dp_index % 2
    heads = head_count // ctx_count
    head_size = width // head_count
    own_width = heads * head_size
    experts = w_router.shape[1]
    top_count = routes.shape[3]
    capacity = (5 * rows_dev * top_count + 4 * experts - 1) // (4 * experts)
    slots = -(-capacity // 16) * 16
    ff = w_gate.shape[2]
    half_ff = ff // 2
    weight_rows = w_query.shape[0]
    plane = dp_count * ctx_count
    plane_index = dp_index * ctx_count + ctx_index
    act = activations[:, 0]
    cot = cotangent[:, 0]
    deal = dealing[:, 0]
    length = lengths[:, 0]
    route = routes[:, 0]

    extras = jnp.concatenate(
        [w_router, norm_first[:, None], norm_second[:, None]], axis=1
    )
    extras = jnp.pad(extras, ((0, 0), (0, 128 - extras.shape[1])))
    column_parts = [
        jnp.split(weight, ctx_count, axis=1) for weight in (w_query, w_key, w_value)
    ]
    packs = [
        jnp.concatenate([part[c] for part in column_parts] + [extras], axis=1)
        for c in range(ctx_count)
    ]
    packs = reorder(packs, ctx_index)
    packs = [packs[0]] + [swap(packs[k], "context", k) for k in range(1, ctx_count)]
    packs = jnp.stack(reorder(packs, ctx_index))
    dense = lax.all_gather(packs, ("dp", "experts"), axis=0, tiled=False)
    dense = dense.reshape((dp_count, expert_count) + packs.shape)
    dense = jnp.transpose(dense, (0, 2, 1, 3, 4)).reshape(width, -1)
    qkv_w = dense[:, : 3 * own_width]
    router_w = dense[:, 3 * own_width : 3 * own_width + experts]
    gain_one = dense[:, 3 * own_width + experts].astype(F32)
    gain_two = dense[:, 3 * own_width + experts + 1].astype(F32)
    out_w = lax.all_gather(w_out, ALL, axis=0, tiled=True)

    gate_up = [
        jnp.concatenate([w_gate[0, :, h * half_ff : (h + 1) * half_ff], w_up[0, :, h * half_ff : (h + 1) * half_ff]], axis=1)
        for h in range(2)
    ]
    halves = reorder(gate_up, low)
    gate_blocks = []
    for j in range(plane):
        dp_offset, ctx_offset = j // ctx_count, j % ctx_count
        piece = halves[dp_offset % 2]
        if dp_offset:
            piece = swap(piece, "dp", dp_offset)
        if ctx_offset:
            piece = swap(piece, "context", ctx_offset) if not dp_offset else piece
        gate_blocks.append(piece)
    for j in range(plane):
        dp_offset, ctx_offset = j // ctx_count, j % ctx_count
        if dp_offset and ctx_offset:
            gate_blocks[j] = swap(gate_blocks[dp_offset * ctx_count], "context", ctx_offset)
    gate_up_w = jnp.concatenate(gate_blocks, axis=0)
    down_w = jnp.zeros((half_ff, width), BF16)
    down_rows = w_down.shape[1]
    for ctx_offset in range(ctx_count):
        for core in range(2):
            pairs = down_routes(dp_count, ctx_count, expert_count, core, ctx_offset)
            piece = lax.ppermute(w_down[0], ALL, pairs)
            from_core = jnp.where(low == high, core, 1 - core)
            place = (from_core * ctx_count + (ctx_index ^ ctx_offset)) * down_rows
            down_w = lax.dynamic_update_slice(down_w, piece, (place, 0))

    act_all = jnp.concatenate(
        reorder([act] + [swap(act, "context", k) for k in range(1, ctx_count)], ctx_index), axis=1
    )
    cot_all = jnp.concatenate(
        reorder([cot] + [swap(cot, "context", k) for k in range(1, ctx_count)], ctx_index), axis=1
    )
    position_ids = jnp.arange(seq, dtype=jnp.int32)
    slot_blocks = [
        lax.dynamic_slice_in_dim(deal, (ctx_index ^ k) * rows_dev, rows_dev, axis=1)
        for k in range(ctx_count)
    ]
    hot = [
        (block[:, :, None] == position_ids[None, None, :]).astype(BF16) for block in slot_blocks
    ]
    my_positions = ctx_index * rows_dev + jnp.arange(rows_dev, dtype=jnp.int32)
    hot_mine = [
        (block[:, :, None] == my_positions[None, None, :]).astype(BF16) for block in slot_blocks
    ]
    live = slot_blocks[0] < length[:, None]
    live_rows = live.astype(F32)[:, :, None]
    bucket_hot = (buckets[:, None] == jnp.arange(bucket_count)[None, :]).astype(BF16)
    own_table = lax.dynamic_slice_in_dim(bias_table, ctx_index * heads, heads, axis=1)
    lookup = dot_f32("sb,bh->hs", bucket_hot, own_table)
    lines = jnp.concatenate(
        [lookup[:, :1], jnp.zeros((heads, seq), F32), lookup[:, :0:-1]], axis=1
    )

    rows_all = act_all.astype(F32)
    inverse_one = lax.rsqrt(jnp.mean(rows_all * rows_all, axis=-1, keepdims=True) + epsilon)
    normed = (rows_all * inverse_one * gain_one).astype(BF16)
    qkv = dot_f32("mpd,dw->mpw", normed, qkv_w).astype(BF16)
    mixed_own = attend(qkv, lines, length, heads)
    mixed_parts = [
        dot_f32("msp,mpw->msw", hot[k], mixed_own).astype(BF16) for k in range(ctx_count)
    ]
    mixed_parts = [mixed_parts[0]] + [
        swap(mixed_parts[k], "context", k) for k in range(1, ctx_count)
    ]
    mixed = jnp.concatenate(reorder(mixed_parts, ctx_index), axis=-1)

    rows_in = dot_f32("msp,mpd->msd", hot[0], act_all)
    cot_rows = dot_f32("msp,mpd->msd", hot[0], cot_all)
    branch = dot_f32("msi,io->mso", mixed, out_w)
    hidden = rows_in + branch * live_rows
    inverse_two = lax.rsqrt(jnp.mean(hidden * hidden, axis=-1, keepdims=True) + epsilon)
    normed_two = (hidden * inverse_two * gain_two).astype(BF16)
    logits = dot_f32("msd,de->mse", normed_two, router_w)
    route_hot = (route[..., None] == jnp.arange(experts)).astype(F32)
    chosen = jnp.sum(route_hot * logits[:, :, None, :], axis=3)
    gate_probs = jax.nn.softmax(chosen, axis=-1)

    flat_hot = (route_hot * live_rows[..., None]).reshape(micro, rows_dev * top_count, experts)
    pair_ids = jnp.arange(rows_dev * top_count)
    before = (pair_ids[:, None] > pair_ids[None, :]).astype(BF16)
    earlier = dot_f32("ab,mbe->mae", before, flat_hot.astype(BF16))
    rank = jnp.sum(earlier * flat_hot, axis=2).astype(jnp.int32).reshape(route.shape)
    kept = live[:, :, None] & (rank < capacity)
    target = jnp.where(kept, (route ^ expert_index) * slots + rank, -1)
    place_ids = jnp.arange(experts * slots, dtype=jnp.int32)
    pick = [
        (target[:, None, :, j] == place_ids[None, :, None]) for j in range(top_count)
    ]
    pick_any = functools.reduce(jnp.logical_or, pick).astype(BF16)
    pick_bf = [p.astype(BF16) for p in pick]
    prob_rows = sum(
        jnp.sum(jnp.where(pick[j], gate_probs[:, None, :, j], 0.0), axis=2)
        for j in range(top_count)
    )

    def by_expert(value):
        shaped = value.reshape((micro, experts, slots) + value.shape[2:])
        return jnp.moveaxis(shaped, 1, 0)

    def exchange(value):
        parts = [value[0]] + [swap(value[k], "experts", k) for k in range(1, expert_count)]
        return jnp.stack(parts)

    normed_rel = reorder_lanes(normed_two, plane, plane_index)
    sent_rows = by_expert(dot_f32("mrs,msd->mrd", pick_any, normed_rel).astype(BF16))
    sent_up = by_expert(
        dot_f32("mrs,msd->mrd", pick_any, cot_rows.astype(BF16)).astype(BF16)
    )
    row_count = expert_count * micro * slots
    own_x = exchange(sent_rows).reshape(row_count, width)
    own_u = exchange(sent_up).reshape(row_count, width)
    own_p = exchange(by_expert(prob_rows)).reshape(row_count, 1)
    own_g = (own_p * own_u.astype(F32)).astype(BF16)

    def core_swap(value):
        blocks = jnp.split(value, plane, axis=-1)
        return jnp.concatenate([blocks[j ^ ctx_count] for j in range(plane)], axis=-1)

    all_x = jnp.concatenate([own_x, core_swap(swap(own_x, "dp", 1))], axis=0)
    all_g = jnp.concatenate([own_g, swap(own_g, "dp", 1)], axis=0)

    pre_up = dot_f32("rd,df->rf", all_x, gate_up_w)
    gelu_value, gelu_slope = gelu_parts(pre_up[:, :half_ff])
    up_part = pre_up[:, half_ff:]
    activated = (gelu_value * up_part).astype(BF16)
    act_grad = dot_f32("rd,fd->rf", all_g, down_w)
    pre_grad = (act_grad * up_part * gelu_slope).astype(BF16)
    up_grad = (act_grad * gelu_value).astype(BF16)
    both_grad = jnp.concatenate([pre_grad, up_grad], axis=1)
    back_part = dot_f32("rf,df->rd", both_grad, gate_up_w)
    out_part = dot_f32("rf,fd->rd", activated, down_w)
    out_own = (
        out_part[:row_count] + swap(out_part[row_count:].astype(BF16), "dp", 1).astype(F32)
    ).astype(BF16)
    back_own = (
        back_part[:row_count]
        + swap(core_swap(back_part[row_count:].astype(BF16)), "dp", 1).astype(F32)
    ).astype(BF16)
    gate_rows = jnp.sum(own_u.astype(F32) * out_own.astype(F32), axis=-1)

    def to_source(value):
        parts = value.reshape((expert_count, micro, slots) + value.shape[1:])
        parts = exchange(parts)
        return jnp.moveaxis(parts, 0, 1).reshape((micro, experts * slots) + value.shape[1:])

    back_rows = to_source(back_own)
    gate_back = to_source(gate_rows)
    out_rows = to_source(out_own)

    gate_up_total = dot_f32("rd,rf->df", all_x, both_grad)
    down_total = dot_f32("rf,rd->fd", activated, all_g)

    gate_up_sums = [0.0, 0.0]
    for j in range(plane):
        dp_offset, ctx_offset = j // ctx_count, j % ctx_count
        block = gate_up_total[j * (width // plane) : (j + 1) * (width // plane)].astype(BF16)
        pairs = [
            (
                (d * ctx_count + c) * expert_count + e,
                ((d ^ dp_offset) * ctx_count + (c ^ ctx_offset)) * expert_count + e,
            )
            for d in range(dp_count)
            for c in range(ctx_count)
            for e in range(expert_count)
        ]
        if j:
            block = lax.ppermute(block, ALL, pairs)
        gate_up_sums[dp_offset % 2] = gate_up_sums[dp_offset % 2] + block.astype(F32)
    first_half, second_half = reorder(gate_up_sums, low)
    grad_gate = jnp.concatenate([first_half[:, :half_ff], second_half[:, :half_ff]], axis=1)
    grad_up = jnp.concatenate([first_half[:, half_ff:], second_half[:, half_ff:]], axis=1)
    grad_down = 0.0
    for ctx_offset in range(ctx_count):
        for core in range(2):
            pairs = down_routes(dp_count, ctx_count, expert_count, core, ctx_offset)
            from_core = jnp.where(low == high, core, 1 - core)
            place = (from_core * ctx_count + (ctx_index ^ ctx_offset)) * down_rows
            piece = lax.dynamic_slice_in_dim(down_total, place, down_rows, axis=0).astype(BF16)
            arrived = lax.ppermute(piece, ALL, [(b, a) for a, b in pairs])
            grad_down = grad_down + arrived.astype(F32)

    pair_out = [dot_f32("mrs,mrd->msd", pick_bf[j], out_rows) for j in range(top_count)]
    final = hidden + sum(gate_probs[:, :, j, None] * pair_out[j] for j in range(top_count))
    final = final.astype(BF16)
    gate_grad = jnp.stack(
        [
            jnp.sum(jnp.where(pick[j], gate_back[:, :, None], 0.0), axis=1)
            for j in range(top_count)
        ],
        axis=-1,
    )
    chosen_grad = gate_probs * (
        gate_grad - jnp.sum(gate_probs * gate_grad, axis=-1, keepdims=True)
    )
    logit_grad = jnp.sum(route_hot * chosen_grad[..., None], axis=2).astype(BF16)
    normed_grad = reorder_lanes(
        dot_f32("mrs,mrd->msd", pick_any, back_rows), plane, plane_index
    ) + dot_f32("mse,de->msd", logit_grad, router_w)
    router_total = dot_f32("msd,mse->de", normed_two, logit_grad)
    hidden_norm_grad, second_total = norm_pull(hidden, inverse_two, gain_two, normed_grad)
    hidden_grad = cot_rows + hidden_norm_grad
    branch_grad = (hidden_grad * live_rows).astype(BF16)
    hidden_low = hidden_grad.astype(BF16)
    out_total = dot_f32("msi,mso->io", mixed, branch_grad)
    mixed_grad = dot_f32("mso,io->msi", branch_grad, out_w).astype(BF16)
    grad_parts = reorder(jnp.split(mixed_grad, ctx_count, axis=-1), ctx_index)
    grad_parts = [grad_parts[0]] + [
        swap(grad_parts[k], "context", k) for k in range(1, ctx_count)
    ]
    mixed_back = sum(
        dot_f32("msp,msw->mpw", hot[k], grad_parts[k]) for k in range(ctx_count)
    ).astype(BF16)
    qkv_grad, diagonals = attend_back(qkv, mixed_back, lines, length, heads)
    qkv_total = dot_f32("mpd,mpw->dw", normed, qkv_grad)
    first_part = dot_f32("mpw,dw->mpd", qkv_grad, qkv_w)
    first_total = jnp.sum(first_part * rows_all * inverse_one, axis=(0, 1))
    blocks = [
        lax.dynamic_slice_in_dim(first_part, (ctx_index ^ k) * rows_dev, rows_dev, axis=1)
        for k in range(ctx_count)
    ]
    first_grad = blocks[0] + sum(
        swap(blocks[k].astype(BF16), "context", k).astype(F32) for k in range(1, ctx_count)
    )

    def to_positions(value):
        parts = [value] + [swap(value, "context", k) for k in range(1, ctx_count)]
        return sum(dot_f32("msp,msd->mpd", hot_mine[k], parts[k]) for k in range(ctx_count))

    rows_mine = act.astype(F32)
    inverse_mine = lax.rsqrt(jnp.mean(rows_mine * rows_mine, axis=-1, keepdims=True) + epsilon)
    rows_back, _ = norm_pull(rows_mine, inverse_mine, gain_one, first_grad)
    grad_input = (to_positions(hidden_low) + rows_back).astype(BF16)[:, None]
    output = to_positions(final).astype(BF16)[:, None]

    sums = plain_sums(
        qkv_total, out_total, router_total, first_total, second_total, own_width
    )
    grad_query, grad_key, grad_value, grad_out, grad_router, grad_first, grad_second = sums
    diag_all = lax.all_gather(
        lax.psum(diagonals, ("dp", "experts")), "context", axis=0, tiled=True
    )
    offsets = jnp.concatenate([diag_all[:, :1], diag_all[:, : seq : -1]], axis=1)
    grad_table = jnp.einsum(
        "hs,sb->bh", offsets, bucket_hot.astype(F32), precision=lax.Precision.HIGHEST
    )
    return (
        output,
        grad_input,
        grad_query,
        grad_key,
        grad_value,
        grad_out,
        grad_router,
        grad_first,
        grad_second,
        grad_table,
        grad_gate[None],
        grad_up[None],
        grad_down[None],
    )


class Wires:
    def __init__(self, sends, receives, homes):
        self.sends, self.receives, self.homes = sends, receives, homes
        self.used, self.used_home = 0, 0

    def take(self):
        self.used += 1
        return self.used - 1

    def copy(self, source, place, peer, index):
        return remote(source, place, self.sends.at[index], self.receives.at[index], peer)

    def home(self, source, place):
        copy = pltpu.make_async_copy(source, place, self.homes.at[self.used_home])
        self.used_home += 1
        return copy


class Spread:
    def __init__(self, wires, buf, ctx_axis):
        self.wires, self.buf = wires, buf
        dp, ctx, exp = (lax.axis_index(name) for name in ALL)
        self.high, self.low, self.exp = dp // 2, dp % 2, exp
        self.last = lax.axis_size("experts") - 1
        self.core_peer = (flip(dp, 1), ctx, exp)
        self.x_peer = (flip(dp, 2), ctx, exp)
        self.up_peer = (dp, ctx, jnp.minimum(exp + 1, self.last))
        self.down_peer = (dp, ctx, jnp.maximum(exp - 1, 0))
        self.labels = [(0, 0)] + [(h, d) for h in range(1, self.last + 1) for d in (1, -1)]
        self.z_wire, self.x_wire, self.own_wire, self.far_wire = (
            {label: wires.take() for label in self.labels} for _ in range(4)
        )

    def block(self, label):
        hop, way = label
        return jnp.clip(self.exp - hop * way, 0, self.last) if hop else self.exp

    def when(self, label):
        hop, way = label
        if hop == 0:
            return lambda f: f()
        here = self.exp - hop * way
        return pl.when((here >= 0) & (here <= self.last))

    def can_send(self, label, act):
        hop, way = label
        held = self.exp - (hop - 1) * way
        ahead = self.exp + way
        pl.when((held >= 0) & (held <= self.last) & (ahead >= 0) & (ahead <= self.last))(act)

    def z_copy(self, label):
        hop, way = label
        held = jnp.clip(self.exp - (hop - 1) * way, 0, self.last)
        part = self.buf.at[self.high, self.low, :, held]
        peer = self.up_peer if way == 1 else self.down_peer
        return self.wires.copy(part, part, peer, self.z_wire[label])

    def part_copy(self, label, high, wire, peer):
        part = self.buf.at[high, self.low, :, self.block(label)]
        return self.wires.copy(part, part, peer, wire[label])

    def x_copy(self, label):
        return self.part_copy(label, self.high, self.x_wire, self.x_peer)

    def own_copy(self, label):
        return self.part_copy(label, self.high, self.own_wire, self.core_peer)

    def far_copy(self, label):
        return self.part_copy(label, 1 - self.high, self.far_wire, self.core_peer)

    def spread(self, label):
        self.x_copy(label).start()
        self.own_copy(label).start()

    def begin(self):
        for way in (1, -1):
            self.can_send((1, way), lambda way=way: self.z_copy((1, way)).start())
        self.spread((0, 0))

    def hop(self, hop):
        for way in (1, -1):
            label = (hop, way)

            @self.when(label)
            def _(label=label):
                part = self.buf.at[self.high, self.low, :, self.block(label)]
                self.wires.copy(part, part, self.up_peer, self.z_wire[label]).wait_recv()

            if hop < self.last:
                nxt = (hop + 1, way)
                self.can_send(nxt, lambda nxt=nxt: self.z_copy(nxt).start())

            @self.when(label)
            def _(label=label):
                self.spread(label)

        for label in self.labels:
            if label[0] == hop - 1:
                self.pass_far(label)

    def pass_far(self, label):
        @self.when(label)
        def _():
            self.x_copy(label).wait_recv()
            self.far_copy(label).start()

    def end(self):
        for label in self.labels:
            if label[0] == self.last:
                self.pass_far(label)
        for label in self.labels:

            @self.when(label)
            def _(label=label):
                self.own_copy(label).wait_recv()
                self.far_copy(label).wait_recv()

    def drain(self):
        for label in self.labels:
            if label[0]:
                self.can_send(label, lambda label=label: self.z_copy(label).wait_send())

            @self.when(label)
            def _(label=label):
                self.x_copy(label).wait_send()
                self.own_copy(label).wait_send()
                self.far_copy(label).wait_send()


def front_kernel(
    sizes,
    act_ref,
    cot_ref,
    deal_lanes,
    length_ref,
    route_lanes,
    bucket_lanes,
    bias_ref,
    query_ref,
    key_ref,
    value_ref,
    out_ref,
    extra_ref,
    gate_ref,
    up_ref,
    down_ref,
    hidden_ref,
    logit_ref,
    mixed,
    cot_rows_ref,
    deal_ref,
    route_ref,
    line_ref,
    dense_save,
    out_save,
    act_save,
    normed_save,
    qkv_save,
    x_save,
    u_save,
    g_save,
    gate_save,
    down_save,
    both_save,
    activated_save,
    dense,
    out_w,
    act_all,
    normed_ref,
    qkv_ref,
    all_x,
    all_u,
    all_p,
    all_g,
    gate_up,
    down,
    both,
    activated,
    cot_all,
    mixed_own,
    mixed_sent,
    sent_x,
    sent_u,
    sent_p,
    line_all,
    sends,
    receives,
    homes,
):
    heads, head_size, experts, capacity, slots = sizes
    micro, rows_dev, width = act_ref.shape
    own_width = heads * head_size
    half = gate_ref.shape[1] // 2
    dp, ctx, exp = (lax.axis_index(name) for name in ALL)
    high, low = dp // 2, dp % 2
    block = dp * 2 + ctx
    core_peer, x_peer, x_core = ((flip(dp, 1), ctx, exp), (flip(dp, 2), ctx, exp), (3 - dp, ctx, exp))
    x_core = (flip(flip(dp, 2), 1), ctx, exp)
    y_peer, y_core = (dp, 1 - ctx, exp), (flip(dp, 1), 1 - ctx, exp)
    z_peers = [None] + [(dp, ctx, flip(exp, 1)), (dp, ctx, flip(exp, 2)), (dp, ctx, 3 - exp)]
    z_index = [exp, flip(exp, 1), flip(exp, 2), 3 - exp]
    greet([core_peer, x_peer, x_core, y_peer, y_core] + z_peers[1:])
    wires = Wires(sends, receives, homes)
    drains = []
    home_copies = []

    def send(source, place, peer):
        copy = wires.copy(source, place, peer, wires.take())
        copy.start()
        drains.append(copy)
        return copy

    def multiple(index, size):
        return pl.ds(pl.multiple_of(index * size, size), size)

    def save(source, place):
        copy = wires.home(source, place)
        copy.start()
        home_copies.append(copy)

    mine, other = multiple(ctx, own_width), multiple(1 - ctx, own_width)
    first = []
    for i, ref in enumerate((query_ref, key_ref, value_ref)):
        place = dense.at[high, low, ctx, exp, :, i * own_width : (i + 1) * own_width]
        first.append(send(ref.at[:, other], place, y_peer))
    first.append(send(extra_ref, dense.at[high, low, ctx, exp, :, 3 * own_width :], y_peer))
    out_first = send(out_ref, out_w.at[high, low, ctx, exp], y_peer)
    here = multiple(ctx, rows_dev)
    act_first = send(act_ref, act_all.at[:, here], y_peer)
    def gate_sends(core, peer):
        cols = multiple(core, half)
        return [
            send(gate_ref.at[:, cols], gate_up.at[block, :, 0:half], peer),
            send(up_ref.at[:, cols], gate_up.at[block, :, half:], peer),
        ]

    own_gate = []
    for ref, start in ((gate_ref, 0), (up_ref, half)):
        copy = wires.home(ref.at[:, multiple(low, half)], gate_up.at[block, :, start : start + half])
        copy.start()
        own_gate.append(copy)

    for i, ref in enumerate((query_ref, key_ref, value_ref)):
        dense[high, low, ctx, exp, :, i * own_width : (i + 1) * own_width] = ref[:, mine]
    dense[high, low, ctx, exp, :, 3 * own_width :] = extra_ref[...]
    out_w[high, low, ctx, exp] = out_ref[...]
    act_all[:, here, :] = act_ref[...]
    cot_all[:, here, :] = cot_ref[...]

    spread = Spread(wires, dense, 2)
    spread_out = Spread(wires, out_w, 2)
    for copy in first:
        copy.wait_recv()
    spread.begin()
    cot_first = send(cot_ref, cot_all.at[:, here], y_peer)
    from_y_core = gate_sends(1 - low, y_core)
    from_y = gate_sends(low, y_peer)
    from_core = gate_sends(1 - low, core_peer)

    spread.hop(1)

    own_down = low * 2 + ctx
    home_down = wires.home(down_ref, down.at[own_down])
    down_wire = {name: wires.take() for name in ("core", "x", "xc", "y", "yc", "rx", "ry")}
    at_home = low == high

    def down_copy(name, peer, source=None):
        source = down_ref if source is None else source
        return wires.copy(source, down.at[own_down], peer, down_wire[name])

    down_sends = [
        ("core", core_peer, False),
        ("x", x_peer, True),
        ("xc", x_core, False),
        ("y", y_peer, True),
        ("yc", y_core, False),
    ]

    def down_start():
        @pl.when(at_home)
        def _():
            home_down.start()

        for name, peer, straight in down_sends:
            pl.when(at_home == straight)(lambda name=name, peer=peer: down_copy(name, peer).start())

    def as_column(line):
        return jnp.broadcast_to(line.astype(F32), (128, line.shape[1])).T[:, 0:1].astype(jnp.int32)

    for m in range(micro):
        deal_ref[m] = as_column(deal_lanes[m : m + 1, :])
        for j in range(2):
            route_ref[m, :, j : j + 1] = as_column(route_lanes[m, j : j + 1, :])
    bucket_rows = lax.broadcasted_iota(
        jnp.int32, (bias_ref.shape[0], bucket_lanes.shape[1]), 0
    )
    bucket_hot = jnp.where(bucket_rows == bucket_lanes[...], 1.0, 0.0).astype(BF16)
    line_all[...] = dot_rows(bias_ref[...], bucket_hot)
    line_ref[...] = line_all[pl.ds(pl.multiple_of(ctx * heads, heads), heads), :]

    lane = lax.broadcasted_iota(jnp.int32, (rows_dev, 128), 1)
    lane_f = lane.astype(F32)
    row_id = lax.broadcasted_iota(jnp.int32, (rows_dev, rows_dev), 0)
    col_id = lax.broadcasted_iota(jnp.int32, (rows_dev, rows_dev), 1)
    before = (row_id > col_id).astype(BF16)
    seq = deal_ref.shape[1]
    seq_lane = lax.broadcasted_iota(jnp.int32, (rows_dev, seq), 1)

    def hot(m, k):
        index = ctx if k == 0 else 1 - ctx
        return (deal_ref[m, multiple(index, rows_dev), :] == seq_lane).astype(BF16)

    def live_slots(m):
        return deal_ref[m, here, :] < length_ref[m]

    def ranks(m):
        live = live_slots(m)
        hots = [(route_ref[m, :, j : j + 1] == lane) for j in range(2)]
        used = jnp.where((hots[0] | hots[1]) & live, 1.0, 0.0).astype(BF16)
        earlier = jnp.dot(before, used, preferred_element_type=F32)
        found = []
        for j in range(2):
            rank = jnp.sum(jnp.where(hots[j], earlier, 0.0), axis=1, keepdims=True)
            found.append(jnp.where(live & (rank < capacity), rank, -1.0))
        return found

    def picks(m, k, rank):
        return [
            (route_ref[m, :, j : j + 1] == z_index[k]) & (rank[j] == lane_f) for j in range(2)
        ]

    def as_rows(pick, value):
        chosen = lax.dot_general(
            pick, value, (((0,), (0,)), ((), ())), preferred_element_type=F32
        )
        return chosen[:slots].astype(BF16)

    spread.hop(2)
    rank_of = [ranks(m) for m in range(micro)]
    act_first.wait_recv()
    spread.hop(3)
    cot_first.wait_recv()
    pick_of = {}
    for m in range(micro):
        hot_mine = hot(m, 0)
        cot_rows = jnp.dot(hot_mine, cot_all[m], preferred_element_type=F32).astype(BF16)
        cot_rows_ref[m] = cot_rows
        for k in range(experts):
            pick = picks(m, k, rank_of[m])
            pick_any = jnp.where(pick[0] | pick[1], 1.0, 0.0).astype(BF16)
            rows = as_rows(pick_any, cot_rows)
            if k == 0:
                all_u[0, 0, m] = rows
            else:
                sent_u[k - 1, m] = rows
    out_first.wait_recv()
    spread.end()
    from_x = gate_sends(low, x_peer)
    from_x_core = gate_sends(1 - low, x_core)
    spread_out.begin()
    save(dense, dense_save)
    save(act_all, act_save)
    u_first, u_core = {}, []

    def send_u(m):
        for k in range(1, experts):
            u_first[k, m] = send(sent_u.at[k - 1, m], all_u.at[0, k, m], z_peers[k])
        u_core.append(send(all_u.at[0, 0, m], all_u.at[1, 0, m], core_peer))

    def pass_u(m):
        for k in range(1, experts):
            u_first[k, m].wait_recv()
            u_core.append(send(all_u.at[0, k, m], all_u.at[1, k, m], core_peer))

    send_u(0)

    extras = dense[:, :, :, :, :, 3 * own_width :].reshape(width, 128).astype(F32)
    turned = extras.T
    gain_one, gain_two = turned[experts : experts + 1], turned[experts + 1 : experts + 2]
    for m in range(micro):
        rows = act_all[m].astype(F32)
        inverse = lax.rsqrt(jnp.mean(rows * rows, axis=-1, keepdims=True) + epsilon)
        normed_ref[m] = (rows * inverse * gain_one).astype(BF16)
    for i in range(3):
        weight = dense[:, :, :, :, :, i * own_width : (i + 1) * own_width].reshape(width, own_width)
        for m in range(micro):
            qkv_ref[m, :, i * own_width : (i + 1) * own_width] = jnp.dot(
                normed_ref[m], weight, preferred_element_type=F32
            ).astype(BF16)
    spread_out.hop(1)

    scale = head_size ** (-0.5)
    mixed_first = []
    save(normed_ref, normed_save)
    save(qkv_ref, qkv_save)
    for m in range(micro):
        length = length_ref[m]
        for head in range(heads):
            at = [
                slice(part * own_width + head * head_size, part * own_width + (head + 1) * head_size)
                for part in range(3)
            ]
            scores = masked_scores(
                qkv_ref[m, :, at[0]], qkv_ref[m, :, at[1]], line_ref[head : head + 1, :], length, scale
            )
            probs = soft(scores).astype(BF16)
            mixed_own[:, at[0]] = jnp.dot(
                probs, qkv_ref[m, :, at[2]], preferred_element_type=F32
            ).astype(BF16)
        own = mixed_own[...]
        mixed_sent[m] = jnp.dot(hot(m, 1), own, preferred_element_type=F32).astype(BF16)
        mixed_first.append(send(mixed_sent.at[m], mixed.at[m, :, mine], y_peer))
        mixed[m, :, mine] = jnp.dot(hot(m, 0), own, preferred_element_type=F32).astype(BF16)
        spread_out.hop(2 + m)
    spread_out.end()

    router_w = dense[:, :, :, :, :, 3 * own_width :].reshape(width, 128)
    x_first, p_first, x_core_copy, core_copies = {}, {}, {}, []
    for m in range(micro):
        mixed_first[m].wait_recv()
        branch = jnp.dot(
            mixed[m], out_w[...].reshape(width, width), preferred_element_type=F32
        )
        rows_in = jnp.dot(hot(m, 0), act_all[m], preferred_element_type=F32)
        live = live_slots(m)
        hidden = rows_in + jnp.where(live, branch, 0.0)
        hidden_ref[m] = hidden
        inverse = lax.rsqrt(jnp.mean(hidden * hidden, axis=-1, keepdims=True) + epsilon)
        normed_two = (hidden * inverse * gain_two).astype(BF16)
        logits = jnp.dot(normed_two, router_w, preferred_element_type=F32)
        logit_ref[m] = logits
        chosen = [
            jnp.sum(jnp.where(route_ref[m, :, j : j + 1] == lane, logits, 0.0), axis=1, keepdims=True)
            for j in range(2)
        ]
        top = jnp.maximum(chosen[0], chosen[1])
        raised = [jnp.exp(c - top) for c in chosen]
        total = raised[0] + raised[1]
        gates = [r / total for r in raised]
        for k in range(experts):
            pick = picks(m, k, rank_of[m])
            pick_any = jnp.where(pick[0] | pick[1], 1.0, 0.0).astype(BF16)
            rows = as_rows(pick_any, normed_two)
            weights = jnp.sum(
                jnp.where(pick[0], gates[0], 0.0) + jnp.where(pick[1], gates[1], 0.0),
                axis=0,
                keepdims=True,
            )
            weights = jnp.broadcast_to(weights, (8, 128))
            if k == 0:
                all_x[0, 0, m] = rows
                all_p[0, 0, m] = weights
                x_core_copy[0, m] = send(all_x.at[0, 0, m], all_x.at[1, 0, m], core_peer)
                core_copies.append(send(all_p.at[0, 0, m], all_p.at[1, 0, m], core_peer))
            else:
                sent_x[k - 1, m] = rows
                sent_p[k - 1, m] = weights
                x_first[k, m] = send(sent_x.at[k - 1, m], all_x.at[0, k, m], z_peers[k])
                p_first[k, m] = send(sent_p.at[k - 1, m], all_p.at[0, k, m], z_peers[k])

    for m in range(1, micro):
        send_u(m)
    save(out_w, out_save)
    for copy in from_x:
        copy.wait_recv()
    x_block = flip(dp, 2) * 2 + ctx
    relay_y = send(gate_up.at[x_block], gate_up.at[x_block], y_peer)
    for copy in from_y_core:
        copy.wait_recv()
    y_block = flip(dp, 1) * 2 + 1 - ctx
    relay_x = send(gate_up.at[y_block], gate_up.at[y_block], x_peer)

    down_start()
    pass_u(0)

    def pass_rows(k):
        for m in range(micro):
            x_first[k, m].wait_recv()
            x_core_copy[k, m] = send(all_x.at[0, k, m], all_x.at[1, k, m], core_peer)
            p_first[k, m].wait_recv()
            core_copies.append(send(all_p.at[0, k, m], all_p.at[1, k, m], core_peer))

    def hidden_units(k):
        for m in range(micro):
            x_core_copy[k, m].wait_recv()
        count = 2 * micro * slots
        shape = (2, micro, slots)

        def tile(start, size):
            rows = all_x[:, k].reshape(count, width)
            gate_w = gate_up[:, :, pl.ds(start, size)].reshape(width, size)
            up_w = gate_up[:, :, pl.ds(half + start, size)].reshape(width, size)
            pre = jnp.dot(rows, gate_w, preferred_element_type=F32)
            up_part = jnp.dot(rows, up_w, preferred_element_type=F32)
            value, slope = gelu_parts(pre)
            activated[:, k, :, :, pl.ds(start, size)] = (
                (value * up_part).astype(BF16).reshape(shape + (size,))
            )
            both[:, k, :, :, pl.ds(start, size)] = (
                (up_part * slope).astype(BF16).reshape(shape + (size,))
            )
            both[:, k, :, :, pl.ds(half + start, size)] = value.astype(BF16).reshape(shape + (size,))

        wide = half // 256

        def step(i, carry):
            tile(pl.multiple_of(i * 256, 256), 256)
            return carry

        lax.fori_loop(0, wide, step, 0)
        if half % 256:
            tile(wide * 256, half - wide * 256)
        save(both.at[:, k], both_save.at[:, k])
        save(activated.at[:, k], activated_save.at[:, k])
        save(all_x.at[:, k], x_save.at[:, k])

    for k in (1, 2):
        pass_rows(k)
    for copy in from_core + from_y + from_x_core + [relay_x, relay_y]:
        copy.wait_recv()
    for copy in own_gate:
        copy.wait()
    save(gate_up, gate_save)
    hidden_units(0)
    hidden_units(1)
    away = jnp.logical_not(at_home)
    rx_place = low * 2 + 1 - ctx
    ry_place = (1 - low) * 2 + ctx

    @pl.when(at_home)
    def _():
        down_copy("y", y_peer).wait_recv()
        wires.copy(down.at[rx_place], down.at[rx_place], x_peer, down_wire["rx"]).start()

    @pl.when(away)
    def _():
        down_copy("xc", x_core).wait_recv()
        wires.copy(down.at[ry_place], down.at[ry_place], y_peer, down_wire["ry"]).start()

    pass_rows(3)
    hidden_units(2)

    def output_rows(m):
        for part in range(2):
            for k in range(experts):
                column = jnp.broadcast_to(all_p[part, k, m, 0:1, :], (128, 128)).T[:slots, 0:1]
                all_g[part, k, m] = (column * all_u[part, k, m].astype(F32)).astype(BF16)
        save(all_g.at[:, :, m], g_save.at[:, :, m])

    passed = len(u_core)
    for copy in u_core + core_copies:
        copy.wait_recv()
    output_rows(0)
    hidden_units(3)
    for m in range(1, micro):
        pass_u(m)
    for copy in u_core[passed:]:
        copy.wait_recv()
    save(all_u.at[0], u_save)
    for m in range(1, micro):
        output_rows(m)

    @pl.when(at_home)
    def _():
        for name in ("core", "yc"):
            down_copy(name, core_peer).wait_recv()
        home_down.wait()
        down_copy("rx", x_peer).wait_send()

    @pl.when(away)
    def _():
        for name in ("x", "rx", "ry"):
            down_copy(name, core_peer).wait_recv()
        down_copy("ry", y_peer).wait_send()

    save(down, down_save)
    for name, peer, straight in down_sends:
        pl.when(at_home == straight)(lambda name=name, peer=peer: down_copy(name, peer).wait_send())
    for copy in home_copies:
        copy.wait()
    for copy in drains:
        copy.wait_send()
    spread.drain()
    spread_out.drain()


def front(
    sizes, act, cot, deal, length, route, bucket_lanes, table, weights, extras, w_gate, w_up, w_down
):
    heads, head_size, experts, capacity, slots = sizes
    micro, rows_dev, width = act.shape
    own_width = heads * head_size
    per_row = weights[0].shape[0]
    seq = deal.shape[1]
    half = w_gate.shape[1] // 2
    in_vmem, in_hbm = pl.BlockSpec(memory_space=pltpu.VMEM), pl.BlockSpec(memory_space=pltpu.HBM)
    wide = 3 * own_width + 128
    rows = (2, experts, micro, slots)
    outs = [
        ((micro, rows_dev, width), F32),
        ((micro, rows_dev, 128), F32),
        ((micro, rows_dev, width), BF16),
        ((micro, rows_dev, width), BF16),
        ((micro, seq, 1), jnp.int32),
        ((micro, rows_dev, 2), jnp.int32),
        ((heads, 2 * seq), F32),
    ]
    saved = [
        ((2, 2, 2, 4, per_row, wide), BF16),
        ((2, 2, 2, 4, per_row, width), BF16),
        ((micro, seq, width), BF16),
        ((micro, seq, width), BF16),
        ((micro, seq, 3 * own_width), BF16),
        (rows + (width,), BF16),
        (rows[1:] + (width,), BF16),
        (rows + (width,), BF16),
        ((8,) + (w_gate.shape[0], 2 * half), BF16),
        ((4,) + w_down.shape, BF16),
        (rows + (2 * half,), BF16),
        (rows + (half,), BF16),
    ]
    held = (
        saved[:6]
        + [(rows + (width,), BF16), ((2, experts, micro, 8, 128), F32)]
        + saved[7:]
    )
    return pl.pallas_call(
        functools.partial(front_kernel, sizes),
        out_shape=tuple(jax.ShapeDtypeStruct(*out) for out in outs + saved),
        in_specs=[in_vmem] * 3 + [pl.BlockSpec(memory_space=pltpu.SMEM)] + [in_vmem] * 8 + [in_hbm] * 3,
        out_specs=(in_vmem,) * len(outs) + (in_hbm,) * len(saved),
        scratch_shapes=[pltpu.VMEM(*shape) for shape in held]
        + [
            pltpu.VMEM((micro, seq, width), BF16),
            pltpu.VMEM((seq, own_width), BF16),
            pltpu.VMEM((micro, rows_dev, own_width), BF16),
            pltpu.VMEM((experts - 1, micro, slots, width), BF16),
            pltpu.VMEM((experts - 1, micro, slots, width), BF16),
            pltpu.VMEM((experts - 1, micro, 8, 128), F32),
            pltpu.VMEM((table.shape[1], 2 * seq), F32),
            pltpu.SemaphoreType.DMA((160,)),
            pltpu.SemaphoreType.DMA((160,)),
            pltpu.SemaphoreType.DMA((32,)),
        ],
        compiler_params=pltpu.CompilerParams(
            collective_id=1, has_side_effects=True, vmem_limit_bytes=60 * 2**20
        ),
    )(
        act, cot, deal, length, route, bucket_lanes, table, *weights, extras, w_gate, w_up, w_down
    )


class Plan:
    def __init__(self, deal_ref, length_ref, route_ref, rows_dev, capacity):
        self.deal, self.length, self.route = deal_ref, length_ref, route_ref
        self.rows, self.capacity = rows_dev, capacity
        self.ctx, exp = lax.axis_index("context"), lax.axis_index("experts")
        self.z_index = [exp, flip(exp, 1), flip(exp, 2), 3 - exp]
        self.lane = lax.broadcasted_iota(jnp.int32, (rows_dev, 128), 1)
        self.lane_f = self.lane.astype(F32)

    def at(self, k):
        index = self.ctx if k == 0 else 1 - self.ctx
        return pl.ds(pl.multiple_of(index * self.rows, self.rows), self.rows)

    def hot(self, m, k):
        seq = self.deal.shape[1]
        lane = lax.broadcasted_iota(jnp.int32, (self.rows, seq), 1)
        return (self.deal[m, self.at(k), :] == lane).astype(BF16)

    def hot_mine(self, m, k):
        lane = lax.broadcasted_iota(jnp.int32, (self.rows, self.rows), 1) + self.ctx * self.rows
        return (self.deal[m, self.at(k), :] == lane).astype(BF16)

    def live(self, m):
        return self.deal[m, self.at(0), :] < self.length[m]

    def named(self, m, j):
        return self.route[m, :, j : j + 1]

    def ranks(self, m):
        row_id = lax.broadcasted_iota(jnp.int32, (self.rows, self.rows), 0)
        col_id = lax.broadcasted_iota(jnp.int32, (self.rows, self.rows), 1)
        before = (row_id > col_id).astype(BF16)
        live = self.live(m)
        hots = [self.named(m, j) == self.lane for j in range(2)]
        used = jnp.where((hots[0] | hots[1]) & live, 1.0, 0.0).astype(BF16)
        earlier = jnp.dot(before, used, preferred_element_type=F32)
        found = []
        for j in range(2):
            rank = jnp.sum(jnp.where(hots[j], earlier, 0.0), axis=1, keepdims=True)
            found.append(jnp.where(live & (rank < self.capacity), rank, -1.0))
        return found

    def picks(self, m, k, rank):
        return [
            (self.named(m, j) == self.z_index[k]) & (rank[j] == self.lane_f) for j in range(2)
        ]

    def places(self, m, rank, experts, slots):
        lane = lax.broadcasted_iota(jnp.int32, (self.rows, experts * slots), 1).astype(F32)
        picks = []
        for j in range(2):
            place = rank[j]
            for k in range(1, experts):
                place = place + jnp.where(self.named(m, j) == self.z_index[k], 1.0 * k * slots, 0.0)
            place = jnp.where(rank[j] < 0, -1.0, place)
            picks.append(jnp.where(place == lane, 1.0, 0.0).astype(BF16))
        return picks

    def gates(self, m, logits):
        chosen = [
            jnp.sum(jnp.where(self.named(m, j) == self.lane, logits, 0.0), axis=1, keepdims=True)
            for j in range(2)
        ]
        top = jnp.maximum(chosen[0], chosen[1])
        raised = [jnp.exp(c - top) for c in chosen]
        total = raised[0] + raised[1]
        return [r / total for r in raised]


def dot_rows(left, right):
    return lax.dot_general(left, right, (((0,), (0,)), ((), ())), preferred_element_type=F32)


def dot_lanes(left, right):
    return lax.dot_general(left, right, (((1,), (1,)), ((), ())), preferred_element_type=F32)


STAGES = {"x": 0, "zl": 3, "zh": 2, "y": 1}


class Reduce:
    def __init__(self, wires, source, columns, order, bufs, peers, indices, finish):
        self.wires, self.source, self.columns = wires, source, columns
        self.order, self.bufs, self.peers, self.indices = order, bufs, peers, indices
        self.finish = finish
        self.flying, self.step = [], 0

    def launch(self, source, place, name):
        copy = self.wires.copy(source, place, self.peers[name], self.wires.take())
        copy.start()
        self.flying.append(copy)

    def begin(self):
        low = self.indices["core"]
        self.launch(self.source.at[:, 1 - low, :, self.columns], self.bufs[0], "core")

    def advance(self):
        if self.step > len(self.order):
            return False
        low = self.indices["core"]
        self.flying[-1].wait_recv()
        if self.step == 0:
            total = self.source[:, low, :, self.columns].astype(F32) + self.bufs[0][...].astype(F32)
            self.bufs[1][...] = total.astype(BF16).reshape(self.bufs[1].shape)
        else:
            kept = self.bufs[2 * self.step - 1]
            arrived = self.bufs[2 * self.step][...].astype(F32)
            mine = kept[self.cut(self.order[self.step - 1], True)].astype(F32)
            if self.step == len(self.order):
                self.finish(mine, arrived)
                self.step += 1
                return False
            self.bufs[2 * self.step + 1][...] = (mine + arrived).astype(BF16)
        name = self.order[self.step]
        kept = self.bufs[2 * self.step + 1]
        self.launch(kept.at[self.cut(name, False)], self.bufs[2 * self.step + 2], name)
        self.step += 1
        return True

    def cut(self, name, own):
        gone = set(self.order[: self.order.index(name)])
        axis = sum(1 for n, place in STAGES.items() if place < STAGES[name] and n not in gone)
        index = self.indices[name] if own else 1 - self.indices[name]
        return (slice(None),) * axis + (index,)


def reduce_buffers(order, rows, per_row, size):
    left = {"x", "zl", "zh", "y"}
    shapes = [(2, rows // 4, size)]
    for name in order:
        shapes.append((2,) * len(left) + (per_row, size))
        left.discard(name)
        shapes.append((2,) * len(left) + (per_row, size))
    return [pltpu.VMEM(shape, BF16) for shape in shapes]


X_FIRST, Z_FIRST = ("x", "zl", "zh", "y"), ("zl", "zh", "x", "y")
ORDERS = [X_FIRST, Z_FIRST, X_FIRST] * 2 + [Z_FIRST] * 2 + [X_FIRST]


def back_kernel(
    sizes,
    hidden_ref,
    logit_ref,
    mixed,
    cot_rows_ref,
    act_ref,
    deal_ref,
    route_ref,
    line_ref,
    length_ref,
    dense_in,
    out_in,
    act_in,
    normed_in,
    qkv_in,
    x_in,
    u_in,
    g_in,
    gate_w_in,
    down_w_in,
    both_in,
    activated_in,
    output_ref,
    grad_input_ref,
    query_out,
    key_out,
    value_out,
    out_out,
    small_out,
    diag_out,
    gate_in,
    down_in,
    gate_w,
    down_w,
    down_got,
    relay_got,
    back_got,
    out_got,
    sent_back,
    sent_out,
    sent_gate,
    ret_back,
    ret_out,
    ret_gate,
    final_all,
    hidden_all,
    mixed_got,
    grad_sent,
    first_sent,
    first_got,
    diag_buf,
    *rest,
):
    heads, head_size, experts, capacity, slots = sizes
    chunk_bufs, (sends, receives, homes) = rest[:-3], rest[-3:]
    micro, rows_dev, width = hidden_ref.shape
    seq = deal_ref.shape[1]
    own_width = heads * head_size
    dp, ctx, exp = (lax.axis_index(name) for name in ALL)
    high, low = dp // 2, dp % 2
    other_core, other_x, both_dp = flip(dp, 1), flip(dp, 2), flip(flip(dp, 1), 2)
    core_peer, x_peer, x_core = (other_core, ctx, exp), (other_x, ctx, exp), (both_dp, ctx, exp)
    y_peer, y_core = (dp, 1 - ctx, exp), (other_core, 1 - ctx, exp)
    z_peers = [None] + [(dp, ctx, flip(exp, 1)), (dp, ctx, flip(exp, 2)), (dp, ctx, 3 - exp)]
    greet([core_peer, x_peer, x_core, y_peer, y_core] + z_peers[1:])
    wires = Wires(sends, receives, homes)
    drains = []

    class Sent:
        def __init__(self, like, source, place, peer):
            self.like, self.peer, self.index = like, peer, wires.take()
            wires.copy(source, place, peer, self.index).start()
            drains.append(self)

        def again(self):
            part = self.like()
            return wires.copy(part, part, self.peer, self.index)

        def wait_recv(self):
            self.again().wait_recv()

        def wait_send(self):
            self.again().wait_send()

    def send(source, place, peer, like=None):
        return Sent(like or (lambda: source), source, place, peer)

    def like_rows():
        return ret_back.at[0, 0]

    def like_gate():
        return ret_gate.at[0, 0]

    def like_block():
        return gate_w.at[0]

    plan = Plan(deal_ref, length_ref, route_ref, rows_dev, capacity)
    mine = pl.ds(pl.multiple_of(ctx * own_width, own_width), own_width)
    other = pl.ds(pl.multiple_of((1 - ctx) * own_width, own_width), own_width)

    def load(source, place):
        copy = wires.home(source, place)
        copy.start()
        return copy

    block = dp * 2 + ctx
    at_home = low == high
    away = jnp.logical_not(at_home)
    down_wire = [wires.take() for _ in range(8)]
    down_sends = [
        (None, False, low * 2 + ctx, 0),
        (core_peer, False, (1 - low) * 2 + ctx, 0),
        (y_peer, False, low * 2 + 1 - ctx, 1),
        (y_core, False, (1 - low) * 2 + 1 - ctx, 1),
        (x_peer, True, low * 2 + ctx, 2),
        (x_core, True, (1 - low) * 2 + ctx, 2),
        (x_peer, True, low * 2 + 1 - ctx, None),
        (x_peer, True, (1 - low) * 2 + 1 - ctx, None),
    ]

    def down_copy(i):
        peer, _, place, slot = down_sends[i]
        target = down_got.at[i - 6] if slot is None else down_in.at[slot]
        return wires.copy(down_w.at[place], target, peer or core_peer, down_wire[i])

    def down_sums():
        @pl.when(at_home)
        def _():
            for i in range(2):
                down_copy(6 + i).wait_recv()
                place = down_sends[2 + i][2]
                down_w[place] = (
                    down_w[place].astype(F32) + down_got[i].astype(F32)
                ).astype(BF16)
                down_copy(2 + i).start()

    home_wire = wires.used_home
    wires.used_home += 2

    def home_block():
        return pltpu.make_async_copy(gate_w.at[block], gate_in.at[0], homes.at[home_wire])

    def home_down():
        return pltpu.make_async_copy(
            down_w.at[low * 2 + ctx], down_in.at[0], homes.at[home_wire + 1]
        )

    bulk, relayed = [], []
    far_places = (other_x * 2 + 1 - ctx, both_dp * 2 + 1 - ctx)
    y_places = (dp * 2 + 1 - ctx, other_core * 2 + 1 - ctx)
    x_places = (other_x * 2 + ctx, both_dp * 2 + ctx)

    def bulk_send(place, slot, peer):
        bulk.append(send(gate_w.at[place], gate_in.at[slot], peer, like_block))

    def relay_sums():
        for i, (place, slot, peer) in enumerate(
            ((y_places[0], 4, y_peer), (x_places[1], 3, x_core))
        ):
            relayed[i].wait_recv()
            gate_w[place] = (gate_w[place].astype(F32) + relay_got[i].astype(F32)).astype(BF16)
            bulk_send(place, slot, peer)

    def start_down(which):
        for i in which:
            peer, is_away, _, _ = down_sends[i]
            pl.when(away if is_away else at_home)(
                lambda i=i, peer=peer: (home_down() if peer is None else down_copy(i)).start()
            )

    ret_first = {}
    both_rows = experts * slots

    def expert_phase(both, rows_x, rows_g, activated, rows_u, back_part):
        half = activated.shape[-1]
        first = [load(g_in, rows_g), load(down_w_in, down_w)]
        second = [load(both_in.at[:, :, m], both.at[:, :, m]) for m in range(micro)]
        second.append(load(gate_w_in, gate_w))
        third = [load(activated_in, activated), load(x_in, rows_x), load(u_in, rows_u)]
        for copy in first:
            copy.wait()
        shape = (2, experts, slots)
        count = 2 * experts * slots

        def act_tile(m, start, size):
            rows = rows_g[:, :, m].reshape(count, width)
            weight = down_w[...].reshape(half, width) if size == half else down_flat(start, size)
            grad = dot_lanes(rows, weight)
            for shift in (0, half):
                cols = pl.ds(shift + start, size)
                kept = both[:, :, m, :, cols].reshape(count, size).astype(F32)
                both[:, :, m, :, cols] = (grad * kept).astype(BF16).reshape(shape + (size,))

        def down_flat(start, size):
            per = down_w.shape[1]
            parts = []
            while size:
                index, offset = start // per, start % per
                taken = min(size, per - offset)
                parts.append(down_w[index, offset : offset + taken, :])
                start, size = start + taken, size - taken
            return parts[0] if len(parts) == 1 else jnp.concatenate(parts, axis=0)

        def back_rows(m):
            def step(i, carry):
                rows = both[:, :, m].reshape(count, 2 * half)
                weight = gate_w[pl.ds(i * 2, 2)].reshape(256, 2 * half)
                part = dot_lanes(rows, weight).astype(BF16)
                cols = pl.ds(pl.multiple_of(i * 256, 256), 256)
                back_part[:, :, m, :, cols] = part.reshape(shape + (256,))
                return carry

            lax.fori_loop(0, width // 256, step, 0)

        back_core = []
        for m in range(micro):
            second[m].wait()
            for start in range(0, half, 256):
                act_tile(m, start, min(256, half - start))
            if m == 0:
                second[-1].wait()
            back_rows(m)
            back_core.append(send(back_part.at[1, :, m], back_got.at[m], core_peer))

        def give_back(m):
            back_core[m].wait_recv()
            for k in range(experts):
                rows = (
                    back_part[0, k, m].astype(F32) + back_got[m, k].astype(F32)
                ).astype(BF16)
                if k == 0:
                    ret_back[m, 0] = rows
                else:
                    sent_back[m, k - 1] = rows
                    ret_first["back", m, k] = send(
                        sent_back.at[m, k - 1], ret_back.at[m, k], z_peers[k], like_rows
                    )

        for copy in third:
            copy.wait()
        depth = width // gate_w.shape[0]

        def gate_grad(place):
            cols = pl.ds(pl.multiple_of(place * depth, depth), depth)
            total = jnp.zeros((depth, 2 * half), F32)
            rows = rows_x[:, :, :, :, cols].reshape(micro * count, depth)
            total = dot_rows(rows, both[...].reshape(micro * count, 2 * half))
            gate_w[place] = total.astype(BF16)

        for i, (place, peer) in enumerate(zip(far_places, (x_peer, y_peer))):
            gate_grad(place)
            relayed.append(send(gate_w.at[place], relay_got.at[i], peer, like_block))
        give_back(0)
        for place, slot, peer in (
            (x_places[0], 2, x_peer),
            (y_places[1], 5, y_core),
            (other_core * 2 + ctx, 1, core_peer),
        ):
            gate_grad(place)
            bulk_send(place, slot, peer)
        give_back(1)
        gate_grad(y_places[0])
        gate_grad(x_places[1])
        gate_grad(block)
        home_block().start()

        out_part = back_part
        for copy in back_core:
            copy.wait_send()
        out_core = []
        for m in range(micro):

            def step(i, carry):
                cols = pl.ds(pl.multiple_of(i * 256, 256), 256)
                rows = activated[:, :, m].reshape(count, half)
                weight = down_w[:, :, cols].reshape(half, 256)
                part = jnp.dot(rows, weight, preferred_element_type=F32).astype(BF16)
                out_part[:, :, m, :, cols] = part.reshape(shape + (256,))
                return carry

            lax.fori_loop(0, width // 256, step, 0)
            out_core.append(send(out_part.at[1, :, m], out_got.at[m], core_peer))

        ones = jnp.ones((8, width), F32)
        for m in range(micro):
            out_core[m].wait_recv()
            for k in range(experts):
                rows = (
                    out_part[0, k, m].astype(F32) + out_got[m, k].astype(F32)
                ).astype(BF16)
                worth = lax.dot_general(
                    ones,
                    rows.astype(F32) * rows_u[k, m].astype(F32),
                    (((1,), (1,)), ((), ())),
                    precision=lax.Precision.HIGHEST,
                    preferred_element_type=F32,
                )
                if k == 0:
                    ret_out[m, 0] = rows
                    ret_gate[m, 0, :, :slots] = worth
                else:
                    sent_out[m, k - 1] = rows
                    sent_gate[m, k - 1, :, :slots] = worth
                    ret_first["gate", m, k] = send(
                        sent_gate.at[m, k - 1], ret_gate.at[m, k], z_peers[k], like_gate
                    )

        totals = {}
        per = down_w.shape[1]
        for start in range(0, half, 128):
            rows = activated[:, :, :, :, start : start + 128].reshape(micro * count, 128)
            total = dot_rows(rows, rows_g[...].reshape(micro * count, width)).astype(BF16)
            done = 0
            while done < 128:
                index, offset = (start + done) // per, (start + done) % per
                taken = min(128 - done, per - offset)
                down_w[index, offset : offset + taken, :] = total[done : done + taken]
                done += taken
        start_down((0, 1, 6, 7, 4, 5))
        for m in range(micro):
            for k in range(1, experts):
                ret_first["out", m, k] = send(
                    sent_out.at[m, k - 1], ret_out.at[m, k], z_peers[k], like_rows
                )
        for copy in out_core:
            copy.wait_send()
        gone = {id(copy) for copy in back_core + out_core}
        drains[:] = [copy for copy in drains if id(copy) not in gone]

    def token_phase(
        dense,
        out_w,
        act_all,
        normed_ref,
        qkv_ref,
        first_own,
        grad_own,
        qkv_grad,
        qkv_total,
        out_low,
        small_f,
        small_low,
        branch_all,
    ):
        loads = [
            load(source, place)
            for source, place in (
                (dense_in, dense),
                (out_in, out_w),
                (qkv_in, qkv_ref),
                (act_in, act_all),
                (normed_in, normed_ref),
            )
        ]
        for copy in loads:
            copy.wait()
        before_tokens = len(drains)
        extras = dense[:, :, :, :, :, 3 * own_width :].reshape(width, 128)
        turned = extras.astype(F32).T
        gain_one, gain_two = turned[experts : experts + 1], turned[experts + 1 : experts + 2]
        lanes = lax.broadcasted_iota(jnp.int32, (width, 128), 1)
        rank_of = [plan.ranks(m) for m in range(micro)]
        gate_of = [plan.gates(m, logit_ref[m]) for m in range(micro)]
        mixed_first, hidden_first = [], []
        second = jnp.zeros((1, width), F32)
        out_matrix = out_w[...].reshape(width, width)
        here = plan.at(0)
        for m in range(micro):
            for k in range(1, experts):
                ret_first["back", m, k].wait_recv()
                ret_first["gate", m, k].wait_recv()
            worths = []
            for j in range(2):
                worth = jnp.zeros((rows_dev, 1), F32)
                for k in range(experts):
                    pick = plan.picks(m, k, rank_of[m])[j]
                    worth = worth + jnp.sum(
                        jnp.where(pick, ret_gate[m, k, 0:1, :], 0.0), axis=1, keepdims=True
                    )
                worths.append(worth)
            gates = gate_of[m]
            mean_worth = gates[0] * worths[0] + gates[1] * worths[1]
            logit_grad = sum(
                jnp.where(plan.named(m, j) == plan.lane, gates[j] * (worths[j] - mean_worth), 0.0)
                for j in range(2)
            ).astype(BF16)
            places = plan.places(m, rank_of[m], experts, slots)
            normed_grad = jnp.dot(
                places[0] + places[1],
                ret_back[m].reshape(experts * slots, width),
                preferred_element_type=F32,
            ) + dot_lanes(logit_grad, extras)
            hidden = hidden_ref[m]
            inverse = lax.rsqrt(jnp.mean(hidden * hidden, axis=-1, keepdims=True) + epsilon)
            scaled = hidden * inverse
            normed_two = (scaled * gain_two).astype(BF16)
            router = dot_rows(normed_two, logit_grad)
            small_f[...] = router if m == 0 else small_f[...] + router
            second = second + jnp.sum(normed_grad * scaled, axis=0, keepdims=True)
            lifted = gain_two * normed_grad
            mean_part = jnp.mean(lifted * hidden, axis=-1, keepdims=True)
            hidden_grad = (
                cot_rows_ref[m].astype(F32)
                + inverse * lifted
                - hidden * (inverse * inverse * inverse) * mean_part
            )
            hidden_all[m, 0] = hidden_grad.astype(BF16)
            branch_grad = jnp.where(plan.live(m), hidden_grad, 0.0).astype(BF16)
            mixed_grad = dot_lanes(branch_grad, out_matrix).astype(BF16)
            grad_sent[m] = mixed_grad
            mixed_first.append(send(grad_sent.at[m, :, other], mixed_got.at[m], y_peer))
            branch_all[m] = branch_grad
        for m in range(micro):
            hidden_first.append(send(hidden_all.at[m, 0], hidden_all.at[m, 1], y_peer))

        out_low[...] = (
            dot_rows(
                mixed[...].reshape(micro * rows_dev, width),
                branch_all[...].reshape(micro * rows_dev, width),
            )
            .astype(BF16)
            .reshape(out_low.shape)
        )

        relay_sums()
        indices = {"core": low, "x": high, "y": ctx, "zl": exp % 2, "zh": exp // 2}
        peers = {"core": core_peer, "x": x_peer, "y": y_peer, "zl": z_peers[1], "zh": z_peers[2]}

        def finish_qkv(place, start):
            def store(kept, arrived):
                size = own_width // 2
                for index, value in ((ctx, kept), (1 - ctx, arrived)):
                    first = pl.multiple_of(index * own_width + start, size)
                    place[:, pl.ds(first, size)] = value

            return store

        def finish_out(start):
            def store(kept, arrived):
                out_out[:, start : start + own_width] = kept + arrived

            return store

        def finish_small(kept, arrived):
            small_out[...] = kept + arrived

        chunks = []
        at = 0
        for i, order in enumerate(ORDERS):
            bufs = chunk_bufs[at : at + 9]
            at += 9
            if i < 6:
                shift = (i // 3) * (own_width // 2)
                source, start = qkv_total, (i % 3) * own_width + shift
                finish = finish_qkv((query_out, key_out, value_out)[i % 3], shift)
            elif i < 8:
                source, start = out_low, (i - 6) * own_width
                finish = finish_out(start)
            else:
                source, start, finish = small_low, 0, finish_small
            size = bufs[0].shape[-1]
            chunks.append(
                Reduce(wires, source, slice(start, start + size), order, bufs, peers, indices, finish)
            )
        chunks[6].begin()
        chunks[7].begin()

        def advance(*which):
            for i in which:
                chunks[i].advance()

        scale = head_size ** (-0.5)

        def head_back(m, head):
            cols = [
                slice(part * own_width + head * head_size, part * own_width + (head + 1) * head_size)
                for part in range(3)
            ]
            query, key, value = (qkv_ref[m, :, part] for part in cols)
            grad = grad_own[m, :, cols[0]]
            scores = masked_scores(
                query, key, line_ref[head : head + 1, :], length_ref[m], scale
            )
            probs = soft(scores)
            prob_grad = dot_lanes(grad, value)
            delta = jnp.sum(probs * prob_grad, axis=-1, keepdims=True)
            score_grad = (probs * (prob_grad - delta)).astype(BF16)
            diagonal = diagonal_sums(score_grad.astype(F32))
            if m:
                diagonal = diagonal + diag_buf[0, head : head + 1, :]
            diag_buf[0, head : head + 1, :] = diagonal
            qkv_grad[m, :, cols[0]] = (
                jnp.dot(score_grad, key, preferred_element_type=F32) * scale
            ).astype(BF16)
            qkv_grad[m, :, cols[1]] = (dot_rows(score_grad, query) * scale).astype(BF16)
            qkv_grad[m, :, cols[2]] = dot_rows(probs.astype(BF16), grad).astype(BF16)

        for group in range(2):
            for m in range(micro):
                if group == 0:
                    mixed_first[m].wait_recv()
                    grad_own[m] = (
                        dot_rows(plan.hot(m, 0), grad_sent[m, :, mine])
                        + dot_rows(plan.hot(m, 1), mixed_got[m])
                    ).astype(BF16)
                for head in range(group * heads // 2, (group + 1) * heads // 2):
                    head_back(m, head)
                advance(6, 7)
                if group == 1:
                    advance(0, 1, 2)
            for i in range(3):
                start = i * own_width + group * (own_width // 2)
                cols = slice(start, start + own_width // 2)
                total = dot_rows(
                    normed_ref[...].reshape(micro * seq, width),
                    qkv_grad[:, :, cols].reshape(micro * seq, own_width // 2),
                )
                qkv_total[:, :, :, cols] = total.astype(BF16).reshape(
                    2, 2, width // 4, own_width // 2
                )
                chunks[3 * group + i].begin()
            if group == 0:
                down_sums()

        diag_peers = [core_peer, x_peer, z_peers[1], z_peers[2], y_peer]
        diag_copies = []

        def diag_step(stage):
            if stage:
                diag_copies[stage - 1].wait_recv()
            if 0 < stage < 5:
                diag_buf[2 * stage] = diag_buf[2 * stage - 2] + diag_buf[2 * stage - 1]
            if stage < 5:
                diag_copies.append(
                    send(diag_buf.at[2 * stage], diag_buf.at[2 * stage + 1], diag_peers[stage])
                )

        diag_step(0)
        first_total = jnp.zeros((1, width), F32)
        first_first = []
        for m in range(micro):
            part = jnp.zeros((seq, width), F32)
            for i in range(3):
                cols = slice(i * own_width, (i + 1) * own_width)
                part = part + dot_lanes(
                    qkv_grad[m, :, cols], dense[:, :, :, :, :, cols].reshape(width, own_width)
                )
            rows = act_all[m].astype(F32)
            inverse = lax.rsqrt(jnp.mean(rows * rows, axis=-1, keepdims=True) + epsilon)
            first_total = first_total + jnp.sum(part * rows * inverse, axis=0, keepdims=True)
            first_own[...] = part
            first_sent[m] = first_own[plan.at(1), :].astype(BF16)
            first_got[m, 0] = first_own[here, :].astype(BF16)
            first_first.append(send(first_sent.at[m], first_got.at[m, 1], y_peer))
            advance(3, 4, 5)
            diag_step(1 + m)
            advance(0, 1, 2)
        columns = jnp.where(
            lanes == experts,
            jnp.broadcast_to(second, (128, width)).T,
            jnp.where(
                lanes == experts + 1, jnp.broadcast_to(first_total, (128, width)).T, small_f[...]
            ),
        )
        small_low[...] = columns.astype(BF16).reshape(small_low.shape)
        chunks[8].begin()
        advance(3, 4, 5)

        final_first = []
        for m in range(micro):
            for k in range(1, experts):
                ret_first["out", m, k].wait_recv()
            places = plan.places(m, rank_of[m], experts, slots)
            rows = ret_out[m].reshape(experts * slots, width)
            final = hidden_ref[m]
            for j in range(2):
                final = final + gate_of[m][j] * jnp.dot(places[j], rows, preferred_element_type=F32)
            final_all[m, 0] = final.astype(BF16)
            final_first.append(send(final_all.at[m, 0], final_all.at[m, 1], y_peer))
            if m == 0:
                advance(8, 3, 4, 5, 6, 7, 0, 1, 2)
                diag_step(3)
        advance(8)
        diag_step(4)
        advance(3, 4, 5)

        for m in range(micro):
            hidden_first[m].wait_recv()
            first_first[m].wait_recv()
            first = first_got[m, 0].astype(F32) + first_got[m, 1].astype(F32)
            rows = act_ref[m].astype(F32)
            inverse = lax.rsqrt(jnp.mean(rows * rows, axis=-1, keepdims=True) + epsilon)
            lifted = gain_one * first
            mean_part = jnp.mean(lifted * rows, axis=-1, keepdims=True)
            back = inverse * lifted - rows * (inverse * inverse * inverse) * mean_part
            moved = sum(dot_rows(plan.hot_mine(m, k), hidden_all[m, k]) for k in range(2))
            grad_input_ref[m] = (moved + back).astype(BF16)
            if m == 0:
                advance(8)
        for m in range(micro):
            final_first[m].wait_recv()
            moved = sum(dot_rows(plan.hot_mine(m, k), final_all[m, k]) for k in range(2))
            output_ref[m] = moved.astype(BF16)
        busy = True
        while busy:
            busy = False
            for i in range(len(chunks)):
                if chunks[i].step <= len(chunks[i].order):
                    chunks[i].advance()
                    busy = True
        diag_step(5)
        diag_out[ctx] = diag_buf[8]
        diag_out[1 - ctx] = diag_buf[9]
        for chunk in chunks:
            for copy in chunk.flying:
                copy.wait_send()
        for copy in drains[before_tokens:]:
            copy.wait_send()
        del drains[before_tokens:]

    rows_shape = (2, experts, micro, slots)
    half_ff = both_in.shape[-1] // 2
    pl.run_scoped(
        expert_phase,
        pltpu.VMEM(rows_shape + (2 * half_ff,), BF16),
        pltpu.VMEM(rows_shape + (width,), BF16),
        pltpu.VMEM(rows_shape + (width,), BF16),
        pltpu.VMEM(rows_shape + (half_ff,), BF16),
        pltpu.VMEM(rows_shape[1:] + (width,), BF16),
        pltpu.VMEM(rows_shape + (width,), BF16),
    )
    pl.run_scoped(
        token_phase,
        pltpu.VMEM(dense_in.shape, BF16),
        pltpu.VMEM(out_in.shape, BF16),
        pltpu.VMEM(act_in.shape, BF16),
        pltpu.VMEM(normed_in.shape, BF16),
        pltpu.VMEM(qkv_in.shape, BF16),
        pltpu.VMEM((seq, width), F32),
        pltpu.VMEM((micro, seq, own_width), BF16),
        pltpu.VMEM((micro, seq, 3 * own_width), BF16),
        pltpu.VMEM((2, 2, width // 4, 3 * own_width), BF16),
        pltpu.VMEM((2, 2, width // 4, width), BF16),
        pltpu.VMEM((width, 128), F32),
        pltpu.VMEM((2, 2, width // 4, 128), BF16),
        pltpu.VMEM((micro, rows_dev, width), BF16),
    )
    for copy in bulk:
        copy.wait_recv()
    for i, (peer, is_away, _, _) in enumerate(down_sends):
        if peer is None:
            pl.when(at_home)(lambda: home_down().wait())
            continue
        pl.when(away if is_away else at_home)(lambda i=i: down_copy(i).wait_send())
    @pl.when(at_home)
    def _():
        for i in (2, 4):
            down_copy(i).wait_recv()

    @pl.when(away)
    def _():
        for i in (1, 3, 5):
            down_copy(i).wait_recv()

    home_block().wait()
    for copy in drains:
        copy.wait_send()


def back(sizes, values, saved):
    heads, head_size, experts, capacity, slots = sizes
    hidden, lines = values[0], values[7]
    dense, gate_w, down_w = saved[0], saved[8], saved[9]
    micro, rows_dev, width = hidden.shape
    own_width = heads * head_size
    per_row = dense.shape[4]
    in_vmem, in_hbm = pl.BlockSpec(memory_space=pltpu.VMEM), pl.BlockSpec(memory_space=pltpu.HBM)
    smem = pl.BlockSpec(memory_space=pltpu.SMEM)
    outs = (
        [((micro, rows_dev, width), BF16)] * 2
        + [((per_row, width), F32)] * 4
        + [((per_row, 128), F32), ((2,) + lines.shape, F32)]
        + [((6,) + gate_w.shape[1:], BF16), ((3,) + down_w.shape[1:], BF16)]
    )
    rows = (micro, experts, slots, width)
    sent = (micro, experts - 1, slots, width)
    scratch = [
        pltpu.VMEM(gate_w.shape, BF16),
        pltpu.VMEM(down_w.shape, BF16),
        pltpu.VMEM((2,) + down_w.shape[1:], BF16),
        pltpu.VMEM((2,) + gate_w.shape[1:], BF16),
        pltpu.VMEM(rows, BF16),
        pltpu.VMEM(rows, BF16),
        pltpu.VMEM(sent, BF16),
        pltpu.VMEM(sent, BF16),
        pltpu.VMEM((micro, experts - 1, 8, 128), F32),
        pltpu.VMEM(rows, BF16),
        pltpu.VMEM(rows, BF16),
        pltpu.VMEM((micro, experts, 8, 128), F32),
        pltpu.VMEM((micro, 2, rows_dev, width), BF16),
        pltpu.VMEM((micro, 2, rows_dev, width), BF16),
        pltpu.VMEM((micro, rows_dev, own_width), BF16),
        pltpu.VMEM((micro, rows_dev, width), BF16),
        pltpu.VMEM((micro, rows_dev, width), BF16),
        pltpu.VMEM((micro, 2, rows_dev, width), BF16),
        pltpu.VMEM((10,) + lines.shape, F32),
    ]
    chunk_sizes = [own_width // 2] * 6 + [own_width] * 2 + [128]
    for order, size in zip(ORDERS, chunk_sizes):
        scratch += reduce_buffers(order, width, per_row, size)
    scratch += [
        pltpu.SemaphoreType.DMA((192,)),
        pltpu.SemaphoreType.DMA((192,)),
        pltpu.SemaphoreType.DMA((24,)),
    ]
    return pl.pallas_call(
        functools.partial(back_kernel, sizes),
        out_shape=tuple(jax.ShapeDtypeStruct(*out) for out in outs),
        in_specs=[in_vmem] * 8 + [smem] + [in_hbm] * len(saved),
        out_specs=(in_vmem,) * 8 + (in_hbm,) * 2,
        scratch_shapes=scratch,
        compiler_params=pltpu.CompilerParams(
            collective_id=2, has_side_effects=True, vmem_limit_bytes=61 * 2**20
        ),
    )(*values, *saved)


def finish_kernel(
    experts,
    gate_in,
    down_in,
    output_in,
    grad_in,
    query_in,
    key_in,
    value_in,
    out_in,
    small_in,
    diag_in,
    lane_ref,
    gate_out,
    up_out,
    down_out,
    output_out,
    grad_out,
    query_out,
    key_out,
    value_out,
    out_out,
    router_out,
    first_out,
    second_out,
    table_out,
):
    low = lax.axis_index("dp") % 2
    half = gate_out.shape[1] // 2
    own = pl.ds(pl.multiple_of(low * half, half), half)
    other = pl.ds(pl.multiple_of((1 - low) * half, half), half)
    for cols, slots in ((own, (0, 2, 4)), (other, (1, 3, 5))):
        gate_out[:, cols] = sum(gate_in[j, :, :half].astype(F32) for j in slots)
        up_out[:, cols] = sum(gate_in[j, :, half:].astype(F32) for j in slots)
    down_out[...] = sum(down_in[j].astype(F32) for j in range(down_in.shape[0]))

    @pl.when(pl.program_id(0) == 0)
    def _():
        for source, place in (
            (output_in, output_out),
            (grad_in, grad_out),
            (query_in, query_out),
            (key_in, key_out),
            (value_in, value_out),
            (out_in, out_out),
        ):
            place[...] = source[...]
        small = small_in[...]
        router_out[...] = small[:, :experts]
        turned = jnp.concatenate([small] * (128 // small.shape[0]), axis=0).T
        second_out[...] = turned[experts : experts + 1, : small.shape[0]]
        first_out[...] = turned[experts + 1 : experts + 2, : small.shape[0]]
        buckets, lanes = table_out.shape[0], lane_ref.shape[1]
        rows = lax.broadcasted_iota(jnp.int32, (buckets, lanes), 0)
        hot = jnp.where(rows == lane_ref[...], 1.0, 0.0)
        heads = diag_in.shape[0] * diag_in.shape[1]
        table_out[...] = lax.dot_general(
            hot,
            diag_in[...].reshape(heads, lanes),
            (((1,), (1,)), ((), ())),
            precision=lax.Precision.HIGHEST,
            preferred_element_type=F32,
        )


def finish(values, bucket_lanes, experts, table_shape):
    gate_in, down_in, output, grad_input, query, key, value, out, small, diag = values
    steps = 2
    rows, ff = gate_in.shape[1:]
    per_row = small.shape[0]
    fixed = lambda v: pl.BlockSpec(v.shape, lambda i: (0,) * len(v.shape))
    cut = lambda v: pl.BlockSpec(
        (v.shape[0], v.shape[1] // steps, v.shape[2]), lambda i: (0, i, 0)
    )
    outs = [
        jax.ShapeDtypeStruct((rows, ff), F32),
        jax.ShapeDtypeStruct((rows, ff), F32),
        jax.ShapeDtypeStruct(down_in.shape[1:], F32),
    ] + [jax.ShapeDtypeStruct(v.shape, v.dtype) for v in (output, grad_input, query, key, value, out)]
    small_outs = [
        jax.ShapeDtypeStruct((per_row, experts), F32),
        jax.ShapeDtypeStruct((1, per_row), F32),
        jax.ShapeDtypeStruct((1, per_row), F32),
        jax.ShapeDtypeStruct(table_shape, F32),
    ]
    sliced = lambda v: pl.BlockSpec((v.shape[0] // steps, v.shape[1]), lambda i: (i, 0))
    return pl.pallas_call(
        functools.partial(finish_kernel, experts),
        grid=(steps,),
        out_shape=tuple(outs + small_outs),
        in_specs=[cut(gate_in), cut(down_in)] + [fixed(v) for v in values[2:]] + [fixed(bucket_lanes)],
        out_specs=tuple([sliced(v) for v in outs[:3]] + [fixed(v) for v in outs[3:] + small_outs]),
        compiler_params=pltpu.CompilerParams(vmem_limit_bytes=60 * 2**20),
    )(*values, bucket_lanes)


def tuned_body(
    activations,
    cotangent,
    dealing,
    lengths,
    routes,
    buckets,
    w_query,
    w_key,
    w_value,
    w_out,
    w_router,
    norm_first,
    norm_second,
    bias_table,
    w_gate,
    w_up,
    w_down,
):
    micro, _, rows_dev, width = activations.shape
    seq = dealing.shape[2]
    bucket_count, head_count = bias_table.shape
    dp_count, ctx_count, expert_count = (lax.axis_size(name) for name in ALL)
    dp_index, ctx_index, expert_index = (lax.axis_index(name) for name in ALL)
    high, low = dp_index // 2, dp_index % 2
    heads = head_count // ctx_count
    head_size = width // head_count
    own_width = heads * head_size
    experts = w_router.shape[1]
    top_count = routes.shape[3]
    capacity = (5 * rows_dev * top_count + 4 * experts - 1) // (4 * experts)
    slots = -(-capacity // 16) * 16
    half_ff = w_gate.shape[2] // 2
    down_rows = w_down.shape[1]
    plane = dp_count * ctx_count
    plane_index = dp_index * ctx_count + ctx_index
    act = activations[:, 0]
    cot = cotangent[:, 0]
    deal = dealing[:, 0]
    length = lengths[:, 0]
    route = routes[:, 0]
    sizes = (heads, head_size, experts, capacity, slots)
    extras = jnp.concatenate([w_router, norm_first[:, None], norm_second[:, None]], axis=1)
    extras = jnp.pad(extras, ((0, 0), (0, 128 - extras.shape[1])))
    bucket_lanes = jnp.concatenate(
        [buckets[:1], jnp.full((seq,), -1, jnp.int32), buckets[:0:-1]]
    )[None, :]
    hidden, logits, mixed, cot_low, deal_column, route_column, lines, *saved = front(
        sizes,
        act,
        cot,
        deal,
        length,
        jnp.swapaxes(route, 1, 2),
        bucket_lanes,
        bias_table,
        (w_query, w_key, w_value, w_out),
        extras,
        w_gate[0],
        w_up[0],
        w_down[0],
    )
    (
        output,
        grad_input,
        grad_query,
        grad_key,
        grad_value,
        grad_out,
        small_sum,
        diag_all,
        gate_in,
        down_in,
    ) = back(
        sizes,
        (hidden, logits, mixed, cot_low, act, deal_column, route_column, lines, length),
        saved,
    )
    (
        grad_gate,
        grad_up,
        grad_down,
        output,
        grad_input,
        grad_query,
        grad_key,
        grad_value,
        grad_out,
        grad_router,
        grad_first,
        grad_second,
        grad_table,
    ) = finish(
        (
            gate_in,
            down_in,
            output,
            grad_input,
            grad_query,
            grad_key,
            grad_value,
            grad_out,
            small_sum,
            diag_all,
        ),
        bucket_lanes,
        experts,
        bias_table.shape,
    )
    return (
        output[:, None],
        grad_input[:, None],
        grad_query,
        grad_key,
        grad_value,
        grad_out,
        grad_router,
        grad_first[0],
        grad_second[0],
        grad_table,
        grad_gate[None],
        grad_up[None],
        grad_down[None],
    )


def body(*arguments):
    counts = tuple(lax.axis_size(name) for name in ALL)
    activations, w_query, bias_table, w_gate = (arguments[i] for i in (0, 6, 13, 14))
    own_width = activations.shape[3] // counts[1]
    fits = (
        counts == (4, 2, 4)
        and w_gate.shape[0] == 1
        and w_query.shape[0] % 16 == 0
        and 128 % w_query.shape[0] == 0
        and own_width % 128 == 0
        and bias_table.shape[1] % (8 * counts[1]) == 0
        and arguments[2].shape[2] % 128 == 0
        and arguments[4].shape[3] == 2
    )
    return (tuned_body if fits else plain_body)(*arguments)


def solution(mesh):
    tokens = P(None, ("dp", "experts"), "context", None)
    sequences = P(None, ("dp", "experts"))
    rows = P(("dp", "context", "experts"), None)
    gains = P(("dp", "context", "experts"))
    experts = P("experts", ("dp", "context"), None)
    placed = (
        (tokens, tokens, P(None, ("dp", "experts"), None), sequences, tokens, P())
        + (rows,) * 5
        + (gains, gains, P())
        + (experts,) * 3
    )
    return jax.shard_map(
        body,
        mesh=mesh,
        in_specs=placed,
        out_specs=(tokens, tokens) + (rows,) * 5 + (gains, gains, P()) + (experts,) * 3,
        check_vma=False,
    )
```
